32 devices in a mesh: section: 2 (over x), slab: 4 (over y, core), batch: 4 (over z).
Axes of the slice: x: 2, y: 2, z: 4, core: 2. Of those that a mesh axis runs over, the one named last changes fastest.
Arguments:
- image: float32 [2, 4, 8, 68, 68, 4], P('section', 'batch', 'slab'), may hold values from -6 to 6
- modality_mask: int32 [2, 4, 4], P('section', 'batch'), may hold values 0 or 1
- extents: int32 [2, 4], replicated, may hold values from 2 to 8, as said below
- crop_offsets: int32 [2, 4, 2], P('section', 'batch'), may hold values from 0 to 16
- coarse: float32 [2, 4, 4, 24, 24, 128], P('section', 'batch', 'slab'), may hold values from -6 to 6
- conv_first: float32 [3, 3, 3, 4, 32], replicated, may hold values from -0.625 to 0.625
- gain_first: float32 [32], replicated, may hold values from 0.1 to 1.9
- shift_first: float32 [32], replicated, may hold values from -3 to 3
- conv_second: float32 [3, 3, 3, 32, 64], replicated, may hold values from -0.21875 to 0.21875
- gain_second: float32 [64], replicated, may hold values from 0.1 to 1.9
- shift_second: float32 [64], replicated, may hold values from -3 to 3
- up_kernel: float32 [2, 2, 2, 128, 128], replicated, may hold values from -0.5 to 0.5
- conv_third: float32 [3, 3, 3, 192, 64], replicated, may hold values from -0.078125 to 0.078125
- gain_third: float32 [64], replicated, may hold values from 0.1 to 1.9
- shift_third: float32 [64], replicated, may hold values from -3 to 3
- conv_fourth: float32 [3, 3, 3, 64, 64], replicated, may hold values from -0.15625 to 0.15625
- gain_fourth: float32 [64], replicated, may hold values from 0.1 to 1.9
- shift_fourth: float32 [64], replicated, may hold values from -3 to 3
- pool_grad: float32 [2, 4, 4, 32, 32, 64], P('section', 'batch', 'slab'), may hold values from -6 to 6
- output_grad: float32 [2, 4, 8, 44, 44, 64], P('section', 'batch', 'slab'), may hold values from -6 to 6
Outputs:
- pooled: float32 [2, 4, 4, 32, 32, 64], P('section', 'batch', 'slab')
- decoded: float32 [2, 4, 8, 44, 44, 64], P('section', 'batch', 'slab')
- image_grad: float32 [2, 4, 8, 68, 68, 4], P('section', 'batch', 'slab')
- coarse_grad: float32 [2, 4, 4, 24, 24, 128], P('section', 'batch', 'slab')
- conv_first_grad: float32 [3, 3, 3, 4, 32], replicated
- gain_first_grad: float32 [32], replicated
- shift_first_grad: float32 [32], replicated
- conv_second_grad: float32 [3, 3, 3, 32, 64], replicated
- gain_second_grad: float32 [64], replicated
- shift_second_grad: float32 [64], replicated
- up_kernel_grad: float32 [2, 2, 2, 128, 128], replicated
- conv_third_grad: float32 [3, 3, 3, 192, 64], replicated
- gain_third_grad: float32 [64], replicated
- shift_third_grad: float32 [64], replicated
- conv_fourth_grad: float32 [3, 3, 3, 64, 64], replicated
- gain_fourth_grad: float32 [64], replicated
- shift_fourth_grad: float32 [64], replicated
The draws below stay inside these ranges and needn't reach their ends.
Inputs may be any that keep to these rules, and one draw needn't show every extreme that they name: `extents`: each extent is even, and in each half some volume fills all 8 planes.
All inputs are finite; a program needn't handle non-finite values. No bound on the sum of `modality_mask` on one device may be relied on, other than what follows from the above.
Results may differ from the reference program's by a relative error of at most 0.00029.
Values sent between devices are 32-bit elements; how exact they have to be, the bound alone decides.
A program may use at most 256 MiB of HBM per device.

```python
import jax
import jax.numpy as jnp
from jax import lax

MODS = 4
ENC1 = 32
ENC2 = 64
COARSE_CH = 128
DEC_CH = 64
IN_W = 68
COARSE_W = 24
DEPTH = 8
SKIP = 64
POOL_W = 32
UP_W = 48
OUT_W = 44
N_SECTION = 2
N_BATCH = 4


def draw_extents(key, part):
    key = jax.random.fold_in(key, 7)
    first_key, second_key = jax.random.split(key)
    lengths = 2 * jax.random.randint(first_key, (N_SECTION, N_BATCH), 1, DEPTH // 2 + 1)
    widest = jax.random.randint(second_key, (N_SECTION,), 0, N_BATCH)
    picked = jnp.arange(N_BATCH)[None, :] == widest[:, None]
    return jnp.where(picked, DEPTH, lengths).astype(jnp.int32)


def set_ends(array, stream_key, least, top_value):
    place = [jax.random.randint(jax.random.fold_in(stream_key, axis), (), 0, length) for axis, length in enumerate(array.shape)]
    main_axis = array.shape.index(max(array.shape))
    neighbour = place[:main_axis] + [(place[main_axis] + 1) % array.shape[main_axis]] + place[main_axis + 1:]
    return array.at[tuple(place)].set(least).at[tuple(neighbour)].set(top_value)


def levels(own_key, shape, shards, smallest, top_value):
    level = 1.0
    for axis_at, parts in shards:
        draws = jax.random.uniform(jax.random.fold_in(jax.random.fold_in(own_key, 6), axis_at), (parts,), jnp.float32, smallest / len(shards), top_value / len(shards))
        level = level * jnp.repeat(jnp.exp(draws), shape[axis_at] // parts).reshape((-1,) + (1,) * (len(shape) - 1 - axis_at))
    return level


def gaussian(stream_key, extent, spread, limit, cuts=(), held_as=jnp.bfloat16):
    values = spread * jax.random.normal(stream_key, extent, jnp.float32)
    if cuts:
        values = values * levels(stream_key, extent, cuts, -0.22, 0.18)
    return jnp.clip(values, -limit, limit).astype(held_as)


def setup_inputs(seed: int = 0) -> dict:
    streams_of = jax.random.split(jax.random.key(seed), 21)
    return {
        "image": gaussian(streams_of[0], (N_SECTION, N_BATCH, DEPTH, IN_W, IN_W, MODS), 1.0, 6.0, ((0, 2), (1, 4), (2, 4)), jnp.float32),
        "modality_mask": set_ends((jax.random.randint(streams_of[1], (N_SECTION, N_BATCH, MODS), 0, 4) < 3).astype(jnp.int32), jax.random.fold_in(streams_of[1], 1), 0, 1),
        "extents": draw_extents(jax.random.fold_in(streams_of[20], 71), 0),
        "crop_offsets": set_ends(jax.random.randint(streams_of[3], (N_SECTION, N_BATCH, 2), 0, SKIP - UP_W + 1), jax.random.fold_in(streams_of[3], 1), 0, SKIP - UP_W).astype(jnp.int32),
        "coarse": gaussian(streams_of[4], (N_SECTION, N_BATCH, DEPTH // 2, COARSE_W, COARSE_W, COARSE_CH), 1.0, 6.0, ((0, 2), (1, 4), (2, 4)), jnp.float32),
        "conv_first": gaussian(streams_of[5], (3, 3, 3, MODS, ENC1), (27 * MODS) ** -0.5, 0.625, (), jnp.float32),
        "gain_first": jnp.clip(1.0 + 0.18 * jax.random.normal(streams_of[6], (ENC1,), jnp.float32), 0.1, 1.9),
        "shift_first": gaussian(streams_of[7], (ENC1,), 0.5, 3.0, (), jnp.float32),
        "conv_second": gaussian(streams_of[8], (3, 3, 3, ENC1, ENC2), (27 * ENC1) ** -0.5, 0.21875, (), jnp.float32),
        "gain_second": jnp.clip(1.0 + 0.18 * jax.random.normal(streams_of[9], (ENC2,), jnp.float32), 0.1, 1.9),
        "shift_second": gaussian(streams_of[10], (ENC2,), 0.5, 3.0, (), jnp.float32),
        "up_kernel": gaussian(streams_of[11], (2, 2, 2, COARSE_CH, COARSE_CH), COARSE_CH ** -0.5, 0.5, (), jnp.float32),
        "conv_third": gaussian(streams_of[12], (3, 3, 3, COARSE_CH + ENC2, DEC_CH), (27 * (COARSE_CH + ENC2)) ** -0.5, 0.078125, (), jnp.float32),
        "gain_third": jnp.clip(1.0 + 0.18 * jax.random.normal(streams_of[13], (DEC_CH,), jnp.float32), 0.1, 1.9),
        "shift_third": gaussian(streams_of[14], (DEC_CH,), 0.5, 3.0, (), jnp.float32),
        "conv_fourth": gaussian(streams_of[15], (3, 3, 3, DEC_CH, DEC_CH), (27 * DEC_CH) ** -0.5, 0.15625, (), jnp.float32),
        "gain_fourth": jnp.clip(1.0 + 0.18 * jax.random.normal(streams_of[16], (DEC_CH,), jnp.float32), 0.1, 1.9),
        "shift_fourth": gaussian(streams_of[17], (DEC_CH,), 0.5, 3.0, (), jnp.float32),
        "pool_grad": gaussian(streams_of[18], (N_SECTION, N_BATCH, DEPTH // 2, POOL_W, POOL_W, ENC2), 1.0, 6.0, ((0, 2), (1, 4), (2, 4)), jnp.float32),
        "output_grad": gaussian(streams_of[19], (N_SECTION, N_BATCH, DEPTH, OUT_W, OUT_W, DEC_CH), 1.0, 6.0, ((0, 2), (1, 4), (2, 4)), jnp.float32),
    }


HIGH = lax.Precision.HIGHEST
EPSILON = 1e-05
LAYOUT = ('NDHWC', 'DHWIO', 'NDHWC')

def correlate(volumes, weight):
    padded = jnp.pad(volumes, ((0, 0), (1, 1), (0, 0), (0, 0), (0, 0)))
    return lax.conv_general_dilated(padded, weight, (1, 1, 1), 'VALID', dimension_numbers=LAYOUT, precision=HIGH)

def norm_act(response, plane_mask, gain_values, shift_values):
    widen = plane_mask[:, :, :, None, None, None]
    voxels = lax.optimization_barrier(jnp.sum(plane_mask, axis=(1, 2))) * (response.shape[3] * response.shape[4])
    voxels = voxels[:, None, None, None, None, None]
    average = lax.optimization_barrier(jnp.sum(response * widen, axis=(1, 2, 3, 4), keepdims=True)) / voxels
    squares = lax.optimization_barrier(jnp.sum(response * widen * response, axis=(1, 2, 3, 4), keepdims=True)) / voxels
    inverse = lax.rsqrt(squares - average * average + EPSILON)
    before = gain_values * ((response - average) * inverse) + shift_values
    return jax.nn.silu(before) * widen

def reference(image, modality_mask, extents, crop_offsets, coarse, conv_first, gain_first, shift_first, conv_second, gain_second, shift_second, up_kernel, conv_third, gain_third, shift_third, conv_fourth, gain_fourth, shift_fourth, pool_grad, output_grad):
    halves = image.shape[0]
    volumes = image.shape[1]
    depth_all = image.shape[2]
    width_up = 2 * coarse.shape[3]
    plane_mask = (jnp.arange(depth_all, dtype=jnp.int32)[None, None, :] < extents[:, :, None]).astype(jnp.float32)
    decoder_mask = plane_mask[::-1]
    keep_in = modality_mask.astype(jnp.float32)[:, :, None, None, None, :] * plane_mask[:, :, :, None, None, None]
    coarse_keep = decoder_mask[:, :, ::2, None, None, None]

    def flatten(array_in):
        return array_in.reshape((halves * volumes,) + array_in.shape[2:])

    def unflatten(array_in):
        return array_in.reshape((halves, volumes) + array_in.shape[1:])

    def crop_one(volume, offset):
        anchor = jnp.zeros((), jnp.int32)
        return lax.dynamic_slice(volume, (anchor, offset[0], offset[1], anchor), (depth_all, width_up, width_up, volume.shape[3]))

    def forward(image_in, coarse_in, kernel_first, gain_one, shift_one, kernel_second, gain_two, shift_two, kernel_up, kernel_third, gain_three, shift_three, kernel_fourth, gain_four, shift_four):
        source = image_in * keep_in
        first_act = norm_act(unflatten(correlate(flatten(source), kernel_first)), plane_mask, gain_one, shift_one)
        second_act = norm_act(unflatten(correlate(flatten(first_act), kernel_second)), plane_mask, gain_two, shift_two)
        shape_act = second_act.shape
        pooled = lax.optimization_barrier(jnp.mean(second_act.reshape(halves, volumes, depth_all // 2, 2, shape_act[3] // 2, 2, shape_act[4] // 2, 2, shape_act[5]), axis=(3, 5, 7)))
        coarse_masked = coarse_in * coarse_keep
        blocks = jnp.einsum('abdhwc,ijkco->abdihjwko', coarse_masked, kernel_up, precision=HIGH)
        upsampled = blocks.reshape(halves, volumes, depth_all, width_up, width_up, kernel_up.shape[4])
        cropped = unflatten(jax.vmap(crop_one)(flatten(second_act), flatten(crop_offsets)))
        joined = jnp.concatenate([upsampled, cropped[::-1]], axis=5)
        third_act = norm_act(unflatten(correlate(flatten(joined), kernel_third)), decoder_mask, gain_three, shift_three)
        decoded = norm_act(unflatten(correlate(flatten(third_act), kernel_fourth)), decoder_mask, gain_four, shift_four)
        return (pooled, decoded)
    outputs, pullback = jax.vjp(forward, image, coarse, conv_first, gain_first, shift_first, conv_second, gain_second, shift_second, up_kernel, conv_third, gain_third, shift_third, conv_fourth, gain_fourth, shift_fourth)
    grads = pullback((pool_grad, output_grad))
    return (outputs[0], outputs[1], grads[0], grads[1], grads[2], grads[3], grads[4], grads[5], grads[6], grads[7], grads[8], grads[9], grads[10], grads[11], grads[12], grads[13], grads[14])
```

```python
import functools

import jax
import jax.numpy as jnp
from jax import lax
from jax.experimental import pallas as pl
from jax.experimental.pallas import tpu as pltpu
from jax.sharding import PartitionSpec as P

f32 = jnp.float32
bf16 = jnp.bfloat16
MESH = pl.DeviceIdType.MESH
EPSILON = 1e-05
NN = (((1,), (0,)), ((), ()))
NT = (((1,), (1,)), ((), ()))
TN = (((0,), (0,)), ((), ()))
VM = pl.BlockSpec(memory_space=pltpu.VMEM)
SM = pl.BlockSpec(memory_space=pltpu.SMEM)
HB = pl.BlockSpec(memory_space=pl.ANY)
LIMIT = 60 * 2**20

OWN = 1408
CROP = 896


def split(x):
    hi = x.astype(bf16)
    return hi, (x - hi.astype(f32)).astype(bf16)


def dot(a, b, dims):
    return lax.dot_general(a, b, dims, preferred_element_type=f32)


def dot3(ah, al, bh, bl, dims):
    return dot(ah, bh, dims) + dot(al, bh, dims) + dot(ah, bl, dims)


def loop(n, f, unroll=1):
    def step(t, c):
        f(t)
        return c

    lax.fori_loop(0, n, step, 0, unroll=unroll)


def fold(v):
    lanes = v.shape[-1]
    v = jnp.broadcast_to(v, (8, lanes))
    if lanes == 256:
        h = v[:, :128] + v[:, 128:]
        h = h + pltpu.roll(h, 64, 1)
        h = jnp.concatenate([h, h], axis=1)
    else:
        h = v + pltpu.roll(v, 64, 1)
        h = h + pltpu.roll(h, 32, 1)
    return h[:1]


def totals(gath, half, lanes):
    per = gath.shape[0] // 2
    tot = jnp.sum(gath[pl.ds(half * per, per)], axis=0)
    return fold(tot[:, :lanes]), fold(tot[:, 256 : 256 + lanes])


def moments(gath, half, count, lanes):
    s, q = totals(gath, half, lanes)
    avg = s / count
    inv = lax.rsqrt(q / count - avg * avg + EPSILON)
    return avg, inv


def affine(par, layer, avg, inv):
    lanes = avg.shape[-1]
    scale = par[2 * layer : 2 * layer + 1, :lanes] * inv
    return scale, par[2 * layer + 1 : 2 * layer + 2, :lanes] - avg * scale


def silu(b):
    return b / (1.0 + jnp.exp(-b))


def silu_back(a, b):
    s = 1.0 / (1.0 + jnp.exp(-b))
    return a * s * (1.0 + b * (1.0 - s))


def cells(shape, rows, cols, row0):
    y = lax.broadcasted_iota(jnp.int32, shape, 0) + row0
    x = lax.broadcasted_iota(jnp.int32, shape, 1)
    return (y < rows) & (x < cols)


def put_sums(st, s, q):
    lanes = s.shape[-1]
    st[...] = jnp.zeros(st.shape, f32)
    st[:, :lanes] = s
    st[:, 256 : 256 + lanes] = q


def im2col(ah, al, p, f, ny, pitch, lanes, x0=0, y0=0):
    def pair(t):
        for a in range(2):
            for b in range(2):
                x = f[pl.ds(y0 + 2 * t + a, 2), x0 + b : x0 + b + pitch, :]
                hi, lo = split(x.reshape(2 * pitch, lanes))
                rows = pl.ds(pl.multiple_of(t * 2 * pitch, 2 * pitch), 2 * pitch)
                at = (2 * a + b) * lanes
                ah[p, rows, at : at + lanes] = hi
                al[p, rows, at : at + lanes] = lo

    loop(ny // 2, pair)


def call(kernel, outs, args, specs=None, scratch=(), name="k", out_specs=None, cost=None):
    return pl.pallas_call(
        kernel,
        out_shape=[jax.ShapeDtypeStruct(s, d) for s, d in outs],
        in_specs=specs or [VM] * len(args),
        out_specs=out_specs or [VM] * len(outs),
        scratch_shapes=list(scratch),
        compiler_params=pltpu.CompilerParams(vmem_limit_bytes=LIMIT),
        cost_estimate=cost,
        name=name,
    )(*args)


def exchange_kernel(dims, nh, *refs):
    stats = refs[0]
    planes = refs[1 : 1 + nh]
    gath = refs[1 + nh]
    halos = refs[2 + nh : 2 + 3 * nh]
    ssem, rsem = refs[2 + 3 * nh : 4 + 3 * nh]
    S, K, B = dims
    n = S * K * B
    s = lax.axis_index("section")
    k = lax.axis_index("slab")
    b = lax.axis_index("batch")
    me = (s * K + k) * B + b

    def coords(d):
        return (d // (K * B), (d // B) % K, d % B)

    barrier = pltpu.get_barrier_semaphore()

    def greet(p, c):
        pl.semaphore_signal(
            barrier, inc=1, device_id=coords((me + p) % n), device_id_type=MESH
        )
        return c

    lax.fori_loop(1, n, greet, 0)
    gath[me] = stats[...]
    pl.semaphore_wait(barrier, n - 1)

    def desc(p, slot):
        return pltpu.make_async_remote_copy(
            src_ref=stats,
            dst_ref=gath.at[slot],
            send_sem=ssem.at[p],
            recv_sem=rsem.at[p],
            device_id=coords((me + p) % n),
            device_id_type=MESH,
        )

    def halo_copies(j):
        hs, hr = refs[4 + 3 * nh : 6 + 3 * nh]
        last = planes[j].shape[0] - 1
        to_left = pltpu.make_async_remote_copy(
            src_ref=planes[j].at[0],
            dst_ref=halos[2 * j + 1],
            send_sem=hs.at[2 * j],
            recv_sem=hr.at[2 * j],
            device_id=(s, (k + K - 1) % K, b),
            device_id_type=MESH,
        )
        to_right = pltpu.make_async_remote_copy(
            src_ref=planes[j].at[last],
            dst_ref=halos[2 * j],
            send_sem=hs.at[2 * j + 1],
            recv_sem=hr.at[2 * j + 1],
            device_id=(s, (k + 1) % K, b),
            device_id_type=MESH,
        )
        return to_left, to_right

    pairs = [halo_copies(j) for j in range(nh)]
    if nh:

        @pl.when(k > 0)
        def _():
            for left, _ in pairs:
                left.start()

        @pl.when(k < K - 1)
        def _():
            for _, right in pairs:
                right.start()

    def send(p, c):
        desc(p, me).start()
        return c

    def got(p, c):
        desc(p, (me + n - p) % n).wait_recv()
        return c

    def sent(p, c):
        desc(p, me).wait_send()
        return c

    lax.fori_loop(1, n, send, 0)
    lax.fori_loop(1, n, got, 0)
    lax.fori_loop(1, n, sent, 0)
    if nh:

        @pl.when(k > 0)
        def _():
            for left, right in pairs:
                left.wait_send()
                right.wait_recv()

        @pl.when(k < K - 1)
        def _():
            for left, right in pairs:
                right.wait_send()
                left.wait_recv()


def exchange(dims, stats, planes, cid):
    n = dims[0] * dims[1] * dims[2]
    nh = len(planes)
    outs = [jax.ShapeDtypeStruct((n,) + stats.shape, f32)]
    for p in planes:
        outs += [jax.ShapeDtypeStruct(p.shape[1:], f32)] * 2
    scratch = [pltpu.SemaphoreType.DMA((n,))] * 2
    if nh:
        scratch += [pltpu.SemaphoreType.DMA((2 * nh,))] * 2
    return pl.pallas_call(
        functools.partial(exchange_kernel, dims, nh),
        out_shape=outs,
        in_specs=[VM] + [HB] * nh,
        out_specs=[VM] + [HB] * (2 * nh),
        scratch_shapes=scratch,
        compiler_params=pltpu.CompilerParams(collective_id=cid, has_side_effects=True),
        name=f"exchange{cid}",
    )(stats, *planes)


def toeplitz(w, c0, chans, th, tl, dh, dl):
    def pick(i, j, k):
        if 0 <= j <= 2 and 0 <= k <= 2:
            return w[i * 9 + j * 3 + k, c0 : c0 + chans, :]
        return jnp.zeros((chans, 64), f32)

    def tap(i):
        for r in range(4):
            for s in range(4):
                a, py, b, px = r // 2, r % 2, s // 2, s % 2
                block = (2 * a + b) * 4 + py * 2 + px
                for h in range(2):
                    part = jnp.concatenate([pick(i, r - h, s), pick(i, r - h, s - 1)], axis=1)
                    hi, lo = split(part)
                    rows = slice(block * chans, (block + 1) * chans)
                    th[i, rows, 128 * h : 128 * h + 128] = hi
                    tl[i, rows, 128 * h : 128 * h + 128] = lo
                    if dh is not None:
                        rows = slice((py * 2 + px) * chans, (py * 2 + px + 1) * chans)
                        at = ((1 - a) * 2 + (1 - b)) * 256 + 128 * h
                        dh[2 - i, rows, at : at + 128] = hi
                        dl[2 - i, rows, at : at + 128] = lo

    loop(3, tap)


def weights_kernel(
    w2, w3, w4, up,
    t2h, t2l, t3h, t3l, t4h, t4l, tuh, tul, d2h, d2l, d3h, d3l, d4h, d4l,
    uph, upl, uh, ul, ubh, ubl, usc,
):
    toeplitz(w2, 0, 32, t2h, t2l, d2h, d2l)
    toeplitz(w3, 128, 64, t3h, t3l, d3h, d3l)
    toeplitz(w4, 0, 64, t4h, t4l, d4h, d4l)
    toeplitz(w3, 0, 128, tuh, tul, None, None)
    for ip in range(2):
        for q in range(4):
            hi, lo = split(up[ip * 4 + q])
            uph[ip * 128 : ip * 128 + 128, q * 128 : q * 128 + 128] = hi
            upl[ip * 128 : ip * 128 + 128, q * 128 : q * 128 + 128] = lo
    usc[...] = jnp.zeros(usc.shape, f32)
    ah, al = uph[...], upl[...]
    for i in range(3):
        def block(ab, i=i):
            rows = pl.ds(pl.multiple_of(ab * 512, 512), 512)
            p = dot3(ah, al, tuh[i, rows, :], tul[i, rows, :], NN)
            out = pl.ds(pl.multiple_of(ab * 128, 128), 128)
            for ip in range(2):
                usc[slot_of(i, ip), out, :] += p[ip * 128 : ip * 128 + 128]

        loop(4, block)
    for e in range(4):
        for ab in range(4):
            hi, lo = split(usc[e, ab * 128 : ab * 128 + 128, :])
            uh[e, ab * 128 : ab * 128 + 128, :] = hi
            ul[e, ab * 128 : ab * 128 + 128, :] = lo
            p = (3, 1, 2, 0)[e]
            at = (3 - ab) * 256
            ubh[p, :, at : at + 256] = hi
            ubl[p, :, at : at + 256] = lo


def slot_of(i, ip):
    pd = (ip + i + 1) % 2
    t = (pd + i - 1) // 2 - pd + 1
    return pd * 2 + t


def weights(w2, w3, w4, up):
    outs = []
    for shape in [
        (3, 512, 256), (3, 1024, 256), (3, 1024, 256), (3, 2048, 256),
        (3, 128, 1024), (3, 256, 1024), (3, 256, 1024),
        (256, 512), (4, 512, 256), (4, 128, 1024),
    ]:
        outs += [(shape, bf16)] * 2
    return call(
        weights_kernel, outs, (w2, w3, w4, up), scratch=[pltpu.VMEM((4, 512, 256), f32)], name="weights"
    )


def first_kernel(sw, w1, sc, r1, r1c, st, sh, sl, ch, cl):
    wh, wl = split(w1[...])
    for p in range(6):
        own = sw[p, :, :OWN]
        crop = sw[p, :, OWN:]
        for ab in range(4):
            a, b = ab // 2, ab % 2
            rows = slice(p * 64 + ab * 16, p * 64 + ab * 16 + 16)
            hi, lo = split(own if ab == 0 else pltpu.roll(own, OWN - 40 * a - b, 1))
            sh[rows, :] = hi
            sl[rows, :] = lo
            hi, lo = split(crop if ab == 0 else pltpu.roll(crop, CROP - 32 * a - b, 1))
            ch[rows, :] = hi
            cl[rows, :] = lo

    def conv(d):
        rows = pl.ds(pl.multiple_of(d * 64, 64), 192)
        r1[d, :OWN, :] = dot3(sh[rows, :], sl[rows, :], wh, wl, TN)
        r1[d, OWN:, :] = jnp.zeros((1440 - OWN, 128), f32)
        r1c[d] = dot3(ch[rows, :], cl[rows, :], wh, wl, TN)

    loop(4, conv)
    tot = jnp.zeros((1, 128), f32), jnp.zeros((1, 128), f32)
    for d in range(2):
        def part(t, c):
            x = r1[1 + d, pl.ds(pl.multiple_of(t * 160, 160), 160), :].reshape(4, 40, 128)
            x = jnp.where(cells(x.shape, 33, 33, 4 * t), x, 0.0)
            return c[0] + jnp.sum(x, axis=0), c[1] + jnp.sum(x * x, axis=0)

        s, q = lax.fori_loop(0, 9, part, (jnp.zeros((40, 128), f32), jnp.zeros((40, 128), f32)))
        m = sc[1 + d]
        tot = (
            tot[0] + m * jnp.sum(s, axis=0, keepdims=True),
            tot[1] + m * jnp.sum(q, axis=0, keepdims=True),
        )
    put_sums(st, *tot)


def first(sw, w1, sc):
    return call(
        first_kernel,
        [((4, 1440, 128), f32), ((4, CROP, 128), f32), ((1, 512), f32), ((384, OWN), bf16), ((384, OWN), bf16)],
        (sw, w1, sc),
        specs=[VM, VM, SM],
        scratch=[pltpu.VMEM((384, CROP), bf16)] * 2,
        name="first",
    )


def second_kernel(r1, r1c, g1, par, th, tl, sc, si, r2, r2c, st, ah, al, f, bh, bl):
    half = si[0]
    f[...] = jnp.zeros(f.shape, f32)
    scale, off = affine(par, 0, *moments(g1, half, sc[8] * 4356.0, 128))

    def own(p):
        m = sc[p]

        def rows(t):
            x = silu(r1[p, pl.ds(4 * t, 4)] * scale + off)
            f[pl.ds(4 * t, 4), :40, :] = jnp.where(m > 0, x, 0.0)

        loop(9, rows)
        im2col(ah, al, p, f, 32, 32, 128)

    loop(4, own)

    def conv(d):
        acc = jnp.zeros((1024, 256), f32)
        for i in range(3):
            acc += dot3(ah[d + i], al[d + i], th[i], tl[i], NN)
        r2[d] = acc

    loop(2, conv)
    scale_c, off_c = affine(par, 0, *moments(g1, 1 - half, sc[9] * 4356.0, 128))

    def crop(p):
        m = sc[4 + p]

        def rows(t):
            x = silu(r1c[p, pl.ds(4 * t, 4)] * scale_c + off_c)
            f[pl.ds(4 * t, 4), :32, :] = jnp.where(m > 0, x, 0.0)

        loop(7, rows)
        im2col(bh, bl, p, f, 24, 24, 128)

    loop(4, crop)

    def conv_crop(d):
        acc = jnp.zeros((576, 256), f32)
        for i in range(3):
            acc += dot3(bh[d + i], bl[d + i], th[i], tl[i], NN)
        r2c[d] = acc

    loop(2, conv_crop)
    s = jnp.zeros((1, 256), f32)
    q = jnp.zeros((1, 256), f32)
    for d in range(2):
        def part(t, c):
            x = r2[d, pl.ds(pl.multiple_of(t * 128, 128), 128), :].reshape(16, 8, 256)
            return c[0] + jnp.sum(x, axis=0), c[1] + jnp.sum(x * x, axis=0)

        ps, pq = lax.fori_loop(0, 8, part, (jnp.zeros((8, 256), f32), jnp.zeros((8, 256), f32)))
        s = s + sc[1 + d] * jnp.sum(ps, axis=0, keepdims=True)
        q = q + sc[1 + d] * jnp.sum(pq, axis=0, keepdims=True)
    put_sums(st, s, q)


def second(r1, r1c, g1, par, th, tl, sc, si):
    return call(
        second_kernel,
        [((2, 1024, 256), f32), ((2, 576, 256), f32), ((1, 512), f32), ((4, 1024, 512), bf16), ((4, 1024, 512), bf16)],
        (r1.reshape(4, 36, 40, 128), r1c.reshape(4, 28, 32, 128), g1, par, th, tl, sc, si),
        specs=[VM] * 6 + [SM, SM],
        scratch=[pltpu.VMEM((36, 48, 128), f32)] + [pltpu.VMEM((4, 576, 512), bf16)] * 2,
        name="second",
    )


def field_sums(r, d, n, rows, cols, mask):
    def part(t, c):
        x = r[d, pl.ds(pl.multiple_of(t * 96, 96), 96), :].reshape(4, 24, 256)
        x = jnp.where(cells(x.shape, rows, cols, 4 * t), x, 0.0)
        return c[0] + jnp.sum(x, axis=0), c[1] + jnp.sum(x * x, axis=0)

    zero = jnp.zeros((24, 256), f32)
    full = n // 96
    s, q = lax.fori_loop(0, full, part, (zero, zero))
    if n % 96:
        x = r[d, full * 96 : n, :].reshape((n - full * 96) // 24, 24, 256)
        x = jnp.where(cells(x.shape, rows, cols, 4 * full), x, 0.0)
        s = s + jnp.sum(x, axis=0)
        q = q + jnp.sum(x * x, axis=0)
    return mask * jnp.sum(s, axis=0, keepdims=True), mask * jnp.sum(q, axis=0, keepdims=True)


def third_kernel(
    r2, r2c, hl, hr, co, col, cor, g2, par, th, tl, uh, ul, sc, si,
    pooled, r3, st, ah, al, cuh, cul, f, f2,
):
    half = si[0]
    scale, off = affine(par, 1, *moments(g2, half, sc[8] * 4096.0, 256))

    def pool(t):
        rows = pl.ds(pl.multiple_of(t * 64, 64), 64)
        v = sc[1] * silu(r2[0, rows, :] * scale + off) + sc[2] * silu(r2[1, rows, :] * scale + off)
        v = v[:, :128] + v[:, 128:]
        v = (v + pltpu.roll(v, 64, 1)) * 0.125
        pooled[rows, :] = v[:, :64]

    loop(16, pool)
    scale_c, off_c = affine(par, 1, *moments(g2, 1 - half, sc[9] * 4096.0, 256))
    f[...] = jnp.zeros(f.shape, f32)

    def put(p, get):
        m = sc[4 + p]

        def rows(t):
            x = silu(get(t) * scale_c + off_c)
            f[pl.ds(4 * t, 4), :24, :] = jnp.where(m > 0, x, 0.0)

        loop(6, rows)
        im2col(ah, al, p, f, 24, 24, 256)

    put(0, lambda t: hl[pl.ds(4 * t, 4)])
    loop(2, lambda p: put(p + 1, lambda t: r2c[p, pl.ds(4 * t, 4)]))
    put(3, lambda t: hr[pl.ds(4 * t, 4)])
    f2[...] = jnp.zeros(f2.shape, f32)
    for p, (src, m) in enumerate(((col, sc[4]), (co, sc[5]), (cor, sc[7]))):
        f2[:24, :24, :] = jnp.where(m > 0, src[...], 0.0)
        im2col(cuh, cul, p, f2, 24, 24, 128)

    def conv(d):
        acc = jnp.zeros((576, 256), f32)
        for i in range(3):
            acc += dot3(ah[d + i], al[d + i], th[i], tl[i], NN)
        for t in range(2):
            acc += dot3(cuh[d + t], cul[d + t], uh[2 * d + t], ul[2 * d + t], NN)
        r3[d] = acc

    loop(2, conv)
    s0, q0 = field_sums(r3, 0, 576, 23, 23, sc[5])
    s1, q1 = field_sums(r3, 1, 576, 23, 23, sc[6])
    put_sums(st, s0 + s1, q0 + q1)


def third(r2, r2c, hl, hr, co, col, cor, g2, par, th, tl, uh, ul, sc, si):
    return call(
        third_kernel,
        [
            ((1024, 64), f32), ((2, 576, 256), f32), ((1, 512), f32),
            ((4, 576, 1024), bf16), ((4, 576, 1024), bf16), ((3, 576, 512), bf16), ((3, 576, 512), bf16),
        ],
        (
            r2, r2c.reshape(2, 24, 24, 256), hl.reshape(24, 24, 256), hr.reshape(24, 24, 256),
            co, col, cor, g2, par, th, tl, uh, ul, sc, si,
        ),
        specs=[VM] * 13 + [SM, SM],
        scratch=[pltpu.VMEM((26, 32, 256), f32), pltpu.VMEM((26, 32, 128), f32)],
        name="third",
    )


def fourth_kernel(r3, hl, hr, g3, par, th, tl, sc, si, r4, st, ah, al, f):
    scale, off = affine(par, 2, *moments(g3, si[0], sc[9] * 2116.0, 256))
    f[...] = jnp.zeros(f.shape, f32)

    def put(p, get):
        m = sc[4 + p]

        def rows(t):
            x = silu(get(t) * scale + off)
            f[pl.ds(4 * t, 4), :24, :] = jnp.where(m > 0, x, 0.0)

        loop(6, rows)
        im2col(ah, al, p, f, 22, 24, 256)

    put(0, lambda t: hl[pl.ds(4 * t, 4)])
    loop(2, lambda p: put(p + 1, lambda t: r3[p, pl.ds(4 * t, 4)]))
    put(3, lambda t: hr[pl.ds(4 * t, 4)])

    def conv(d):
        acc = jnp.zeros((528, 256), f32)
        for i in range(3):
            acc += dot3(ah[d + i], al[d + i], th[i], tl[i], NN)
        r4[d] = acc

    loop(2, conv)
    s0, q0 = field_sums(r4, 0, 528, 22, 22, sc[5])
    s1, q1 = field_sums(r4, 1, 528, 22, 22, sc[6])
    put_sums(st, s0 + s1, q0 + q1)


def fourth(r3, hl, hr, g3, par, th, tl, sc, si):
    return call(
        fourth_kernel,
        [((2, 528, 256), f32), ((1, 512), f32), ((4, 528, 1024), bf16), ((4, 528, 1024), bf16)],
        (r3.reshape(2, 24, 24, 256), hl.reshape(24, 24, 256), hr.reshape(24, 24, 256), g3, par, th, tl, sc, si),
        specs=[VM] * 7 + [SM, SM],
        scratch=[pltpu.VMEM((26, 32, 256), f32)],
        name="fourth",
    )


def back_parts(par, layer, avg, inv, r, a):
    lanes = avg.shape[-1]
    normed = (r - avg) * inv
    b = par[2 * layer : 2 * layer + 1, :lanes] * normed + par[2 * layer + 1 : 2 * layer + 2, :lanes]
    return normed, silu_back(a, b)


def response_back(par, layer, avg, inv, tg, tc, count, r, a):
    lanes = avg.shape[-1]
    gain = par[2 * layer : 2 * layer + 1, :lanes]
    normed, bg = back_parts(par, layer, avg, inv, r, a)
    return inv * gain * (bg - (tg + normed * tc) / count)


def output_kernel(r4, og, g4, par, sc, si, dec, st):
    avg, inv = moments(g4, si[0], sc[9] * 1936.0, 256)
    scale, off = affine(par, 3, avg, inv)
    s = jnp.zeros((1, 256), f32)
    q = jnp.zeros((1, 256), f32)
    for d in range(2):
        m = sc[5 + d]

        def part(t, c):
            rows = pl.ds(pl.multiple_of(t * 48, 48), 48)
            r = r4[d, rows, :]
            b = r * scale + off
            sg = 1.0 / (1.0 + jnp.exp(-b))
            dec[d, rows, :] = m * (b * sg)
            bg = og[d, rows, :] * sg * (1.0 + b * (1.0 - sg))
            normed = (r - avg) * inv
            bg3 = bg.reshape(6, 8, 256)
            return c[0] + jnp.sum(bg3, axis=0), c[1] + jnp.sum(bg3 * normed.reshape(6, 8, 256), axis=0)

        ps, pq = lax.fori_loop(0, 11, part, (jnp.zeros((8, 256), f32), jnp.zeros((8, 256), f32)))
        s = s + m * jnp.sum(ps, axis=0, keepdims=True)
        q = q + m * jnp.sum(pq, axis=0, keepdims=True)
    put_sums(st, s, q)


def output(r4, og, g4, par, sc, si):
    return call(
        output_kernel,
        [((2, 528, 256), f32), ((1, 512), f32)],
        (r4, og, g4, par, sc, si),
        specs=[VM] * 4 + [SM, SM],
        name="output",
    )


def fourth_back_kernel(
    r4, r4l, r4r, og, ogl, ogr, g4, g5, r3, g3, par, dh, dl, sc, si,
    a3, st, e4, f, ah, al,
):
    half = si[0]
    count = sc[9] * 1936.0
    avg, inv = moments(g4, half, count, 256)
    tg, tc = totals(g5, half, 256)
    f[...] = jnp.zeros(f.shape, f32)

    def put(p, get_r, get_a, keep):
        m = sc[4 + p]

        def rows(t):
            e = response_back(par, 3, avg, inv, tg, tc, count, get_r(t), get_a(t))
            e = jnp.where(cells(e.shape, 22, 22, 0) & (m > 0), e, 0.0)
            f[pl.ds(1 + 2 * t, 2), 8:32, :] = e
            if keep is not None:
                e4[keep, pl.ds(2 * t, 2)] = e

        loop(11, rows)
        im2col(ah, al, p, f, 24, 24, 256, x0=7)

    put(0, lambda t: r4l[pl.ds(2 * t, 2)], lambda t: ogl[pl.ds(2 * t, 2)], None)
    loop(
        2,
        lambda p: put(
            p + 1, lambda t: r4[p, pl.ds(2 * t, 2)], lambda t: og[p, pl.ds(2 * t, 2)], p
        ),
    )
    put(3, lambda t: r4r[pl.ds(2 * t, 2)], lambda t: ogr[pl.ds(2 * t, 2)], None)

    def conv(d):
        acc = jnp.zeros((576, 256), f32)
        for i in range(3):
            acc += dot3(ah[d + i], al[d + i], dh[i], dl[i], NT)
        a3[d] = acc

    loop(2, conv)
    avg3, inv3 = moments(g3, half, sc[9] * 2116.0, 256)
    s = jnp.zeros((1, 256), f32)
    q = jnp.zeros((1, 256), f32)
    for d in range(2):
        def part(t, c):
            rows = pl.ds(pl.multiple_of(t * 48, 48), 48)
            normed, bg = back_parts(par, 2, avg3, inv3, r3[d, rows, :], a3[d, rows, :])
            bg = bg.reshape(2, 24, 256)
            bg = jnp.where(cells(bg.shape, 23, 23, 2 * t), bg, 0.0)
            return c[0] + jnp.sum(bg, axis=0), c[1] + jnp.sum(bg * normed.reshape(2, 24, 256), axis=0)

        ps, pq = lax.fori_loop(0, 12, part, (jnp.zeros((24, 256), f32), jnp.zeros((24, 256), f32)))
        s = s + sc[5 + d] * jnp.sum(ps, axis=0, keepdims=True)
        q = q + sc[5 + d] * jnp.sum(pq, axis=0, keepdims=True)
    put_sums(st, s, q)


def fourth_back(r4, r4l, r4r, og, ogl, ogr, g4, g5, r3, g3, par, dh, dl, sc, si):
    box = (22, 24, 256)
    return call(
        fourth_back_kernel,
        [((2, 576, 256), f32), ((1, 512), f32), ((2, 22, 24, 256), f32)],
        (
            r4.reshape((2,) + box), r4l.reshape(box), r4r.reshape(box),
            og.reshape((2,) + box), ogl.reshape(box), ogr.reshape(box),
            g4, g5, r3, g3, par, dh, dl, sc, si,
        ),
        specs=[VM] * 13 + [SM, SM],
        scratch=[pltpu.VMEM((26, 40, 256), f32)] + [pltpu.VMEM((4, 576, 1024), bf16)] * 2,
        name="fourth_back",
    )


def unfold(g, i, j, k, chans, out, row0):
    def block(r, s):
        at = (2 * (r // 2) + s // 2) * 4 + (r % 2) * 2 + s % 2
        return slice(at * chans, (at + 1) * chans)

    x = g[block(j, k), 0:128] + g[block(j + 1, k), 128:256]
    y = g[block(j, k + 1), 0:128] + g[block(j + 1, k + 1), 128:256]
    out[i * 9 + j * 3 + k, row0 : row0 + chans, :] = (x + pltpu.roll(y, 64, 1))[:, :64]


def fourth_weight_kernel(ah, al, e4, dw, g):
    for i in range(3):
        for d in range(2):
            eh, el = split(e4[d])
            v = dot3(ah[d + i], al[d + i], eh, el, TN)
            if d == 0:
                g[...] = v
            else:
                g[...] += v
        for j in range(3):
            for k in range(3):
                unfold(g, i, j, k, 64, dw, 0)


def fourth_weight(ah, al, e4):
    return call(
        fourth_weight_kernel,
        [((27, 64, 64), f32)],
        (ah, al, e4),
        scratch=[pltpu.VMEM((1024, 256), f32)],
        name="fourth_weight",
    )[0]


def third_back_kernel(
    a3, a3l, a3r, r3, r3l, r3r, g3, g6, par, dh, dl, sc, si, skip, e3, ah, al, f
):
    half = si[0]
    count = sc[9] * 2116.0
    avg, inv = moments(g3, half, count, 256)
    tg, tc = totals(g6, half, 256)
    f[...] = jnp.zeros(f.shape, f32)

    def put(p, get_r, get_a, keep):
        m = sc[4 + p]

        def rows(t):
            e = response_back(par, 2, avg, inv, tg, tc, count, get_r(t), get_a(t))
            e = jnp.where(cells(e.shape, 23, 23, 2 * t) & (m > 0), e, 0.0)
            f[pl.ds(1 + 2 * t, 2), 8:32, :] = e
            if keep is not None:
                e3[keep, pl.ds(2 * t, 2)] = e

        loop(12, rows)
        im2col(ah, al, p, f, 24, 24, 256, x0=7)

    put(0, lambda t: r3l[pl.ds(2 * t, 2)], lambda t: a3l[pl.ds(2 * t, 2)], None)
    loop(
        2,
        lambda p: put(
            p + 1, lambda t: r3[p, pl.ds(2 * t, 2)], lambda t: a3[p, pl.ds(2 * t, 2)], p
        ),
    )
    put(3, lambda t: r3r[pl.ds(2 * t, 2)], lambda t: a3r[pl.ds(2 * t, 2)], None)

    def conv(d):
        acc = jnp.zeros((576, 256), f32)
        for i in range(3):
            acc += dot3(ah[d + i], al[d + i], dh[i], dl[i], NT)
        skip[d] = acc

    loop(2, conv)


def third_back(a3, a3l, a3r, r3, r3l, r3r, g3, g6, par, dh, dl, sc, si):
    box = (24, 24, 256)
    return call(
        third_back_kernel,
        [((2, 576, 256), f32), ((2, 24, 24, 256), f32), ((4, 576, 1024), bf16), ((4, 576, 1024), bf16)],
        (
            a3.reshape((2,) + box), a3l.reshape(box), a3r.reshape(box),
            r3.reshape((2,) + box), r3l.reshape(box), r3r.reshape(box),
            g3, g6, par, dh, dl, sc, si,
        ),
        specs=[VM] * 11 + [SM, SM],
        scratch=[pltpu.VMEM((26, 40, 256), f32)],
        name="third_back",
    )


def coarse_back_kernel(ah, al, ubh, ubl, sc, cg):
    acc = jnp.zeros((576, 128), f32)
    for p in range(4):
        acc += dot3(ah[p], al[p], ubh[p], ubl[p], NT)
    cg[...] = acc * sc[5]


def coarse_back(ah, al, ubh, ubl, sc):
    return call(
        coarse_back_kernel,
        [((576, 128), f32)],
        (ah, al, ubh, ubl, sc),
        specs=[VM] * 4 + [SM],
        name="coarse_back",
    )[0]


def third_weight_kernel(ah, al, cuh, cul, e3, tuh, tul, uph, upl, dw, dup, g, gu, gd, eh, el):
    for d in range(2):
        hi, lo = split(e3[d])
        eh[d] = hi
        el[d] = lo
    for i in range(3):
        g[:1024, :] = dot3(ah[i], al[i], eh[0], el[0], TN) + dot3(ah[i + 1], al[i + 1], eh[1], el[1], TN)
        for j in range(3):
            for k in range(3):
                unfold(g, i, j, k, 64, dw, 128)
    for pd in range(2):
        for t in range(2):
            gu[pd * 2 + t] = dot3(cuh[pd + t], cul[pd + t], eh[pd], el[pd], TN)
    gd[...] = jnp.zeros(gd.shape, f32)
    for i in range(3):
        def block(ab, i=i):
            out = pl.ds(pl.multiple_of(ab * 128, 128), 128)
            p = jnp.concatenate([gu[slot_of(i, 0), out, :], gu[slot_of(i, 1), out, :]], axis=0)
            ph, plo = split(p)
            rows = pl.ds(pl.multiple_of(ab * 512, 512), 512)
            gd[...] += dot3(ph, plo, tuh[i, rows, :], tul[i, rows, :], NT)
            g[rows, :] = dot3(uph[...], upl[...], ph, plo, TN)

        loop(4, block)
        for j in range(3):
            for k in range(3):
                unfold(g, i, j, k, 128, dw, 0)
    for ip in range(2):
        for q in range(4):
            dup[ip * 4 + q] = gd[ip * 128 : ip * 128 + 128, q * 128 : q * 128 + 128]


def third_weight(ah, al, cuh, cul, e3, tuh, tul, uph, upl):
    return call(
        third_weight_kernel,
        [((27, 192, 64), f32), ((8, 128, 128), f32)],
        (ah, al, cuh, cul, e3, tuh, tul, uph, upl),
        scratch=[
            pltpu.VMEM((2048, 256), f32), pltpu.VMEM((4, 512, 256), f32), pltpu.VMEM((256, 512), f32),
            pltpu.VMEM((2, 576, 256), bf16), pltpu.VMEM((2, 576, 256), bf16),
        ],
        name="third_weight",
    )


def skip_kernel(skip, pg, r2, g2, par, sc, si, bg2, st, z):
    avg, inv = moments(g2, si[0], sc[8] * 4096.0, 256)
    oy, ox = si[1], si[2]
    qx = ox // 2
    rx = ox - 2 * qx
    odd = rx > 0
    s = jnp.zeros((1, 256), f32)
    q = jnp.zeros((1, 256), f32)
    lane = lax.broadcasted_iota(jnp.int32, (32, 128), 1)
    pad = jnp.zeros((8, 128), f32)
    for d in range(2):
        z[...] = jnp.zeros(z.shape, f32)

        def place(t):
            for h in range(2):
                v = jnp.concatenate([skip[d, t, :, 128 * h : 128 * h + 128], pad], axis=0)
                v = jnp.where(odd, pltpu.roll(v, 64, 1), v)
                v = jnp.where(lane < 64, pltpu.roll(v, qx + rx, 0), pltpu.roll(v, qx, 0))
                z[oy + 2 * t + h] = v

        loop(24, place)

        def part(t, c):
            pv = pg[t] * 0.125
            pv = jnp.concatenate([pv, pv], axis=1)
            a = jnp.concatenate([z[2 * t] + pv, z[2 * t + 1] + pv], axis=1)
            rows = pl.ds(pl.multiple_of(t * 32, 32), 32)
            normed, bg = back_parts(par, 1, avg, inv, r2[d, rows, :], a)
            bg = sc[1 + d] * bg
            bg2[d, rows, :] = bg
            bg = bg.reshape(4, 8, 256)
            return c[0] + jnp.sum(bg, axis=0), c[1] + jnp.sum(bg * normed.reshape(4, 8, 256), axis=0)

        ps, pq = lax.fori_loop(0, 32, part, (jnp.zeros((8, 256), f32), jnp.zeros((8, 256), f32)))
        s = s + jnp.sum(ps, axis=0, keepdims=True)
        q = q + jnp.sum(pq, axis=0, keepdims=True)
    put_sums(st, s, q)


def skip_back(skip, pg, r2, g2, par, sc, si):
    return call(
        skip_kernel,
        [((2, 1024, 256), f32), ((1, 512), f32)],
        (skip.reshape(2, 24, 24, 256), pg, r2, g2, par, sc, si),
        specs=[VM] * 5 + [SM, SM],
        scratch=[pltpu.VMEM((64, 32, 128), f32)],
        name="skip_back",
    )


def second_back_kernel(bg2, r2, g2, g7, par, dh, dl, sc, si, e2, a1, side, f, ah, al):
    half = si[0]
    count = sc[8] * 4096.0
    avg, inv = moments(g2, half, count, 256)
    tg, tc = totals(g7, half, 256)
    k = par[2:3, :] * inv
    f[...] = jnp.zeros(f.shape, f32)

    def put(p):
        m = sc[1 + p]

        def rows(t):
            at = pl.ds(pl.multiple_of(t * 64, 64), 64)
            normed = (r2[p, at, :] - avg) * inv
            e = k * (bg2[p, at, :] - m * ((tg + normed * tc) / count))
            e2[p, at, :] = e
            f[pl.ds(1 + 2 * t, 2), 8:40, :] = e.reshape(2, 32, 256)

        loop(16, rows)
        im2col(ah, al, p, f, 34, 40, 256, x0=7)

    loop(2, put)
    rh = dh[...].reshape(384, 1024)
    rl = dl[...].reshape(384, 1024)
    v = dot3(ah[0], al[0], rh, rl, NT)
    a1[1, :1360] = v[:, :128]
    a1[0, :1360] = v[:, 128:256]
    side[0, :1360] = v[:, 256:]
    v = dot3(ah[1], al[1], rh, rl, NT)
    side[1, :1360] = v[:, :128]
    a1[1, :1360] += v[:, 128:256]
    a1[0, :1360] += v[:, 256:]
    for d in range(2):
        a1[d, 1360:] = jnp.zeros((48, 128), f32)
        side[d, 1360:] = jnp.zeros((48, 128), f32)


def second_back(bg2, r2, g2, g7, par, dh, dl, sc, si):
    return call(
        second_back_kernel,
        [((2, 1024, 256), f32), ((2, OWN, 128), f32), ((2, OWN, 128), f32)],
        (bg2, r2, g2, g7, par, dh, dl, sc, si),
        specs=[VM] * 7 + [SM, SM],
        scratch=[pltpu.VMEM((36, 56, 256), f32)] + [pltpu.VMEM((2, 1360, 1024), bf16)] * 2,
        name="second_back",
    )


def second_weight_kernel(ah, al, e2, dw, g, eh, el):
    for d in range(2):
        hi, lo = split(e2[d])
        eh[d] = hi
        el[d] = lo
    for i in range(3):
        g[...] = dot3(ah[i], al[i], eh[0], el[0], TN) + dot3(ah[i + 1], al[i + 1], eh[1], el[1], TN)
        for j in range(3):
            for k in range(3):
                unfold(g, i, j, k, 32, dw, 0)


def second_weight(ah, al, e2):
    return call(
        second_weight_kernel,
        [((27, 32, 64), f32)],
        (ah, al, e2),
        scratch=[pltpu.VMEM((512, 256), f32), pltpu.VMEM((2, 1024, 256), bf16), pltpu.VMEM((2, 1024, 256), bf16)],
        name="second_weight",
    )[0]


def first_sums_kernel(a1p, sl, sr, r1, g1, par, sc, si, a1, st):
    avg, inv = moments(g1, si[0], sc[8] * 4356.0, 128)
    s = jnp.zeros((1, 128), f32)
    q = jnp.zeros((1, 128), f32)
    for d in range(2):
        other = sl if d == 0 else sr
        here = sc[10 + d]

        def part(t, c):
            rows = pl.ds(pl.multiple_of(t * 160, 160), 160)
            a = a1p[d, rows, :] + jnp.where(here > 0, other[rows, :], 0.0)
            a1[d, rows, :] = a
            normed, bg = back_parts(par, 0, avg, inv, r1[1 + d, rows, :], a)
            bg = bg.reshape(4, 40, 128)
            bg = jnp.where(cells(bg.shape, 33, 33, 4 * t), bg, 0.0)
            return c[0] + jnp.sum(bg, axis=0), c[1] + jnp.sum(bg * normed.reshape(4, 40, 128), axis=0)

        ps, pq = lax.fori_loop(0, 8, part, (jnp.zeros((40, 128), f32), jnp.zeros((40, 128), f32)))
        rows = slice(1280, OWN)
        a = a1p[d, rows, :] + jnp.where(here > 0, other[rows, :], 0.0)
        a1[d, rows, :] = a
        rows = slice(1280, 1320)
        normed, bg = back_parts(par, 0, avg, inv, r1[1 + d, rows, :], a[:40])
        bg = jnp.where(lax.broadcasted_iota(jnp.int32, (40, 128), 0) < 33, bg, 0.0)
        ps = ps + bg
        pq = pq + bg * normed
        s = s + sc[1 + d] * jnp.sum(ps, axis=0, keepdims=True)
        q = q + sc[1 + d] * jnp.sum(pq, axis=0, keepdims=True)
    put_sums(st, s, q)


def first_sums(a1p, sl, sr, r1, g1, par, sc, si):
    return call(
        first_sums_kernel,
        [((2, OWN, 128), f32), ((1, 512), f32)],
        (a1p, sl, sr, r1, g1, par, sc, si),
        specs=[VM] * 6 + [SM, SM],
        name="first_sums",
    )


def first_back_kernel(a1, a1l, a1r, r1, g1, g8, par, w1, sh, sl, sc, si, ig, dw, eh, el):
    half = si[0]
    count = sc[8] * 4356.0
    avg, inv = moments(g1, half, count, 128)
    tg, tc = totals(g8, half, 128)
    wh, wl = split(w1[...])

    def put(p, get_a):
        m = sc[p]
        eh[p, 1280:, :] = jnp.zeros((OWN - 1280, 128), bf16)
        el[p, 1280:, :] = jnp.zeros((OWN - 1280, 128), bf16)

        def rows(t):
            at = pl.ds(pl.multiple_of(t * 80, 80), 80)
            e = response_back(par, 0, avg, inv, tg, tc, count, r1[p, at, :], get_a(at))
            e = e.reshape(2, 40, 128)
            e = jnp.where(cells(e.shape, 33, 33, 2 * t) & (m > 0), e, 0.0)
            hi, lo = split(e.reshape(80, 128))
            eh[p, at, :] = hi
            el[p, at, :] = lo

        loop(17, rows)

    put(0, lambda at: a1l[at, :])
    loop(2, lambda p: put(p + 1, lambda at: a1[p, at, :]))
    put(3, lambda at: a1r[at, :])
    acc = jnp.zeros((192, 128), f32)
    for d in range(2):
        rows = slice((d + 1) * 64, (d + 1) * 64 + 192)
        acc += dot3(sh[rows, :], sl[rows, :], eh[d + 1], el[d + 1], NN)
    dw[...] = acc
    parts = [dot3(wh, wl, eh[p], el[p], NT) for p in range(4)]
    for d in range(2):
        tot = jnp.zeros((16, OWN), f32)
        for ab in range(4):
            v = jnp.zeros((16, OWN), f32)
            for i in range(3):
                at = i * 64 + ab * 16
                v += parts[d + 2 - i][at : at + 16, :]
            a, b = ab // 2, ab % 2
            tot += v if ab == 0 else pltpu.roll(v, 40 * a + b, 1)
        ig[d] = tot


def first_back(a1, a1l, a1r, r1, g1, g8, par, w1, sh, sl, sc, si):
    return call(
        first_back_kernel,
        [((2, 16, OWN), f32), ((192, 128), f32)],
        (a1, a1l, a1r, r1, g1, g8, par, w1, sh, sl, sc, si),
        specs=[VM] * 10 + [SM, SM],
        scratch=[pltpu.VMEM((4, OWN, 128), bf16)] * 2,
        name="first_back",
    )


def planar(x, pitch, lanes):
    planes, side = x.shape[0], x.shape[1] // 2
    x = x.reshape(planes, side, 2, side, 2, 4).transpose(0, 2, 4, 5, 1, 3).reshape(planes, 16, side, side)
    x = jnp.pad(x, ((0, 0), (0, 0), (0, 0), (0, pitch - side))).reshape(planes, 16, side * pitch)
    return jnp.pad(x, ((0, 0), (0, 0), (0, lanes - side * pitch)))


def body(
    dims,
    image, modality_mask, extents, crop_offsets, coarse,
    conv_first, gain_first, shift_first, conv_second, gain_second, shift_second,
    up_kernel, conv_third, gain_third, shift_third, conv_fourth, gain_fourth, shift_fourth,
    pool_grad, output_grad,
):
    S, K, B = dims
    n = S * K * B
    section = lax.axis_index("section")
    slab = lax.axis_index("slab")
    batch = lax.axis_index("batch")
    planes = image.shape[2]
    enc_len = extents[section]
    dec_len = extents[1 - section]
    window = slab * planes + jnp.arange(-1, planes + 1, dtype=jnp.int32)
    enc_mask = ((window < enc_len[batch]) & (window >= 0)).astype(f32)
    dec_mask = ((window < dec_len[batch]) & (window >= 0)).astype(f32)
    sc = jnp.concatenate(
        [
            enc_mask, dec_mask,
            jnp.stack(
                [
                    jnp.sum(enc_len).astype(f32), jnp.sum(dec_len).astype(f32),
                    (slab > 0).astype(f32), (slab < K - 1).astype(f32),
                ]
            ),
            jnp.zeros((4,), f32),
        ]
    )
    offsets = crop_offsets[0, 0]
    si = jnp.concatenate([jnp.stack([section.astype(jnp.int32)]), offsets, jnp.zeros((5,), jnp.int32)])

    def lanes(v):
        return jnp.tile(v, 256 // v.shape[0])

    par = jnp.stack(
        [
            lanes(v)
            for v in (
                gain_first, shift_first, gain_second, shift_second,
                gain_third, shift_third, gain_fourth, shift_fourth,
            )
        ]
    )
    w1 = jnp.stack(
        [
            jnp.pad(conv_first, ((0, 0), (qy, 1 - qy), (qx, 1 - qx), (0, 0), (0, 0)))
            for qy in range(2)
            for qx in range(2)
        ],
        axis=4,
    )
    w1 = w1.reshape(3, 2, 2, 2, 2, 4, 128).transpose(0, 1, 3, 2, 4, 5, 6).reshape(192, 128)

    keep_in = modality_mask[0, 0].astype(f32)[None, None, None, :] * enc_mask[1:3, None, None, None]
    source = image[0, 0] * keep_in
    zero = jnp.zeros((), jnp.int32)
    crop = lax.dynamic_slice(source, (zero, offsets[0], offsets[1], zero), (planes, 52, 52, 4))
    swap = [(i, 1 - i) for i in range(2)]
    right = [(i, i + 1) for i in range(K - 1)]
    left = [(i + 1, i) for i in range(K - 1)]
    crop = lax.ppermute(planar(crop, 32, CROP), "section", swap)
    own = jnp.concatenate([planar(source, 40, OWN), crop], axis=2)
    sw = jnp.concatenate([lax.ppermute(own, "slab", right), own, lax.ppermute(own, "slab", left)], axis=0)

    og = output_grad[0, 0].reshape(2, 22, 2, 22, 2, 64).transpose(0, 1, 3, 2, 4, 5).reshape(2, 22, 22, 256)
    og = jnp.pad(og, ((0, 0), (0, 0), (0, 2), (0, 0))).reshape(2, 528, 256)

    (
        t2h, t2l, t3h, t3l, t4h, t4l, tuh, tul, d2h, d2l, d3h, d3l, d4h, d4l,
        uph, upl, uh, ul, ubh, ubl,
    ) = weights(
        conv_second.reshape(27, 32, 64), conv_third.reshape(27, 192, 64),
        conv_fourth.reshape(27, 64, 64), up_kernel.reshape(8, 128, 128),
    )

    r1, r1c, st, sh, sl = first(sw, w1, sc)
    co = coarse[0, 0]
    g1, col, cor = exchange(dims, st, [co], 1)
    r2, r2c, st, a2h, a2l = second(r1, r1c, g1, par, t2h, t2l, sc, si)
    g2, hl, hr = exchange(dims, st, [r2c], 2)
    pooled, r3, st, a3h, a3l, cuh, cul = third(
        r2, r2c, hl, hr, co[0], col, cor, g2, par, t3h, t3l, uh, ul, sc, si
    )
    g3, r3l, r3r = exchange(dims, st, [r3], 2)
    r4, st, a4h, a4l = fourth(r3, r3l, r3r, g3, par, t4h, t4l, sc, si)
    g4, r4l, r4r, ogl, ogr = exchange(dims, st, [r4, og], 3)
    dec, st = output(r4, og, g4, par, sc, si)
    (g5,) = exchange(dims, st, [], 4)
    a3, st, e4 = fourth_back(r4, r4l, r4r, og, ogl, ogr, g4, g5, r3, g3, par, d4h, d4l, sc, si)
    g6, a3l_, a3r_ = exchange(dims, st, [a3], 2)
    dw4 = fourth_weight(a4h, a4l, e4.reshape(2, 528, 256))
    skip, e3, e3h, e3l = third_back(a3, a3l_, a3r_, r3, r3l, r3r, g3, g6, par, d3h, d3l, sc, si)
    skip = lax.ppermute(skip, "section", swap)
    coarse_grad = coarse_back(e3h, e3l, ubh, ubl, sc)
    dw3, dup = third_weight(a3h, a3l, cuh, cul, e3.reshape(2, 576, 256), tuh, tul, uph, upl)
    bg2, st = skip_back(skip, pool_grad[0, 0, 0], r2, g2, par, sc, si)
    (g7,) = exchange(dims, st, [], 4)
    e2, a1p, side = second_back(bg2, r2, g2, g7, par, d2h, d2l, sc, si)
    _, s_l, s_r = exchange(dims, st, [side], 5)
    dw2 = second_weight(a2h, a2l, e2)
    a1, st = first_sums(a1p, s_l, s_r, r1, g1, par, sc, si)
    g8, a1l, a1r = exchange(dims, st, [a1], 5)
    ig, dw1 = first_back(a1, a1l, a1r, r1, g1, g8, par, w1, sh, sl, sc, si)

    dw1 = dw1.reshape(3, 2, 2, 2, 2, 4, 2, 2, 32).transpose(0, 1, 3, 2, 4, 5, 6, 7, 8)
    dw1 = dw1.reshape(3, 4, 4, 4, 2, 2, 32)
    dw1 = sum(
        dw1[:, qy : qy + 3, qx : qx + 3, :, qy, qx] for qy in range(2) for qx in range(2)
    )
    axes = ("section", "slab", "batch")
    dw4, dw3, dup = lax.psum((dw4, dw3, dup), axes)
    dw1, dw2 = lax.psum((dw1, dw2), axes)

    def affine_grads(g, width):
        t = jnp.sum(g, axis=(0, 1)).reshape(2, 256 // width, width).sum(axis=1)
        return t[1], t[0]

    gg1, gs1 = affine_grads(g8, 32)
    gg2, gs2 = affine_grads(g7, 64)
    gg3, gs3 = affine_grads(g6, 64)
    gg4, gs4 = affine_grads(g5, 64)

    dec = dec.reshape(2, 22, 24, 2, 2, 64)[:, :, :22].transpose(0, 1, 3, 2, 4, 5).reshape(2, 44, 44, 64)
    ig = ig[:, :, :1360].reshape(2, 2, 2, 4, 34, 40)[..., :34].transpose(0, 4, 1, 5, 2, 3)
    ig = ig.reshape(2, 68, 68, 4) * keep_in
    return (
        pooled.reshape(1, 1, 1, 32, 32, 64),
        dec[None, None],
        ig[None, None],
        coarse_grad.reshape(1, 1, 1, 24, 24, 128),
        dw1,
        gg1,
        gs1,
        dw2.reshape(3, 3, 3, 32, 64),
        gg2,
        gs2,
        dup.reshape(2, 2, 2, 128, 128),
        dw3.reshape(3, 3, 3, 192, 64),
        gg3,
        gs3,
        dw4.reshape(3, 3, 3, 64, 64),
        gg4,
        gs4,
    )


def solution(mesh):
    dims = tuple(mesh.shape[a] for a in ("section", "slab", "batch"))
    field = P("section", "batch", "slab", None, None, None)
    volume = P("section", "batch", None)
    rep = P()
    return jax.shard_map(
        functools.partial(body, dims),
        mesh=mesh,
        in_specs=(field, volume, rep, volume, field) + (rep,) * 13 + (field, field),
        out_specs=(field,) * 4 + (rep,) * 13,
        check_vma=False,
    )
```

```python
import functools

import jax
import jax.numpy as jnp
import numpy as np
from jax import lax
from jax.experimental import pallas as pl
from jax.experimental.pallas import tpu as pltpu
from jax.sharding import PartitionSpec as P

f32 = jnp.float32
bf16 = jnp.bfloat16
MESH = pl.DeviceIdType.MESH
EPSILON = 1e-05
NN = (((1,), (0,)), ((), ()))
NT = (((1,), (1,)), ((), ()))
TN = (((0,), (0,)), ((), ()))
VM = pl.BlockSpec(memory_space=pltpu.VMEM)
SM = pl.BlockSpec(memory_space=pltpu.SMEM)
HB = pl.BlockSpec(memory_space=pl.ANY)
LIMIT = 60 * 2**20

OWN = 1408
CROP = 896


def split(x):
    hi = x.astype(bf16)
    return hi, (x - hi.astype(f32)).astype(bf16)


def dot(a, b, dims):
    return lax.dot_general(a, b, dims, preferred_element_type=f32)


def dot3(ah, al, bh, bl, dims):
    return dot(ah, bh, dims) + dot(al, bh, dims) + dot(ah, bl, dims)


def loop(n, f, unroll=1):
    def step(t, c):
        f(t)
        return c

    lax.fori_loop(0, n, step, 0, unroll=unroll)


def fold(v):
    lanes = v.shape[-1]
    v = jnp.broadcast_to(v, (8, lanes))
    if lanes == 256:
        h = v[:, :128] + v[:, 128:]
        h = h + pltpu.roll(h, 64, 1)
        h = jnp.concatenate([h, h], axis=1)
    else:
        h = v + pltpu.roll(v, 64, 1)
        h = h + pltpu.roll(h, 32, 1)
    return h[:1]


def totals(gath, half, lanes):
    if half is None:
        tot = jnp.sum(gath[...], axis=0)
    else:
        per = gath.shape[0] // 2
        tot = jnp.sum(gath[pl.ds(half * per, per)], axis=0)
    return fold(tot[:, :lanes]), fold(tot[:, 256 : 256 + lanes])


def moments(gath, half, count, lanes):
    s, q = totals(gath, half, lanes)
    avg = s / count
    inv = lax.rsqrt(q / count - avg * avg + EPSILON)
    return avg, inv


def affine(par, layer, avg, inv):
    lanes = avg.shape[-1]
    scale = par[2 * layer : 2 * layer + 1, :lanes] * inv
    return scale, par[2 * layer + 1 : 2 * layer + 2, :lanes] - avg * scale


def silu(b):
    return b / (1.0 + jnp.exp(-b))


def silu_back(a, b):
    s = 1.0 / (1.0 + jnp.exp(-b))
    return a * s * (1.0 + b * (1.0 - s))


def cells(shape, rows, cols, row0):
    y = lax.broadcasted_iota(jnp.int32, shape, 0) + row0
    x = lax.broadcasted_iota(jnp.int32, shape, 1)
    return (y < rows) & (x < cols)


def put_sums(st, s, q):
    lanes = s.shape[-1]
    st[...] = jnp.zeros(st.shape, f32)
    st[:, :lanes] = s
    st[:, 256 : 256 + lanes] = q


def im2col(ah, al, p, f, ny, pitch, lanes, x0=0, y0=0):
    def pair(t):
        for a in range(2):
            for b in range(2):
                x = f[pl.ds(y0 + 2 * t + a, 2), x0 + b : x0 + b + pitch, :]
                hi, lo = split(x.reshape(2 * pitch, lanes))
                rows = pl.ds(pl.multiple_of(t * 2 * pitch, 2 * pitch), 2 * pitch)
                at = (2 * a + b) * lanes
                ah[p, rows, at : at + lanes] = hi
                al[p, rows, at : at + lanes] = lo

    loop(ny // 2, pair)


def call(kernel, outs, args, specs=None, scratch=(), name="k", out_specs=None, cid=None):
    return pl.pallas_call(
        kernel,
        out_shape=[jax.ShapeDtypeStruct(s, d) for s, d in outs],
        in_specs=specs or [VM] * len(args),
        out_specs=out_specs or [VM] * len(outs),
        scratch_shapes=list(scratch),
        compiler_params=pltpu.CompilerParams(
            vmem_limit_bytes=LIMIT, collective_id=cid, has_side_effects=cid is not None
        ),
        name=name,
    )(*args)


class Net:
    def __init__(self, dims, wide, sems):
        S, K, B = dims
        self.s = lax.axis_index("section")
        self.k = lax.axis_index("slab")
        self.b = lax.axis_index("batch")
        self.K = K
        self.sems = sems
        if wide:
            self.n = S * K * B
            self.me = (self.s * K + self.k) * B + self.b
            self.coords = lambda d: (d // (K * B), (d // B) % K, d % B)
        else:
            self.n = K * B
            self.me = self.k * B + self.b
            self.coords = lambda d: (self.s, d // B, d % B)
        self.halos = []

    def each(self, f):
        def step(p, c):
            f(p)
            return c

        lax.fori_loop(1, self.n, step, 0)

    def enter(self):
        barrier = pltpu.get_barrier_semaphore()
        self.each(
            lambda p: pl.semaphore_signal(
                barrier, inc=1, device_id=self.coords((self.me + p) % self.n), device_id_type=MESH
            )
        )

    def ready(self):
        pl.semaphore_wait(pltpu.get_barrier_semaphore(), self.n - 1)

    def _copy(self, src, dst, p, group):
        return pltpu.make_async_remote_copy(
            src_ref=src,
            dst_ref=dst,
            send_sem=self.sems[2 * group].at[p],
            recv_sem=self.sems[2 * group + 1].at[p],
            device_id=self.coords((self.me + p) % self.n),
            device_id_type=MESH,
        )

    def share(self, src, slots, group=0):
        slots[self.me] = src[...]
        self.each(lambda p: self._copy(src, slots.at[self.me], p, group).start())

    def shared(self, src, slots, group=0):
        n = self.n
        self.each(lambda p: self._copy(src, slots.at[(self.me + n - p) % n], p, group).wait_recv())
        self.each(lambda p: self._copy(src, slots.at[self.me], p, group).wait_send())

    def scatter(self, src, slots, group):
        slots[self.me] = src[self.me]
        n = self.n
        self.each(lambda p: self._copy(src.at[(self.me + p) % n], slots.at[self.me], p, group).start())

    def scattered(self, src, slots, group):
        n = self.n
        self.each(
            lambda p: self._copy(
                src.at[(self.me + p) % n], slots.at[(self.me + n - p) % n], p, group
            ).wait_recv()
        )
        self.each(lambda p: self._copy(src.at[(self.me + p) % n], slots.at[self.me], p, group).wait_send())

    def _side(self, src, dst, j, step):
        return pltpu.make_async_remote_copy(
            src_ref=src,
            dst_ref=dst,
            send_sem=self.sems[-2].at[j],
            recv_sem=self.sems[-1].at[j],
            device_id=(self.s, (self.k + self.K + step) % self.K, self.b),
            device_id_type=MESH,
        )

    def to_left(self, src, dst, j):
        copy = self._side(src, dst, 2 * j, -1)

        @pl.when(self.k > 0)
        def _():
            copy.start()

        self.halos.append((copy, -1))

    def to_right(self, src, dst, j):
        copy = self._side(src, dst, 2 * j + 1, 1)

        @pl.when(self.k < self.K - 1)
        def _():
            copy.start()

        self.halos.append((copy, 1))

    def sides(self):
        @pl.when(self.k > 0)
        def _():
            for copy, step in self.halos:
                if step < 0:
                    copy.wait_send()
                else:
                    copy.wait_recv()

        @pl.when(self.k < self.K - 1)
        def _():
            for copy, step in self.halos:
                if step > 0:
                    copy.wait_send()
                else:
                    copy.wait_recv()


def net_sems(n, halos, groups=1):
    sems = [pltpu.SemaphoreType.DMA((n,))] * (2 * groups)
    if halos:
        sems += [pltpu.SemaphoreType.DMA((2 * halos,))] * 2
    return sems


def toeplitz(w, c0, chans, th, tl, dh, dl):
    def pick(i, j, k):
        if 0 <= j <= 2 and 0 <= k <= 2:
            return w[i * 9 + j * 3 + k, c0 : c0 + chans, :]
        return jnp.zeros((chans, 64), f32)

    def tap(i):
        for r in range(4):
            for s in range(4):
                a, py, b, px = r // 2, r % 2, s // 2, s % 2
                block = (2 * a + b) * 4 + py * 2 + px
                for h in range(2):
                    part = jnp.concatenate([pick(i, r - h, s), pick(i, r - h, s - 1)], axis=1)
                    hi, lo = split(part)
                    rows = slice(block * chans, (block + 1) * chans)
                    th[i, rows, 128 * h : 128 * h + 128] = hi
                    tl[i, rows, 128 * h : 128 * h + 128] = lo
                    if dh is not None:
                        rows = slice((py * 2 + px) * chans, (py * 2 + px + 1) * chans)
                        at = ((1 - a) * 2 + (1 - b)) * 256 + 128 * h
                        dh[2 - i, rows, at : at + 128] = hi
                        dl[2 - i, rows, at : at + 128] = lo

    loop(3, tap)


def source_copies(dims, own, crop, so, sr, ss, rs):
    K = dims[1]
    s = lax.axis_index("section")
    k = lax.axis_index("slab")
    b = lax.axis_index("batch")
    barrier = pltpu.get_barrier_semaphore()
    here, left, right = k, (k + K - 1) % K, (k + 1) % K
    for dev in ((s, left, b), (s, right, b), (1 - s, here, b), (1 - s, left, b), (1 - s, right, b)):
        pl.semaphore_signal(barrier, inc=1, device_id=dev, device_id_type=MESH)

    def copy(j, src, dst, dev):
        return pltpu.make_async_remote_copy(
            src_ref=src,
            dst_ref=dst,
            send_sem=ss.at[j],
            recv_sem=rs.at[j],
            device_id=dev,
            device_id_type=MESH,
        )

    so[2:4] = own[...]
    lefts = [
        copy(0, own, so.at[4:6], (s, left, b)),
        copy(1, crop, sr.at[4:6], (1 - s, left, b)),
    ]
    rights = [
        copy(2, own, so.at[0:2], (s, right, b)),
        copy(3, crop, sr.at[0:2], (1 - s, right, b)),
    ]
    across = copy(4, crop, sr.at[2:4], (1 - s, here, b))

    def start():
        pl.semaphore_wait(barrier, 5)
        across.start()

        @pl.when(k > 0)
        def _():
            for c in lefts:
                c.start()

        @pl.when(k < K - 1)
        def _():
            for c in rights:
                c.start()

    def finish():
        across.wait()

        @pl.when(k > 0)
        def _():
            for c in lefts:
                c.wait_send()
            for c in rights:
                c.wait_recv()

        @pl.when(k < K - 1)
        def _():
            for c in rights:
                c.wait_send()
            for c in lefts:
                c.wait_recv()

        @pl.when(k == 0)
        def _():
            so[0:2] = jnp.zeros((2, 16, OWN), f32)
            sr[0:2] = jnp.zeros((2, 16, CROP), f32)

        @pl.when(k == K - 1)
        def _():
            so[4:6] = jnp.zeros((2, 16, OWN), f32)
            sr[4:6] = jnp.zeros((2, 16, CROP), f32)

    return start, finish


def weights_kernel(
    dims, w2, w3, w4, up, own, crop,
    t2h, t2l, t3h, t3l, t4h, t4l, tuh, tul, d2h, d2l, d3h, d3l, d4h, d4l,
    uph, upl, uh, ul, ubh, ubl, so, sr, usc, ss, rs,
):
    start, finish = source_copies(dims, own, crop, so, sr, ss, rs)
    start()
    toeplitz(w2, 0, 32, t2h, t2l, d2h, d2l)
    toeplitz(w3, 128, 64, t3h, t3l, d3h, d3l)
    toeplitz(w4, 0, 64, t4h, t4l, d4h, d4l)
    toeplitz(w3, 0, 128, tuh, tul, None, None)
    for ip in range(2):
        for q in range(4):
            hi, lo = split(up[ip * 4 + q])
            uph[ip * 128 : ip * 128 + 128, q * 128 : q * 128 + 128] = hi
            upl[ip * 128 : ip * 128 + 128, q * 128 : q * 128 + 128] = lo
    usc[...] = jnp.zeros(usc.shape, f32)
    ah, al = uph[...], upl[...]
    for i in range(3):
        def block(ab, i=i):
            rows = pl.ds(pl.multiple_of(ab * 512, 512), 512)
            p = dot3(ah, al, tuh[i, rows, :], tul[i, rows, :], NN)
            out = pl.ds(pl.multiple_of(ab * 128, 128), 128)
            for ip in range(2):
                usc[slot_of(i, ip), out, :] += p[ip * 128 : ip * 128 + 128]

        loop(4, block)
    for e in range(4):
        for ab in range(4):
            hi, lo = split(usc[e, ab * 128 : ab * 128 + 128, :])
            uh[e, ab * 128 : ab * 128 + 128, :] = hi
            ul[e, ab * 128 : ab * 128 + 128, :] = lo
            p = (3, 1, 2, 0)[e]
            at = (3 - ab) * 256
            ubh[p, :, at : at + 256] = hi
            ubl[p, :, at : at + 256] = lo
    finish()


def slot_of(i, ip):
    pd = (ip + i + 1) % 2
    t = (pd + i - 1) // 2 - pd + 1
    return pd * 2 + t


def weights(dims, w2, w3, w4, up, own, crop):
    outs = []
    for shape in [
        (3, 512, 256), (3, 1024, 256), (3, 1024, 256), (3, 2048, 256),
        (3, 128, 1024), (3, 256, 1024), (3, 256, 1024),
        (256, 512), (4, 512, 256), (4, 128, 1024),
    ]:
        outs += [(shape, bf16)] * 2
    outs += [((6, 16, OWN), f32), ((6, 16, CROP), f32)]
    return call(
        functools.partial(weights_kernel, dims),
        outs,
        (w2, w3, w4, up, own, crop),
        scratch=[pltpu.VMEM((4, 512, 256), f32)] + [pltpu.SemaphoreType.DMA((5,))] * 2,
        name="weights",
        cid=1,
    )


def first_kernel(dims, so, sr, w1, co, sc, r1, r1c, sh, sl, gath, col, cor, st, ch, cl, *sems):
    net = Net(dims, True, sems)
    net.enter()
    wh, wl = split(w1[...])
    for p in range(6):
        own = so[p]
        crop = sr[p]
        for ab in range(4):
            a, b = ab // 2, ab % 2
            rows = slice(p * 64 + ab * 16, p * 64 + ab * 16 + 16)
            hi, lo = split(own if ab == 0 else pltpu.roll(own, OWN - 40 * a - b, 1))
            sh[rows, :] = hi
            sl[rows, :] = lo
            hi, lo = split(crop if ab == 0 else pltpu.roll(crop, CROP - 32 * a - b, 1))
            ch[rows, :] = hi
            cl[rows, :] = lo

    def conv(d):
        rows = pl.ds(pl.multiple_of(d * 64, 64), 192)
        r1[d, :OWN, :] = dot3(sh[rows, :], sl[rows, :], wh, wl, TN)
        r1[d, OWN:, :] = jnp.zeros((1440 - OWN, 128), f32)
        r1c[d] = dot3(ch[rows, :], cl[rows, :], wh, wl, TN)

    net.ready()
    net.to_left(co.at[0], cor, 0)
    net.to_right(co.at[0], col, 0)
    loop(4, conv)
    tot = jnp.zeros((1, 128), f32), jnp.zeros((1, 128), f32)
    for d in range(2):
        def part(t, c):
            x = r1[1 + d, pl.ds(pl.multiple_of(t * 160, 160), 160), :].reshape(4, 40, 128)
            x = jnp.where(cells(x.shape, 33, 33, 4 * t), x, 0.0)
            return c[0] + jnp.sum(x, axis=0), c[1] + jnp.sum(x * x, axis=0)

        s, q = lax.fori_loop(0, 9, part, (jnp.zeros((40, 128), f32), jnp.zeros((40, 128), f32)))
        m = sc[1 + d]
        tot = (
            tot[0] + m * jnp.sum(s, axis=0, keepdims=True),
            tot[1] + m * jnp.sum(q, axis=0, keepdims=True),
        )
    put_sums(st, *tot)
    net.share(st, gath)
    net.shared(st, gath)
    net.sides()


def first(dims, so, sr, w1, co, sc):
    n = dims[0] * dims[1] * dims[2]
    return call(
        functools.partial(first_kernel, dims),
        [
            ((4, 1440, 128), f32), ((4, CROP, 128), f32), ((384, OWN), bf16), ((384, OWN), bf16),
            ((n, 1, 512), f32), (co.shape[1:], f32), (co.shape[1:], f32),
        ],
        (so, sr, w1, co, sc),
        specs=[VM, VM, VM, HB, SM],
        out_specs=[VM] * 5 + [HB] * 2,
        scratch=[pltpu.VMEM((1, 512), f32)] + [pltpu.VMEM((384, CROP), bf16)] * 2 + net_sems(n, 1),
        name="first",
        cid=2,
    )


def second_kernel(dims, r1, r1c, g1, par, th, tl, sc, r2, r2c, ah, al, gath, hl, hr, st, f, bh, bl, *sems):
    net = Net(dims, True, sems)
    net.enter()
    half = net.s
    f[...] = jnp.zeros(f.shape, f32)
    scale, off = affine(par, 0, *moments(g1, half, sc[8] * 4356.0, 128))
    scale_c, off_c = affine(par, 0, *moments(g1, 1 - half, sc[9] * 4356.0, 128))

    def crop(p):
        m = sc[4 + p]

        def rows(t):
            x = silu(r1c[p, pl.ds(4 * t, 4)] * scale_c + off_c)
            f[pl.ds(4 * t, 4), :32, :] = jnp.where(m > 0, x, 0.0)

        loop(7, rows)
        im2col(bh, bl, p, f, 24, 24, 128)

    loop(4, crop)

    def conv_crop(d):
        acc = jnp.zeros((576, 256), f32)
        for i in range(3):
            acc += dot3(bh[d + i], bl[d + i], th[i], tl[i], NN)
        r2c[d] = acc

    conv_crop(0)
    net.ready()
    net.to_left(r2c.at[0], hr, 0)
    conv_crop(1)
    net.to_right(r2c.at[1], hl, 0)
    def own(p):
        m = sc[p]

        def rows(t):
            x = silu(r1[p, pl.ds(4 * t, 4)] * scale + off)
            f[pl.ds(4 * t, 4), :40, :] = jnp.where(m > 0, x, 0.0)

        loop(9, rows)
        im2col(ah, al, p, f, 32, 32, 128)

    loop(4, own)

    def conv(d):
        acc = jnp.zeros((1024, 256), f32)
        for i in range(3):
            acc += dot3(ah[d + i], al[d + i], th[i], tl[i], NN)
        r2[d] = acc

    loop(2, conv)
    s = jnp.zeros((1, 256), f32)
    q = jnp.zeros((1, 256), f32)
    for d in range(2):
        def part(t, c):
            x = r2[d, pl.ds(pl.multiple_of(t * 128, 128), 128), :].reshape(16, 8, 256)
            return c[0] + jnp.sum(x, axis=0), c[1] + jnp.sum(x * x, axis=0)

        ps, pq = lax.fori_loop(0, 8, part, (jnp.zeros((8, 256), f32), jnp.zeros((8, 256), f32)))
        s = s + sc[1 + d] * jnp.sum(ps, axis=0, keepdims=True)
        q = q + sc[1 + d] * jnp.sum(pq, axis=0, keepdims=True)
    put_sums(st, s, q)
    net.share(st, gath)
    net.shared(st, gath)
    net.sides()


def second(dims, r1, r1c, g1, par, th, tl, sc):
    n = dims[0] * dims[1] * dims[2]
    return call(
        functools.partial(second_kernel, dims),
        [
            ((2, 1024, 256), f32), ((2, 576, 256), f32), ((4, 1024, 512), bf16), ((4, 1024, 512), bf16),
            ((n, 1, 512), f32), ((576, 256), f32), ((576, 256), f32),
        ],
        (r1.reshape(4, 36, 40, 128), r1c.reshape(4, 28, 32, 128), g1, par, th, tl, sc),
        specs=[VM] * 6 + [SM],
        out_specs=[VM] * 5 + [HB] * 2,
        scratch=[pltpu.VMEM((1, 512), f32), pltpu.VMEM((36, 48, 128), f32)]
        + [pltpu.VMEM((4, 576, 512), bf16)] * 2
        + net_sems(n, 1),
        name="second",
        cid=3,
    )


def field_sums(r, d, n, rows, cols, mask):
    def part(t, c):
        x = r[d, pl.ds(pl.multiple_of(t * 96, 96), 96), :].reshape(4, 24, 256)
        x = jnp.where(cells(x.shape, rows, cols, 4 * t), x, 0.0)
        return c[0] + jnp.sum(x, axis=0), c[1] + jnp.sum(x * x, axis=0)

    zero = jnp.zeros((24, 256), f32)
    full = n // 96
    s, q = lax.fori_loop(0, full, part, (zero, zero))
    if n % 96:
        x = r[d, full * 96 : n, :].reshape((n - full * 96) // 24, 24, 256)
        x = jnp.where(cells(x.shape, rows, cols, 4 * full), x, 0.0)
        s = s + jnp.sum(x, axis=0)
        q = q + jnp.sum(x * x, axis=0)
    return mask * jnp.sum(s, axis=0, keepdims=True), mask * jnp.sum(q, axis=0, keepdims=True)


def third_kernel(
    dims, r2, r2c, hl, hr, co, col, cor, g2, par, th, tl, uh, ul, sc,
    pooled, r3, ah, al, cuh, cul, gath, nl, nr, st, f, f2, *sems,
):
    net = Net(dims, False, sems)
    net.enter()
    half = net.s
    scale, off = affine(par, 1, *moments(g2, half, sc[8] * 4096.0, 256))

    def pool(t):
        rows = pl.ds(pl.multiple_of(t * 64, 64), 64)
        v = sc[1] * silu(r2[0, rows, :] * scale + off) + sc[2] * silu(r2[1, rows, :] * scale + off)
        v = v[:, :128] + v[:, 128:]
        v = (v + pltpu.roll(v, 64, 1)) * 0.125
        pooled[rows, :] = v[:, :64]

    loop(16, pool)
    scale_c, off_c = affine(par, 1, *moments(g2, 1 - half, sc[9] * 4096.0, 256))
    f[...] = jnp.zeros(f.shape, f32)

    def put(p, get):
        m = sc[4 + p]

        def rows(t):
            x = silu(get(t) * scale_c + off_c)
            f[pl.ds(4 * t, 4), :24, :] = jnp.where(m > 0, x, 0.0)

        loop(6, rows)
        im2col(ah, al, p, f, 24, 24, 256)

    put(0, lambda t: hl[pl.ds(4 * t, 4)])
    loop(2, lambda p: put(p + 1, lambda t: r2c[p, pl.ds(4 * t, 4)]))
    put(3, lambda t: hr[pl.ds(4 * t, 4)])
    f2[...] = jnp.zeros(f2.shape, f32)
    for p, (src, m) in enumerate(((col, sc[4]), (co, sc[5]), (cor, sc[7]))):
        f2[:24, :24, :] = jnp.where(m > 0, src[...], 0.0)
        im2col(cuh, cul, p, f2, 24, 24, 128)

    def conv(d):
        acc = jnp.zeros((576, 256), f32)
        for i in range(3):
            acc += dot3(ah[d + i], al[d + i], th[i], tl[i], NN)
        for t in range(2):
            acc += dot3(cuh[d + t], cul[d + t], uh[2 * d + t], ul[2 * d + t], NN)
        r3[d] = acc

    conv(0)
    net.ready()
    net.to_left(r3.at[0], nr, 0)
    conv(1)
    net.to_right(r3.at[1], nl, 0)
    s0, q0 = field_sums(r3, 0, 576, 23, 23, sc[5])
    s1, q1 = field_sums(r3, 1, 576, 23, 23, sc[6])
    put_sums(st, s0 + s1, q0 + q1)
    net.share(st, gath)
    net.shared(st, gath)
    net.sides()


def third(dims, r2, r2c, hl, hr, co, col, cor, g2, par, th, tl, uh, ul, sc):
    n = dims[1] * dims[2]
    return call(
        functools.partial(third_kernel, dims),
        [
            ((1024, 64), f32), ((2, 576, 256), f32),
            ((4, 576, 1024), bf16), ((4, 576, 1024), bf16), ((3, 576, 512), bf16), ((3, 576, 512), bf16),
            ((n, 1, 512), f32), ((576, 256), f32), ((576, 256), f32),
        ],
        (
            r2, r2c.reshape(2, 24, 24, 256), hl.reshape(24, 24, 256), hr.reshape(24, 24, 256),
            co, col, cor, g2, par, th, tl, uh, ul, sc,
        ),
        specs=[VM] * 13 + [SM],
        out_specs=[VM] * 7 + [HB] * 2,
        scratch=[pltpu.VMEM((1, 512), f32), pltpu.VMEM((26, 32, 256), f32), pltpu.VMEM((26, 32, 128), f32)]
        + net_sems(n, 1),
        name="third",
        cid=4,
    )


def fourth_kernel(
    dims, r3, hl, hr, g3, og, par, th, tl, sc, r4, ah, al, gath, nl, nr, ogl, ogr, st, f, *sems
):
    net = Net(dims, False, sems)
    net.enter()
    scale, off = affine(par, 2, *moments(g3, None, sc[9] * 2116.0, 256))
    f[...] = jnp.zeros(f.shape, f32)

    def put(p, get):
        m = sc[4 + p]

        def rows(t):
            x = silu(get(t) * scale + off)
            f[pl.ds(4 * t, 4), :24, :] = jnp.where(m > 0, x, 0.0)

        loop(6, rows)
        im2col(ah, al, p, f, 22, 24, 256)

    put(0, lambda t: hl[pl.ds(4 * t, 4)])
    loop(2, lambda p: put(p + 1, lambda t: r3[p, pl.ds(4 * t, 4)]))
    put(3, lambda t: hr[pl.ds(4 * t, 4)])

    def conv(d):
        acc = jnp.zeros((528, 256), f32)
        for i in range(3):
            acc += dot3(ah[d + i], al[d + i], th[i], tl[i], NN)
        r4[d] = acc

    net.ready()
    net.to_left(og.at[0], ogr, 1)
    net.to_right(og.at[1], ogl, 1)
    conv(0)
    net.to_left(r4.at[0], nr, 0)
    conv(1)
    net.to_right(r4.at[1], nl, 0)
    s0, q0 = field_sums(r4, 0, 528, 22, 22, sc[5])
    s1, q1 = field_sums(r4, 1, 528, 22, 22, sc[6])
    put_sums(st, s0 + s1, q0 + q1)
    net.share(st, gath)
    net.shared(st, gath)
    net.sides()


def fourth(dims, r3, hl, hr, g3, og, par, th, tl, sc):
    n = dims[1] * dims[2]
    return call(
        functools.partial(fourth_kernel, dims),
        [((2, 528, 256), f32), ((4, 528, 1024), bf16), ((4, 528, 1024), bf16), ((n, 1, 512), f32)]
        + [((528, 256), f32)] * 4,
        (r3.reshape(2, 24, 24, 256), hl.reshape(24, 24, 256), hr.reshape(24, 24, 256), g3, og, par, th, tl, sc),
        specs=[VM] * 4 + [HB] + [VM] * 3 + [SM],
        out_specs=[VM] * 4 + [HB] * 4,
        scratch=[pltpu.VMEM((1, 512), f32), pltpu.VMEM((26, 32, 256), f32)] + net_sems(n, 2),
        name="fourth",
        cid=5,
    )


def back_parts(par, layer, avg, inv, r, a):
    lanes = avg.shape[-1]
    normed = (r - avg) * inv
    b = par[2 * layer : 2 * layer + 1, :lanes] * normed + par[2 * layer + 1 : 2 * layer + 2, :lanes]
    return normed, silu_back(a, b)


def response_back(par, layer, avg, inv, tg, tc, count, r, a):
    lanes = avg.shape[-1]
    gain = par[2 * layer : 2 * layer + 1, :lanes]
    normed, bg = back_parts(par, layer, avg, inv, r, a)
    return inv * gain * (bg - (tg + normed * tc) / count)


def output_kernel(dims, r4, og, g4, par, sc, dec, gath, st, *sems):
    net = Net(dims, False, sems)
    net.enter()
    avg, inv = moments(g4, None, sc[9] * 1936.0, 256)
    scale, off = affine(par, 3, avg, inv)
    s = jnp.zeros((1, 256), f32)
    q = jnp.zeros((1, 256), f32)
    for d in range(2):
        m = sc[5 + d]

        def part(t, c):
            rows = pl.ds(pl.multiple_of(t * 48, 48), 48)
            r = r4[d, rows, :]
            b = r * scale + off
            sg = 1.0 / (1.0 + jnp.exp(-b))
            dec[d, rows, :] = m * (b * sg)
            bg = og[d, rows, :] * sg * (1.0 + b * (1.0 - sg))
            normed = (r - avg) * inv
            bg3 = bg.reshape(6, 8, 256)
            return c[0] + jnp.sum(bg3, axis=0), c[1] + jnp.sum(bg3 * normed.reshape(6, 8, 256), axis=0)

        ps, pq = lax.fori_loop(0, 11, part, (jnp.zeros((8, 256), f32), jnp.zeros((8, 256), f32)))
        s = s + m * jnp.sum(ps, axis=0, keepdims=True)
        q = q + m * jnp.sum(pq, axis=0, keepdims=True)
    put_sums(st, s, q)
    net.ready()
    net.share(st, gath)
    net.shared(st, gath)


def output(dims, r4, og, g4, par, sc):
    n = dims[1] * dims[2]
    return call(
        functools.partial(output_kernel, dims),
        [((2, 528, 256), f32), ((n, 1, 512), f32), ((1, 512), f32)],
        (r4, og, g4, par, sc),
        specs=[VM] * 4 + [SM],
        scratch=net_sems(n, 0),
        name="output",
        cid=6,
    )


def fourth_back_kernel(
    dims, r4, r4l, r4r, og, ogl, ogr, g4, g5, r3, g3, par, dh, dl, sc,
    a3, e4, gath, nl, nr, st, f, ah, al, *sems,
):
    net = Net(dims, False, sems)
    net.enter()
    count = sc[9] * 1936.0
    avg, inv = moments(g4, None, count, 256)
    tg, tc = totals(g5, None, 256)
    f[...] = jnp.zeros(f.shape, f32)

    def put(p, get_r, get_a, keep):
        m = sc[4 + p]

        def rows(t):
            e = response_back(par, 3, avg, inv, tg, tc, count, get_r(t), get_a(t))
            e = jnp.where(cells(e.shape, 22, 22, 0) & (m > 0), e, 0.0)
            f[pl.ds(1 + 2 * t, 2), 8:32, :] = e
            if keep is not None:
                e4[keep, pl.ds(2 * t, 2)] = e

        loop(11, rows)
        im2col(ah, al, p, f, 24, 24, 256, x0=7)

    put(0, lambda t: r4l[pl.ds(2 * t, 2)], lambda t: ogl[pl.ds(2 * t, 2)], None)
    loop(
        2,
        lambda p: put(
            p + 1, lambda t: r4[p, pl.ds(2 * t, 2)], lambda t: og[p, pl.ds(2 * t, 2)], p
        ),
    )
    put(3, lambda t: r4r[pl.ds(2 * t, 2)], lambda t: ogr[pl.ds(2 * t, 2)], None)

    def conv(d):
        acc = jnp.zeros((576, 256), f32)
        for i in range(3):
            acc += dot3(ah[d + i], al[d + i], dh[i], dl[i], NT)
        a3[d] = acc

    conv(0)
    net.ready()
    net.to_left(a3.at[0], nr, 0)
    conv(1)
    net.to_right(a3.at[1], nl, 0)
    avg3, inv3 = moments(g3, None, sc[9] * 2116.0, 256)
    s = jnp.zeros((1, 256), f32)
    q = jnp.zeros((1, 256), f32)
    for d in range(2):
        def part(t, c):
            rows = pl.ds(pl.multiple_of(t * 48, 48), 48)
            normed, bg = back_parts(par, 2, avg3, inv3, r3[d, rows, :], a3[d, rows, :])
            bg = bg.reshape(2, 24, 256)
            bg = jnp.where(cells(bg.shape, 23, 23, 2 * t), bg, 0.0)
            return c[0] + jnp.sum(bg, axis=0), c[1] + jnp.sum(bg * normed.reshape(2, 24, 256), axis=0)

        ps, pq = lax.fori_loop(0, 12, part, (jnp.zeros((24, 256), f32), jnp.zeros((24, 256), f32)))
        s = s + sc[5 + d] * jnp.sum(ps, axis=0, keepdims=True)
        q = q + sc[5 + d] * jnp.sum(pq, axis=0, keepdims=True)
    put_sums(st, s, q)
    net.share(st, gath)
    net.shared(st, gath)
    net.sides()


def fourth_back(dims, r4, r4l, r4r, og, ogl, ogr, g4, g5, r3, g3, par, dh, dl, sc):
    box = (22, 24, 256)
    n = dims[1] * dims[2]
    return call(
        functools.partial(fourth_back_kernel, dims),
        [
            ((2, 576, 256), f32), ((2, 22, 24, 256), f32), ((n, 1, 512), f32),
            ((576, 256), f32), ((576, 256), f32), ((1, 512), f32),
        ],
        (
            r4.reshape((2,) + box), r4l.reshape(box), r4r.reshape(box),
            og.reshape((2,) + box), ogl.reshape(box), ogr.reshape(box),
            g4, g5, r3, g3, par, dh, dl, sc,
        ),
        specs=[VM] * 13 + [SM],
        out_specs=[VM] * 3 + [HB] * 2 + [VM],
        scratch=[pltpu.VMEM((26, 40, 256), f32)] + [pltpu.VMEM((4, 576, 1024), bf16)] * 2 + net_sems(n, 1),
        name="fourth_back",
        cid=7,
    )


def unfold(g, i, j, k, chans, out, row0):
    out[i * 9 + j * 3 + k, row0 : row0 + chans, :] = folded(g, j, k, chans)[:, :64]


def folded(g, j, k, chans):
    def block(r, s):
        at = (2 * (r // 2) + s // 2) * 4 + (r % 2) * 2 + s % 2
        return slice(at * chans, (at + 1) * chans)

    x = g[block(j, k), 0:128] + g[block(j + 1, k), 128:256]
    y = g[block(j, k + 1), 0:128] + g[block(j + 1, k + 1), 128:256]
    return x + pltpu.roll(y, 64, 1)


def fourth_weight_kernel(ah, al, e4, dw, g):
    for i in range(3):
        for d in range(2):
            eh, el = split(e4[d])
            v = dot3(ah[d + i], al[d + i], eh, el, TN)
            if d == 0:
                g[...] = v
            else:
                g[...] += v
        for j in range(3):
            for k in range(3):
                unfold(g, i, j, k, 64, dw, 0)


def fourth_weight(ah, al, e4):
    return call(
        fourth_weight_kernel,
        [((27, 64, 64), f32)],
        (ah, al, e4),
        scratch=[pltpu.VMEM((1024, 256), f32)],
        name="fourth_weight",
    )[0]


def third_back_kernel(
    a3, a3l, a3r, r3, r3l, r3r, g3, g6, par, dh, dl, sc, skip, e3, ah, al, f, v
):
    count = sc[9] * 2116.0
    avg, inv = moments(g3, None, count, 256)
    tg, tc = totals(g6, None, 256)
    f[...] = jnp.zeros(f.shape, f32)

    def put(p, get_r, get_a, keep):
        m = sc[4 + p]

        def rows(t):
            e = response_back(par, 2, avg, inv, tg, tc, count, get_r(t), get_a(t))
            e = jnp.where(cells(e.shape, 23, 23, 2 * t) & (m > 0), e, 0.0)
            f[pl.ds(1 + 2 * t, 2), 8:32, :] = e
            if keep is not None:
                e3[keep, pl.ds(2 * t, 2)] = e

        loop(12, rows)
        im2col(ah, al, p, f, 24, 24, 256, x0=7)

    put(0, lambda t: r3l[pl.ds(2 * t, 2)], lambda t: a3l[pl.ds(2 * t, 2)], None)
    loop(
        2,
        lambda p: put(
            p + 1, lambda t: r3[p, pl.ds(2 * t, 2)], lambda t: a3[p, pl.ds(2 * t, 2)], p
        ),
    )
    put(3, lambda t: r3r[pl.ds(2 * t, 2)], lambda t: a3r[pl.ds(2 * t, 2)], None)

    def conv(d):
        acc = jnp.zeros((576, 256), f32)
        for i in range(3):
            acc += dot3(ah[d + i], al[d + i], dh[i], dl[i], NT)
        v[...] = acc.reshape(24, 24, 256)

        def row(t):
            skip[d, 2 * t] = v[t, :, :128]
            skip[d, 2 * t + 1] = v[t, :, 128:]

        loop(24, row)

    loop(2, conv)


def third_back(a3, a3l, a3r, r3, r3l, r3r, g3, g6, par, dh, dl, sc):
    box = (24, 24, 256)
    return call(
        third_back_kernel,
        [((2, 48, 24, 128), f32), ((2, 24, 24, 256), f32), ((4, 576, 1024), bf16), ((4, 576, 1024), bf16)],
        (
            a3.reshape((2,) + box), a3l.reshape(box), a3r.reshape(box),
            r3.reshape((2,) + box), r3l.reshape(box), r3r.reshape(box),
            g3, g6, par, dh, dl, sc,
        ),
        specs=[VM] * 11 + [SM],
        scratch=[pltpu.VMEM((26, 40, 256), f32), pltpu.VMEM((24, 24, 256), f32)],
        name="third_back",
    )


def coarse_back_kernel(ah, al, ubh, ubl, sc, cg):
    acc = jnp.zeros((576, 128), f32)
    for p in range(4):
        acc += dot3(ah[p], al[p], ubh[p], ubl[p], NT)
    cg[...] = acc * sc[5]


def coarse_back(ah, al, ubh, ubl, sc):
    return call(
        coarse_back_kernel,
        [((576, 128), f32)],
        (ah, al, ubh, ubl, sc),
        specs=[VM] * 4 + [SM],
        name="coarse_back",
    )[0]


def third_weight_kernel(ah, al, cuh, cul, e3, tuh, tul, uph, upl, dw, dup, g, gu, gd, eh, el):
    for d in range(2):
        hi, lo = split(e3[d])
        eh[d] = hi
        el[d] = lo
    for i in range(3):
        g[:1024, :] = dot3(ah[i], al[i], eh[0], el[0], TN) + dot3(ah[i + 1], al[i + 1], eh[1], el[1], TN)
        for j in range(3):
            for k in range(3):
                unfold(g, i, j, k, 64, dw, 128)
    for pd in range(2):
        for t in range(2):
            gu[pd * 2 + t] = dot3(cuh[pd + t], cul[pd + t], eh[pd], el[pd], TN)
    gd[...] = jnp.zeros(gd.shape, f32)
    for i in range(3):
        def block(ab, i=i):
            out = pl.ds(pl.multiple_of(ab * 128, 128), 128)
            p = jnp.concatenate([gu[slot_of(i, 0), out, :], gu[slot_of(i, 1), out, :]], axis=0)
            ph, plo = split(p)
            rows = pl.ds(pl.multiple_of(ab * 512, 512), 512)
            gd[...] += dot3(ph, plo, tuh[i, rows, :], tul[i, rows, :], NT)
            g[rows, :] = dot3(uph[...], upl[...], ph, plo, TN)

        loop(4, block)
        for j in range(3):
            for k in range(3):
                unfold(g, i, j, k, 128, dw, 0)
    for ip in range(2):
        for q in range(4):
            dup[ip * 4 + q] = gd[ip * 128 : ip * 128 + 128, q * 128 : q * 128 + 128]


def third_weight(ah, al, cuh, cul, e3, tuh, tul, uph, upl):
    return call(
        third_weight_kernel,
        [((27, 192, 64), f32), ((8, 128, 128), f32)],
        (ah, al, cuh, cul, e3, tuh, tul, uph, upl),
        scratch=[
            pltpu.VMEM((2048, 256), f32), pltpu.VMEM((4, 512, 256), f32), pltpu.VMEM((256, 512), f32),
            pltpu.VMEM((2, 576, 256), bf16), pltpu.VMEM((2, 576, 256), bf16),
        ],
        name="third_weight",
    )


def skip_kernel(dims, skip, pg, r2, g2, par, sc, si, bg2, gath, st, *sems):
    net = Net(dims, False, sems)
    net.enter()
    avg, inv = moments(g2, net.s, sc[8] * 4096.0, 256)
    oy, ox = si[1], si[2]
    qx = ox // 2
    rx = ox - 2 * qx
    odd = rx > 0
    s = jnp.zeros((1, 256), f32)
    q = jnp.zeros((1, 256), f32)
    lane = lax.broadcasted_iota(jnp.int32, (32, 128), 1)
    pad = jnp.zeros((8, 128), f32)
    for d in range(2):
        def placed(row):
            r = row - oy
            v = skip[d, jnp.clip(r, 0, 47)]
            v = jnp.where((r >= 0) & (r < 48), v, 0.0)
            v = jnp.concatenate([v, pad], axis=0)
            v = jnp.where(odd, pltpu.roll(v, 64, 1), v)
            return jnp.where(lane < 64, pltpu.roll(v, qx + rx, 0), pltpu.roll(v, qx, 0))

        def part(t, c):
            pv = pg[t] * 0.125
            pv = jnp.concatenate([pv, pv], axis=1)
            a = jnp.concatenate([placed(2 * t) + pv, placed(2 * t + 1) + pv], axis=1)
            rows = pl.ds(pl.multiple_of(t * 32, 32), 32)
            normed, bg = back_parts(par, 1, avg, inv, r2[d, rows, :], a)
            bg = sc[1 + d] * bg
            bg2[d, rows, :] = bg
            bg = bg.reshape(4, 8, 256)
            return c[0] + jnp.sum(bg, axis=0), c[1] + jnp.sum(bg * normed.reshape(4, 8, 256), axis=0)

        ps, pq = lax.fori_loop(0, 32, part, (jnp.zeros((8, 256), f32), jnp.zeros((8, 256), f32)))
        s = s + jnp.sum(ps, axis=0, keepdims=True)
        q = q + jnp.sum(pq, axis=0, keepdims=True)
    put_sums(st, s, q)
    net.ready()
    net.share(st, gath)
    net.shared(st, gath)


def skip_back(dims, skip, pg, r2, g2, par, sc, si):
    n = dims[1] * dims[2]
    return call(
        functools.partial(skip_kernel, dims),
        [((2, 1024, 256), f32), ((n, 1, 512), f32), ((1, 512), f32)],
        (skip, pg, r2, g2, par, sc, si),
        specs=[VM] * 5 + [SM, SM],
        scratch=net_sems(n, 0),
        name="skip_back",
        cid=8,
    )


def second_back_kernel(dims, bg2, r2, g2, g7, par, dh, dl, sc, e2, a1, fl, fr, f, ah, al, side, *sems):
    net = Net(dims, False, sems)
    net.enter()
    count = sc[8] * 4096.0
    avg, inv = moments(g2, net.s, count, 256)
    tg, tc = totals(g7, None, 256)
    k = par[2:3, :] * inv
    f[...] = jnp.zeros(f.shape, f32)

    def put(p):
        m = sc[1 + p]

        def rows(t):
            at = pl.ds(pl.multiple_of(t * 64, 64), 64)
            normed = (r2[p, at, :] - avg) * inv
            e = k * (bg2[p, at, :] - m * ((tg + normed * tc) / count))
            e2[p, at, :] = e
            f[pl.ds(1 + 2 * t, 2), 8:40, :] = e.reshape(2, 32, 256)

        loop(16, rows)
        im2col(ah, al, p, f, 34, 40, 256, x0=7)

    loop(2, put)
    rh = dh[...].reshape(384, 1024)
    rl = dl[...].reshape(384, 1024)
    v = dot3(ah[0], al[0], rh, rl, NT)
    a1[1, :1360] = v[:, :128]
    a1[0, :1360] = v[:, 128:256]
    side[0, :1360] = v[:, 256:]
    side[0, 1360:] = jnp.zeros((48, 128), f32)
    net.ready()
    net.to_left(side.at[0], fr, 0)
    v = dot3(ah[1], al[1], rh, rl, NT)
    side[1, :1360] = v[:, :128]
    side[1, 1360:] = jnp.zeros((48, 128), f32)
    net.to_right(side.at[1], fl, 0)
    a1[1, :1360] += v[:, 128:256]
    a1[0, :1360] += v[:, 256:]
    for d in range(2):
        a1[d, 1360:] = jnp.zeros((48, 128), f32)
    net.sides()


def second_back(dims, bg2, r2, g2, g7, par, dh, dl, sc):
    n = dims[1] * dims[2]
    return call(
        functools.partial(second_back_kernel, dims),
        [((2, 1024, 256), f32), ((2, OWN, 128), f32), ((OWN, 128), f32), ((OWN, 128), f32)],
        (bg2, r2, g2, g7, par, dh, dl, sc),
        specs=[VM] * 7 + [SM],
        out_specs=[VM] * 2 + [HB] * 2,
        scratch=[pltpu.VMEM((36, 56, 256), f32)]
        + [pltpu.VMEM((2, 1360, 1024), bf16)] * 2
        + [pltpu.VMEM((2, OWN, 128), f32)]
        + net_sems(n, 1),
        name="second_back",
        cid=9,
    )


def second_weight_kernel(ah, al, e2, dw, g, eh, el):
    for d in range(2):
        hi, lo = split(e2[d])
        eh[d] = hi
        el[d] = lo
    for i in range(3):
        g[...] = dot3(ah[i], al[i], eh[0], el[0], TN) + dot3(ah[i + 1], al[i + 1], eh[1], el[1], TN)
        for j in range(3):
            for k in range(3):
                t = i * 9 + j * 3 + k
                v = folded(g, j, k, 32)
                v = v if t % 2 == 0 else pltpu.roll(v, 64, 1)
                at = 64 * (t % 2)
                dw[32 * (t // 2) : 32 * (t // 2) + 32, at : at + 64] = v[:, at : at + 64]
    dw[416:, 64:] = jnp.zeros((32, 64), f32)


def second_weight(ah, al, e2):
    return call(
        second_weight_kernel,
        [((448, 128), f32)],
        (ah, al, e2),
        scratch=[pltpu.VMEM((512, 256), f32), pltpu.VMEM((2, 1024, 256), bf16), pltpu.VMEM((2, 1024, 256), bf16)],
        name="second_weight",
    )[0]


def first_sums_kernel(dims, a1p, sl, sr, r1, g1, par, sc, a1, gath, nl, nr, st, *sems):
    net = Net(dims, False, sems)
    net.enter()
    avg, inv = moments(g1, net.s, sc[8] * 4356.0, 128)
    s = jnp.zeros((1, 128), f32)
    q = jnp.zeros((1, 128), f32)
    for d in range(2):
        other = sl if d == 0 else sr
        here = sc[10 + d]

        def part(t, c):
            rows = pl.ds(pl.multiple_of(t * 160, 160), 160)
            a = a1p[d, rows, :] + jnp.where(here > 0, other[rows, :], 0.0)
            a1[d, rows, :] = a
            normed, bg = back_parts(par, 0, avg, inv, r1[1 + d, rows, :], a)
            bg = bg.reshape(4, 40, 128)
            bg = jnp.where(cells(bg.shape, 33, 33, 4 * t), bg, 0.0)
            return c[0] + jnp.sum(bg, axis=0), c[1] + jnp.sum(bg * normed.reshape(4, 40, 128), axis=0)

        ps, pq = lax.fori_loop(0, 8, part, (jnp.zeros((40, 128), f32), jnp.zeros((40, 128), f32)))
        rows = slice(1280, OWN)
        a = a1p[d, rows, :] + jnp.where(here > 0, other[rows, :], 0.0)
        a1[d, rows, :] = a
        rows = slice(1280, 1320)
        normed, bg = back_parts(par, 0, avg, inv, r1[1 + d, rows, :], a[:40])
        bg = jnp.where(lax.broadcasted_iota(jnp.int32, (40, 128), 0) < 33, bg, 0.0)
        ps = ps + bg
        pq = pq + bg * normed
        s = s + sc[1 + d] * jnp.sum(ps, axis=0, keepdims=True)
        q = q + sc[1 + d] * jnp.sum(pq, axis=0, keepdims=True)
        if d == 0:
            net.ready()
            net.to_left(a1.at[0], nr, 0)
        else:
            net.to_right(a1.at[1], nl, 0)
    put_sums(st, s, q)
    net.share(st, gath)
    net.shared(st, gath)
    net.sides()


def first_sums(dims, a1p, sl, sr, r1, g1, par, sc):
    n = dims[1] * dims[2]
    return call(
        functools.partial(first_sums_kernel, dims),
        [((2, OWN, 128), f32), ((n, 1, 512), f32), ((OWN, 128), f32), ((OWN, 128), f32), ((1, 512), f32)],
        (a1p, sl, sr, r1, g1, par, sc),
        specs=[VM] * 6 + [SM],
        out_specs=[VM] * 2 + [HB] * 2 + [VM],
        scratch=net_sems(n, 1),
        name="first_sums",
        cid=10,
    )


def first_back_kernel(
    dims, a1, a1l, a1r, r1, g1, g8, par, w1, sh, sl, keep, pick, gather, dw2, sums, sc,
    ig, red, eh, el, bucket, slots, mine, *sems,
):
    net = Net(dims, True, sems)
    net.enter()
    count = sc[8] * 4356.0
    avg, inv = moments(g1, net.s, count, 128)
    tg, tc = totals(g8, None, 128)
    wh, wl = split(w1[...])

    def put(p, get_a):
        m = sc[p]
        eh[p, 1280:, :] = jnp.zeros((OWN - 1280, 128), bf16)
        el[p, 1280:, :] = jnp.zeros((OWN - 1280, 128), bf16)

        def rows(t):
            at = pl.ds(pl.multiple_of(t * 80, 80), 80)
            e = response_back(par, 0, avg, inv, tg, tc, count, r1[p, at, :], get_a(at))
            e = e.reshape(2, 40, 128)
            e = jnp.where(cells(e.shape, 33, 33, 2 * t) & (m > 0), e, 0.0)
            hi, lo = split(e.reshape(80, 128))
            eh[p, at, :] = hi
            el[p, at, :] = lo

        loop(17, rows)

    loop(2, lambda p: put(p + 1, lambda at: a1[p, at, :]))
    acc = jnp.zeros((192, 128), f32)
    for d in range(2):
        rows = slice((d + 1) * 64, (d + 1) * 64 + 192)
        acc += dot3(sh[rows, :], sl[rows, :], eh[d + 1], el[d + 1], NN)
    lane = lax.broadcasted_iota(jnp.int32, (32, 128), 1)
    tot = jnp.zeros((32, 128), f32)
    for tap in range(4):
        v = jnp.zeros((32, 128), f32)
        for q in range(4):
            x = acc if q == tap else pltpu.roll(acc, ((tap - q) % 4) * 32, 1)
            hi, lo = split(x)
            sel = pick[tap * 4 + q]
            v += dot(sel, hi, NN) + dot(sel, lo, NN)
        tot += jnp.where(lane // 32 == tap, v, 0.0)

    per = 512 // net.n

    def store(x, row0):
        for r in range(0, x.shape[0], per):
            bucket[(row0 + r) // per] = x[r : r + per]

    store(dw2[...], 0)
    store(tot, 448)
    store(sums[...], 480)
    store(jnp.zeros((16, 128), f32), 496)
    net.ready()
    net.scatter(bucket, slots, 0)
    put(0, lambda at: a1l[at, :])
    put(3, lambda at: a1r[at, :])
    parts = [dot3(wh, wl, eh[p], el[p], NT) for p in range(4)]
    net.scattered(bucket, slots, 0)
    mine[...] = jnp.sum(slots[...], axis=0)
    net.share(mine, red, 1)
    for d in range(2):
        tot = jnp.zeros((16, OWN), f32)
        for ab in range(4):
            v = jnp.zeros((16, OWN), f32)
            for i in range(3):
                at = i * 64 + ab * 16
                v += parts[d + 2 - i][at : at + 16, :]
            a, b = ab // 2, ab % 2
            tot += v if ab == 0 else pltpu.roll(v, 40 * a + b, 1)
        tot = tot * (keep[...] * sc[1 + d])
        rows = []
        for y in range(34):
            tile, off = (40 * y) // 128, (40 * y) % 128
            pair = []
            for px in range(2):
                v = tot[8 * px : 8 * px + 8, 128 * tile : 128 * tile + 128]
                if off + 34 > 128:
                    nxt = tot[8 * px : 8 * px + 8, 128 * tile + 128 : 128 * tile + 256]
                    v = jnp.where(lane[:8] >= off, v, nxt)
                pair.append(v if off == 0 else pltpu.roll(v, 128 - off, 1))
            rows.append(jnp.concatenate(pair, axis=1))
        hi, lo = split(jnp.concatenate(rows, axis=0))
        out = dot(hi, gather[...], NT) + dot(lo, gather[...], NT)
        ig[d] = out.reshape(34, 8, 68)
    net.shared(mine, red, 1)


def first_back(dims, a1, a1l, a1r, r1, g1, g8, par, w1, sh, sl, keep, dw2, sums, sc):
    n = dims[0] * dims[1] * dims[2]
    per = 512 // n
    return call(
        functools.partial(first_back_kernel, dims),
        [((2, 34, 8, 68), f32), ((n, per, 128), f32)],
        (a1, a1l, a1r, r1, g1, g8, par, w1, sh, sl, keep, tap_picks(), deinterleave(), dw2, sums, sc),
        specs=[VM] * 15 + [SM],
        scratch=[pltpu.VMEM((4, OWN, 128), bf16)] * 2
        + [pltpu.VMEM((n, per, 128), f32)] * 2
        + [pltpu.VMEM((per, 128), f32)]
        + net_sems(n, 0, 2),
        name="first_back",
        cid=11,
    )


def tap_picks():
    sel = np.zeros((4, 4, 32, 192), np.float32)
    for t in range(27):
        i, j, k = t // 9, (t // 3) % 3, t % 3
        for q in range(4):
            r, s = j + q // 2, k + q % 2
            for c in range(4):
                col = i * 64 + (2 * (r // 2) + s // 2) * 16 + (s % 2) * 8 + (r % 2) * 4 + c
                sel[t % 4, q, (t // 4) * 4 + c, col] = 1.0
    return jnp.asarray(sel.reshape(16, 32, 192), bf16)


def deinterleave():
    sel = np.zeros((68, 256), np.float32)
    for x in range(68):
        sel[x, (x % 2) * 128 + x // 2] = 1.0
    return jnp.asarray(sel, bf16)


def source_kernel(img, keep, even, sc, si, own, crop):
    oy, ox = si[1], si[2]
    x = lax.broadcasted_iota(jnp.int32, (68, 256), 0)
    lane = lax.broadcasted_iota(jnp.int32, (68, 256), 1)
    at = 2 * (lane % 128) + lane // 128
    pick = ((x == at + ox) & (lane % 128 < 26)).astype(f32).astype(bf16)
    r = lax.broadcasted_iota(jnp.int32, (208, 272), 0)
    c = lax.broadcasted_iota(jnp.int32, (208, 272), 1)
    rows = (c == r + 4 * oy).astype(f32).astype(bf16)
    lane = lax.broadcasted_iota(jnp.int32, (8, 128), 1)

    def flat(v, side, pitch, tiles):
        out = [[jnp.zeros((8, 128), f32) for _ in range(tiles)] for _ in range(2)]
        for y in range(side):
            tile, off = (pitch * y) // 128, (pitch * y) % 128
            for px in range(2):
                p = v[8 * y : 8 * y + 8, 128 * px : 128 * px + 128]
                p = p if off == 0 else pltpu.roll(p, off, 1)
                if off + side > 128:
                    out[px][tile + 1] += jnp.where(lane < off, p, 0.0)
                    p = jnp.where(lane >= off, p, 0.0)
                out[px][tile] += p
        return jnp.concatenate([jnp.concatenate(o, axis=1) for o in out], axis=0)

    for d in range(2):
        hi, lo = split(img[d].reshape(272, 68))
        k = keep[...] * sc[1 + d]
        own[d] = flat(dot(hi, even[...], NN) + dot(lo, even[...], NN), 34, 40, OWN // 128) * k
        hi = dot(rows, hi, NN).astype(bf16)
        lo = dot(rows, lo, NN).astype(bf16)
        crop[d] = flat(dot(hi, pick, NN) + dot(lo, pick, NN), 26, 32, CROP // 128) * k


def source_planes(img, keep, sc, si):
    return call(
        source_kernel,
        [((2, 16, OWN), f32), ((2, 16, CROP), f32)],
        (img, keep, deinterleave(), sc, si),
        specs=[VM] * 3 + [SM, SM],
        name="source_planes",
    )


def body(
    dims,
    image, modality_mask, extents, crop_offsets, coarse,
    conv_first, gain_first, shift_first, conv_second, gain_second, shift_second,
    up_kernel, conv_third, gain_third, shift_third, conv_fourth, gain_fourth, shift_fourth,
    pool_grad, output_grad,
):
    S, K, B = dims
    n = S * K * B
    section = lax.axis_index("section")
    slab = lax.axis_index("slab")
    batch = lax.axis_index("batch")
    planes = image.shape[2]
    enc_len = extents[section]
    dec_len = extents[1 - section]
    window = slab * planes + jnp.arange(-1, planes + 1, dtype=jnp.int32)
    enc_mask = ((window < enc_len[batch]) & (window >= 0)).astype(f32)
    dec_mask = ((window < dec_len[batch]) & (window >= 0)).astype(f32)
    sc = jnp.concatenate(
        [
            enc_mask, dec_mask,
            jnp.stack(
                [
                    jnp.sum(enc_len).astype(f32), jnp.sum(dec_len).astype(f32),
                    (slab > 0).astype(f32), (slab < K - 1).astype(f32),
                ]
            ),
            jnp.zeros((4,), f32),
        ]
    )
    offsets = crop_offsets[0, 0]
    si = jnp.concatenate([jnp.stack([section.astype(jnp.int32)]), offsets, jnp.zeros((5,), jnp.int32)])

    def lanes(v):
        return jnp.tile(v, 256 // v.shape[0])

    par = jnp.stack(
        [
            lanes(v)
            for v in (
                gain_first, shift_first, gain_second, shift_second,
                gain_third, shift_third, gain_fourth, shift_fourth,
            )
        ]
    )
    w1 = jnp.stack(
        [
            jnp.pad(conv_first, ((0, 0), (qy, 1 - qy), (qx, 1 - qx), (0, 0), (0, 0)))
            for qy in range(2)
            for qx in range(2)
        ],
        axis=4,
    )
    w1 = w1.reshape(3, 2, 2, 2, 2, 4, 128).transpose(0, 1, 3, 4, 2, 5, 6).reshape(192, 128)

    keep = jnp.tile(modality_mask[0, 0].astype(f32), 4)[:, None]
    img = image[0, 0].transpose(0, 1, 3, 2).reshape(2, 34, 8, 68)
    own, crop = source_planes(img, keep, sc, si)
    swap = [(i, 1 - i) for i in range(2)]

    og = output_grad[0, 0].reshape(2, 22, 2, 22, 2, 64).transpose(0, 1, 3, 2, 4, 5).reshape(2, 22, 22, 256)
    og = jnp.pad(og, ((0, 0), (0, 0), (0, 2), (0, 0))).reshape(2, 528, 256)

    (
        t2h, t2l, t3h, t3l, t4h, t4l, tuh, tul, d2h, d2l, d3h, d3l, d4h, d4l,
        uph, upl, uh, ul, ubh, ubl, so, sr,
    ) = weights(
        dims,
        conv_second.reshape(27, 32, 64), conv_third.reshape(27, 192, 64),
        conv_fourth.reshape(27, 64, 64), up_kernel.reshape(8, 128, 128), own, crop,
    )

    co = coarse[0, 0]
    r1, r1c, sh, sl, g1, col, cor = first(dims, so, sr, w1, co, sc)
    r2, r2c, a2h, a2l, g2, hl, hr = second(dims, r1, r1c, g1, par, t2h, t2l, sc)
    pooled, r3, a3h, a3l, cuh, cul, g3, r3l, r3r = third(
        dims, r2, r2c, hl, hr, co[0], col, cor, g2, par, t3h, t3l, uh, ul, sc
    )
    r4, a4h, a4l, g4, r4l, r4r, ogl, ogr = fourth(dims, r3, r3l, r3r, g3, og, par, t4h, t4l, sc)
    dec, g5, st5 = output(dims, r4, og, g4, par, sc)
    a3, e4, g6, a3l_, a3r_, st6 = fourth_back(
        dims, r4, r4l, r4r, og, ogl, ogr, g4, g5, r3, g3, par, d4h, d4l, sc
    )
    skip, e3, e3h, e3l = third_back(a3, a3l_, a3r_, r3, r3l, r3r, g3, g6, par, d3h, d3l, sc)
    skip = lax.ppermute(skip, "section", swap)
    dw3, dup = third_weight(a3h, a3l, cuh, cul, e3.reshape(2, 576, 256), tuh, tul, uph, upl)
    dw4 = fourth_weight(a4h, a4l, e4.reshape(2, 528, 256))
    dw4, dw3, dup = lax.psum((dw4, dw3, dup), ("section", "slab", "batch"))
    coarse_grad = coarse_back(e3h, e3l, ubh, ubl, sc)
    bg2, g7, st7 = skip_back(dims, skip, pool_grad[0, 0, 0], r2, g2, par, sc, si)
    e2, a1p, s_l, s_r = second_back(dims, bg2, r2, g2, g7, par, d2h, d2l, sc)
    dw2 = second_weight(a2h, a2l, e2)
    a1, g8, a1l, a1r, st8 = first_sums(dims, a1p, s_l, s_r, r1, g1, par, sc)
    sums = jnp.concatenate([st8, st7, st6, st5], axis=0).reshape(16, 128)
    ig, red = first_back(dims, a1, a1l, a1r, r1, g1, g8, par, w1, sh, sl, keep, dw2, sums, sc)

    red = red.reshape(512, 128)
    dw2 = red[:448].reshape(14, 32, 2, 64).transpose(0, 2, 1, 3).reshape(28, 32, 64)[:27]
    dw1 = red[448:476].reshape(7, 4, 4, 32).transpose(0, 2, 1, 3).reshape(28, 4, 32)[:27]
    sums = red[480:496].reshape(4, 2, 256)

    def affine_grads(layer, width):
        t = sums[layer].reshape(2, 256 // width, width).sum(axis=1)
        return t[1], t[0]

    gg1, gs1 = affine_grads(0, 32)
    gg2, gs2 = affine_grads(1, 64)
    gg3, gs3 = affine_grads(2, 64)
    gg4, gs4 = affine_grads(3, 64)

    dec = dec.reshape(2, 22, 24, 2, 2, 64)[:, :, :22].transpose(0, 1, 3, 2, 4, 5).reshape(2, 44, 44, 64)
    ig = ig.reshape(2, 68, 4, 68).transpose(0, 1, 3, 2)
    return (
        pooled.reshape(1, 1, 1, 32, 32, 64),
        dec[None, None],
        ig[None, None],
        coarse_grad.reshape(1, 1, 1, 24, 24, 128),
        dw1.reshape(3, 3, 3, 4, 32),
        gg1,
        gs1,
        dw2.reshape(3, 3, 3, 32, 64),
        gg2,
        gs2,
        dup.reshape(2, 2, 2, 128, 128),
        dw3.reshape(3, 3, 3, 192, 64),
        gg3,
        gs3,
        dw4.reshape(3, 3, 3, 64, 64),
        gg4,
        gs4,
    )


def solution(mesh):
    dims = tuple(mesh.shape[a] for a in ("section", "slab", "batch"))
    field = P("section", "batch", "slab", None, None, None)
    volume = P("section", "batch", None)
    rep = P()
    return jax.shard_map(
        functools.partial(body, dims),
        mesh=mesh,
        in_specs=(field, volume, rep, volume, field) + (rep,) * 13 + (field, field),
        out_specs=(field,) * 4 + (rep,) * 13,
        check_vma=False,
    )
```

```python
import functools
import types

import jax
import jax.numpy as jnp
import numpy as np
from jax import lax
from jax.experimental import pallas as pl
from jax.experimental.pallas import tpu as pltpu
from jax.sharding import PartitionSpec as P

f32 = jnp.float32
bf16 = jnp.bfloat16
MESH = pl.DeviceIdType.MESH
EPSILON = 1e-05
NN = (((1,), (0,)), ((), ()))
NT = (((1,), (1,)), ((), ()))
TN = (((0,), (0,)), ((), ()))
VM = pl.BlockSpec(memory_space=pltpu.VMEM)
SM = pl.BlockSpec(memory_space=pltpu.SMEM)
HB = pl.BlockSpec(memory_space=pl.ANY)
LIMIT = 62 * 2**20

OWN = 1408
CROP = 896


def split(x):
    hi = x.astype(bf16)
    return hi, (x - hi.astype(f32)).astype(bf16)


def dot(a, b, dims):
    return lax.dot_general(a, b, dims, preferred_element_type=f32)


def dot3(ah, al, bh, bl, dims):
    return dot(ah, bh, dims) + dot(al, bh, dims) + dot(ah, bl, dims)


def loop(n, f, unroll=1):
    def step(t, c):
        f(t)
        return c

    lax.fori_loop(0, n, step, 0, unroll=unroll)


def fold(v):
    lanes = v.shape[-1]
    v = jnp.broadcast_to(v, (8, lanes))
    if lanes == 256:
        h = v[:, :128] + v[:, 128:]
        h = h + pltpu.roll(h, 64, 1)
        h = jnp.concatenate([h, h], axis=1)
    else:
        h = v + pltpu.roll(v, 64, 1)
        h = h + pltpu.roll(h, 32, 1)
    return h[:1]


def totals(gath, half, lanes):
    if half is None:
        tot = jnp.sum(gath[...], axis=0)
    else:
        per = gath.shape[0] // 2
        tot = jnp.sum(gath[pl.ds(half * per, per)], axis=0)
    return fold(tot[:, :lanes]), fold(tot[:, 256 : 256 + lanes])


def moments(gath, half, count, lanes):
    s, q = totals(gath, half, lanes)
    avg = s / count
    inv = lax.rsqrt(q / count - avg * avg + EPSILON)
    return avg, inv


def affine(par, layer, avg, inv):
    lanes = avg.shape[-1]
    scale = par[2 * layer : 2 * layer + 1, :lanes] * inv
    return scale, par[2 * layer + 1 : 2 * layer + 2, :lanes] - avg * scale


def silu(b):
    return b / (1.0 + jnp.exp(-b))


def silu_back(a, b):
    s = 1.0 / (1.0 + jnp.exp(-b))
    return a * s * (1.0 + b * (1.0 - s))


def cells(shape, rows, cols, row0):
    y = lax.broadcasted_iota(jnp.int32, shape, 0) + row0
    x = lax.broadcasted_iota(jnp.int32, shape, 1)
    return (y < rows) & (x < cols)


def put_sums(st, s, q):
    lanes = s.shape[-1]
    st[...] = jnp.zeros(st.shape, f32)
    st[:, :lanes] = s
    st[:, 256 : 256 + lanes] = q


def im2col(ah, al, p, f, ny, pitch, lanes, x0=0):
    def pair(t):
        for a in range(2):
            for b in range(2):
                x = f[pl.ds(2 * t + a, 2), x0 + b : x0 + b + pitch, :]
                hi, lo = split(x.reshape(2 * pitch, lanes))
                rows = pl.ds(pl.multiple_of(p * (ny * pitch) + t * (2 * pitch), 16), 2 * pitch)
                at = (2 * a + b) * lanes
                ah[rows, at : at + lanes] = hi
                al[rows, at : at + lanes] = lo

    loop(ny // 2, pair)


def launch(body, name, cid, ins, outs, scratch):
    names = [i[0] for i in ins] + [o[0] for o in outs] + [x[0] for x in scratch]

    def kernel(*refs):
        body(types.SimpleNamespace(**dict(zip(names, refs))))

    res = pl.pallas_call(
        kernel,
        out_shape=[jax.ShapeDtypeStruct(o[1], o[2]) for o in outs],
        in_specs=[i[2] for i in ins],
        out_specs=[o[3] for o in outs],
        scratch_shapes=[x[1] for x in scratch],
        compiler_params=pltpu.CompilerParams(
            vmem_limit_bytes=LIMIT, collective_id=cid, has_side_effects=cid is not None
        ),
        name=name,
    )(*[i[1] for i in ins])
    return types.SimpleNamespace(**dict(zip([o[0] for o in outs], res)))


def both(name, shape):
    return [(name + "h", pltpu.VMEM(shape, bf16)), (name + "l", pltpu.VMEM(shape, bf16))]


def both_out(name, shape):
    return [(name + "h", shape, bf16, HB), (name + "l", shape, bf16, HB)]


def sems(*sizes):
    return [(f"sem{i}", pltpu.SemaphoreType.DMA((n,))) for i, n in enumerate(sizes)]


class Moves:
    def __init__(self, sem):
        self.sem = sem
        self.used = 0
        self.pending = []

    def start(self, src, dst):
        copy = pltpu.make_async_copy(src, dst, self.sem.at[self.used])
        self.used += 1
        copy.start()
        return copy

    def out(self, *pairs):
        for src, dst in pairs:
            self.pending.append(self.start(src, dst))

    def finish(self):
        for copy in self.pending:
            copy.wait()


def fetch(mv, *pairs):
    copies = [mv.start(src, dst) for src, dst in pairs]

    def wait():
        for copy in copies:
            copy.wait()

    return wait


class Net:
    def __init__(self, dims, wide, sems):
        S, K, B = dims
        self.s = lax.axis_index("section")
        self.k = lax.axis_index("slab")
        self.b = lax.axis_index("batch")
        self.K = K
        self.sems = sems
        if wide:
            self.n = S * K * B
            self.me = (self.s * K + self.k) * B + self.b
            self.coords = lambda d: (d // (K * B), (d // B) % K, d % B)
        else:
            self.n = K * B
            self.me = self.k * B + self.b
            self.coords = lambda d: (self.s, d // B, d % B)
        self.halos = []

    def each(self, f):
        def step(p, c):
            f(p)
            return c

        lax.fori_loop(1, self.n, step, 0)

    def enter(self):
        barrier = pltpu.get_barrier_semaphore()
        self.each(
            lambda p: pl.semaphore_signal(
                barrier, inc=1, device_id=self.coords((self.me + p) % self.n), device_id_type=MESH
            )
        )

    def ready(self):
        pl.semaphore_wait(pltpu.get_barrier_semaphore(), self.n - 1)

    def _copy(self, src, dst, p, group):
        return pltpu.make_async_remote_copy(
            src_ref=src,
            dst_ref=dst,
            send_sem=self.sems[2 * group].at[p],
            recv_sem=self.sems[2 * group + 1].at[p],
            device_id=self.coords((self.me + p) % self.n),
            device_id_type=MESH,
        )

    def share(self, src, slots, group=0):
        slots[self.me] = src[...]
        self.each(lambda p: self._copy(src, slots.at[self.me], p, group).start())

    def shared(self, src, slots, group=0):
        n = self.n
        self.each(lambda p: self._copy(src, slots.at[(self.me + n - p) % n], p, group).wait_recv())
        self.each(lambda p: self._copy(src, slots.at[self.me], p, group).wait_send())

    def scatter(self, src, slots, group):
        slots[self.me] = src[self.me]
        n = self.n
        self.each(lambda p: self._copy(src.at[(self.me + p) % n], slots.at[self.me], p, group).start())

    def scattered(self, src, slots, group):
        n = self.n
        self.each(
            lambda p: self._copy(
                src.at[(self.me + p) % n], slots.at[(self.me + n - p) % n], p, group
            ).wait_recv()
        )
        self.each(lambda p: self._copy(src.at[(self.me + p) % n], slots.at[self.me], p, group).wait_send())

    def _side(self, src, dst, j, step):
        return pltpu.make_async_remote_copy(
            src_ref=src,
            dst_ref=dst,
            send_sem=self.sems[-2].at[j],
            recv_sem=self.sems[-1].at[j],
            device_id=(self.s, (self.k + self.K + step) % self.K, self.b),
            device_id_type=MESH,
        )

    def to_left(self, src, dst, j):
        copy = self._side(src, dst, 2 * j, -1)

        @pl.when(self.k > 0)
        def _():
            copy.start()

        self.halos.append((copy, -1))

    def to_right(self, src, dst, j):
        copy = self._side(src, dst, 2 * j + 1, 1)

        @pl.when(self.k < self.K - 1)
        def _():
            copy.start()

        self.halos.append((copy, 1))

    def sides(self):
        @pl.when(self.k > 0)
        def _():
            for copy, step in self.halos:
                if step < 0:
                    copy.wait_send()
                else:
                    copy.wait_recv()

        @pl.when(self.k < self.K - 1)
        def _():
            for copy, step in self.halos:
                if step > 0:
                    copy.wait_send()
                else:
                    copy.wait_recv()


def toeplitz(w, c0, chans, th, tl, dh=None, dl=None):
    def tap(i):
        zero = jnp.zeros((chans, 64), f32)
        none = jnp.zeros((chans, 128), bf16)
        for s in range(4):
            part = []
            for j in range(3):
                here = w[i * 9 + j * 3 + s, c0 : c0 + chans, :] if s <= 2 else zero
                prev = w[i * 9 + j * 3 + s - 1, c0 : c0 + chans, :] if s >= 1 else zero
                part.append(split(jnp.concatenate([here, prev], axis=1)))
            for r in range(4):
                a, py, b, px = r // 2, r % 2, s // 2, s % 2
                block = (2 * a + b) * 4 + py * 2 + px
                for h in range(2):
                    hi, lo = part[r - h] if 0 <= r - h <= 2 else (none, none)
                    rows = slice(block * chans, (block + 1) * chans)
                    th[i, rows, 128 * h : 128 * h + 128] = hi
                    tl[i, rows, 128 * h : 128 * h + 128] = lo
                    if dh is not None:
                        rows = slice((py * 2 + px) * chans, (py * 2 + px + 1) * chans)
                        at = ((1 - a) * 2 + (1 - b)) * 256 + 128 * h
                        dh[2 - i, rows, at : at + 128] = hi
                        dl[2 - i, rows, at : at + 128] = lo

    loop(3, tap)


def slot_of(i, ip):
    pd = (ip + i + 1) % 2
    t = (pd + i - 1) // 2 - pd + 1
    return pd * 2 + t


def compose(r):
    r.usc[...] = jnp.zeros(r.usc.shape, f32)
    ah, al = r.uph[...], r.upl[...]
    for i in range(3):
        def block(ab, i=i):
            rows = pl.ds(pl.multiple_of(ab * 512, 512), 512)
            p = dot3(ah, al, r.tuh[i, rows, :], r.tul[i, rows, :], NN)
            out = pl.ds(pl.multiple_of(ab * 128, 128), 128)
            for ip in range(2):
                r.usc[slot_of(i, ip), out, :] += p[ip * 128 : ip * 128 + 128]

        loop(4, block)
    for e in range(4):
        for ab in range(4):
            hi, lo = split(r.usc[e, ab * 128 : ab * 128 + 128, :])
            r.uh[e, ab * 128 : ab * 128 + 128, :] = hi
            r.ul[e, ab * 128 : ab * 128 + 128, :] = lo
            p = (3, 1, 2, 0)[e]
            at = (3 - ab) * 256
            r.ubh[p, :, at : at + 256] = hi
            r.ubl[p, :, at : at + 256] = lo


def source_copies(dims, own, crop, so, sr, ss, rs):
    K = dims[1]
    s = lax.axis_index("section")
    k = lax.axis_index("slab")
    b = lax.axis_index("batch")
    here, left, right = k, (k + K - 1) % K, (k + 1) % K

    def copy(j, src, dst, dev):
        return pltpu.make_async_remote_copy(
            src_ref=src,
            dst_ref=dst,
            send_sem=ss.at[j],
            recv_sem=rs.at[j],
            device_id=dev,
            device_id_type=MESH,
        )

    so[2:4] = own[...]
    lefts = [
        copy(0, own, so.at[4:6], (s, left, b)),
        copy(1, crop, sr.at[4:6], (1 - s, left, b)),
    ]
    rights = [
        copy(2, own, so.at[0:2], (s, right, b)),
        copy(3, crop, sr.at[0:2], (1 - s, right, b)),
    ]
    across = copy(4, crop, sr.at[2:4], (1 - s, here, b))

    def start():
        across.start()

        @pl.when(k > 0)
        def _():
            for c in lefts:
                c.start()

        @pl.when(k < K - 1)
        def _():
            for c in rights:
                c.start()

    def finish():
        across.wait()

        @pl.when(k > 0)
        def _():
            for c in lefts:
                c.wait_send()
            for c in rights:
                c.wait_recv()

        @pl.when(k < K - 1)
        def _():
            for c in rights:
                c.wait_send()
            for c in lefts:
                c.wait_recv()

        @pl.when(k == 0)
        def _():
            so[0:2] = jnp.zeros((2, 16, OWN), f32)
            sr[0:2] = jnp.zeros((2, 16, CROP), f32)

        @pl.when(k == K - 1)
        def _():
            so[4:6] = jnp.zeros((2, 16, OWN), f32)
            sr[4:6] = jnp.zeros((2, 16, CROP), f32)

    return start, finish


def field_sums(r, d, n, rows, cols, mask):
    base = d * n

    def part(t, c):
        x = r[pl.ds(pl.multiple_of(base + t * 96, 16), 96), :].reshape(4, 24, 256)
        x = jnp.where(cells(x.shape, rows, cols, 4 * t), x, 0.0)
        return c[0] + jnp.sum(x, axis=0), c[1] + jnp.sum(x * x, axis=0)

    zero = jnp.zeros((24, 256), f32)
    full = n // 96
    s, q = lax.fori_loop(0, full, part, (zero, zero))
    if n % 96:
        x = r[base + full * 96 : base + n, :].reshape((n - full * 96) // 24, 24, 256)
        x = jnp.where(cells(x.shape, rows, cols, 4 * full), x, 0.0)
        s = s + jnp.sum(x, axis=0)
        q = q + jnp.sum(x * x, axis=0)
    return mask * jnp.sum(s, axis=0, keepdims=True), mask * jnp.sum(q, axis=0, keepdims=True)


def back_parts(par, layer, avg, inv, r, a):
    lanes = avg.shape[-1]
    normed = (r - avg) * inv
    b = par[2 * layer : 2 * layer + 1, :lanes] * normed + par[2 * layer + 1 : 2 * layer + 2, :lanes]
    return normed, silu_back(a, b)


def response_back(par, layer, avg, inv, tg, tc, count, r, a):
    lanes = avg.shape[-1]
    gain = par[2 * layer : 2 * layer + 1, :lanes]
    normed, bg = back_parts(par, layer, avg, inv, r, a)
    return inv * gain * (bg - (tg + normed * tc) / count)


def folded(g, j, k, chans):
    def block(r, s):
        at = (2 * (r // 2) + s // 2) * 4 + (r % 2) * 2 + s % 2
        return slice(at * chans, (at + 1) * chans)

    x = g[block(j, k), 0:128] + g[block(j + 1, k), 128:256]
    y = g[block(j, k + 1), 0:128] + g[block(j + 1, k + 1), 128:256]
    return x + pltpu.roll(y, 64, 1)


def tap_picks():
    sel = np.zeros((4, 4, 32, 192), np.float32)
    for t in range(27):
        i, j, k = t // 9, (t // 3) % 3, t % 3
        for q in range(4):
            r, s = j + q // 2, k + q % 2
            for c in range(4):
                col = i * 64 + (2 * (r // 2) + s // 2) * 16 + (s % 2) * 8 + (r % 2) * 4 + c
                sel[t % 4, q, (t // 4) * 4 + c, col] = 1.0
    return jnp.asarray(sel.reshape(16, 32, 192), bf16)


def deinterleave():
    sel = np.zeros((68, 256), np.float32)
    for x in range(68):
        sel[x, (x % 2) * 128 + x // 2] = 1.0
    return jnp.asarray(sel, bf16)


def prepare_kernel(r):
    s = lax.axis_index("section")
    k = lax.axis_index("slab")
    b = lax.axis_index("batch")
    ends = (r.ext[s, b], r.ext[1 - s, b])
    for h in range(2):
        for p in range(4):
            g = 2 * k - 1 + p
            r.sc[4 * h + p] = jnp.where((g >= 0) & (g < ends[h]), 1.0, 0.0)
        tot = jnp.int32(0)
        for v in range(r.ext.shape[1]):
            tot = tot + (r.ext[s, v] if h == 0 else r.ext[1 - s, v])
        r.sc[8 + h] = tot.astype(f32)
    r.sc[10] = jnp.where(k > 0, 1.0, 0.0)
    r.sc[11] = jnp.where(k < r.slabs - 1, 1.0, 0.0)
    for j in range(12, 16):
        r.sc[j] = jnp.float32(0.0)
    for j, v in enumerate((r.v0, r.v1, r.v2, r.v3, r.v4, r.v5, r.v6, r.v7)):
        v = v[...]
        while v.shape[1] < 256:
            v = jnp.concatenate([v, v], axis=1)
        r.par[j : j + 1, :] = v
    row = lax.broadcasted_iota(jnp.int32, (16, 1), 0) % 4
    col = jnp.zeros((16, 1), f32)
    for c in range(4):
        col = jnp.where(row == c, r.mods[0, c].astype(f32), col)
    r.keep[...] = col
    img, keep, even, sc, own, crop = r.img, r.keep, r.even, r.sc, r.own, r.crop
    oy, ox = r.si[1], r.si[2]
    x = lax.broadcasted_iota(jnp.int32, (68, 256), 0)
    lane = lax.broadcasted_iota(jnp.int32, (68, 256), 1)
    at = 2 * (lane % 128) + lane // 128
    pick = ((x == at + ox) & (lane % 128 < 26)).astype(f32).astype(bf16)
    r = lax.broadcasted_iota(jnp.int32, (208, 272), 0)
    c = lax.broadcasted_iota(jnp.int32, (208, 272), 1)
    rows = (c == r + 4 * oy).astype(f32).astype(bf16)
    lane = lax.broadcasted_iota(jnp.int32, (8, 128), 1)

    def flat(v, side, pitch, tiles):
        out = [[jnp.zeros((8, 128), f32) for _ in range(tiles)] for _ in range(2)]
        for y in range(side):
            tile, off = (pitch * y) // 128, (pitch * y) % 128
            for px in range(2):
                p = v[8 * y : 8 * y + 8, 128 * px : 128 * px + 128]
                p = p if off == 0 else pltpu.roll(p, off, 1)
                if off + side > 128:
                    out[px][tile + 1] += jnp.where(lane < off, p, 0.0)
                    p = jnp.where(lane >= off, p, 0.0)
                out[px][tile] += p
        return jnp.concatenate([jnp.concatenate(o, axis=1) for o in out], axis=0)

    for d in range(2):
        hi, lo = split(img[d].reshape(272, 68))
        k = keep[...] * sc[1 + d]
        own[d] = flat(dot(hi, even[...], NN) + dot(lo, even[...], NN), 34, 40, OWN // 128) * k
        hi = dot(rows, hi, NN).astype(bf16)
        lo = dot(rows, lo, NN).astype(bf16)
        crop[d] = flat(dot(hi, pick, NN) + dot(lo, pick, NN), 26, 32, CROP // 128) * k


def prepare(dims, img, ext, mods, si, vectors):
    def body(r):
        r.slabs = dims[1]
        prepare_kernel(r)

    return launch(
        body, "prepare", None,
        [("img", img, VM), ("even", deinterleave(), VM), ("ext", ext, SM), ("mods", mods, SM), ("si", si, SM)]
        + [(f"v{j}", v.reshape(1, -1), VM) for j, v in enumerate(vectors)],
        [("own", (2, 16, OWN), f32, VM), ("crop", (2, 16, CROP), f32, VM), ("par", (8, 256), f32, VM),
         ("keep", (16, 1), f32, VM), ("sc", (16,), f32, SM)],
        [],
    )


def tap_spread():
    sel = np.zeros((4, 192, 112), np.float32)
    for t in range(27):
        i, j, k = t // 9, (t // 3) % 3, t % 3
        for q in range(4):
            r, s = j + q // 2, k + q % 2
            for c in range(4):
                row = i * 64 + (2 * (r // 2) + s // 2) * 16 + (s % 2) * 8 + (r % 2) * 4 + c
                sel[q, row, t * 4 + c] = 1.0
    return jnp.asarray(sel, bf16)


def first_weights(r):
    r.wf4[...] = jnp.zeros(r.wf4.shape, f32)
    w = r.wf[...]
    r.wf4[:108, :] = jnp.concatenate([w, w, w, w], axis=1)
    hi, lo = split(r.wf4[...])
    lane = lax.broadcasted_iota(jnp.int32, (192, 128), 1) // 32
    wh = jnp.zeros((192, 128), f32)
    wl = jnp.zeros((192, 128), f32)
    for q in range(4):
        wh += jnp.where(lane == q, dot(r.spread[q], hi, NN), 0.0)
        wl += jnp.where(lane == q, dot(r.spread[q], lo, NN), 0.0)
    r.w1h[...] = wh.astype(bf16)
    r.w1l[...] = wl.astype(bf16)


def first_stage(r):
    for p in range(6):
        own = r.so[p]
        crop = r.sr[p]
        for ab in range(4):
            a, b = ab // 2, ab % 2
            rows = slice(p * 64 + ab * 16, p * 64 + ab * 16 + 16)
            hi, lo = split(own if ab == 0 else pltpu.roll(own, OWN - 40 * a - b, 1))
            r.sh[rows, :] = hi
            r.sl[rows, :] = lo
            hi, lo = split(crop if ab == 0 else pltpu.roll(crop, CROP - 32 * a - b, 1))
            r.ch[rows, :] = hi
            r.cl[rows, :] = lo
    for w, out in ((r.w1h, r.wdh), (r.w1l, r.wdl)):
        out[...] = jnp.zeros(out.shape, bf16)
        out[:192, :128] = w[...]
        out[64:, 128:] = w[...]
    wh, wl = r.wdh[...], r.wdl[...]
    for d in (0, 2):
        rows = slice(d * 64, d * 64 + 256)
        v = dot3(r.sh[rows, :], r.sl[rows, :], wh, wl, TN)
        r.r1[d, :OWN, :] = v[:, :128]
        r.r1[d + 1, :OWN, :] = v[:, 128:]
        v = dot3(r.ch[rows, :], r.cl[rows, :], wh, wl, TN)
        r.r1c[d] = v[:, :128]
        r.r1c[d + 1] = v[:, 128:]
    for d in range(4):
        r.r1[d, OWN:, :] = jnp.zeros((1440 - OWN, 128), f32)
    s = jnp.zeros((1, 128), f32)
    q = jnp.zeros((1, 128), f32)
    for d in range(2):
        def part(t, c):
            x = r.r1[1 + d, pl.ds(pl.multiple_of(t * 160, 160), 160), :].reshape(4, 40, 128)
            x = jnp.where(cells(x.shape, 33, 33, 4 * t), x, 0.0)
            return c[0] + jnp.sum(x, axis=0), c[1] + jnp.sum(x * x, axis=0)

        ps, pq = lax.fori_loop(0, 9, part, (jnp.zeros((40, 128), f32), jnp.zeros((40, 128), f32)))
        s = s + r.sc[1 + d] * jnp.sum(ps, axis=0, keepdims=True)
        q = q + r.sc[1 + d] * jnp.sum(pq, axis=0, keepdims=True)
    put_sums(r.st1, s, q)


def front_kernel(dims, r):
    net = Net(dims, True, [r.sem0, r.sem1, r.sem2, r.sem3, r.sem4, r.sem5])
    net.enter()
    mv = Moves(r.sem8)
    first_weights(r)
    toeplitz(r.w2, 0, 32, r.t2h, r.t2l, r.d2h, r.d2l)
    mv.out((r.d2h, r.od2h), (r.d2l, r.od2l), (r.w1h, r.ow1h), (r.w1l, r.ow1l))
    net.ready()
    start, finish = source_copies(dims, r.own, r.crop, r.so, r.sr, r.sem6, r.sem7)
    start()
    net.to_left(r.co.at[0], r.cor, 0)
    net.to_right(r.co.at[0], r.col, 0)
    toeplitz(r.w3, 128, 64, r.t3h, r.t3l, r.d3h, r.d3l)
    mv.out((r.t3h, r.ot3h), (r.t3l, r.ot3l), (r.d3h, r.od3h), (r.d3l, r.od3l))
    finish()
    first_stage(r)
    mv.out((r.sh, r.osh), (r.sl, r.osl), (r.r1, r.or1))
    net.share(r.st1, r.g1, 0)
    toeplitz(r.w3, 0, 128, r.tuh, r.tul)
    for ip in range(2):
        for q in range(4):
            hi, lo = split(r.up[ip * 4 + q])
            r.uph[ip * 128 : ip * 128 + 128, q * 128 : q * 128 + 128] = hi
            r.upl[ip * 128 : ip * 128 + 128, q * 128 : q * 128 + 128] = lo
    mv.out((r.tuh, r.otuh), (r.tul, r.otul), (r.uph, r.ouph), (r.upl, r.oupl))
    net.shared(r.st1, r.g1, 0)

    half = net.s
    f = r.f
    f[...] = jnp.zeros(f.shape, f32)
    scale_c, off_c = affine(r.par, 0, *moments(r.g1, 1 - half, r.sc[9] * 4356.0, 128))

    def crop(p):
        m = r.sc[4 + p]

        def rows(t):
            x = r.r1c[p, pl.ds(pl.multiple_of(t * 128, 128), 128), :].reshape(4, 32, 128)
            f[pl.ds(4 * t, 4), :32, :] = jnp.where(m > 0, silu(x * scale_c + off_c), 0.0)

        loop(7, rows)
        im2col(r.ah, r.al, p, f, 24, 24, 128)

    loop(4, crop)
    conv(r.r2c, r.ah, r.al, r.t2h, r.t2l, 576, NN)
    net.to_left(r.r2c.at[0:576], r.hr, 1)
    net.to_right(r.r2c.at[576:1152], r.hl, 1)
    mv.out((r.r2c, r.or2c))
    scale, off = affine(r.par, 0, *moments(r.g1, half, r.sc[8] * 4356.0, 128))

    def own(p):
        m = r.sc[p]

        def rows(t):
            x = r.r1[p, pl.ds(pl.multiple_of(t * 160, 160), 160), :].reshape(4, 40, 128)
            f[pl.ds(4 * t, 4), :40, :] = jnp.where(m > 0, silu(x * scale + off), 0.0)

        loop(9, rows)
        im2col(r.ah, r.al, p, f, 32, 32, 128)

    loop(4, own)
    mv.out((r.ah, r.oah), (r.al, r.oal))
    conv(r.r2, r.ah, r.al, r.t2h, r.t2l, 1024, NN)
    mv.out((r.r2, r.or2))
    s = jnp.zeros((1, 256), f32)
    q = jnp.zeros((1, 256), f32)
    for d in range(2):
        def part(t, c):
            x = r.r2[pl.ds(pl.multiple_of(d * 1024 + t * 128, 128), 128), :].reshape(16, 8, 256)
            return c[0] + jnp.sum(x, axis=0), c[1] + jnp.sum(x * x, axis=0)

        ps, pq = lax.fori_loop(0, 8, part, (jnp.zeros((8, 256), f32), jnp.zeros((8, 256), f32)))
        s = s + r.sc[1 + d] * jnp.sum(ps, axis=0, keepdims=True)
        q = q + r.sc[1 + d] * jnp.sum(pq, axis=0, keepdims=True)
    put_sums(r.st2, s, q)
    net.share(r.st2, r.g2, 1)
    compose(r)
    mv.out((r.uh, r.ouh), (r.ul, r.oul), (r.ubh, r.oubh), (r.ubl, r.oubl))
    net.shared(r.st2, r.g2, 1)
    net.sides()
    mv.finish()


def conv(out, ah, al, th, tl, rows, dims):
    for i in range(3):
        at = slice(i * rows, (i + 2) * rows)
        v = dot3(ah[at, :], al[at, :], th[i], tl[i], dims)
        if i == 0:
            out[...] = v
        else:
            out[...] += v


def front(dims, own, crop, wf, w2, w3, up, co, par, sc):
    n = dims[0] * dims[1] * dims[2]
    V = pltpu.VMEM
    forms = [("t3", (3, 1024, 256)), ("d2", (3, 128, 1024)), ("d3", (3, 256, 1024)), ("tu", (3, 2048, 256)),
             ("up", (256, 512)), ("u", (4, 512, 256)), ("ub", (4, 128, 1024)), ("s", (384, OWN)),
             ("a", (4096, 512)), ("w1", (192, 128))]
    outs = [("g1", (n, 1, 512), f32, VM), ("g2", (n, 1, 512), f32, VM),
            ("or1", (4, 1440, 128), f32, HB), ("or2", (2048, 256), f32, HB), ("or2c", (1152, 256), f32, HB),
            ("col", co.shape[1:], f32, HB), ("cor", co.shape[1:], f32, HB),
            ("hl", (576, 256), f32, HB), ("hr", (576, 256), f32, HB)]
    scratch = []
    for name, shape in forms:
        outs += both_out("o" + name, shape)
        scratch += both(name, shape)
    scratch += both("t2", (3, 512, 256)) + both("c", (384, CROP)) + both("wd", (256, 256))
    scratch += [("st1", V((1, 512), f32)), ("st2", V((1, 512), f32)), ("so", V((6, 16, OWN), f32)),
                ("sr", V((6, 16, CROP), f32)), ("wf4", V((112, 128), f32)), ("usc", V((4, 512, 256), f32)),
                ("r1", V((4, 1440, 128), f32)), ("r1c", V((4, CROP, 128), f32)), ("r2", V((2048, 256), f32)),
                ("r2c", V((1152, 256), f32)), ("f", V((36, 48, 128), f32))]
    return launch(
        functools.partial(front_kernel, dims), "front", 1,
        [("own", own, VM), ("crop", crop, VM), ("wf", wf, VM), ("spread", tap_spread(), VM), ("w2", w2, VM),
         ("w3", w3, VM), ("up", up, VM), ("co", co, HB), ("par", par, VM), ("sc", sc, SM)],
        outs, scratch + sems(n, n, n, n, 4, 4, 5, 5, 32),
    )


def third_kernel(dims, r):
    net = Net(dims, False, [r.sem0, r.sem1, r.sem2, r.sem3])
    net.enter()
    mv = Moves(r.sem4)
    weights = fetch(mv, (r.it3h, r.t3h), (r.it3l, r.t3l), (r.iuh, r.uh), (r.iul, r.ul))
    f, f2, sc = r.f, r.f2, r.sc
    scale_c, off_c = affine(r.par, 1, *moments(r.g2, 1 - net.s, sc[9] * 4096.0, 256))
    f[...] = jnp.zeros(f.shape, f32)

    def put(p, get):
        m = sc[4 + p]

        def rows(t):
            x = silu(get(t * 96) * scale_c + off_c).reshape(4, 24, 256)
            f[pl.ds(4 * t, 4), :24, :] = jnp.where(m > 0, x, 0.0)

        loop(6, rows)
        im2col(r.ah, r.al, p, f, 24, 24, 256)

    def of(ref, base):
        return lambda at: ref[pl.ds(pl.multiple_of(base + at, 32), 96), :]

    put(0, of(r.hl, 0))
    loop(2, lambda p: put(p + 1, of(r.r2c, p * 576)))
    put(3, of(r.hr, 0))
    mv.out((r.ah, r.oah), (r.al, r.oal))
    f2[...] = jnp.zeros(f2.shape, f32)
    for p, (src, m) in enumerate(((r.col, sc[4]), (r.co, sc[5]), (r.cor, sc[7]))):
        f2[:24, :24, :] = jnp.where(m > 0, src[...], 0.0)
        im2col(r.cuh, r.cul, p, f2, 24, 24, 128)
    mv.out((r.cuh, r.ocuh), (r.cul, r.ocul))
    weights()
    conv(r.r3, r.ah, r.al, r.t3h, r.t3l, 576, NN)
    for d in range(2):
        for t in range(2):
            at = slice((d + t) * 576, (d + t + 1) * 576)
            r.r3[d * 576 : d * 576 + 576, :] += dot3(
                r.cuh[at, :], r.cul[at, :], r.uh[2 * d + t], r.ul[2 * d + t], NN
            )
    net.ready()
    net.to_left(r.r3.at[0:576], r.nr, 0)
    net.to_right(r.r3.at[576:1152], r.nl, 0)
    s0, q0 = field_sums(r.r3, 0, 576, 23, 23, sc[5])
    s1, q1 = field_sums(r.r3, 1, 576, 23, 23, sc[6])
    put_sums(r.st, s0 + s1, q0 + q1)
    net.share(r.st, r.g3)
    mv.out((r.r3, r.or3))
    scale, off = affine(r.par, 1, *moments(r.g2, net.s, sc[8] * 4096.0, 256))

    def pool(t):
        v = jnp.zeros((128, 256), f32)
        for d in range(2):
            x = r.r2[pl.ds(pl.multiple_of(d * 1024 + t * 128, 128), 128), :]
            v = v + sc[1 + d] * silu(x * scale + off)
        v = v[:, :128] + v[:, 128:]
        v = (v + pltpu.roll(v, 64, 1)) * 0.125
        r.pooled[pl.ds(pl.multiple_of(t * 128, 128), 128), :] = v[:, :64]

    loop(8, pool)
    toeplitz(r.w4, 0, 64, r.t4h, r.t4l, r.d4h, r.d4l)
    mv.out((r.t4h, r.ot4h), (r.t4l, r.ot4l), (r.d4h, r.od4h), (r.d4l, r.od4l))
    net.shared(r.st, r.g3)
    net.sides()
    mv.finish()


def third(dims, k, co, w4, par, sc):
    n = dims[1] * dims[2]
    V = pltpu.VMEM
    outs = [("pooled", (1024, 64), f32, VM), ("g3", (n, 1, 512), f32, VM), ("or3", (1152, 256), f32, HB),
            ("nl", (576, 256), f32, HB), ("nr", (576, 256), f32, HB)]
    scratch = []
    for name, shape in [("a", (2304, 1024)), ("cu", (1728, 512)), ("t4", (3, 1024, 256)), ("d4", (3, 256, 1024))]:
        outs += both_out("o" + name, shape)
        scratch += both(name, shape)
    scratch += both("t3", (3, 1024, 256)) + both("u", (4, 512, 256))
    scratch += [("st", V((1, 512), f32)), ("r3", V((1152, 256), f32)), ("f", V((26, 32, 256), f32)),
                ("f2", V((26, 32, 128), f32))]
    return launch(
        functools.partial(third_kernel, dims), "third", 2,
        [("r2", k.or2, VM), ("r2c", k.or2c, VM), ("hl", k.hl, VM), ("hr", k.hr, VM), ("co", co[0], VM),
         ("col", k.col, VM), ("cor", k.cor, VM), ("g2", k.g2, VM), ("par", par, VM),
         ("it3h", k.ot3h, HB), ("it3l", k.ot3l, HB), ("iuh", k.ouh, HB), ("iul", k.oul, HB),
         ("w4", w4, VM), ("sc", sc, SM)],
        outs, scratch + sems(n, n, 2, 2, 32),
    )


def fourth_kernel(dims, r):
    net = Net(dims, False, [r.sem0, r.sem1, r.sem2, r.sem3, r.sem4, r.sem5, r.sem6, r.sem7])
    net.enter()
    mv = Moves(r.sem8)
    forward = fetch(mv, (r.it4h, r.t4h), (r.it4l, r.t4l))
    backward = fetch(mv, (r.id4h, r.d4h), (r.id4l, r.d4l))
    sc, f, par = r.sc, r.f, r.par
    avg3, inv3 = moments(r.g3, None, sc[9] * 2116.0, 256)
    scale, off = affine(par, 2, avg3, inv3)
    f[...] = jnp.zeros(f.shape, f32)

    def put(p, get):
        m = sc[4 + p]

        def rows(t):
            x = silu(get(t * 96) * scale + off).reshape(4, 24, 256)
            f[pl.ds(4 * t, 4), :24, :] = jnp.where(m > 0, x, 0.0)

        loop(6, rows)
        im2col(r.ah, r.al, p, f, 22, 24, 256)

    def of(ref, base, step):
        return lambda at: ref[pl.ds(pl.multiple_of(base + at, 16), step), :]

    put(0, of(r.r3l, 0, 96))
    loop(2, lambda p: put(p + 1, of(r.r3, p * 576, 96)))
    put(3, of(r.r3r, 0, 96))
    forward()
    conv(r.r4, r.ah, r.al, r.t4h, r.t4l, 528, NN)
    net.ready()
    net.to_left(r.r4.at[0:528], r.r4r, 0)
    net.to_right(r.r4.at[528:1056], r.r4l, 0)
    s0, q0 = field_sums(r.r4, 0, 528, 22, 22, sc[5])
    s1, q1 = field_sums(r.r4, 1, 528, 22, 22, sc[6])
    put_sums(r.st4, s0 + s1, q0 + q1)
    net.share(r.st4, r.g4, 0)
    r.og[...] = jnp.zeros(r.og.shape, f32)

    def gather(t):
        for d in range(2):
            for py in range(2):
                x0 = r.ograw[d, 2 * t + py, pl.ds(0, 22, stride=2), :]
                x1 = r.ograw[d, 2 * t + py, pl.ds(1, 22, stride=2), :]
                r.og[d, t, pl.ds(0, 22), py * 128 : py * 128 + 128] = jnp.concatenate([x0, x1], axis=1)

    loop(22, gather)
    net.to_left(r.og.at[0], r.ogr, 1)
    net.to_right(r.og.at[1], r.ogl, 1)
    net.shared(r.st4, r.g4, 0)

    count = sc[9] * 1936.0
    avg, inv = moments(r.g4, None, count, 256)
    scale4, off4 = affine(par, 3, avg, inv)
    s = jnp.zeros((1, 256), f32)
    q = jnp.zeros((1, 256), f32)
    for d in range(2):
        m = sc[5 + d]

        def part(t, c):
            x = r.r4[pl.ds(pl.multiple_of(d * 528 + t * 48, 16), 48), :]
            b = x * scale4 + off4
            sg = 1.0 / (1.0 + jnp.exp(-b))
            r.dec[d, pl.ds(2 * t, 2)] = (m * (b * sg)).reshape(2, 24, 256)
            bg = r.og[d, pl.ds(2 * t, 2)].reshape(48, 256) * sg * (1.0 + b * (1.0 - sg))
            normed = (x - avg) * inv
            return (
                c[0] + jnp.sum(bg.reshape(6, 8, 256), axis=0),
                c[1] + jnp.sum((bg * normed).reshape(6, 8, 256), axis=0),
            )

        ps, pq = lax.fori_loop(0, 11, part, (jnp.zeros((8, 256), f32), jnp.zeros((8, 256), f32)))
        s = s + m * jnp.sum(ps, axis=0, keepdims=True)
        q = q + m * jnp.sum(pq, axis=0, keepdims=True)
    put_sums(r.st5, s, q)
    net.share(r.st5, r.g5, 1)

    def spread(t):
        for d in range(2):
            for py in range(2):
                v = r.dec[d, t, pl.ds(0, 22), py * 128 : py * 128 + 128]
                r.decoded[d, 2 * t + py, pl.ds(0, 22, stride=2), :] = v[:, :64]
                r.decoded[d, 2 * t + py, pl.ds(1, 22, stride=2), :] = v[:, 64:]

    loop(22, spread)
    net.shared(r.st5, r.g5, 1)
    net.sides()

    tg, tc = totals(r.g5, None, 256)
    f[...] = jnp.zeros(f.shape, f32)

    def put_back(p, get_r, get_a, keep):
        m = sc[4 + p]

        def rows(t):
            a = get_a(2 * t).reshape(48, 256)
            e = response_back(par, 3, avg, inv, tg, tc, count, get_r(t * 48), a).reshape(2, 24, 256)
            e = jnp.where(cells(e.shape, 22, 22, 0) & (m > 0), e, 0.0)
            f[pl.ds(1 + 2 * t, 2), 8:32, :] = e
            if keep is not None:
                hi, lo = split(e.reshape(48, 256))
                at = pl.ds(pl.multiple_of(keep * 528 + t * 48, 16), 48)
                r.eh[at, :] = hi
                r.el[at, :] = lo

        loop(11, rows)
        im2col(r.bh, r.bl, p, f, 24, 24, 256, x0=7)

    put_back(0, of(r.r4l, 0, 48), lambda y: r.ogl[pl.ds(y, 2)], None)
    loop(2, lambda p: put_back(p + 1, of(r.r4, p * 528, 48), lambda y: r.og[p, pl.ds(y, 2)], p))
    put_back(3, of(r.r4r, 0, 48), lambda y: r.ogr[pl.ds(y, 2)], None)
    backward()
    conv(r.a3, r.bh, r.bl, r.d4h, r.d4l, 576, NT)
    net.halos = []
    net.sems = [r.sem0, r.sem1, r.sem2, r.sem3, r.sem4, r.sem5, r.sem9, r.sem10]
    net.to_left(r.a3.at[0:576], r.a3r, 0)
    net.to_right(r.a3.at[576:1152], r.a3l, 0)
    mv.out((r.a3, r.oa3))
    s = jnp.zeros((1, 256), f32)
    q = jnp.zeros((1, 256), f32)
    for d in range(2):
        def part(t, c):
            at = pl.ds(pl.multiple_of(d * 576 + t * 48, 16), 48)
            normed, bg = back_parts(par, 2, avg3, inv3, r.r3[at, :], r.a3[at, :])
            bg = bg.reshape(2, 24, 256)
            bg = jnp.where(cells(bg.shape, 23, 23, 2 * t), bg, 0.0)
            return c[0] + jnp.sum(bg, axis=0), c[1] + jnp.sum(bg * normed.reshape(2, 24, 256), axis=0)

        ps, pq = lax.fori_loop(0, 12, part, (jnp.zeros((24, 256), f32), jnp.zeros((24, 256), f32)))
        s = s + sc[5 + d] * jnp.sum(ps, axis=0, keepdims=True)
        q = q + sc[5 + d] * jnp.sum(pq, axis=0, keepdims=True)
    put_sums(r.st6, s, q)
    net.share(r.st6, r.g6, 2)
    for i in range(3):
        at = slice(i * 528, (i + 2) * 528)
        r.g[...] = dot3(r.ah[at, :], r.al[at, :], r.eh[...], r.el[...], TN)
        put_taps(r.dw4, r.g, i, 64, 64, 0, 0)
    r.dw4[832:, 64:] = jnp.zeros((64, 64), f32)
    net.shared(r.st6, r.g6, 2)
    net.sides()
    mv.finish()


def put_taps(out, g, i, chans, total, row0, base):
    for j in range(3):
        for k in range(3):
            t = i * 9 + j * 3 + k
            v = folded(g, j, k, chans)
            v = v if t % 2 == 0 else pltpu.roll(v, 64, 1)
            at = 64 * (t % 2)
            row = base + (t // 2) * total + row0
            out[row : row + chans, at : at + 64] = v[:, at : at + 64]


def fourth(dims, r3, r3l, r3r, g3, og, k, par, sc):
    n = dims[1] * dims[2]
    V = pltpu.VMEM
    box = (22, 24, 256)
    return launch(
        functools.partial(fourth_kernel, dims), "fourth", 3,
        [("r3", r3, VM), ("r3l", r3l, VM), ("r3r", r3r, VM), ("g3", g3, VM), ("ograw", og, VM), ("par", par, VM),
         ("it4h", k.ot4h, HB), ("it4l", k.ot4l, HB), ("id4h", k.od4h, HB), ("id4l", k.od4l, HB), ("sc", sc, SM)],
        [("decoded", (2, 44, 44, 64), f32, VM), ("oa3", (1152, 256), f32, HB), ("a3l", (576, 256), f32, HB),
         ("a3r", (576, 256), f32, HB), ("g6", (n, 1, 512), f32, VM), ("st5", (1, 512), f32, VM),
         ("st6", (1, 512), f32, VM), ("dw4", (896, 128), f32, VM)],
        both("t4", (3, 1024, 256)) + both("d4", (3, 256, 1024)) + both("a", (2112, 1024)) + both("b", (2304, 1024))
        + both("e", (1056, 256))
        + [("f", V((26, 40, 256), f32)), ("r4", V((1056, 256), f32)), ("r4l", V((528, 256), f32)),
           ("r4r", V((528, 256), f32)), ("og", V((2,) + box, f32)), ("ogl", V(box, f32)), ("ogr", V(box, f32)),
           ("dec", V((2,) + box, f32)), ("a3", V((1152, 256), f32)), ("g", V((1024, 256), f32)),
           ("g4", V((n, 1, 512), f32)), ("g5", V((n, 1, 512), f32)), ("st4", V((1, 512), f32))]
        + sems(n, n, n, n, n, n, 4, 4, 8, 2, 2),
    )


def third_back_kernel(dims, r):
    net = Net(dims, False, [])
    barrier = pltpu.get_barrier_semaphore()
    partner = (1 - net.s, net.k, net.b)
    pair = (net.s, net.k + 1 - 2 * (net.k % 2), net.b)
    for device in (partner, pair):
        pl.semaphore_signal(barrier, inc=1, device_id=device, device_id_type=MESH)
    mv = Moves(r.sem0)
    backward = fetch(mv, (r.id3h, r.d3h), (r.id3l, r.d3l))
    ready_a = fetch(mv, (r.iah, r.ah), (r.ial, r.al), (r.icuh, r.cuh), (r.icul, r.cul))
    ready_t = [
        fetch(mv, (r.ituh.at[i], r.tuh.at[i]), (r.itul.at[i], r.tul.at[i])) for i in range(2)
    ]
    ready_u = fetch(mv, (r.iuph, r.uph), (r.iupl, r.upl), (r.iubh, r.ubh), (r.iubl, r.ubl))
    sc, f, par = r.sc, r.f, r.par
    count = sc[9] * 2116.0
    avg, inv = moments(r.g3, None, count, 256)
    tg, tc = totals(r.g6, None, 256)
    f[...] = jnp.zeros(f.shape, f32)

    def of(ref, base):
        return lambda at: ref[pl.ds(pl.multiple_of(base + at, 16), 48), :]

    def put(p, get_r, get_a, keep):
        m = sc[4 + p]

        def rows(t):
            e = response_back(par, 2, avg, inv, tg, tc, count, get_r(t * 48), get_a(t * 48)).reshape(2, 24, 256)
            e = jnp.where(cells(e.shape, 23, 23, 2 * t) & (m > 0), e, 0.0)
            f[pl.ds(1 + 2 * t, 2), 8:32, :] = e
            if keep is not None:
                hi, lo = split(e.reshape(48, 256))
                at = pl.ds(pl.multiple_of(keep * 576 + t * 48, 16), 48)
                r.eh[at, :] = hi
                r.el[at, :] = lo

        loop(12, rows)
        im2col(r.bh, r.bl, p, f, 24, 24, 256, x0=7)

    put(0, of(r.r3l, 0), of(r.a3l, 0), None)
    loop(2, lambda p: put(p + 1, of(r.r3, p * 576), of(r.a3, p * 576), p))
    put(3, of(r.r3r, 0), of(r.a3r, 0), None)
    backward()
    conv(r.g.at[:1152], r.bh, r.bl, r.d3h, r.d3l, 576, NT)

    def row(t):
        at = pl.ds(pl.multiple_of(t * 24, 24), 24)
        r.skip[2 * t] = r.g[at, :128]
        r.skip[2 * t + 1] = r.g[at, 128:]

    loop(48, row)
    pl.semaphore_wait(barrier, 2)
    across = pltpu.make_async_remote_copy(
        src_ref=r.skip, dst_ref=r.oskip, send_sem=r.sem1.at[0], recv_sem=r.sem1.at[1],
        device_id=partner, device_id_type=MESH,
    )
    across.start()

    ready_a()
    bucket = r.bucket
    for i in range(3):
        at = slice(i * 576, (i + 2) * 576)
        r.g[:1024, :] = dot3(r.ah[at, :], r.al[at, :], r.eh[...], r.el[...], TN)
        put_taps(bucket, r.g, i, 64, 192, 128, 0)
    for pd in range(2):
        for t in range(2):
            at = slice((pd + t) * 576, (pd + t + 1) * 576)
            e = slice(pd * 576, pd * 576 + 576)
            r.gu[pd * 2 + t] = dot3(r.cuh[at, :], r.cul[at, :], r.eh[e, :], r.el[e, :], TN)
    r.gd[...] = jnp.zeros(r.gd.shape, f32)
    ready_u()
    acc = dot3(r.bh[0:576, :], r.bl[0:576, :], r.ubh[0], r.ubl[0], NT)
    for p in range(1, 4):
        at = slice(p * 576, p * 576 + 576)
        acc += dot3(r.bh[at, :], r.bl[at, :], r.ubh[p], r.ubl[p], NT)
    r.cg[...] = acc * sc[5]
    for i in range(3):
        ready_t[i]()

        def block(ab, i=i):
            out = pl.ds(pl.multiple_of(ab * 128, 128), 128)
            p = jnp.concatenate([r.gu[slot_of(i, 0), out, :], r.gu[slot_of(i, 1), out, :]], axis=0)
            ph, plo = split(p)
            rows = pl.ds(pl.multiple_of(ab * 512, 512), 512)
            r.gd[...] += dot3(ph, plo, r.tuh[i % 2, rows, :], r.tul[i % 2, rows, :], NT)
            r.g[rows, :] = dot3(r.uph[...], r.upl[...], ph, plo, TN)

        loop(4, block)
        if i == 0:
            ready_t.append(fetch(mv, (r.ituh.at[2], r.tuh.at[0]), (r.itul.at[2], r.tul.at[0])))
        put_taps(bucket, r.g, i, 128, 192, 0, 0)
    bucket[2496:2688, 64:] = jnp.zeros((192, 64), f32)
    bucket[2688:3584, :] = r.dw4[...]
    for ip in range(2):
        for q in range(4):
            at = 3584 + (ip * 4 + q) * 128
            bucket[at : at + 128, :] = r.gd[ip * 128 : ip * 128 + 128, q * 128 : q * 128 + 128]
    if bucket.shape[0] > 4608:
        bucket[4608:, :] = jnp.zeros((bucket.shape[0] - 4608, 128), f32)

    size = bucket.shape[0] // 2
    core = net.k % 2
    swap = pltpu.make_async_remote_copy(
        src_ref=bucket.at[pl.ds(pl.multiple_of((1 - core) * size, 8), size)], dst_ref=r.slot,
        send_sem=r.sem1.at[2], recv_sem=r.sem1.at[3],
        device_id=pair, device_id_type=MESH,
    )
    swap.start()
    swap.wait()

    def add(t):
        at = pl.ds(pl.multiple_of(t * (size // 16), 8), size // 16)
        own = pl.ds(pl.multiple_of(core * size + t * (size // 16), 8), size // 16)
        r.slot[at, :] += bucket[own, :]

    loop(16, add)
    mv.out((r.slot, r.mine1))
    across.wait()
    mv.finish()


def bucket_rows(dims):
    n = dims[0] * dims[1] * dims[2]
    return -(-4608 // (8 * n)) * 8


def third_back(dims, fb, r3, r3l, r3r, g3, k, t, dw4, par, sc):
    n = dims[0] * dims[1] * dims[2]
    V = pltpu.VMEM
    rows = n * bucket_rows(dims)
    return launch(
        functools.partial(third_back_kernel, dims), "third_back", 4,
        [("a3", fb.oa3, VM), ("a3l", fb.a3l, VM), ("a3r", fb.a3r, VM), ("r3", r3, VM), ("r3l", r3l, VM),
         ("r3r", r3r, VM), ("g3", g3, VM), ("g6", fb.g6, VM), ("dw4", dw4, VM), ("par", par, VM),
         ("id3h", k.od3h, HB), ("id3l", k.od3l, HB), ("iah", t.oah, HB), ("ial", t.oal, HB),
         ("icuh", t.ocuh, HB), ("icul", t.ocul, HB), ("ituh", k.otuh, HB), ("itul", k.otul, HB),
         ("iuph", k.ouph, HB), ("iupl", k.oupl, HB), ("iubh", k.oubh, HB), ("iubl", k.oubl, HB), ("sc", sc, SM)],
        [("oskip", (96, 24, 128), f32, HB), ("cg", (576, 128), f32, VM), ("mine1", (rows // 2, 128), f32, HB)],
        both("d3", (3, 256, 1024)) + both("a", (2304, 1024)) + both("cu", (1728, 512)) + both("tu", (2, 2048, 256))
        + both("up", (256, 512)) + both("ub", (4, 128, 1024)) + both("b", (2304, 1024)) + both("e", (1152, 256))
        + [("f", V((26, 40, 256), f32)), ("skip", V((96, 24, 128), f32)),
           ("g", V((2048, 256), f32)), ("gu", V((4, 512, 256), f32)), ("gd", V((256, 512), f32)),
           ("bucket", V((rows, 128), f32)), ("slot", V((rows // 2, 128), f32))]
        + sems(24, 4),
    )


class Reduction:
    def __init__(self, dims, r, net):
        S, K, B = dims
        self.r, self.net = r, net
        self.per = bucket_rows(dims)
        self.Q, self.B, self.half = S * K // 2, B, S * K * B // 2
        self.core = net.k % 2
        self.y = net.k // 2
        self.q = net.s * (K // 2) + self.y
        self.rows = K // 2

    def ds(self, first, count):
        return pl.ds(pl.multiple_of(first * self.per, 8), count * self.per)

    def at_square(self, q):
        return (q // self.rows, 2 * (q % self.rows) + self.core, self.net.b)

    def copies(self, sem, items):
        out = []
        for j, (src, dst, dev) in enumerate(items):
            out.append(
                pltpu.make_async_remote_copy(
                    src_ref=src, dst_ref=dst, send_sem=sem.at[2 * j], recv_sem=sem.at[2 * j + 1],
                    device_id=dev, device_id_type=MESH,
                )
            )
        for c in out:
            c.start()
        self.open = out

    def wait(self):
        for c in self.open:
            c.wait()

    def square(self, sem):
        items = []
        for t in range(1, self.Q):
            q = (self.q + t) % self.Q
            items.append((self.r.mine1.at[self.ds(q * self.B, self.B)], self.r.slot2.at[t - 1], self.at_square(q)))
        self.copies(sem, items)

    def square_done(self):
        self.wait()
        v = self.r.mine1[self.ds(self.q * self.B, self.B), :]
        for t in range(self.Q - 1):
            v = v + self.r.slot2[t]
        self.r.mine2[...] = v

    def line(self, sem):
        items = []
        for t in range(1, self.B):
            b = (self.net.b + t) % self.B
            items.append((self.r.mine2.at[self.ds(b, 1)], self.r.slot3.at[t - 1], (self.net.s, self.net.k, b)))
        self.copies(sem, items)

    def line_done(self):
        self.wait()
        v = self.r.mine2[self.ds(self.net.b, 1), :]
        for t in range(self.B - 1):
            v = v + self.r.slot3[t]
        self.place = self.core * self.half + self.q * self.B + self.net.b
        self.r.res[self.ds(self.place, 1), :] = v

    def line_back(self, sem):
        own = self.r.res.at[self.ds(self.place, 1)]
        self.copies(
            sem,
            [(own, own, (self.net.s, self.net.k, (self.net.b + t) % self.B)) for t in range(1, self.B)],
        )

    def square_back(self, sem):
        own = self.r.res.at[self.ds(self.core * self.half + self.q * self.B, self.B)]
        self.copies(sem, [(own, own, self.at_square((self.q + t) % self.Q)) for t in range(1, self.Q)])

    def pair_back(self, sem):
        own = self.r.res.at[self.ds(self.core * self.half, self.half)]
        self.copies(sem, [(own, own, (self.net.s, self.net.k + 1 - 2 * self.core, self.net.b))])


def skip_stage(r, net, avg, inv):
    sc, par = r.sc, r.par
    oy, ox = r.si[1], r.si[2]
    qx = ox // 2
    rx = ox - 2 * qx
    odd = rx > 0
    s = jnp.zeros((1, 256), f32)
    q = jnp.zeros((1, 256), f32)
    lane = lax.broadcasted_iota(jnp.int32, (32, 128), 1)
    pad = jnp.zeros((8, 128), f32)
    for d in range(2):
        def placed(row):
            at = row - oy
            v = r.skip[d * 48 + jnp.clip(at, 0, 47)]
            v = jnp.where((at >= 0) & (at < 48), v, 0.0)
            v = jnp.concatenate([v, pad], axis=0)
            v = jnp.where(odd, pltpu.roll(v, 64, 1), v)
            return jnp.where(lane < 64, pltpu.roll(v, qx + rx, 0), pltpu.roll(v, qx, 0))

        def part(t, c):
            pv = r.pg[t] * 0.125
            pv = jnp.concatenate([pv, pv], axis=1)
            a = jnp.concatenate([placed(2 * t) + pv, placed(2 * t + 1) + pv], axis=1)
            rows = pl.ds(pl.multiple_of(d * 1024 + t * 32, 32), 32)
            normed, bg = back_parts(par, 1, avg, inv, r.r2[rows, :], a)
            bg = sc[1 + d] * bg
            r.bg2[rows, :] = bg
            bg = bg.reshape(4, 8, 256)
            return c[0] + jnp.sum(bg, axis=0), c[1] + jnp.sum(bg * normed.reshape(4, 8, 256), axis=0)

        ps, pq = lax.fori_loop(0, 32, part, (jnp.zeros((8, 256), f32), jnp.zeros((8, 256), f32)))
        s = s + jnp.sum(ps, axis=0, keepdims=True)
        q = q + jnp.sum(pq, axis=0, keepdims=True)
    put_sums(r.st7, s, q)


def tail_kernel(dims, r):
    net = Net(dims, False, [r.sem0, r.sem1, r.sem2, r.sem3, r.sem4, r.sem5])
    world = Net(dims, True, [r.sem6, r.sem7, r.sem8, r.sem9])
    world.enter()
    mv = Moves(r.sem10)
    backward = fetch(mv, (r.id2h, r.d2h), (r.id2l, r.d2l))
    ready_a = fetch(mv, (r.iah, r.ah), (r.ial, r.al))
    ready_s = fetch(mv, (r.ish, r.sh), (r.isl, r.sl), (r.ir1, r.r1))
    sc, par, f = r.sc, r.par, r.f
    count = sc[8] * 4096.0
    avg, inv = moments(r.g2, net.s, count, 256)
    world.ready()
    large = Reduction(dims, r, net)
    large.square(r.sem11)
    skip_stage(r, net, avg, inv)
    net.share(r.st7, r.g7, 0)
    f[...] = jnp.zeros(f.shape, f32)
    net.shared(r.st7, r.g7, 0)

    tg, tc = totals(r.g7, None, 256)
    k = par[2:3, :] * inv

    def put(p):
        m = sc[1 + p]

        def rows(t):
            at = pl.ds(pl.multiple_of(p * 1024 + t * 64, 64), 64)
            normed = (r.r2[at, :] - avg) * inv
            e = k * (r.bg2[at, :] - m * ((tg + normed * tc) / count))
            hi, lo = split(e)
            r.e2h[at, :] = hi
            r.e2l[at, :] = lo
            f[pl.ds(1 + 2 * t, 2), 8:40, :] = e.reshape(2, 32, 256)

        loop(16, rows)
        im2col(r.bh, r.bl, 0, f, 34, 40, 256, x0=7)

    put(0)
    backward()
    v = dot3(r.bh[...], r.bl[...], r.d2h[...], r.d2l[...], NT)
    r.a1[1, :1360] = v[:, :128]
    r.a1[0, :1360] = v[:, 128:256]
    r.side[0, :1360] = v[:, 256:]
    r.side[0, 1360:] = jnp.zeros((48, 128), f32)
    net.to_left(r.side.at[0], r.fr, 0)
    put(1)
    v = dot3(r.bh[...], r.bl[...], r.d2h[...], r.d2l[...], NT)
    r.side[1, :1360] = v[:, :128]
    r.side[1, 1360:] = jnp.zeros((48, 128), f32)
    net.to_right(r.side.at[1], r.fl, 0)
    r.a1[1, :1360] += v[:, 128:256]
    r.a1[0, :1360] += v[:, 256:]
    for d in range(2):
        r.a1[d, 1360:] = jnp.zeros((48, 128), f32)
    large.square_done()
    large.line(r.sem12)

    ready_a()
    for i in range(3):
        at = slice(i * 1024, (i + 2) * 1024)
        r.g[...] = dot3(r.ah[at, :], r.al[at, :], r.e2h[...], r.e2l[...], TN)
        put_taps(r.dw2, r.g, i, 32, 32, 0, 0)
    r.dw2[416:, 64:] = jnp.zeros((32, 64), f32)
    large.line_done()
    large.line_back(r.sem13)
    net.sides()

    ready_s()
    count1 = sc[8] * 4356.0
    avg1, inv1 = moments(r.g1, net.s, count1, 128)
    s = jnp.zeros((1, 128), f32)
    q = jnp.zeros((1, 128), f32)
    net.halos = []
    for d in range(2):
        other = r.fl if d == 0 else r.fr
        here = sc[10 + d]

        def part(t, c):
            rows = pl.ds(pl.multiple_of(t * 160, 160), 160)
            a = r.a1[d, rows, :] + jnp.where(here > 0, other[rows, :], 0.0)
            r.a1[d, rows, :] = a
            normed, bg = back_parts(par, 0, avg1, inv1, r.r1[1 + d, rows, :], a)
            bg = bg.reshape(4, 40, 128)
            bg = jnp.where(cells(bg.shape, 33, 33, 4 * t), bg, 0.0)
            return c[0] + jnp.sum(bg, axis=0), c[1] + jnp.sum(bg * normed.reshape(4, 40, 128), axis=0)

        ps, pq = lax.fori_loop(0, 8, part, (jnp.zeros((40, 128), f32), jnp.zeros((40, 128), f32)))
        rows = slice(1280, OWN)
        a = r.a1[d, rows, :] + jnp.where(here > 0, other[rows, :], 0.0)
        r.a1[d, rows, :] = a
        normed, bg = back_parts(par, 0, avg1, inv1, r.r1[1 + d, 1280:1320, :], a[:40])
        bg = jnp.where(lax.broadcasted_iota(jnp.int32, (40, 128), 0) < 33, bg, 0.0)
        ps = ps + bg
        pq = pq + bg * normed
        s = s + sc[1 + d] * jnp.sum(ps, axis=0, keepdims=True)
        q = q + sc[1 + d] * jnp.sum(pq, axis=0, keepdims=True)
        if d == 0:
            net.to_left(r.a1.at[0], r.a1r, 1)
        else:
            net.to_right(r.a1.at[1], r.a1l, 1)
    put_sums(r.st8, s, q)
    net.share(r.st8, r.g8, 1)
    large.wait()
    large.square_back(r.sem14)
    net.shared(r.st8, r.g8, 1)

    tg1, tc1 = totals(r.g8, None, 128)
    wh, wl = r.w1h[...], r.w1l[...]
    eh, el = r.eh, r.el

    def put_first(p, get_a):
        m = sc[p]
        eh[p, 1280:, :] = jnp.zeros((OWN - 1280, 128), bf16)
        el[p, 1280:, :] = jnp.zeros((OWN - 1280, 128), bf16)

        def rows(t):
            at = pl.ds(pl.multiple_of(t * 80, 80), 80)
            e = response_back(par, 0, avg1, inv1, tg1, tc1, count1, r.r1[p, at, :], get_a(at))
            e = e.reshape(2, 40, 128)
            e = jnp.where(cells(e.shape, 33, 33, 2 * t) & (m > 0), e, 0.0)
            hi, lo = split(e.reshape(80, 128))
            eh[p, at, :] = hi
            el[p, at, :] = lo

        loop(17, rows)

    loop(2, lambda p: put_first(p + 1, lambda at: r.a1[p, at, :]))
    acc = jnp.zeros((192, 128), f32)
    for d in range(2):
        rows = slice((d + 1) * 64, (d + 1) * 64 + 192)
        acc += dot3(r.sh[rows, :], r.sl[rows, :], eh[d + 1], el[d + 1], NN)
    lane = lax.broadcasted_iota(jnp.int32, (32, 128), 1)
    tot = jnp.zeros((32, 128), f32)
    for tap in range(4):
        v = jnp.zeros((32, 128), f32)
        for q in range(4):
            x = acc if q == tap else pltpu.roll(acc, ((tap - q) % 4) * 32, 1)
            hi, lo = split(x)
            sel = r.pick[tap * 4 + q]
            v += dot(sel, hi, NN) + dot(sel, lo, NN)
        tot += jnp.where(lane // 32 == tap, v, 0.0)

    per = 512 // world.n

    def store(x, row0):
        for at in range(0, x.shape[0], per):
            r.small[(row0 + at) // per] = x[at : at + per]

    store(r.dw2[...], 0)
    store(tot, 448)
    for j, st in enumerate((r.st8, r.st7, r.st6, r.st5)):
        v = st[...]
        rows = jnp.concatenate([v[:, 128 * c : 128 * c + 128] for c in range(4)], axis=0)
        if per > 4:
            at = 480 + 4 * j
            r.small[at // per, at % per : at % per + 4, :] = rows
        else:
            store(rows, 480 + 4 * j)
    store(jnp.zeros((16, 128), f32), 496)
    world.scatter(r.small, r.slots, 0)
    net.sides()
    put_first(0, lambda at: r.a1l[at, :])
    put_first(3, lambda at: r.a1r[at, :])
    parts = [dot3(wh, wl, eh[p], el[p], NT) for p in range(4)]
    world.scattered(r.small, r.slots, 0)
    r.mine[...] = jnp.sum(r.slots[...], axis=0)
    world.share(r.mine, r.red, 1)
    large.wait()
    large.pair_back(r.sem15)
    for d in range(2):
        tot = jnp.zeros((16, OWN), f32)
        for ab in range(4):
            v = jnp.zeros((16, OWN), f32)
            for i in range(3):
                at = i * 64 + ab * 16
                v += parts[d + 2 - i][at : at + 16, :]
            a, b = ab // 2, ab % 2
            tot += v if ab == 0 else pltpu.roll(v, 40 * a + b, 1)
        tot = tot * (r.keep[...] * sc[1 + d])
        rows = []
        for y in range(34):
            tile, off = (40 * y) // 128, (40 * y) % 128
            pair = []
            for px in range(2):
                v = tot[8 * px : 8 * px + 8, 128 * tile : 128 * tile + 128]
                if off + 34 > 128:
                    nxt = tot[8 * px : 8 * px + 8, 128 * tile + 128 : 128 * tile + 256]
                    v = jnp.where(lane[:8] >= off, v, nxt)
                pair.append(v if off == 0 else pltpu.roll(v, 128 - off, 1))
            rows.append(jnp.concatenate(pair, axis=1))
        hi, lo = split(jnp.concatenate(rows, axis=0))
        out = dot(hi, r.even[...], NT) + dot(lo, r.even[...], NT)
        r.ig[d] = out.reshape(34, 8, 68)
    world.shared(r.mine, r.red, 1)
    large.wait()
    mv.finish()


def tail(dims, tb, pg, k, fo, keep, par, sc, si):
    n = dims[0] * dims[1] * dims[2]
    m = dims[1] * dims[2]
    V = pltpu.VMEM
    per = 512 // n
    big = bucket_rows(dims)
    Q, B = dims[0] * dims[1] // 2, dims[2]
    return launch(
        functools.partial(tail_kernel, dims), "tail", 5,
        [("skip", tb.oskip, VM), ("mine1", tb.mine1, VM), ("pg", pg, VM), ("r2", k.or2, VM), ("g2", k.g2, VM),
         ("g1", k.g1, VM), ("keep", keep, VM), ("w1h", k.ow1h, VM), ("w1l", k.ow1l, VM), ("pick", tap_picks(), VM),
         ("even", deinterleave(), VM), ("st5", fo.st5, VM), ("st6", fo.st6, VM), ("par", par, VM),
         ("id2h", k.od2h, HB), ("id2l", k.od2l, HB), ("iah", k.oah, HB), ("ial", k.oal, HB),
         ("ish", k.osh, HB), ("isl", k.osl, HB), ("ir1", k.or1, HB), ("sc", sc, SM), ("si", si, SM)],
        [("ig", (2, 34, 8, 68), f32, VM), ("red", (n, per, 128), f32, VM), ("res", (n * big, 128), f32, VM)],
        both("d2", (384, 1024)) + both("a", (4096, 512)) + both("b", (1360, 1024)) + both("e2", (2048, 256))
        + both("s", (384, OWN)) + both("e", (4, OWN, 128))
        + [("f", V((36, 56, 256), f32)), ("bg2", V((2048, 256), f32)), ("r1", V((4, 1440, 128), f32)),
           ("a1", V((2, OWN, 128), f32)), ("side", V((2, OWN, 128), f32)), ("fl", V((OWN, 128), f32)),
           ("fr", V((OWN, 128), f32)), ("a1l", V((OWN, 128), f32)), ("a1r", V((OWN, 128), f32)),
           ("g", V((512, 256), f32)), ("dw2", V((448, 128), f32)), ("small", V((n, per, 128), f32)),
           ("slots", V((n, per, 128), f32)), ("mine", V((per, 128), f32)), ("g7", V((m, 1, 512), f32)),
           ("g8", V((m, 1, 512), f32)), ("st7", V((1, 512), f32)), ("st8", V((1, 512), f32)),
           ("slot2", V((Q - 1, B * big, 128), f32)), ("mine2", V((B * big, 128), f32)),
           ("slot3", V((B - 1, big, 128), f32))]
        + sems(m, m, m, m, 4, 4, n, n, n, n, 8, 2 * (Q - 1), 2 * (B - 1), 2 * (B - 1), 2 * (Q - 1), 2),
    )


def body(
    dims,
    image, modality_mask, extents, crop_offsets, coarse,
    conv_first, gain_first, shift_first, conv_second, gain_second, shift_second,
    up_kernel, conv_third, gain_third, shift_third, conv_fourth, gain_fourth, shift_fourth,
    pool_grad, output_grad,
):
    si = jnp.pad(crop_offsets[0, 0], (1, 5))
    img = image[0, 0].transpose(0, 1, 3, 2).reshape(2, 34, 8, 68)
    p = prepare(
        dims, img, extents, modality_mask[0], si,
        (gain_first, shift_first, gain_second, shift_second, gain_third, shift_third, gain_fourth, shift_fourth),
    )
    co = coarse[0, 0]
    k = front(
        dims, p.own, p.crop, conv_first.reshape(108, 32), conv_second.reshape(27, 32, 64),
        conv_third.reshape(27, 192, 64), up_kernel.reshape(8, 128, 128), co, p.par, p.sc,
    )
    t = third(dims, k, co, conv_fourth.reshape(27, 64, 64), p.par, p.sc)
    fo = fourth(dims, t.or3, t.nl, t.nr, t.g3, output_grad[0, 0], t, p.par, p.sc)
    tb = third_back(dims, fo, t.or3, t.nl, t.nr, t.g3, k, t, fo.dw4, p.par, p.sc)
    k.od2h = k.od2h.reshape(384, 1024)
    k.od2l = k.od2l.reshape(384, 1024)
    e = tail(dims, tb, pool_grad[0, 0, 0], k, fo, p.keep, p.par, p.sc, si)

    def taps(rows, chans):
        return rows.reshape(14, chans, 2, 64).transpose(0, 2, 1, 3).reshape(28, chans, 64)[:27].reshape(3, 3, 3, chans, 64)

    red = e.red.reshape(512, 128)
    dw2 = taps(red[:448], 32)
    dw1 = red[448:476].reshape(7, 4, 4, 32).transpose(0, 2, 1, 3).reshape(28, 4, 32)[:27]
    sums = red[480:496].reshape(4, 2, 256)
    dw3 = taps(e.res[:2688], 192)
    dw4 = taps(e.res[2688:3584], 64)
    dup = e.res[3584:4608]

    def affine_grads(layer, width):
        v = sums[layer].reshape(2, 256 // width, width).sum(axis=1)
        return v[1], v[0]

    gg1, gs1 = affine_grads(0, 32)
    gg2, gs2 = affine_grads(1, 64)
    gg3, gs3 = affine_grads(2, 64)
    gg4, gs4 = affine_grads(3, 64)
    return (
        t.pooled.reshape(1, 1, 1, 32, 32, 64),
        fo.decoded[None, None],
        e.ig.reshape(2, 68, 4, 68).transpose(0, 1, 3, 2)[None, None],
        tb.cg.reshape(1, 1, 1, 24, 24, 128),
        dw1.reshape(3, 3, 3, 4, 32),
        gg1,
        gs1,
        dw2,
        gg2,
        gs2,
        dup.reshape(2, 2, 2, 128, 128),
        dw3,
        gg3,
        gs3,
        dw4,
        gg4,
        gs4,
    )


def solution(mesh):
    dims = tuple(mesh.shape[a] for a in ("section", "slab", "batch"))
    field = P("section", "batch", "slab", None, None, None)
    volume = P("section", "batch", None)
    rep = P()
    return jax.shard_map(
        functools.partial(body, dims),
        mesh=mesh,
        in_specs=(field, volume, rep, volume, field) + (rep,) * 13 + (field, field),
        out_specs=(field,) * 4 + (rep,) * 13,
        check_vma=False,
    )
```

```python
import functools
import types

import jax
import jax.numpy as jnp
import numpy as np
from jax import lax
from jax.experimental import pallas as pl
from jax.experimental.pallas import tpu as pltpu
from jax.sharding import PartitionSpec as P

f32 = jnp.float32
bf16 = jnp.bfloat16
MESH = pl.DeviceIdType.MESH
EPSILON = 1e-05
NN = (((1,), (0,)), ((), ()))
NT = (((1,), (1,)), ((), ()))
TN = (((0,), (0,)), ((), ()))
VM = pl.BlockSpec(memory_space=pltpu.VMEM)
SM = pl.BlockSpec(memory_space=pltpu.SMEM)
HB = pl.BlockSpec(memory_space=pl.ANY)
LIMIT = 62 * 2**20

OWN = 1408
CROP = 896
BUCKET = 2880 + 960 + 1024


def split(x):
    hi = x.astype(bf16)
    return hi, (x - hi.astype(f32)).astype(bf16)


def dot(a, b, dims):
    return lax.dot_general(a, b, dims, preferred_element_type=f32)


def dot3(ah, al, bh, bl, dims):
    return dot(ah, bh, dims) + dot(al, bh, dims) + dot(ah, bl, dims)


def loop(n, f, unroll=1):
    def step(t, c):
        f(t)
        return c

    lax.fori_loop(0, n, step, 0, unroll=unroll)


def fold(v):
    lanes = v.shape[-1]
    v = jnp.broadcast_to(v, (8, lanes))
    if lanes == 256:
        h = v[:, :128] + v[:, 128:]
        h = h + pltpu.roll(h, 64, 1)
        h = jnp.concatenate([h, h], axis=1)
    else:
        h = v + pltpu.roll(v, 64, 1)
        h = h + pltpu.roll(h, 32, 1)
    return h[:1]


def totals(gath, half, lanes):
    if half is None:
        tot = jnp.sum(gath[...], axis=0)
    else:
        per = gath.shape[0] // 2
        tot = jnp.sum(gath[pl.ds(half * per, per)], axis=0)
    return fold(tot[:, :lanes]), fold(tot[:, 256 : 256 + lanes])


def moments(gath, half, count, lanes):
    s, q = totals(gath, half, lanes)
    avg = s / count
    inv = lax.rsqrt(q / count - avg * avg + EPSILON)
    return avg, inv


def affine(par, layer, avg, inv):
    lanes = avg.shape[-1]
    scale = par[2 * layer : 2 * layer + 1, :lanes] * inv
    return scale, par[2 * layer + 1 : 2 * layer + 2, :lanes] - avg * scale


def silu(b):
    return b / (1.0 + jnp.exp(-b))


def silu_back(a, b):
    s = 1.0 / (1.0 + jnp.exp(-b))
    return a * s * (1.0 + b * (1.0 - s))


def cells(shape, rows, cols, row0):
    y = lax.broadcasted_iota(jnp.int32, shape, 0) + row0
    x = lax.broadcasted_iota(jnp.int32, shape, 1)
    return (y < rows) & (x < cols)


def put_sums(st, s, q):
    lanes = s.shape[-1]
    st[...] = jnp.zeros(st.shape, f32)
    st[:, :lanes] = s
    st[:, 256 : 256 + lanes] = q


def im2col(ah, al, p, f, ny, pitch, lanes, x0=0):
    def pair(t):
        for a in range(2):
            for b in range(2):
                x = f[pl.ds(2 * t + a, 2), x0 + b : x0 + b + pitch, :]
                hi, lo = split(x.reshape(2 * pitch, lanes))
                rows = pl.ds(pl.multiple_of(p * (ny * pitch) + t * (2 * pitch), 16), 2 * pitch)
                at = (2 * a + b) * lanes
                ah[rows, at : at + lanes] = hi
                al[rows, at : at + lanes] = lo

    loop(ny // 2, pair)


def launch(body, name, cid, ins, outs, scratch):
    names = [i[0] for i in ins] + [o[0] for o in outs] + [x[0] for x in scratch]

    def kernel(*refs):
        body(types.SimpleNamespace(**dict(zip(names, refs))))

    res = pl.pallas_call(
        kernel,
        out_shape=[jax.ShapeDtypeStruct(o[1], o[2]) for o in outs],
        in_specs=[i[2] for i in ins],
        out_specs=[o[3] for o in outs],
        scratch_shapes=[x[1] for x in scratch],
        compiler_params=pltpu.CompilerParams(
            vmem_limit_bytes=LIMIT, collective_id=cid, has_side_effects=cid is not None
        ),
        name=name,
    )(*[i[1] for i in ins])
    return types.SimpleNamespace(**dict(zip([o[0] for o in outs], res)))


def both(name, shape):
    return [(name + "h", pltpu.VMEM(shape, bf16)), (name + "l", pltpu.VMEM(shape, bf16))]


def both_out(name, shape):
    return [(name + "h", shape, bf16, HB), (name + "l", shape, bf16, HB)]


def sems(*sizes):
    return [(f"sem{i}", pltpu.SemaphoreType.DMA((n,))) for i, n in enumerate(sizes)]


class Moves:
    def __init__(self, sem):
        self.sem = sem
        self.used = 0
        self.pending = []

    def start(self, src, dst):
        copy = pltpu.make_async_copy(src, dst, self.sem.at[self.used])
        self.used += 1
        copy.start()
        return copy

    def out(self, *pairs):
        for src, dst in pairs:
            self.pending.append(self.start(src, dst))

    def finish(self):
        for copy in self.pending:
            copy.wait()


def fetch(mv, *pairs):
    copies = [mv.start(src, dst) for src, dst in pairs]

    def wait():
        for copy in copies:
            copy.wait()

    return wait


class Net:
    def __init__(self, dims, wide, sems):
        S, K, B = dims
        self.s = lax.axis_index("section")
        self.k = lax.axis_index("slab")
        self.b = lax.axis_index("batch")
        self.K = K
        self.sems = sems
        if wide:
            self.n = S * K * B
            self.me = (self.s * K + self.k) * B + self.b
            self.coords = lambda d: (d // (K * B), (d // B) % K, d % B)
        else:
            self.n = K * B
            self.me = self.k * B + self.b
            self.coords = lambda d: (self.s, d // B, d % B)
        self.halos = []

    def each(self, f):
        def step(p, c):
            f(p)
            return c

        lax.fori_loop(1, self.n, step, 0)

    def enter(self):
        barrier = pltpu.get_barrier_semaphore()
        self.each(
            lambda p: pl.semaphore_signal(
                barrier, inc=1, device_id=self.coords((self.me + p) % self.n), device_id_type=MESH
            )
        )

    def ready(self):
        pl.semaphore_wait(pltpu.get_barrier_semaphore(), self.n - 1)

    def _copy(self, src, dst, p, group):
        return pltpu.make_async_remote_copy(
            src_ref=src,
            dst_ref=dst,
            send_sem=self.sems[2 * group].at[p],
            recv_sem=self.sems[2 * group + 1].at[p],
            device_id=self.coords((self.me + p) % self.n),
            device_id_type=MESH,
        )

    def share(self, src, slots, group=0):
        slots[self.me] = src[...]
        self.each(lambda p: self._copy(src, slots.at[self.me], p, group).start())

    def shared(self, src, slots, group=0):
        n = self.n
        self.each(lambda p: self._copy(src, slots.at[(self.me + n - p) % n], p, group).wait_recv())
        self.each(lambda p: self._copy(src, slots.at[self.me], p, group).wait_send())

    def scatter(self, src, slots, group):
        slots[self.me] = src[self.me]
        n = self.n
        self.each(lambda p: self._copy(src.at[(self.me + p) % n], slots.at[self.me], p, group).start())

    def scattered(self, src, slots, group):
        n = self.n
        self.each(
            lambda p: self._copy(
                src.at[(self.me + p) % n], slots.at[(self.me + n - p) % n], p, group
            ).wait_recv()
        )
        self.each(lambda p: self._copy(src.at[(self.me + p) % n], slots.at[self.me], p, group).wait_send())

    def _side(self, src, dst, j, step):
        return pltpu.make_async_remote_copy(
            src_ref=src,
            dst_ref=dst,
            send_sem=self.sems[-2].at[j],
            recv_sem=self.sems[-1].at[j],
            device_id=(self.s, (self.k + self.K + step) % self.K, self.b),
            device_id_type=MESH,
        )

    def to_left(self, src, dst, j):
        copy = self._side(src, dst, 2 * j, -1)

        @pl.when(self.k > 0)
        def _():
            copy.start()

        self.halos.append((copy, -1))

    def to_right(self, src, dst, j):
        copy = self._side(src, dst, 2 * j + 1, 1)

        @pl.when(self.k < self.K - 1)
        def _():
            copy.start()

        self.halos.append((copy, 1))

    def sides(self):
        @pl.when(self.k > 0)
        def _():
            for copy, step in self.halos:
                if step < 0:
                    copy.wait_send()
                else:
                    copy.wait_recv()

        @pl.when(self.k < self.K - 1)
        def _():
            for copy, step in self.halos:
                if step > 0:
                    copy.wait_send()
                else:
                    copy.wait_recv()


def toeplitz(w, c0, chans, th, tl, dh=None, dl=None):
    loop(3, lambda i: toeplitz_tap(w, c0, chans, i, i, th, tl, dh, dl))


def toeplitz_tap(w, c0, chans, i, slot, th, tl, dh=None, dl=None):
    zero = jnp.zeros((chans, 64), f32)
    none = jnp.zeros((chans, 128), bf16)
    for s in range(4):
        part = []
        for j in range(3):
            here = w[i * 9 + j * 3 + s, c0 : c0 + chans, :] if s <= 2 else zero
            prev = w[i * 9 + j * 3 + s - 1, c0 : c0 + chans, :] if s >= 1 else zero
            part.append(split(jnp.concatenate([here, prev], axis=1)))
        for r in range(4):
            a, py, b, px = r // 2, r % 2, s // 2, s % 2
            block = (2 * a + b) * 4 + py * 2 + px
            for h in range(2):
                hi, lo = part[r - h] if 0 <= r - h <= 2 else (none, none)
                if th is not None:
                    rows = slice(block * chans, (block + 1) * chans)
                    th[slot, rows, 128 * h : 128 * h + 128] = hi
                    tl[slot, rows, 128 * h : 128 * h + 128] = lo
                if dh is not None:
                    rows = slice((py * 2 + px) * chans, (py * 2 + px + 1) * chans)
                    at = ((1 - a) * 2 + (1 - b)) * 256 + 128 * h
                    dh[2 - i, rows, at : at + 128] = hi
                    dl[2 - i, rows, at : at + 128] = lo


def slot_of(i, ip):
    pd = (ip + i + 1) % 2
    t = (pd + i - 1) // 2 - pd + 1
    return pd * 2 + t


def up_blocks(r):
    for ip in range(2):
        for q in range(4):
            hi, lo = split(r.up[ip * 4 + q])
            r.uph[ip * 128 : ip * 128 + 128, q * 128 : q * 128 + 128] = hi
            r.upl[ip * 128 : ip * 128 + 128, q * 128 : q * 128 + 128] = lo


def compose(r, i):
    def block(ab):
        rows = pl.ds(pl.multiple_of(ab * 512, 512), 512)
        p = dot3(r.uph[...], r.upl[...], r.tuh[i, rows, :], r.tul[i, rows, :], NN)
        out = pl.ds(pl.multiple_of(ab * 128, 128), 128)
        for ip in range(2):
            r.usc[slot_of(i, ip), out, :] += p[ip * 128 : ip * 128 + 128]

    loop(4, block)


def composed(r):
    for e in range(4):
        for ab in range(4):
            hi, lo = split(r.usc[e, ab * 128 : ab * 128 + 128, :])
            r.uh[e, ab * 128 : ab * 128 + 128, :] = hi
            r.ul[e, ab * 128 : ab * 128 + 128, :] = lo
            p = (3, 1, 2, 0)[e]
            at = (3 - ab) * 256
            r.ubh[p, :, at : at + 256] = hi
            r.ubl[p, :, at : at + 256] = lo


def source_copies(dims, own, crop, so, sr, ss, rs):
    K = dims[1]
    s = lax.axis_index("section")
    k = lax.axis_index("slab")
    b = lax.axis_index("batch")
    here, left, right = k, (k + K - 1) % K, (k + 1) % K

    def copy(j, src, dst, dev):
        return pltpu.make_async_remote_copy(
            src_ref=src,
            dst_ref=dst,
            send_sem=ss.at[j],
            recv_sem=rs.at[j],
            device_id=dev,
            device_id_type=MESH,
        )

    so[2:4] = own[...]
    lefts = [
        copy(0, own, so.at[4:6], (s, left, b)),
        copy(1, crop, sr.at[4:6], (1 - s, left, b)),
    ]
    rights = [
        copy(2, own, so.at[0:2], (s, right, b)),
        copy(3, crop, sr.at[0:2], (1 - s, right, b)),
    ]
    across = copy(4, crop, sr.at[2:4], (1 - s, here, b))

    def start():
        across.start()

        @pl.when(k > 0)
        def _():
            for c in lefts:
                c.start()

        @pl.when(k < K - 1)
        def _():
            for c in rights:
                c.start()

    def finish():
        across.wait()

        @pl.when(k > 0)
        def _():
            for c in lefts:
                c.wait_send()
            for c in rights:
                c.wait_recv()

        @pl.when(k < K - 1)
        def _():
            for c in rights:
                c.wait_send()
            for c in lefts:
                c.wait_recv()

        @pl.when(k == 0)
        def _():
            so[0:2] = jnp.zeros((2, 16, OWN), f32)
            sr[0:2] = jnp.zeros((2, 16, CROP), f32)

        @pl.when(k == K - 1)
        def _():
            so[4:6] = jnp.zeros((2, 16, OWN), f32)
            sr[4:6] = jnp.zeros((2, 16, CROP), f32)

    return start, finish


def field_sums(r, d, n, rows, cols, mask):
    base = d * n

    def part(t, c):
        x = r[pl.ds(pl.multiple_of(base + t * 96, 16), 96), :].reshape(4, 24, 256)
        x = jnp.where(cells(x.shape, rows, cols, 4 * t), x, 0.0)
        return c[0] + jnp.sum(x, axis=0), c[1] + jnp.sum(x * x, axis=0)

    zero = jnp.zeros((24, 256), f32)
    full = n // 96
    s, q = lax.fori_loop(0, full, part, (zero, zero))
    if n % 96:
        x = r[base + full * 96 : base + n, :].reshape((n - full * 96) // 24, 24, 256)
        x = jnp.where(cells(x.shape, rows, cols, 4 * full), x, 0.0)
        s = s + jnp.sum(x, axis=0)
        q = q + jnp.sum(x * x, axis=0)
    return mask * jnp.sum(s, axis=0, keepdims=True), mask * jnp.sum(q, axis=0, keepdims=True)


def back_parts(par, layer, avg, inv, r, a):
    lanes = avg.shape[-1]
    normed = (r - avg) * inv
    b = par[2 * layer : 2 * layer + 1, :lanes] * normed + par[2 * layer + 1 : 2 * layer + 2, :lanes]
    return normed, silu_back(a, b)


def response_back(par, layer, avg, inv, tg, tc, count, r, a):
    lanes = avg.shape[-1]
    gain = par[2 * layer : 2 * layer + 1, :lanes]
    normed, bg = back_parts(par, layer, avg, inv, r, a)
    return inv * gain * (bg - (tg + normed * tc) / count)


def folded(g, j, k, chans):
    def block(r, s):
        at = (2 * (r // 2) + s // 2) * 4 + (r % 2) * 2 + s % 2
        return slice(at * chans, (at + 1) * chans)

    x = g[block(j, k), 0:128] + g[block(j + 1, k), 128:256]
    y = g[block(j, k + 1), 0:128] + g[block(j + 1, k + 1), 128:256]
    return x + pltpu.roll(y, 64, 1)


def tap_picks():
    sel = np.zeros((4, 4, 32, 192), np.float32)
    for t in range(27):
        i, j, k = t // 9, (t // 3) % 3, t % 3
        for q in range(4):
            r, s = j + q // 2, k + q % 2
            for c in range(4):
                col = i * 64 + (2 * (r // 2) + s // 2) * 16 + (s % 2) * 8 + (r % 2) * 4 + c
                sel[t % 4, q, (t // 4) * 4 + c, col] = 1.0
    return jnp.asarray(sel.reshape(16, 32, 192), bf16)


def deinterleave():
    sel = np.zeros((68, 256), np.float32)
    for x in range(68):
        sel[x, (x % 2) * 128 + x // 2] = 1.0
    return jnp.asarray(sel, bf16)


def prepare_kernel(r):
    s = lax.axis_index("section")
    k = lax.axis_index("slab")
    b = lax.axis_index("batch")
    ends = (r.ext[s, b], r.ext[1 - s, b])
    for h in range(2):
        for p in range(4):
            g = 2 * k - 1 + p
            r.sc[4 * h + p] = jnp.where((g >= 0) & (g < ends[h]), 1.0, 0.0)
        tot = jnp.int32(0)
        for v in range(r.ext.shape[1]):
            tot = tot + (r.ext[s, v] if h == 0 else r.ext[1 - s, v])
        r.sc[8 + h] = tot.astype(f32)
    r.sc[10] = jnp.where(k > 0, 1.0, 0.0)
    r.sc[11] = jnp.where(k < r.slabs - 1, 1.0, 0.0)
    for j in range(12, 16):
        r.sc[j] = jnp.float32(0.0)
    for j, v in enumerate((r.v0, r.v1, r.v2, r.v3, r.v4, r.v5, r.v6, r.v7)):
        v = v[...]
        while v.shape[1] < 256:
            v = jnp.concatenate([v, v], axis=1)
        r.par[j : j + 1, :] = v
    row = lax.broadcasted_iota(jnp.int32, (16, 1), 0) % 4
    col = jnp.zeros((16, 1), f32)
    for c in range(4):
        col = jnp.where(row == c, r.mods[0, c].astype(f32), col)
    r.keep[...] = col
    img, keep, even, sc, own, crop = r.img, r.keep, r.even, r.sc, r.own, r.crop
    oy, ox = r.si[0, 0], r.si[0, 1]

    def turn(t):
        v = r.w3t[t].T
        r.w3u[t] = v[:128]
        r.w3c[t] = v[128:]

    loop(27, turn)
    x = lax.broadcasted_iota(jnp.int32, (68, 256), 0)
    lane = lax.broadcasted_iota(jnp.int32, (68, 256), 1)
    at = 2 * (lane % 128) + lane // 128
    pick = ((x == at + ox) & (lane % 128 < 26)).astype(f32).astype(bf16)
    r = lax.broadcasted_iota(jnp.int32, (208, 272), 0)
    c = lax.broadcasted_iota(jnp.int32, (208, 272), 1)
    rows = (c == r + 4 * oy).astype(f32).astype(bf16)
    lane = lax.broadcasted_iota(jnp.int32, (8, 128), 1)

    def flat(v, side, pitch, tiles):
        out = [[jnp.zeros((8, 128), f32) for _ in range(tiles)] for _ in range(2)]
        for y in range(side):
            tile, off = (pitch * y) // 128, (pitch * y) % 128
            for px in range(2):
                p = v[8 * y : 8 * y + 8, 128 * px : 128 * px + 128]
                p = p if off == 0 else pltpu.roll(p, off, 1)
                if off + side > 128:
                    out[px][tile + 1] += jnp.where(lane < off, p, 0.0)
                    p = jnp.where(lane >= off, p, 0.0)
                out[px][tile] += p
        return jnp.concatenate([jnp.concatenate(o, axis=1) for o in out], axis=0)

    for d in range(2):
        hi, lo = split(img[d].reshape(272, 68))
        k = keep[...] * sc[1 + d]
        own[d] = flat(dot(hi, even[...], NN) + dot(lo, even[...], NN), 34, 40, OWN // 128) * k
        hi = dot(rows, hi, NN).astype(bf16)
        lo = dot(rows, lo, NN).astype(bf16)
        crop[d] = flat(dot(hi, pick, NN) + dot(lo, pick, NN), 26, 32, CROP // 128) * k


def prepare(dims, img, ext, mods, si, w3t, vectors):
    def body(r):
        r.slabs = dims[1]
        prepare_kernel(r)

    return launch(
        body, "prepare", None,
        [("img", img, VM), ("even", deinterleave(), VM), ("ext", ext, SM), ("mods", mods, SM), ("si", si, SM), ("w3t", w3t, VM)]
        + [(f"v{j}", v.reshape(1, -1), VM) for j, v in enumerate(vectors)],
        [("own", (2, 16, OWN), f32, VM), ("crop", (2, 16, CROP), f32, VM), ("par", (8, 256), f32, VM),
         ("keep", (16, 1), f32, VM), ("sc", (16,), f32, SM), ("w3u", (27, 128, 64), f32, VM), ("w3c", (27, 64, 64), f32, VM)],
        [],
    )


def tap_spread():
    sel = np.zeros((4, 192, 112), np.float32)
    for t in range(27):
        i, j, k = t // 9, (t // 3) % 3, t % 3
        for q in range(4):
            r, s = j + q // 2, k + q % 2
            for c in range(4):
                row = i * 64 + (2 * (r // 2) + s // 2) * 16 + (s % 2) * 8 + (r % 2) * 4 + c
                sel[q, row, t * 4 + c] = 1.0
    return jnp.asarray(sel, bf16)


def first_weights(r):
    r.wf4[...] = jnp.zeros(r.wf4.shape, f32)
    for t in range(27):
        w = r.wf[t]
        r.wf4[4 * t : 4 * t + 4, :] = jnp.concatenate([w, w, w, w], axis=1)
    hi, lo = split(r.wf4[...])
    lane = lax.broadcasted_iota(jnp.int32, (192, 128), 1) // 32
    wh = jnp.zeros((192, 128), f32)
    wl = jnp.zeros((192, 128), f32)
    for q in range(4):
        wh += jnp.where(lane == q, dot(r.spread[q], hi, NN), 0.0)
        wl += jnp.where(lane == q, dot(r.spread[q], lo, NN), 0.0)
    r.w1h[...] = wh.astype(bf16)
    r.w1l[...] = wl.astype(bf16)


def first_stage(r):
    for p in range(6):
        own = r.so[p]
        crop = r.sr[p]
        for ab in range(4):
            a, b = ab // 2, ab % 2
            rows = slice(p * 64 + ab * 16, p * 64 + ab * 16 + 16)
            hi, lo = split(own if ab == 0 else pltpu.roll(own, OWN - 40 * a - b, 1))
            r.sh[rows, :] = hi
            r.sl[rows, :] = lo
            hi, lo = split(crop if ab == 0 else pltpu.roll(crop, CROP - 32 * a - b, 1))
            r.ch[rows, :] = hi
            r.cl[rows, :] = lo
    for w, out in ((r.w1h, r.wdh), (r.w1l, r.wdl)):
        out[...] = jnp.zeros(out.shape, bf16)
        out[:192, :128] = w[...]
        out[64:, 128:] = w[...]
    wh, wl = r.wdh[...], r.wdl[...]
    def pair(t):
        rows = pl.ds(pl.multiple_of(t * 128, 128), 256)
        v = dot3(r.sh[rows, :], r.sl[rows, :], wh, wl, TN)
        r.r1[2 * t, :OWN, :] = v[:, :128]
        r.r1[2 * t + 1, :OWN, :] = v[:, 128:]
        v = dot3(r.ch[rows, :], r.cl[rows, :], wh, wl, TN)
        r.r1c[2 * t] = v[:, :128]
        r.r1c[2 * t + 1] = v[:, 128:]

    loop(2, pair)
    for d in range(4):
        r.r1[d, OWN:, :] = jnp.zeros((1440 - OWN, 128), f32)
    s = jnp.zeros((1, 128), f32)
    q = jnp.zeros((1, 128), f32)
    for d in range(2):
        def part(t, c):
            x = r.r1[1 + d, pl.ds(pl.multiple_of(t * 160, 160), 160), :].reshape(4, 40, 128)
            x = jnp.where(cells(x.shape, 33, 33, 4 * t), x, 0.0)
            return c[0] + jnp.sum(x, axis=0), c[1] + jnp.sum(x * x, axis=0)

        ps, pq = lax.fori_loop(0, 9, part, (jnp.zeros((40, 128), f32), jnp.zeros((40, 128), f32)))
        s = s + r.sc[1 + d] * jnp.sum(ps, axis=0, keepdims=True)
        q = q + r.sc[1 + d] * jnp.sum(pq, axis=0, keepdims=True)
    put_sums(r.st1, s, q)


def front_kernel(dims, r):
    net = Net(dims, True, [r.sem0, r.sem1, r.sem2, r.sem3, r.sem4, r.sem5])
    net.enter()
    mv = Moves(r.sem8)
    first_weights(r)
    mv.out((r.w1h, r.ow1h), (r.w1l, r.ow1l))
    toeplitz(r.w2, 0, 32, r.t2h, r.t2l)
    toeplitz(r.w3, 0, 128, r.tuh, r.tul)
    up_blocks(r)
    net.ready()
    start, finish = source_copies(dims, r.own, r.crop, r.so, r.sr, r.sem6, r.sem7)
    start()
    net.to_left(r.co.at[0], r.cor, 0)
    net.to_right(r.co.at[0], r.col, 0)
    r.usc[...] = jnp.zeros(r.usc.shape, f32)
    compose(r, 0)
    compose(r, 1)
    finish()
    first_stage(r)
    mv.out((r.sh, r.osh), (r.sl, r.osl), (r.r1, r.or1))
    net.share(r.st1, r.g1, 0)
    compose(r, 2)
    composed(r)
    mv.out((r.uh, r.ouh), (r.ul, r.oul), (r.ubh, r.oubh), (r.ubl, r.oubl))
    net.shared(r.st1, r.g1, 0)

    half = net.s
    f = r.f
    f[...] = jnp.zeros(f.shape, f32)
    scale_c, off_c = affine(r.par, 0, *moments(r.g1, 1 - half, r.sc[9] * 4356.0, 128))

    def crop(p):
        m = r.sc[4 + p]

        def rows(t):
            x = r.r1c[p, pl.ds(pl.multiple_of(t * 128, 128), 128), :].reshape(4, 32, 128)
            f[pl.ds(4 * t, 4), :32, :] = jnp.where(m > 0, silu(x * scale_c + off_c), 0.0)

        loop(7, rows)
        im2col(r.ah, r.al, p, f, 24, 24, 128)

    loop(4, crop)
    conv(r.r2c, r.ah, r.al, r.t2h, r.t2l, 576, NN)
    net.to_left(r.r2c.at[0:576], r.hr, 1)
    net.to_right(r.r2c.at[576:1152], r.hl, 1)
    mv.out((r.r2c, r.or2c))
    scale, off = affine(r.par, 0, *moments(r.g1, half, r.sc[8] * 4356.0, 128))

    def own(p):
        m = r.sc[p]

        def rows(t):
            x = r.r1[p, pl.ds(pl.multiple_of(t * 160, 160), 160), :].reshape(4, 40, 128)
            f[pl.ds(4 * t, 4), :40, :] = jnp.where(m > 0, silu(x * scale + off), 0.0)

        loop(9, rows)
        im2col(r.ah, r.al, p, f, 32, 32, 128)

    loop(4, own)
    mv.out((r.ah, r.oah), (r.al, r.oal))
    conv(r.r2, r.ah, r.al, r.t2h, r.t2l, 1024, NN)
    mv.out((r.r2, r.or2))
    s = jnp.zeros((1, 256), f32)
    q = jnp.zeros((1, 256), f32)
    for d in range(2):
        def part(t, c):
            x = r.r2[pl.ds(pl.multiple_of(d * 1024 + t * 128, 128), 128), :].reshape(16, 8, 256)
            return c[0] + jnp.sum(x, axis=0), c[1] + jnp.sum(x * x, axis=0)

        ps, pq = lax.fori_loop(0, 8, part, (jnp.zeros((8, 256), f32), jnp.zeros((8, 256), f32)))
        s = s + r.sc[1 + d] * jnp.sum(ps, axis=0, keepdims=True)
        q = q + r.sc[1 + d] * jnp.sum(pq, axis=0, keepdims=True)
    put_sums(r.st2, s, q)
    net.share(r.st2, r.g2, 1)
    net.shared(r.st2, r.g2, 1)
    net.sides()
    mv.finish()


def conv(out, ah, al, th, tl, rows, dims):
    out[...] = jnp.zeros(out.shape, f32)

    def tap(i):
        at = pl.ds(pl.multiple_of(i * rows, 16), 2 * rows)
        out[...] += dot3(ah[at, :], al[at, :], th[i], tl[i], dims)

    loop(3, tap)


def front(dims, own, crop, wf, w2, w3, up, co, par, sc):
    n = dims[0] * dims[1] * dims[2]
    V = pltpu.VMEM
    forms = [("u", (4, 512, 256)), ("ub", (4, 128, 1024)), ("s", (384, OWN)), ("a", (4096, 512)), ("w1", (192, 128))]
    outs = [("g1", (n, 1, 512), f32, VM), ("g2", (n, 1, 512), f32, VM),
            ("or1", (4, 1440, 128), f32, HB), ("or2", (2048, 256), f32, HB), ("or2c", (1152, 256), f32, HB),
            ("col", co.shape[1:], f32, HB), ("cor", co.shape[1:], f32, HB),
            ("hl", (576, 256), f32, HB), ("hr", (576, 256), f32, HB)]
    scratch = []
    for name, shape in forms:
        outs += both_out("o" + name, shape)
        scratch += both(name, shape)
    scratch += both("t2", (3, 512, 256)) + both("tu", (3, 2048, 256)) + both("up", (256, 512)) + both("c", (384, CROP)) + both("wd", (256, 256))
    scratch += [("st1", V((1, 512), f32)), ("st2", V((1, 512), f32)), ("so", V((6, 16, OWN), f32)),
                ("sr", V((6, 16, CROP), f32)), ("wf4", V((112, 128), f32)), ("usc", V((4, 512, 256), f32)),
                ("r1", V((4, 1440, 128), f32)), ("r1c", V((4, CROP, 128), f32)), ("r2", V((2048, 256), f32)),
                ("r2c", V((1152, 256), f32)), ("f", V((36, 48, 128), f32))]
    return launch(
        functools.partial(front_kernel, dims), "front", 1,
        [("own", own, VM), ("crop", crop, VM), ("wf", wf, VM), ("spread", tap_spread(), VM), ("w2", w2, VM),
         ("w3", w3, VM), ("up", up, VM), ("co", co, HB), ("par", par, VM), ("sc", sc, SM)],
        outs, scratch + sems(n, n, n, n, 4, 4, 5, 5, 32),
    )


def third_kernel(dims, r):
    net = Net(dims, False, [r.sem0, r.sem1, r.sem2, r.sem3])
    net.enter()
    mv = Moves(r.sem4)
    weights = fetch(mv, (r.iuh, r.uh), (r.iul, r.ul))
    ready_r2 = fetch(mv, (r.ir2, r.r2))
    toeplitz(r.w3, 0, 64, r.t3h, r.t3l)
    f, f2, sc = r.f, r.f2, r.sc
    scale_c, off_c = affine(r.par, 1, *moments(r.g2, 1 - net.s, sc[9] * 4096.0, 256))
    f[...] = jnp.zeros(f.shape, f32)

    def put(p, get):
        m = sc[4 + p]

        def rows(t):
            x = silu(get(t * 96) * scale_c + off_c).reshape(4, 24, 256)
            f[pl.ds(4 * t, 4), :24, :] = jnp.where(m > 0, x, 0.0)

        loop(6, rows)
        im2col(r.ah, r.al, p, f, 24, 24, 256)

    def of(ref, base):
        return lambda at: ref[pl.ds(pl.multiple_of(base + at, 32), 96), :]

    put(0, of(r.hl, 0))
    loop(2, lambda p: put(p + 1, of(r.r2c, p * 576)))
    put(3, of(r.hr, 0))
    mv.out((r.ah, r.oah), (r.al, r.oal))
    f2[...] = jnp.zeros(f2.shape, f32)
    for p, (src, m) in enumerate(((r.col, sc[4]), (r.co, sc[5]), (r.cor, sc[7]))):
        f2[:24, :24, :] = jnp.where(m > 0, src[...], 0.0)
        im2col(r.cuh, r.cul, p, f2, 24, 24, 128)
    mv.out((r.cuh, r.ocuh), (r.cul, r.ocul))
    weights()
    conv(r.r3, r.ah, r.al, r.t3h, r.t3l, 576, NN)

    def up(j):
        at = pl.ds(pl.multiple_of((j // 2 + j % 2) * 576, 16), 576)
        out = pl.ds(pl.multiple_of((j // 2) * 576, 16), 576)
        r.r3[out, :] += dot3(r.cuh[at, :], r.cul[at, :], r.uh[j], r.ul[j], NN)

    loop(4, up)
    net.ready()
    net.to_left(r.r3.at[0:576], r.nr, 0)
    net.to_right(r.r3.at[576:1152], r.nl, 0)
    s0, q0 = field_sums(r.r3, 0, 576, 23, 23, sc[5])
    s1, q1 = field_sums(r.r3, 1, 576, 23, 23, sc[6])
    put_sums(r.st, s0 + s1, q0 + q1)
    net.share(r.st, r.g3)
    mv.out((r.r3, r.or3))
    scale, off = affine(r.par, 1, *moments(r.g2, net.s, sc[8] * 4096.0, 256))

    def pool(t):
        v = jnp.zeros((128, 256), f32)
        for d in range(2):
            x = r.r2[pl.ds(pl.multiple_of(d * 1024 + t * 128, 128), 128), :]
            v = v + sc[1 + d] * silu(x * scale + off)
        v = v[:, :128] + v[:, 128:]
        v = (v + pltpu.roll(v, 64, 1)) * 0.125
        r.pooled[pl.ds(pl.multiple_of(t * 128, 128), 128), :] = v[:, :64]

    ready_r2()
    loop(8, pool)
    net.shared(r.st, r.g3)
    net.sides()
    mv.finish()


def third(dims, k, co, w3, par, sc):
    n = dims[1] * dims[2]
    V = pltpu.VMEM
    outs = [("pooled", (1024, 64), f32, VM), ("g3", (n, 1, 512), f32, VM), ("or3", (1152, 256), f32, HB),
            ("nl", (576, 256), f32, HB), ("nr", (576, 256), f32, HB)]
    scratch = []
    for name, shape in [("a", (2304, 1024)), ("cu", (1728, 512))]:
        outs += both_out("o" + name, shape)
        scratch += both(name, shape)
    scratch += both("t3", (3, 1024, 256)) + both("u", (4, 512, 256))
    scratch += [("st", V((1, 512), f32)), ("r3", V((1152, 256), f32)), ("f", V((26, 32, 256), f32)),
                ("f2", V((26, 32, 128), f32)), ("r2", V((2048, 256), f32))]
    return launch(
        functools.partial(third_kernel, dims), "third", 2,
        [("ir2", k.or2, HB), ("r2c", k.or2c, VM), ("hl", k.hl, VM), ("hr", k.hr, VM), ("co", co[0], VM),
         ("col", k.col, VM), ("cor", k.cor, VM), ("g2", k.g2, VM), ("par", par, VM),
         ("iuh", k.ouh, HB), ("iul", k.oul, HB), ("w3", w3, VM), ("sc", sc, SM)],
        outs, scratch + sems(n, n, 2, 2, 32),
    )


def fourth_kernel(dims, r):
    net = Net(dims, False, [r.sem0, r.sem1, r.sem2, r.sem3, r.sem4, r.sem5, r.sem6, r.sem7])
    net.enter()
    mv = Moves(r.sem8)
    toeplitz(r.w4, 0, 64, r.t4h, r.t4l, r.d4h, r.d4l)
    sc, f, par = r.sc, r.f, r.par
    avg3, inv3 = moments(r.g3, None, sc[9] * 2116.0, 256)
    scale, off = affine(par, 2, avg3, inv3)
    f[...] = jnp.zeros(f.shape, f32)

    def put(p, get):
        m = sc[4 + p]

        def rows(t):
            x = silu(get(t * 96) * scale + off).reshape(4, 24, 256)
            f[pl.ds(4 * t, 4), :24, :] = jnp.where(m > 0, x, 0.0)

        loop(6, rows)
        im2col(r.ah, r.al, p, f, 22, 24, 256)

    def of(ref, base, step):
        return lambda at: ref[pl.ds(pl.multiple_of(base + at, 16), step), :]

    put(0, of(r.r3l, 0, 96))
    loop(2, lambda p: put(p + 1, of(r.r3, p * 576, 96)))
    put(3, of(r.r3r, 0, 96))
    conv(r.r4, r.ah, r.al, r.t4h, r.t4l, 528, NN)
    net.ready()
    net.to_left(r.r4.at[0:528], r.r4r, 0)
    net.to_right(r.r4.at[528:1056], r.r4l, 0)
    s0, q0 = field_sums(r.r4, 0, 528, 22, 22, sc[5])
    s1, q1 = field_sums(r.r4, 1, 528, 22, 22, sc[6])
    put_sums(r.st4, s0 + s1, q0 + q1)
    net.share(r.st4, r.g4, 0)
    r.og[...] = jnp.zeros(r.og.shape, f32)

    def gather(t):
        for d in range(2):
            for py in range(2):
                x0 = r.ograw[d, 2 * t + py, pl.ds(0, 22, stride=2), :]
                x1 = r.ograw[d, 2 * t + py, pl.ds(1, 22, stride=2), :]
                r.og[d, t, pl.ds(0, 22), py * 128 : py * 128 + 128] = jnp.concatenate([x0, x1], axis=1)

    loop(22, gather)
    net.to_left(r.og.at[0], r.ogr, 1)
    net.to_right(r.og.at[1], r.ogl, 1)
    net.shared(r.st4, r.g4, 0)

    count = sc[9] * 1936.0
    avg, inv = moments(r.g4, None, count, 256)
    scale4, off4 = affine(par, 3, avg, inv)
    s = jnp.zeros((1, 256), f32)
    q = jnp.zeros((1, 256), f32)
    for d in range(2):
        m = sc[5 + d]

        def part(t, c):
            x = r.r4[pl.ds(pl.multiple_of(d * 528 + t * 48, 16), 48), :]
            b = x * scale4 + off4
            sg = 1.0 / (1.0 + jnp.exp(-b))
            r.dec[d, pl.ds(2 * t, 2)] = (m * (b * sg)).reshape(2, 24, 256)
            bg = r.og[d, pl.ds(2 * t, 2)].reshape(48, 256) * sg * (1.0 + b * (1.0 - sg))
            normed = (x - avg) * inv
            return (
                c[0] + jnp.sum(bg.reshape(6, 8, 256), axis=0),
                c[1] + jnp.sum((bg * normed).reshape(6, 8, 256), axis=0),
            )

        ps, pq = lax.fori_loop(0, 11, part, (jnp.zeros((8, 256), f32), jnp.zeros((8, 256), f32)))
        s = s + m * jnp.sum(ps, axis=0, keepdims=True)
        q = q + m * jnp.sum(pq, axis=0, keepdims=True)
    put_sums(r.st5, s, q)
    net.share(r.st5, r.g5, 1)

    def spread(t):
        for d in range(2):
            for py in range(2):
                v = r.dec[d, t, pl.ds(0, 22), py * 128 : py * 128 + 128]
                r.decoded[d, 2 * t + py, pl.ds(0, 22, stride=2), :] = v[:, :64]
                r.decoded[d, 2 * t + py, pl.ds(1, 22, stride=2), :] = v[:, 64:]

    loop(22, spread)
    net.shared(r.st5, r.g5, 1)
    net.sides()

    tg, tc = totals(r.g5, None, 256)
    f[...] = jnp.zeros(f.shape, f32)

    def put_back(p, get_r, get_a, keep):
        m = sc[4 + p]

        def rows(t):
            a = get_a(2 * t).reshape(48, 256)
            e = response_back(par, 3, avg, inv, tg, tc, count, get_r(t * 48), a).reshape(2, 24, 256)
            e = jnp.where(cells(e.shape, 22, 22, 0) & (m > 0), e, 0.0)
            f[pl.ds(1 + 2 * t, 2), 8:32, :] = e
            if keep is not None:
                hi, lo = split(e.reshape(48, 256))
                at = pl.ds(pl.multiple_of(keep * 528 + t * 48, 16), 48)
                r.eh[at, :] = hi
                r.el[at, :] = lo

        loop(11, rows)
        im2col(r.bh, r.bl, p, f, 24, 24, 256, x0=7)

    put_back(0, of(r.r4l, 0, 48), lambda y: r.ogl[pl.ds(y, 2)], None)
    loop(2, lambda p: put_back(p + 1, of(r.r4, p * 528, 48), lambda y: r.og[p, pl.ds(y, 2)], p))
    put_back(3, of(r.r4r, 0, 48), lambda y: r.ogr[pl.ds(y, 2)], None)
    conv(r.a3, r.bh, r.bl, r.d4h, r.d4l, 576, NT)
    net.halos = []
    net.sems = [r.sem0, r.sem1, r.sem2, r.sem3, r.sem4, r.sem5, r.sem9, r.sem10]
    net.to_left(r.a3.at[0:576], r.a3r, 0)
    net.to_right(r.a3.at[576:1152], r.a3l, 0)
    mv.out((r.a3, r.oa3))
    s = jnp.zeros((1, 256), f32)
    q = jnp.zeros((1, 256), f32)
    for d in range(2):
        def part(t, c):
            at = pl.ds(pl.multiple_of(d * 576 + t * 48, 16), 48)
            normed, bg = back_parts(par, 2, avg3, inv3, r.r3[at, :], r.a3[at, :])
            bg = bg.reshape(2, 24, 256)
            bg = jnp.where(cells(bg.shape, 23, 23, 2 * t), bg, 0.0)
            return c[0] + jnp.sum(bg, axis=0), c[1] + jnp.sum(bg * normed.reshape(2, 24, 256), axis=0)

        ps, pq = lax.fori_loop(0, 12, part, (jnp.zeros((24, 256), f32), jnp.zeros((24, 256), f32)))
        s = s + sc[5 + d] * jnp.sum(ps, axis=0, keepdims=True)
        q = q + sc[5 + d] * jnp.sum(pq, axis=0, keepdims=True)
    put_sums(r.st6, s, q)
    net.share(r.st6, r.g6, 2)

    def tap(i):
        at = pl.ds(pl.multiple_of(i * 528, 16), 1056)
        r.g[...] = dot3(r.ah[at, :], r.al[at, :], r.eh[...], r.el[...], TN)
        put_taps(r.dw4, r.g, i, 64, 64, 0, 0)

    loop(3, tap)
    net.shared(r.st6, r.g6, 2)
    net.sides()
    mv.finish()


def put_taps(out, g, i, chans, total, row0, base):
    def rows(p):
        return pl.ds(pl.multiple_of(base + (i * 5 + p // 2) * total + row0, 8), chans)

    for p in range(9):
        v = folded(g, p // 3, p % 3, chans)
        v = v if p % 2 == 0 else pltpu.roll(v, 64, 1)
        at = 64 * (p % 2)
        out[rows(p), at : at + 64] = v[:, at : at + 64]
    out[rows(8), 64:] = jnp.zeros((chans, 64), f32)


def fourth(dims, r3, r3l, r3r, g3, og, w4, par, sc):
    n = dims[1] * dims[2]
    V = pltpu.VMEM
    box = (22, 24, 256)
    return launch(
        functools.partial(fourth_kernel, dims), "fourth", 3,
        [("r3", r3, VM), ("r3l", r3l, VM), ("r3r", r3r, VM), ("g3", g3, VM), ("ograw", og, VM), ("par", par, VM),
         ("w4", w4, VM), ("sc", sc, SM)],
        [("decoded", (2, 44, 44, 64), f32, VM), ("oa3", (1152, 256), f32, HB), ("a3l", (576, 256), f32, HB),
         ("a3r", (576, 256), f32, HB), ("g6", (n, 1, 512), f32, VM), ("st5", (1, 512), f32, VM),
         ("st6", (1, 512), f32, VM), ("dw4", (960, 128), f32, VM)],
        both("t4", (3, 1024, 256)) + both("d4", (3, 256, 1024)) + both("a", (2112, 1024)) + both("b", (2304, 1024))
        + both("e", (1056, 256))
        + [("f", V((26, 40, 256), f32)), ("r4", V((1056, 256), f32)), ("r4l", V((528, 256), f32)),
           ("r4r", V((528, 256), f32)), ("og", V((2,) + box, f32)), ("ogl", V(box, f32)), ("ogr", V(box, f32)),
           ("dec", V((2,) + box, f32)), ("a3", V((1152, 256), f32)), ("g", V((1024, 256), f32)),
           ("g4", V((n, 1, 512), f32)), ("g5", V((n, 1, 512), f32)), ("st4", V((1, 512), f32))]
        + sems(n, n, n, n, n, n, 4, 4, 8, 2, 2),
    )


def third_back_kernel(dims, r):
    net = Net(dims, False, [])
    barrier = pltpu.get_barrier_semaphore()
    partner = (1 - net.s, net.k, net.b)
    pl.semaphore_signal(barrier, inc=1, device_id=partner, device_id_type=MESH)
    mv = Moves(r.sem0)
    ready_a = fetch(mv, (r.iah, r.ah), (r.ial, r.al))
    ready_u = fetch(mv, (r.icuh, r.cuh), (r.icul, r.cul), (r.iubh, r.ubh), (r.iubl, r.ubl))
    toeplitz(r.w3c, 0, 64, None, None, r.d3h, r.d3l)
    sc, f, par = r.sc, r.f, r.par
    count = sc[9] * 2116.0
    avg, inv = moments(r.g3, None, count, 256)
    tg, tc = totals(r.g6, None, 256)
    f[...] = jnp.zeros(f.shape, f32)

    def of(ref, base):
        return lambda at: ref[pl.ds(pl.multiple_of(base + at, 16), 48), :]

    def put(p, get_r, get_a, keep):
        m = sc[4 + p]

        def rows(t):
            e = response_back(par, 2, avg, inv, tg, tc, count, get_r(t * 48), get_a(t * 48)).reshape(2, 24, 256)
            e = jnp.where(cells(e.shape, 23, 23, 2 * t) & (m > 0), e, 0.0)
            f[pl.ds(1 + 2 * t, 2), 8:32, :] = e
            if keep is not None:
                hi, lo = split(e.reshape(48, 256))
                at = pl.ds(pl.multiple_of(keep * 576 + t * 48, 16), 48)
                r.eh[at, :] = hi
                r.el[at, :] = lo

        loop(12, rows)
        im2col(r.bh, r.bl, p, f, 24, 24, 256, x0=7)

    put(0, of(r.r3l, 0), of(r.a3l, 0), None)
    loop(2, lambda p: put(p + 1, of(r.r3, p * 576), of(r.a3, p * 576), p))
    put(3, of(r.r3r, 0), of(r.a3r, 0), None)
    conv(r.g.at[:1152], r.bh, r.bl, r.d3h, r.d3l, 576, NT)

    def row(t):
        at = pl.ds(pl.multiple_of(t * 24, 24), 24)
        r.skip[2 * t] = r.g[at, :128]
        r.skip[2 * t + 1] = r.g[at, 128:]

    loop(48, row)
    pl.semaphore_wait(barrier, 1)
    across = pltpu.make_async_remote_copy(
        src_ref=r.skip, dst_ref=r.oskip, send_sem=r.sem1.at[0], recv_sem=r.sem1.at[1],
        device_id=partner, device_id_type=MESH,
    )
    across.start()

    ready_a()
    bucket = r.bucket

    def tap(i):
        at = pl.ds(pl.multiple_of(i * 576, 16), 1152)
        r.g[:1024, :] = dot3(r.ah[at, :], r.al[at, :], r.eh[...], r.el[...], TN)
        put_taps(bucket, r.g, i, 64, 192, 128, 0)

    loop(3, tap)
    ready_u()

    def coarse(j):
        at = pl.ds(pl.multiple_of((j // 2 + j % 2) * 576, 16), 576)
        e = pl.ds(pl.multiple_of((j // 2) * 576, 16), 576)
        r.gu[j] = dot3(r.cuh[at, :], r.cul[at, :], r.eh[e, :], r.el[e, :], TN)

    loop(4, coarse)
    r.cg[...] = jnp.zeros(r.cg.shape, f32)

    def back(p):
        at = pl.ds(pl.multiple_of(p * 576, 16), 576)
        r.cg[...] += sc[5] * dot3(r.bh[at, :], r.bl[at, :], r.ubh[p], r.ubl[p], NT)

    loop(4, back)
    up_blocks(r)
    r.gd[...] = jnp.zeros(r.gd.shape, f32)
    for i in range(3):
        loop(1, lambda _, i=i: toeplitz_tap(r.w3u, 0, 128, i, 0, r.tuh, r.tul))

        def block(ab, i=i):
            out = pl.ds(pl.multiple_of(ab * 128, 128), 128)
            p = jnp.concatenate([r.gu[slot_of(i, 0), out, :], r.gu[slot_of(i, 1), out, :]], axis=0)
            ph, plo = split(p)
            rows = pl.ds(pl.multiple_of(ab * 512, 512), 512)
            r.gd[...] += dot3(ph, plo, r.tuh[0, rows, :], r.tul[0, rows, :], NT)
            r.g[rows, :] = dot3(r.uph[...], r.upl[...], ph, plo, TN)

        loop(4, block)
        loop(1, lambda _, i=i: put_taps(bucket, r.g, i, 128, 192, 0, 0))
    bucket[2880:3840, :] = r.dw4[...]
    for ip in range(2):
        for q in range(4):
            at = 3840 + (ip * 4 + q) * 128
            bucket[at : at + 128, :] = r.gd[ip * 128 : ip * 128 + 128, q * 128 : q * 128 + 128]
    if bucket.shape[0] > BUCKET:
        bucket[BUCKET:, :] = jnp.zeros((bucket.shape[0] - BUCKET, 128), f32)
    mv.out((bucket, r.obucket))
    across.wait()
    mv.finish()


def bucket_rows(dims):
    n = dims[0] * dims[1] * dims[2]
    return -(-BUCKET // (8 * n)) * 8


def third_back(dims, fb, r3, r3l, r3r, g3, k, t, dw4, w3u, w3c, up, par, sc):
    n = dims[0] * dims[1] * dims[2]
    V = pltpu.VMEM
    rows = n * bucket_rows(dims)
    return launch(
        functools.partial(third_back_kernel, dims), "third_back", 4,
        [("a3", fb.oa3, VM), ("a3l", fb.a3l, VM), ("a3r", fb.a3r, VM), ("r3", r3, VM), ("r3l", r3l, VM),
         ("r3r", r3r, VM), ("g3", g3, VM), ("g6", fb.g6, VM), ("dw4", dw4, VM), ("par", par, VM),
         ("w3u", w3u, VM), ("w3c", w3c, VM), ("up", up, VM), ("iah", t.oah, HB), ("ial", t.oal, HB),
         ("icuh", t.ocuh, HB), ("icul", t.ocul, HB), ("iubh", k.oubh, HB), ("iubl", k.oubl, HB), ("sc", sc, SM)],
        [("oskip", (96, 24, 128), f32, HB), ("cg", (576, 128), f32, VM), ("obucket", (rows, 128), f32, HB)],
        both("tu", (1, 2048, 256)) + both("d3", (3, 256, 1024)) + both("a", (2304, 1024)) + both("cu", (1728, 512))
        + both("up", (256, 512)) + both("ub", (4, 128, 1024)) + both("b", (2304, 1024)) + both("e", (1152, 256))
        + [("f", V((26, 40, 256), f32)), ("skip", V((96, 24, 128), f32)),
           ("g", V((2048, 256), f32)), ("gu", V((4, 512, 256), f32)), ("gd", V((256, 512), f32)),
           ("bucket", V((rows, 128), f32))]
        + sems(24, 2),
    )


class Reduction:
    def __init__(self, dims, r, net):
        S, K, B = dims
        self.r, self.net = r, net
        self.per = bucket_rows(dims)
        self.Q, self.B, self.half = S * K // 2, B, S * K * B // 2
        self.core = net.k % 2
        self.q = net.s * (K // 2) + net.k // 2
        self.rows = K // 2
        self.pair_of = (net.s, net.k + 1 - 2 * self.core, net.b)
        self.place = self.core * self.half + self.q * self.B + net.b

    def ds(self, first, count):
        return pl.ds(pl.multiple_of(first * self.per, 8), count * self.per)

    def at_square(self, q):
        return (q // self.rows, 2 * (q % self.rows) + self.core, self.net.b)

    def copies(self, sem, items):
        self.open = [
            pltpu.make_async_remote_copy(
                src_ref=src, dst_ref=dst, send_sem=sem.at[2 * j], recv_sem=sem.at[2 * j + 1],
                device_id=dev, device_id_type=MESH,
            )
            for j, (src, dst, dev) in enumerate(items)
        ]
        for c in self.open:
            c.start()

    def wait(self):
        for c in self.open:
            c.wait()

    def pair(self, sem, mv):
        self.own = mv.start(self.r.bucket.at[self.ds(self.core * self.half, self.half)], self.r.mine1)
        src = self.r.bucket.at[self.ds((1 - self.core) * self.half, self.half)]
        self.copies(sem, [(src, self.r.slot1, self.pair_of)])

    def pair_done(self):
        self.wait()
        self.own.wait()
        size = self.half * self.per // 16

        def add(t):
            at = pl.ds(pl.multiple_of(t * size, 8), size)
            self.r.mine1[at, :] += self.r.slot1[at, :]

        loop(16, add)

    def square(self, sem):
        items = []
        for t in range(1, self.Q):
            q = (self.q + t) % self.Q
            items.append((self.r.mine1.at[self.ds(q * self.B, self.B)], self.r.slot2.at[t - 1], self.at_square(q)))
        self.copies(sem, items)

    def square_done(self):
        self.wait()
        v = self.r.mine1[self.ds(self.q * self.B, self.B), :]
        for t in range(self.Q - 1):
            v = v + self.r.slot2[t]
        self.r.mine2[...] = v

    def line(self, sem):
        items = []
        for t in range(1, self.B):
            b = (self.net.b + t) % self.B
            items.append((self.r.mine2.at[self.ds(b, 1)], self.r.slot3.at[t - 1], (self.net.s, self.net.k, b)))
        self.copies(sem, items)

    def line_done(self):
        self.wait()
        v = self.r.mine2[self.ds(self.net.b, 1), :]
        for t in range(self.B - 1):
            v = v + self.r.slot3[t]
        self.r.res[self.ds(self.place, 1), :] = v

    def line_back(self, sem):
        own = self.r.res.at[self.ds(self.place, 1)]
        self.copies(
            sem,
            [(own, own, (self.net.s, self.net.k, (self.net.b + t) % self.B)) for t in range(1, self.B)],
        )

    def square_back(self, sem):
        own = self.r.res.at[self.ds(self.core * self.half + self.q * self.B, self.B)]
        self.copies(sem, [(own, own, self.at_square((self.q + t) % self.Q)) for t in range(1, self.Q)])

    def pair_back(self, sem):
        own = self.r.res.at[self.ds(self.core * self.half, self.half)]
        self.copies(sem, [(own, own, self.pair_of)])


def skip_stage(r, net, avg, inv):
    sc, par = r.sc, r.par
    oy, ox = r.si[0, 0], r.si[0, 1]
    qx = ox // 2
    rx = ox - 2 * qx
    odd = rx > 0
    s = jnp.zeros((1, 256), f32)
    q = jnp.zeros((1, 256), f32)
    lane = lax.broadcasted_iota(jnp.int32, (32, 128), 1)
    pad = jnp.zeros((8, 128), f32)
    for d in range(2):
        def placed(row):
            at = row - oy
            v = r.skip[d * 48 + jnp.clip(at, 0, 47)]
            v = jnp.where((at >= 0) & (at < 48), v, 0.0)
            v = jnp.concatenate([v, pad], axis=0)
            v = jnp.where(odd, pltpu.roll(v, 64, 1), v)
            v = pltpu.roll(v, qx, 0)
            return jnp.where((lane < 64) & odd, pltpu.roll(v, 1, 0), v)

        def part(t, c):
            pv = r.pg[t] * 0.125
            pv = jnp.concatenate([pv, pv], axis=1)
            a = jnp.concatenate([placed(2 * t) + pv, placed(2 * t + 1) + pv], axis=1)
            rows = pl.ds(pl.multiple_of(d * 1024 + t * 32, 32), 32)
            normed, bg = back_parts(par, 1, avg, inv, r.r2[rows, :], a)
            bg = sc[1 + d] * bg
            r.bg2[rows, :] = bg
            bg = bg.reshape(4, 8, 256)
            return c[0] + jnp.sum(bg, axis=0), c[1] + jnp.sum(bg * normed.reshape(4, 8, 256), axis=0)

        ps, pq = lax.fori_loop(0, 32, part, (jnp.zeros((8, 256), f32), jnp.zeros((8, 256), f32)))
        s = s + jnp.sum(ps, axis=0, keepdims=True)
        q = q + jnp.sum(pq, axis=0, keepdims=True)
    put_sums(r.st7, s, q)


def store_slots(slots, x, row0):
    per = slots.shape[1]
    for at in range(0, x.shape[0], per):
        slots[(row0 + at) // per] = x[at : at + per]


def four_rows(st):
    v = st[...]
    return [v[:, 128 * c : 128 * c + 128] for c in range(4)]


def tail_kernel(dims, r):
    net = Net(dims, False, [r.sem0, r.sem1, r.sem2, r.sem3, r.sem4, r.sem5])
    world = Net(dims, True, [r.sem6, r.sem7, r.sem8, r.sem9, r.sem16, r.sem17, r.sem18, r.sem19])
    world.enter()
    mv = Moves(r.sem10)
    ready_a = fetch(mv, (r.iah, r.ah), (r.ial, r.al))
    ready_s = fetch(mv, (r.ish, r.sh), (r.isl, r.sl), (r.ir1.at[1:3], r.r1))
    sc, par, f = r.sc, r.par, r.f
    count = sc[8] * 4096.0
    avg, inv = moments(r.g2, net.s, count, 256)
    toeplitz(r.w2, 0, 32, None, None, r.d2h, r.d2l)
    f[...] = jnp.zeros(f.shape, f32)
    world.ready()
    large = Reduction(dims, r, net)
    large.pair(r.sem20, mv)
    skip_stage(r, net, avg, inv)
    net.share(r.st7, r.g7, 0)
    large.pair_done()
    large.square(r.sem11)
    net.shared(r.st7, r.g7, 0)

    tg, tc = totals(r.g7, None, 256)
    k = par[2:3, :] * inv

    def put(p):
        m = sc[1 + p]

        def rows(t):
            at = pl.ds(pl.multiple_of(p * 1024 + t * 64, 64), 64)
            normed = (r.r2[at, :] - avg) * inv
            e = k * (r.bg2[at, :] - m * ((tg + normed * tc) / count))
            hi, lo = split(e)
            r.e2h[at, :] = hi
            r.e2l[at, :] = lo
            f[pl.ds(1 + 2 * t, 2), 8:40, :] = e.reshape(2, 32, 256)

        loop(16, rows)
        im2col(r.bh, r.bl, 0, f, 34, 40, 256, x0=7)
        r.v[p] = dot3(r.bh[...], r.bl[...], r.d2h[...].reshape(384, 1024), r.d2l[...].reshape(384, 1024), NT)

    loop(2, put)
    for d in range(2):
        r.side[d, :1360] = r.v[0, :, 256:] if d == 0 else r.v[1, :, :128]
        r.side[d, 1360:] = jnp.zeros((48, 128), f32)
        if d == 0:
            net.to_left(r.side.at[0], r.fr, 0)
        else:
            net.to_right(r.side.at[1], r.fl, 0)
    r.a1[1, :1360] = r.v[0, :, :128] + r.v[1, :, 128:256]
    r.a1[0, :1360] = r.v[0, :, 128:256] + r.v[1, :, 256:]
    for d in range(2):
        r.a1[d, 1360:] = jnp.zeros((48, 128), f32)
    large.square_done()
    large.line(r.sem12)

    ready_a()

    def tap(i):
        at = pl.ds(pl.multiple_of(i * 1024, 1024), 2048)
        r.g[...] = dot3(r.ah[at, :], r.al[at, :], r.e2h[...], r.e2l[...], TN)
        put_taps(r.dw2, r.g, i, 32, 32, 0, 0)

    loop(3, tap)
    store_slots(r.small, r.dw2[...], 0)
    rows = jnp.concatenate(
        four_rows(r.st7) + four_rows(r.st6) + four_rows(r.st5) + [jnp.zeros((20, 128), f32)], axis=0
    )
    store_slots(r.small, rows, 480)
    world.scatter(r.small, r.slots, 0)
    large.line_done()
    large.line_back(r.sem13)
    net.sides()

    ready_s()
    count1 = sc[8] * 4356.0
    avg1, inv1 = moments(r.g1, net.s, count1, 128)
    s = jnp.zeros((1, 128), f32)
    q = jnp.zeros((1, 128), f32)
    for d in range(2):
        other = r.fl if d == 0 else r.fr
        here = sc[10 + d]

        def part(t, c):
            rows = pl.ds(pl.multiple_of(t * 160, 160), 160)
            a = r.a1[d, rows, :] + jnp.where(here > 0, other[rows, :], 0.0)
            r.a1[d, rows, :] = a
            normed, bg = back_parts(par, 0, avg1, inv1, r.r1[d, rows, :], a)
            bg = bg.reshape(4, 40, 128)
            bg = jnp.where(cells(bg.shape, 33, 33, 4 * t), bg, 0.0)
            return c[0] + jnp.sum(bg, axis=0), c[1] + jnp.sum(bg * normed.reshape(4, 40, 128), axis=0)

        ps, pq = lax.fori_loop(0, 8, part, (jnp.zeros((40, 128), f32), jnp.zeros((40, 128), f32)))
        rows = slice(1280, OWN)
        a = r.a1[d, rows, :] + jnp.where(here > 0, other[rows, :], 0.0)
        r.a1[d, rows, :] = a
        normed, bg = back_parts(par, 0, avg1, inv1, r.r1[d, 1280:1320, :], a[:40])
        bg = jnp.where(lax.broadcasted_iota(jnp.int32, (40, 128), 0) < 33, bg, 0.0)
        ps = ps + bg
        pq = pq + bg * normed
        s = s + sc[1 + d] * jnp.sum(ps, axis=0, keepdims=True)
        q = q + sc[1 + d] * jnp.sum(pq, axis=0, keepdims=True)
    put_sums(r.st8, s, q)
    net.share(r.st8, r.g8, 1)
    large.wait()
    large.square_back(r.sem14)
    world.scattered(r.small, r.slots, 0)
    r.mine[...] = jnp.sum(r.slots[...], axis=0)
    world.share(r.mine, r.red, 1)
    net.shared(r.st8, r.g8, 1)

    tg1, tc1 = totals(r.g8, None, 128)
    wh, wl = r.w1h[...], r.w1l[...]
    r.dw1[...] = jnp.zeros(r.dw1.shape, f32)

    def put_first(p):
        m = sc[1 + p]
        r.eh[p, 1280:, :] = jnp.zeros((OWN - 1280, 128), bf16)
        r.el[p, 1280:, :] = jnp.zeros((OWN - 1280, 128), bf16)

        def rows(t):
            at = pl.ds(pl.multiple_of(t * 80, 80), 80)
            e = response_back(par, 0, avg1, inv1, tg1, tc1, count1, r.r1[p, at, :], r.a1[p, at, :])
            e = e.reshape(2, 40, 128)
            e = jnp.where(cells(e.shape, 33, 33, 2 * t) & (m > 0), e, 0.0)
            hi, lo = split(e.reshape(80, 128))
            r.eh[p, at, :] = hi
            r.el[p, at, :] = lo

        loop(17, rows)
        rows = pl.ds(pl.multiple_of((p + 1) * 64, 64), 192)
        r.dw1[...] += dot3(r.sh[rows, :], r.sl[rows, :], r.eh[p], r.el[p], NN)

    loop(2, put_first)
    acc = r.dw1[...]
    lane = lax.broadcasted_iota(jnp.int32, (32, 128), 1)
    tot = jnp.zeros((32, 128), f32)
    for tap in range(4):
        v = jnp.zeros((32, 128), f32)
        for q in range(4):
            x = acc if q == tap else pltpu.roll(acc, ((tap - q) % 4) * 32, 1)
            hi, lo = split(x)
            sel = r.pick[tap * 4 + q]
            v += dot(sel, hi, NN) + dot(sel, lo, NN)
        tot += jnp.where(lane // 32 == tap, v, 0.0)
    last = r.small2.shape[0] * r.small2.shape[1]
    rows = jnp.concatenate([tot] + four_rows(r.st8) + [jnp.zeros((last - 36, 128), f32)], axis=0)
    store_slots(r.small2, rows, 0)
    world.scatter(r.small2, r.slots2, 2)

    def image_part(p):
        v = dot3(wh, wl, r.eh[p], r.el[p], NT)
        for i in range(3):
            tot = jnp.zeros((16, OWN), f32)
            for ab in range(4):
                at = i * 64 + ab * 16
                a, b = ab // 2, ab % 2
                x = v[at : at + 16, :]
                tot += x if ab == 0 else pltpu.roll(x, 40 * a + b, 1)
            r.parts[p, i] = tot

    loop(2, image_part)
    net.halos = []
    net.to_left(r.parts.at[0, 0], r.pr, 1)
    net.to_right(r.parts.at[1, 2], r.pl, 1)
    large.wait()
    large.pair_back(r.sem15)
    world.scattered(r.small2, r.slots2, 2)
    r.mine2s[...] = jnp.sum(r.slots2[...], axis=0)
    world.share(r.mine2s, r.red2, 3)
    net.sides()
    for d in range(2):
        other = r.pl if d == 0 else r.pr
        tot = r.parts[0, 1 + d] + r.parts[1, d] + jnp.where(sc[10 + d] > 0, other[...], 0.0)
        tot = tot * (r.keep[...] * sc[1 + d])
        rows = []
        for y in range(34):
            tile, off = (40 * y) // 128, (40 * y) % 128
            pair = []
            for px in range(2):
                v = tot[8 * px : 8 * px + 8, 128 * tile : 128 * tile + 128]
                if off + 34 > 128:
                    nxt = tot[8 * px : 8 * px + 8, 128 * tile + 128 : 128 * tile + 256]
                    v = jnp.where(lane[:8] >= off, v, nxt)
                pair.append(v if off == 0 else pltpu.roll(v, 128 - off, 1))
            rows.append(jnp.concatenate(pair, axis=1))
        hi, lo = split(jnp.concatenate(rows, axis=0))
        out = dot(hi, r.even[...], NT) + dot(lo, r.even[...], NT)
        r.ig[d] = out.reshape(34, 8, 68)
    world.shared(r.mine, r.red, 1)
    world.shared(r.mine2s, r.red2, 3)
    large.wait()
    mv.finish()


def tail(dims, tb, pg, k, fo, w2, keep, par, sc, si):
    n = dims[0] * dims[1] * dims[2]
    m = dims[1] * dims[2]
    V = pltpu.VMEM
    per = 512 // n
    per2 = max(64, n) // n
    big = bucket_rows(dims)
    Q, B = dims[0] * dims[1] // 2, dims[2]
    return launch(
        functools.partial(tail_kernel, dims), "tail", 5,
        [("skip", tb.oskip, VM), ("bucket", tb.obucket, HB), ("pg", pg, VM), ("r2", k.or2, VM), ("g2", k.g2, VM),
         ("g1", k.g1, VM), ("w2", w2, VM), ("keep", keep, VM), ("w1h", k.ow1h, VM), ("w1l", k.ow1l, VM),
         ("pick", tap_picks(), VM), ("even", deinterleave(), VM), ("st5", fo.st5, VM), ("st6", fo.st6, VM),
         ("par", par, VM), ("iah", k.oah, HB), ("ial", k.oal, HB), ("ish", k.osh, HB), ("isl", k.osl, HB),
         ("ir1", k.or1, HB), ("sc", sc, SM), ("si", si, SM)],
        [("ig", (2, 34, 8, 68), f32, VM), ("red", (n, per, 128), f32, VM), ("red2", (n, per2, 128), f32, VM),
         ("res", (n * big, 128), f32, VM)],
        both("d2", (3, 128, 1024)) + both("a", (4096, 512)) + both("b", (1360, 1024)) + both("e2", (2048, 256))
        + both("s", (384, OWN)) + both("e", (2, OWN, 128))
        + [("f", V((36, 56, 256), f32)), ("bg2", V((2048, 256), f32)), ("r1", V((2, 1440, 128), f32)),
           ("a1", V((2, OWN, 128), f32)), ("side", V((2, OWN, 128), f32)), ("fl", V((OWN, 128), f32)),
           ("fr", V((OWN, 128), f32)), ("v", V((2, 1360, 384), f32)), ("parts", V((2, 3, 16, OWN), f32)),
           ("pl", V((16, OWN), f32)), ("pr", V((16, OWN), f32)), ("dw1", V((192, 128), f32)),
           ("g", V((512, 256), f32)), ("dw2", V((480, 128), f32)), ("small", V((n, per, 128), f32)),
           ("slots", V((n, per, 128), f32)), ("mine", V((per, 128), f32)), ("small2", V((n, per2, 128), f32)),
           ("slots2", V((n, per2, 128), f32)), ("mine2s", V((per2, 128), f32)), ("g7", V((m, 1, 512), f32)),
           ("g8", V((m, 1, 512), f32)), ("st7", V((1, 512), f32)), ("st8", V((1, 512), f32)),
           ("mine1", V((n // 2 * big, 128), f32)), ("slot1", V((n // 2 * big, 128), f32)),
           ("slot2", V((Q - 1, B * big, 128), f32)), ("mine2", V((B * big, 128), f32)),
           ("slot3", V((B - 1, big, 128), f32))]
        + sems(m, m, m, m, 4, 4, n, n, n, n, 8, 2 * (Q - 1), 2 * (B - 1), 2 * (B - 1), 2 * (Q - 1), 2,
               n, n, n, n, 2),
    )


def finish_kernel(r):
    def tap(i):
        for p in range(9):
            at = 64 * (p % 2)

            def get(base, chans, at=at, p=p):
                rows = pl.ds(pl.multiple_of(base + (i * 5 + p // 2) * chans, 8), chans)
                v = r.res[rows, :]
                return (v if at == 0 else pltpu.roll(v, 64, 1))[:, :64]

            r.dw3t[i * 9 + p] = get(0, 192).T
            r.dw4[i * 9 + p] = get(2880, 64)
            rows = pl.ds(pl.multiple_of((i * 5 + p // 2) * 32, 32), 32)
            v = r.red[rows, :]
            r.dw2[i * 9 + p] = (v if at == 0 else pltpu.roll(v, 64, 1))[:, :64]

    loop(3, tap)
    r.dup[...] = r.res[3840:4864, :].reshape(8, 128, 128)
    for t in range(27):
        v = r.red2[4 * (t // 4) : 4 * (t // 4) + 4, :]
        v = v if t % 4 == 0 else pltpu.roll(v, 128 - 32 * (t % 4), 1)
        r.dw1[t] = v[:, :32]
    sums = [r.red2[32:36, :]] + [r.red[480 + 4 * j : 484 + 4 * j, :] for j in range(3)]
    for j, v in enumerate(sums):
        for c, out in ((0, (r.s1, r.s2, r.s3, r.s4)[j]), (2, (r.x1, r.x2, r.x3, r.x4)[j])):
            x = jnp.concatenate([v[c : c + 1], v[c + 1 : c + 2]], axis=1)
            if j == 0:
                x = fold(x[:, :128])
            else:
                x = fold(x)
            out[...] = x[:, : out.shape[1]]


def finish(res, red, red2):
    vectors = [(f"{a}{j}", (1, 32 if j == 1 else 64), f32, VM) for j in range(1, 5) for a in "sx"]
    return launch(
        finish_kernel, "finish", None,
        [("res", res, VM), ("red", red, VM), ("red2", red2, VM)],
        [("dw3t", (27, 64, 192), f32, VM), ("dw4", (27, 64, 64), f32, VM), ("dw2", (27, 32, 64), f32, VM),
         ("dup", (8, 128, 128), f32, VM), ("dw1", (27, 4, 32), f32, VM)] + vectors,
        [],
    )


def body(
    dims,
    image, modality_mask, extents, crop_offsets, coarse,
    conv_first, gain_first, shift_first, conv_second, gain_second, shift_second,
    up_kernel, conv_third, gain_third, shift_third, conv_fourth, gain_fourth, shift_fourth,
    pool_grad, output_grad,
):
    si = crop_offsets[0]
    img = image[0, 0].transpose(0, 1, 3, 2).reshape(2, 34, 8, 68)
    p = prepare(
        dims, img, extents, modality_mask[0], si, conv_third.reshape(27, 192, 64).transpose(0, 2, 1),
        (gain_first, shift_first, gain_second, shift_second, gain_third, shift_third, gain_fourth, shift_fourth),
    )
    co = coarse[0, 0]
    w2 = conv_second.reshape(27, 32, 64)
    up = up_kernel.reshape(8, 128, 128)
    k = front(dims, p.own, p.crop, conv_first.reshape(27, 4, 32), w2, p.w3u, up, co, p.par, p.sc)
    t = third(dims, k, co, p.w3c, p.par, p.sc)
    fo = fourth(dims, t.or3, t.nl, t.nr, t.g3, output_grad[0, 0], conv_fourth.reshape(27, 64, 64), p.par, p.sc)
    tb = third_back(dims, fo, t.or3, t.nl, t.nr, t.g3, k, t, fo.dw4, p.w3u, p.w3c, up, p.par, p.sc)
    e = tail(dims, tb, pool_grad[0, 0, 0], k, fo, w2, p.keep, p.par, p.sc, si)
    g = finish(e.res, e.red.reshape(512, 128), e.red2.reshape(-1, 128))
    return (
        t.pooled.reshape(1, 1, 1, 32, 32, 64),
        fo.decoded[None, None],
        e.ig.reshape(2, 68, 4, 68).transpose(0, 1, 3, 2)[None, None],
        tb.cg.reshape(1, 1, 1, 24, 24, 128),
        g.dw1.reshape(3, 3, 3, 4, 32),
        g.x1[0],
        g.s1[0],
        g.dw2.reshape(3, 3, 3, 32, 64),
        g.x2[0],
        g.s2[0],
        g.dup.reshape(2, 2, 2, 128, 128),
        g.dw3t.transpose(0, 2, 1).reshape(3, 3, 3, 192, 64),
        g.x3[0],
        g.s3[0],
        g.dw4.reshape(3, 3, 3, 64, 64),
        g.x4[0],
        g.s4[0],
    )


def solution(mesh):
    dims = tuple(mesh.shape[a] for a in ("section", "slab", "batch"))
    field = P("section", "batch", "slab", None, None, None)
    volume = P("section", "batch", None)
    rep = P()
    return jax.shard_map(
        functools.partial(body, dims),
        mesh=mesh,
        in_specs=(field, volume, rep, volume, field) + (rep,) * 13 + (field, field),
        out_specs=(field,) * 4 + (rep,) * 13,
        check_vma=False,
    )
```

```python
import functools
import types

import jax
import jax.numpy as jnp
import numpy as np
from jax import lax
from jax.experimental import pallas as pl
from jax.experimental.pallas import tpu as pltpu
from jax.sharding import PartitionSpec as P

f32 = jnp.float32
bf16 = jnp.bfloat16
MESH = pl.DeviceIdType.MESH
EPSILON = 1e-05
NN = (((1,), (0,)), ((), ()))
NT = (((1,), (1,)), ((), ()))
TN = (((0,), (0,)), ((), ()))
VM = pl.BlockSpec(memory_space=pltpu.VMEM)
SM = pl.BlockSpec(memory_space=pltpu.SMEM)
HB = pl.BlockSpec(memory_space=pl.ANY)
LIMIT = 62 * 2**20

OWN = 1408
CROP = 896
BUCKET = 2880 + 960 + 1024
FIRST_HALF = 2560


def split(x):
    hi = x.astype(bf16)
    return hi, (x - hi.astype(f32)).astype(bf16)


def dot(a, b, dims):
    return lax.dot_general(a, b, dims, preferred_element_type=f32)


def dot3(ah, al, bh, bl, dims):
    return dot(ah, bh, dims) + dot(al, bh, dims) + dot(ah, bl, dims)


def loop(n, f, unroll=1):
    def step(t, c):
        f(t)
        return c

    lax.fori_loop(0, n, step, 0, unroll=unroll)


def fold(v):
    lanes = v.shape[-1]
    v = jnp.broadcast_to(v, (8, lanes))
    if lanes == 256:
        h = v[:, :128] + v[:, 128:]
        h = h + pltpu.roll(h, 64, 1)
        h = jnp.concatenate([h, h], axis=1)
    else:
        h = v + pltpu.roll(v, 64, 1)
        h = h + pltpu.roll(h, 32, 1)
    return h[:1]


def totals(gath, half, lanes):
    if half is None:
        tot = jnp.sum(gath[...], axis=0)
    else:
        per = gath.shape[0] // 2
        tot = jnp.sum(gath[pl.ds(half * per, per)], axis=0)
    return fold(tot[:, :lanes]), fold(tot[:, 256 : 256 + lanes])


def moments(gath, half, count, lanes):
    s, q = totals(gath, half, lanes)
    avg = s / count
    inv = lax.rsqrt(q / count - avg * avg + EPSILON)
    return avg, inv


def affine(par, layer, avg, inv):
    lanes = avg.shape[-1]
    scale = par[2 * layer : 2 * layer + 1, :lanes] * inv
    return scale, par[2 * layer + 1 : 2 * layer + 2, :lanes] - avg * scale


def silu(b):
    return b / (1.0 + jnp.exp(-b))


def silu_back(a, b):
    s = 1.0 / (1.0 + jnp.exp(-b))
    return a * s * (1.0 + b * (1.0 - s))


def cells(shape, rows, cols, row0):
    y = lax.broadcasted_iota(jnp.int32, shape, 0) + row0
    x = lax.broadcasted_iota(jnp.int32, shape, 1)
    return (y < rows) & (x < cols)


def put_sums(st, s, q):
    lanes = s.shape[-1]
    st[...] = jnp.zeros(st.shape, f32)
    st[:, :lanes] = s
    st[:, 256 : 256 + lanes] = q


def im2col(ah, al, p, f, ny, pitch, lanes, x0=0):
    def pair(t):
        for a in range(2):
            for b in range(2):
                x = f[pl.ds(2 * t + a, 2), x0 + b : x0 + b + pitch, :]
                hi, lo = split(x.reshape(2 * pitch, lanes))
                rows = pl.ds(pl.multiple_of(p * (ny * pitch) + t * (2 * pitch), 16), 2 * pitch)
                at = (2 * a + b) * lanes
                ah[rows, at : at + lanes] = hi
                al[rows, at : at + lanes] = lo

    loop(ny // 2, pair)


def launch(body, name, cid, ins, outs, scratch):
    names = [i[0] for i in ins] + [o[0] for o in outs] + [x[0] for x in scratch]

    def kernel(*refs):
        body(types.SimpleNamespace(**dict(zip(names, refs))))

    res = pl.pallas_call(
        kernel,
        out_shape=[jax.ShapeDtypeStruct(o[1], o[2]) for o in outs],
        in_specs=[i[2] for i in ins],
        out_specs=[o[3] for o in outs],
        scratch_shapes=[x[1] for x in scratch],
        compiler_params=pltpu.CompilerParams(
            vmem_limit_bytes=LIMIT, collective_id=cid, has_side_effects=cid is not None
        ),
        name=name,
    )(*[i[1] for i in ins])
    return types.SimpleNamespace(**dict(zip([o[0] for o in outs], res)))


def both(name, shape):
    return [(name + "h", pltpu.VMEM(shape, bf16)), (name + "l", pltpu.VMEM(shape, bf16))]


def both_out(name, shape):
    return [(name + "h", shape, bf16, HB), (name + "l", shape, bf16, HB)]


def sems(*sizes):
    return [(f"sem{i}", pltpu.SemaphoreType.DMA((n,))) for i, n in enumerate(sizes)]


class Moves:
    def __init__(self, sem):
        self.sem = sem
        self.used = 0
        self.pending = []

    def start(self, src, dst):
        copy = pltpu.make_async_copy(src, dst, self.sem.at[self.used])
        self.used += 1
        copy.start()
        return copy

    def out(self, *pairs):
        for src, dst in pairs:
            self.pending.append(self.start(src, dst))

    def finish(self):
        for copy in self.pending:
            copy.wait()


def fetch(mv, *pairs):
    copies = [mv.start(src, dst) for src, dst in pairs]

    def wait():
        for copy in copies:
            copy.wait()

    return wait


class Net:
    def __init__(self, dims, wide, sems):
        S, K, B = dims
        self.s = lax.axis_index("section")
        self.k = lax.axis_index("slab")
        self.b = lax.axis_index("batch")
        self.K = K
        self.sems = sems
        if wide:
            self.n = S * K * B
            self.me = (self.s * K + self.k) * B + self.b
            self.coords = lambda d: (d // (K * B), (d // B) % K, d % B)
        else:
            self.n = K * B
            self.me = self.k * B + self.b
            self.coords = lambda d: (self.s, d // B, d % B)
        self.halos = []

    def each(self, f):
        def step(p, c):
            f(p)
            return c

        lax.fori_loop(1, self.n, step, 0)

    def enter(self):
        barrier = pltpu.get_barrier_semaphore()
        self.each(
            lambda p: pl.semaphore_signal(
                barrier, inc=1, device_id=self.coords((self.me + p) % self.n), device_id_type=MESH
            )
        )

    def ready(self):
        pl.semaphore_wait(pltpu.get_barrier_semaphore(), self.n - 1)

    def _copy(self, src, dst, p, group):
        return pltpu.make_async_remote_copy(
            src_ref=src,
            dst_ref=dst,
            send_sem=self.sems[2 * group].at[p],
            recv_sem=self.sems[2 * group + 1].at[p],
            device_id=self.coords((self.me + p) % self.n),
            device_id_type=MESH,
        )

    def share(self, src, slots, group=0):
        slots[self.me] = src[...]
        self.each(lambda p: self._copy(src, slots.at[self.me], p, group).start())

    def shared(self, src, slots, group=0):
        n = self.n
        self.each(lambda p: self._copy(src, slots.at[(self.me + n - p) % n], p, group).wait_recv())
        self.each(lambda p: self._copy(src, slots.at[self.me], p, group).wait_send())

    def scatter(self, src, slots, group):
        slots[self.me] = src[self.me]
        n = self.n
        self.each(lambda p: self._copy(src.at[(self.me + p) % n], slots.at[self.me], p, group).start())

    def scattered(self, src, slots, group):
        n = self.n
        self.each(
            lambda p: self._copy(
                src.at[(self.me + p) % n], slots.at[(self.me + n - p) % n], p, group
            ).wait_recv()
        )
        self.each(lambda p: self._copy(src.at[(self.me + p) % n], slots.at[self.me], p, group).wait_send())

    def _side(self, src, dst, j, step):
        return pltpu.make_async_remote_copy(
            src_ref=src,
            dst_ref=dst,
            send_sem=self.sems[-2].at[j],
            recv_sem=self.sems[-1].at[j],
            device_id=(self.s, (self.k + self.K + step) % self.K, self.b),
            device_id_type=MESH,
        )

    def to_left(self, src, dst, j):
        copy = self._side(src, dst, 2 * j, -1)

        @pl.when(self.k > 0)
        def _():
            copy.start()

        self.halos.append((copy, -1))

    def to_right(self, src, dst, j):
        copy = self._side(src, dst, 2 * j + 1, 1)

        @pl.when(self.k < self.K - 1)
        def _():
            copy.start()

        self.halos.append((copy, 1))

    def sides(self):
        @pl.when(self.k > 0)
        def _():
            for copy, step in self.halos:
                if step < 0:
                    copy.wait_send()
                else:
                    copy.wait_recv()

        @pl.when(self.k < self.K - 1)
        def _():
            for copy, step in self.halos:
                if step > 0:
                    copy.wait_send()
                else:
                    copy.wait_recv()


def toeplitz(w, c0, chans, th, tl, dh=None, dl=None):
    loop(3, lambda i: toeplitz_tap(w, c0, chans, i, i, th, tl, dh, dl))


def toeplitz_tap(w, c0, chans, i, slot, th, tl, dh=None, dl=None):
    zero = jnp.zeros((chans, 64), f32)
    none = jnp.zeros((chans, 128), bf16)
    for s in range(4):
        part = []
        for j in range(3):
            here = w[i * 9 + j * 3 + s, c0 : c0 + chans, :] if s <= 2 else zero
            prev = w[i * 9 + j * 3 + s - 1, c0 : c0 + chans, :] if s >= 1 else zero
            part.append(split(jnp.concatenate([here, prev], axis=1)))
        for r in range(4):
            a, py, b, px = r // 2, r % 2, s // 2, s % 2
            block = (2 * a + b) * 4 + py * 2 + px
            for h in range(2):
                hi, lo = part[r - h] if 0 <= r - h <= 2 else (none, none)
                if th is not None:
                    rows = slice(block * chans, (block + 1) * chans)
                    th[slot, rows, 128 * h : 128 * h + 128] = hi
                    tl[slot, rows, 128 * h : 128 * h + 128] = lo
                if dh is not None:
                    rows = slice((py * 2 + px) * chans, (py * 2 + px + 1) * chans)
                    at = ((1 - a) * 2 + (1 - b)) * 256 + 128 * h
                    dh[2 - i, rows, at : at + 128] = hi
                    dl[2 - i, rows, at : at + 128] = lo


def slot_of(i, ip):
    pd = (ip + i + 1) % 2
    t = (pd + i - 1) // 2 - pd + 1
    return pd * 2 + t


def up_blocks(r):
    for ip in range(2):
        for q in range(4):
            hi, lo = split(r.up[ip * 4 + q])
            r.uph[ip * 128 : ip * 128 + 128, q * 128 : q * 128 + 128] = hi
            r.upl[ip * 128 : ip * 128 + 128, q * 128 : q * 128 + 128] = lo


def compose(r, i):
    def block(ab):
        rows = pl.ds(pl.multiple_of(ab * 512, 512), 512)
        p = dot3(r.uph[...], r.upl[...], r.tuh[i, rows, :], r.tul[i, rows, :], NN)
        out = pl.ds(pl.multiple_of(ab * 128, 128), 128)
        for ip in range(2):
            r.usc[slot_of(i, ip), out, :] += p[ip * 128 : ip * 128 + 128]

    loop(4, block)


def composed(r):
    for e in range(4):
        for ab in range(4):
            hi, lo = split(r.usc[e, ab * 128 : ab * 128 + 128, :])
            r.uh[e, ab * 128 : ab * 128 + 128, :] = hi
            r.ul[e, ab * 128 : ab * 128 + 128, :] = lo
            p = (3, 1, 2, 0)[e]
            at = (3 - ab) * 256
            r.ubh[p, :, at : at + 256] = hi
            r.ubl[p, :, at : at + 256] = lo


def source_copies(dims, own, crop, so, sr, ss, rs):
    K = dims[1]
    s = lax.axis_index("section")
    k = lax.axis_index("slab")
    b = lax.axis_index("batch")
    here, left, right = k, (k + K - 1) % K, (k + 1) % K

    def copy(j, src, dst, dev):
        return pltpu.make_async_remote_copy(
            src_ref=src,
            dst_ref=dst,
            send_sem=ss.at[j],
            recv_sem=rs.at[j],
            device_id=dev,
            device_id_type=MESH,
        )

    so[2:4] = own[...]
    lefts = [
        copy(0, own, so.at[4:6], (s, left, b)),
        copy(1, crop, sr.at[4:6], (1 - s, left, b)),
    ]
    rights = [
        copy(2, own, so.at[0:2], (s, right, b)),
        copy(3, crop, sr.at[0:2], (1 - s, right, b)),
    ]
    across = copy(4, crop, sr.at[2:4], (1 - s, here, b))

    def start():
        across.start()

        @pl.when(k > 0)
        def _():
            for c in lefts:
                c.start()

        @pl.when(k < K - 1)
        def _():
            for c in rights:
                c.start()

    def finish():
        across.wait()

        @pl.when(k > 0)
        def _():
            for c in lefts:
                c.wait_send()
            for c in rights:
                c.wait_recv()

        @pl.when(k < K - 1)
        def _():
            for c in rights:
                c.wait_send()
            for c in lefts:
                c.wait_recv()

        @pl.when(k == 0)
        def _():
            so[0:2] = jnp.zeros((2, 16, OWN), f32)
            sr[0:2] = jnp.zeros((2, 16, CROP), f32)

        @pl.when(k == K - 1)
        def _():
            so[4:6] = jnp.zeros((2, 16, OWN), f32)
            sr[4:6] = jnp.zeros((2, 16, CROP), f32)

    return start, finish


def field_sums(r, d, n, rows, cols, mask):
    base = d * n

    def part(t, c):
        x = r[pl.ds(pl.multiple_of(base + t * 96, 16), 96), :].reshape(4, 24, 256)
        x = jnp.where(cells(x.shape, rows, cols, 4 * t), x, 0.0)
        return c[0] + jnp.sum(x, axis=0), c[1] + jnp.sum(x * x, axis=0)

    zero = jnp.zeros((24, 256), f32)
    full = n // 96
    s, q = lax.fori_loop(0, full, part, (zero, zero))
    if n % 96:
        x = r[base + full * 96 : base + n, :].reshape((n - full * 96) // 24, 24, 256)
        x = jnp.where(cells(x.shape, rows, cols, 4 * full), x, 0.0)
        s = s + jnp.sum(x, axis=0)
        q = q + jnp.sum(x * x, axis=0)
    return mask * jnp.sum(s, axis=0, keepdims=True), mask * jnp.sum(q, axis=0, keepdims=True)


def back_parts(par, layer, avg, inv, r, a):
    lanes = avg.shape[-1]
    normed = (r - avg) * inv
    b = par[2 * layer : 2 * layer + 1, :lanes] * normed + par[2 * layer + 1 : 2 * layer + 2, :lanes]
    return normed, silu_back(a, b)


def response_back(par, layer, avg, inv, tg, tc, count, r, a):
    lanes = avg.shape[-1]
    gain = par[2 * layer : 2 * layer + 1, :lanes]
    normed, bg = back_parts(par, layer, avg, inv, r, a)
    return inv * gain * (bg - (tg + normed * tc) / count)


def folded(g, j, k, chans):
    def block(r, s):
        at = (2 * (r // 2) + s // 2) * 4 + (r % 2) * 2 + s % 2
        return slice(at * chans, (at + 1) * chans)

    x = g[block(j, k), 0:128] + g[block(j + 1, k), 128:256]
    y = g[block(j, k + 1), 0:128] + g[block(j + 1, k + 1), 128:256]
    return x + pltpu.roll(y, 64, 1)


def tap_picks():
    sel = np.zeros((4, 4, 32, 192), np.float32)
    for t in range(27):
        i, j, k = t // 9, (t // 3) % 3, t % 3
        for q in range(4):
            r, s = j + q // 2, k + q % 2
            for c in range(4):
                col = i * 64 + (2 * (r // 2) + s // 2) * 16 + (s % 2) * 8 + (r % 2) * 4 + c
                sel[t % 4, q, (t // 4) * 4 + c, col] = 1.0
    return jnp.asarray(sel.reshape(16, 32, 192), bf16)


def deinterleave():
    sel = np.zeros((68, 256), np.float32)
    for x in range(68):
        sel[x, (x % 2) * 128 + x // 2] = 1.0
    return jnp.asarray(sel, bf16)


def source_stage(r):
    s = lax.axis_index("section")
    k = lax.axis_index("slab")
    b = lax.axis_index("batch")
    ends = (r.ext[s, b], r.ext[1 - s, b])
    for h in range(2):
        for p in range(4):
            g = 2 * k - 1 + p
            r.sc[4 * h + p] = jnp.where((g >= 0) & (g < ends[h]), 1.0, 0.0)
        tot = jnp.int32(0)
        for v in range(r.ext.shape[1]):
            tot = tot + (r.ext[s, v] if h == 0 else r.ext[1 - s, v])
        r.sc[8 + h] = tot.astype(f32)
    r.sc[10] = jnp.where(k > 0, 1.0, 0.0)
    r.sc[11] = jnp.where(k < r.slabs - 1, 1.0, 0.0)
    for j in range(12, 16):
        r.sc[j] = jnp.float32(0.0)
    for j, v in enumerate((r.v0, r.v1, r.v2, r.v3, r.v4, r.v5, r.v6, r.v7)):
        v = v[...]
        while v.shape[1] < 256:
            v = jnp.concatenate([v, v], axis=1)
        r.par[j : j + 1, :] = v
    row = lax.broadcasted_iota(jnp.int32, (16, 1), 0) % 4
    col = jnp.zeros((16, 1), f32)
    for c in range(4):
        col = jnp.where(row == c, r.mods[0, c].astype(f32), col)
    r.keep[...] = col
    img, keep, even, sc, own, crop = r.img, r.keep, r.even, r.sc, r.own, r.crop
    oy, ox = r.si[0, 0], r.si[0, 1]
    x = lax.broadcasted_iota(jnp.int32, (68, 256), 0)
    lane = lax.broadcasted_iota(jnp.int32, (68, 256), 1)
    at = 2 * (lane % 128) + lane // 128
    pick = ((x == at + ox) & (lane % 128 < 26)).astype(f32).astype(bf16)
    r = lax.broadcasted_iota(jnp.int32, (208, 272), 0)
    c = lax.broadcasted_iota(jnp.int32, (208, 272), 1)
    rows = (c == r + 4 * oy).astype(f32).astype(bf16)
    lane = lax.broadcasted_iota(jnp.int32, (8, 128), 1)

    def flat(v, side, pitch, tiles):
        out = [[jnp.zeros((8, 128), f32) for _ in range(tiles)] for _ in range(2)]
        for y in range(side):
            tile, off = (pitch * y) // 128, (pitch * y) % 128
            for px in range(2):
                p = v[8 * y : 8 * y + 8, 128 * px : 128 * px + 128]
                p = p if off == 0 else pltpu.roll(p, off, 1)
                if off + side > 128:
                    out[px][tile + 1] += jnp.where(lane < off, p, 0.0)
                    p = jnp.where(lane >= off, p, 0.0)
                out[px][tile] += p
        return jnp.concatenate([jnp.concatenate(o, axis=1) for o in out], axis=0)

    for d in range(2):
        hi, lo = split(img[d].reshape(272, 68))
        k = keep[...] * sc[1 + d]
        own[d] = flat(dot(hi, even[...], NN) + dot(lo, even[...], NN), 34, 40, OWN // 128) * k
        hi = dot(rows, hi, NN).astype(bf16)
        lo = dot(rows, lo, NN).astype(bf16)
        crop[d] = flat(dot(hi, pick, NN) + dot(lo, pick, NN), 26, 32, CROP // 128) * k


def split_third(r):
    def turn(t):
        v = r.w3t[t].T
        r.w3u[t] = v[:128]
        r.w3c[t] = v[128:]

    loop(27, turn)


def gather_output(r):
    r.og[...] = jnp.zeros(r.og.shape, f32)

    def row(t):
        for d in range(2):
            for py in range(2):
                x0 = r.ograw[d, 2 * t + py, pl.ds(0, 22, stride=2), :]
                x1 = r.ograw[d, 2 * t + py, pl.ds(1, 22, stride=2), :]
                r.og[d, t, pl.ds(0, 22), py * 128 : py * 128 + 128] = jnp.concatenate([x0, x1], axis=1)

    loop(22, row)


def tap_spread():
    sel = np.zeros((4, 192, 112), np.float32)
    for t in range(27):
        i, j, k = t // 9, (t // 3) % 3, t % 3
        for q in range(4):
            r, s = j + q // 2, k + q % 2
            for c in range(4):
                row = i * 64 + (2 * (r // 2) + s // 2) * 16 + (s % 2) * 8 + (r % 2) * 4 + c
                sel[q, row, t * 4 + c] = 1.0
    return jnp.asarray(sel, bf16)


def first_weights(r):
    r.wf4[...] = jnp.zeros(r.wf4.shape, f32)
    for t in range(27):
        w = r.wf[t]
        r.wf4[4 * t : 4 * t + 4, :] = jnp.concatenate([w, w, w, w], axis=1)
    hi, lo = split(r.wf4[...])
    lane = lax.broadcasted_iota(jnp.int32, (192, 128), 1) // 32
    wh = jnp.zeros((192, 128), f32)
    wl = jnp.zeros((192, 128), f32)
    for q in range(4):
        wh += jnp.where(lane == q, dot(r.spread[q], hi, NN), 0.0)
        wl += jnp.where(lane == q, dot(r.spread[q], lo, NN), 0.0)
    r.w1h[...] = wh.astype(bf16)
    r.w1l[...] = wl.astype(bf16)


def first_stage(r):
    for p in range(6):
        own = r.so[p]
        crop = r.sr[p]
        for ab in range(4):
            a, b = ab // 2, ab % 2
            rows = slice(p * 64 + ab * 16, p * 64 + ab * 16 + 16)
            hi, lo = split(own if ab == 0 else pltpu.roll(own, OWN - 40 * a - b, 1))
            r.sh[rows, :] = hi
            r.sl[rows, :] = lo
            hi, lo = split(crop if ab == 0 else pltpu.roll(crop, CROP - 32 * a - b, 1))
            r.ch[rows, :] = hi
            r.cl[rows, :] = lo
    for w, out in ((r.w1h, r.wdh), (r.w1l, r.wdl)):
        out[...] = jnp.zeros(out.shape, bf16)
        out[:192, :128] = w[...]
        out[64:, 128:] = w[...]
    wh, wl = r.wdh[...], r.wdl[...]
    def pair(t):
        rows = pl.ds(pl.multiple_of(t * 128, 128), 256)
        v = dot3(r.sh[rows, :], r.sl[rows, :], wh, wl, TN)
        r.r1[2 * t, :OWN, :] = v[:, :128]
        r.r1[2 * t + 1, :OWN, :] = v[:, 128:]
        v = dot3(r.ch[rows, :], r.cl[rows, :], wh, wl, TN)
        r.r1c[2 * t] = v[:, :128]
        r.r1c[2 * t + 1] = v[:, 128:]

    loop(2, pair)
    for d in range(4):
        r.r1[d, OWN:, :] = jnp.zeros((1440 - OWN, 128), f32)
    s = jnp.zeros((1, 128), f32)
    q = jnp.zeros((1, 128), f32)
    for d in range(2):
        def part(t, c):
            x = r.r1[1 + d, pl.ds(pl.multiple_of(t * 160, 160), 160), :].reshape(4, 40, 128)
            x = jnp.where(cells(x.shape, 33, 33, 4 * t), x, 0.0)
            return c[0] + jnp.sum(x, axis=0), c[1] + jnp.sum(x * x, axis=0)

        ps, pq = lax.fori_loop(0, 9, part, (jnp.zeros((40, 128), f32), jnp.zeros((40, 128), f32)))
        s = s + r.sc[1 + d] * jnp.sum(ps, axis=0, keepdims=True)
        q = q + r.sc[1 + d] * jnp.sum(pq, axis=0, keepdims=True)
    put_sums(r.st1, s, q)


def front_kernel(dims, r):
    net = Net(dims, True, [r.sem0, r.sem1, r.sem2, r.sem3, r.sem4, r.sem5])
    net.enter()
    mv = Moves(r.sem8)
    ready_og = fetch(mv, (r.iograw, r.ograw))
    r.slabs = dims[1]
    source_stage(r)
    split_third(r)
    mv.out((r.w3u, r.ow3u), (r.w3c, r.ow3c))
    net.ready()
    start, finish = source_copies(dims, r.own, r.crop, r.so, r.sr, r.sem6, r.sem7)
    start()
    net.to_left(r.co.at[0], r.cor, 0)
    net.to_right(r.co.at[0], r.col, 0)
    first_weights(r)
    mv.out((r.w1h, r.ow1h), (r.w1l, r.ow1l))
    toeplitz(r.w2, 0, 32, r.t2h, r.t2l)
    toeplitz(r.w3u, 0, 128, r.tuh, r.tul)
    up_blocks(r)
    r.usc[...] = jnp.zeros(r.usc.shape, f32)
    compose(r, 0)
    finish()
    first_stage(r)
    mv.out((r.sh, r.osh), (r.sl, r.osl), (r.r1, r.or1))
    net.share(r.st1, r.g1, 0)
    ready_og()
    gather_output(r)
    mv.out((r.og, r.oog))
    net.to_left(r.og.at[0], r.ogr, 2)
    net.to_right(r.og.at[1], r.ogl, 2)
    net.shared(r.st1, r.g1, 0)

    half = net.s
    f = r.f
    f[...] = jnp.zeros(f.shape, f32)
    scale_c, off_c = affine(r.par, 0, *moments(r.g1, 1 - half, r.sc[9] * 4356.0, 128))

    def crop(p):
        m = r.sc[4 + p]

        def rows(t):
            x = r.r1c[p, pl.ds(pl.multiple_of(t * 128, 128), 128), :].reshape(4, 32, 128)
            f[pl.ds(4 * t, 4), :32, :] = jnp.where(m > 0, silu(x * scale_c + off_c), 0.0)

        loop(7, rows)
        im2col(r.ah, r.al, p, f, 24, 24, 128)

    loop(4, crop)
    conv(r.r2c, r.ah, r.al, r.t2h, r.t2l, 576, NN)
    net.to_left(r.r2c.at[0:576], r.hr, 1)
    net.to_right(r.r2c.at[576:1152], r.hl, 1)
    mv.out((r.r2c, r.or2c))
    scale, off = affine(r.par, 0, *moments(r.g1, half, r.sc[8] * 4356.0, 128))

    def own(p):
        m = r.sc[p]

        def rows(t):
            x = r.r1[p, pl.ds(pl.multiple_of(t * 160, 160), 160), :].reshape(4, 40, 128)
            f[pl.ds(4 * t, 4), :40, :] = jnp.where(m > 0, silu(x * scale + off), 0.0)

        loop(9, rows)
        im2col(r.ah, r.al, p, f, 32, 32, 128)

    loop(4, own)
    mv.out((r.ah, r.oah), (r.al, r.oal))
    conv(r.r2, r.ah, r.al, r.t2h, r.t2l, 1024, NN)
    mv.out((r.r2, r.or2))
    s = jnp.zeros((1, 256), f32)
    q = jnp.zeros((1, 256), f32)
    for d in range(2):
        def part(t, c):
            x = r.r2[pl.ds(pl.multiple_of(d * 1024 + t * 128, 128), 128), :].reshape(16, 8, 256)
            return c[0] + jnp.sum(x, axis=0), c[1] + jnp.sum(x * x, axis=0)

        ps, pq = lax.fori_loop(0, 8, part, (jnp.zeros((8, 256), f32), jnp.zeros((8, 256), f32)))
        s = s + r.sc[1 + d] * jnp.sum(ps, axis=0, keepdims=True)
        q = q + r.sc[1 + d] * jnp.sum(pq, axis=0, keepdims=True)
    put_sums(r.st2, s, q)
    net.share(r.st2, r.g2, 1)
    compose(r, 1)
    compose(r, 2)
    composed(r)
    mv.out((r.uh, r.ouh), (r.ul, r.oul), (r.ubh, r.oubh), (r.ubl, r.oubl))
    net.shared(r.st2, r.g2, 1)
    net.sides()
    mv.finish()


def conv(out, ah, al, th, tl, rows, dims):
    out[...] = jnp.zeros(out.shape, f32)

    def tap(i):
        at = pl.ds(pl.multiple_of(i * rows, 16), 2 * rows)
        out[...] += dot3(ah[at, :], al[at, :], th[i], tl[i], dims)

    loop(3, tap)


def front(dims, img, ext, mods, si, vectors, wf, w2, w3t, up, co, og):
    n = dims[0] * dims[1] * dims[2]
    V = pltpu.VMEM
    forms = [("u", (4, 512, 256)), ("ub", (4, 128, 1024)), ("s", (384, OWN)), ("a", (4096, 512)), ("w1", (192, 128))]
    outs = [("g1", (n, 1, 512), f32, VM), ("g2", (n, 1, 512), f32, VM),
            ("or1", (4, 1440, 128), f32, HB), ("or2", (2048, 256), f32, HB), ("or2c", (1152, 256), f32, HB),
            ("col", co.shape[1:], f32, HB), ("cor", co.shape[1:], f32, HB),
            ("par", (8, 256), f32, VM), ("keep", (16, 1), f32, VM), ("sc", (16,), f32, SM),
            ("ow3u", (27, 128, 64), f32, HB), ("ow3c", (27, 64, 64), f32, HB),
            ("oog", (2, 22, 24, 256), f32, HB), ("ogl", (22, 24, 256), f32, HB), ("ogr", (22, 24, 256), f32, HB),
            ("hl", (576, 256), f32, HB), ("hr", (576, 256), f32, HB)]
    scratch = []
    for name, shape in forms:
        outs += both_out("o" + name, shape)
        scratch += both(name, shape)
    scratch += both("t2", (3, 512, 256)) + both("tu", (3, 2048, 256)) + both("up", (256, 512)) + both("c", (384, CROP)) + both("wd", (256, 256))
    scratch += [("st1", V((1, 512), f32)), ("st2", V((1, 512), f32)), ("so", V((6, 16, OWN), f32)),
                ("sr", V((6, 16, CROP), f32)), ("wf4", V((112, 128), f32)), ("usc", V((4, 512, 256), f32)),
                ("r1", V((4, 1440, 128), f32)), ("r1c", V((4, CROP, 128), f32)), ("r2", V((2048, 256), f32)),
                ("r2c", V((1152, 256), f32)), ("f", V((36, 48, 128), f32)), ("own", V((2, 16, OWN), f32)),
                ("crop", V((2, 16, CROP), f32)), ("w3u", V((27, 128, 64), f32)), ("w3c", V((27, 64, 64), f32)),
                ("og", V((2, 22, 24, 256), f32)), ("ograw", V((2, 44, 44, 64), f32))]
    return launch(
        functools.partial(front_kernel, dims), "front", 1,
        [("img", img, VM), ("even", deinterleave(), VM), ("ext", ext, SM), ("mods", mods, SM), ("si", si, SM),
         ("wf", wf, VM), ("spread", tap_spread(), VM), ("w2", w2, VM), ("w3t", w3t, VM), ("up", up, VM),
         ("co", co, HB), ("iograw", og, HB)]
        + [(f"v{j}", v.reshape(1, -1), VM) for j, v in enumerate(vectors)],
        outs, scratch + sems(n, n, n, n, 6, 6, 5, 5, 32),
    )


def decode_kernel(dims, r):
    net = Net(
        dims, False, [r.sem0, r.sem1, r.sem2, r.sem3, r.sem4, r.sem5, r.sem6, r.sem7, r.sem8, r.sem9]
    )
    net.enter()
    mv = Moves(r.sem10)
    par = r.par
    weights = fetch(mv, (r.iuh, r.uh), (r.iul, r.ul))
    ready_r2 = fetch(mv, (r.ir2, r.r2))
    ready_og = fetch(mv, (r.iog, r.og), (r.iogl, r.ogl), (r.iogr, r.ogr))
    toeplitz(r.w3, 0, 64, r.th, r.tl)
    f, f2, sc = r.f, r.f2, r.sc
    scale_c, off_c = affine(r.par, 1, *moments(r.g2, 1 - net.s, sc[9] * 4096.0, 256))
    f[...] = jnp.zeros(f.shape, f32)

    def put(p, get):
        m = sc[4 + p]

        def rows(t):
            x = silu(get(t * 96) * scale_c + off_c).reshape(4, 24, 256)
            f[pl.ds(4 * t, 4), :24, :] = jnp.where(m > 0, x, 0.0)

        loop(6, rows)
        im2col(r.bh, r.bl, p, f, 24, 24, 256)

    def of(ref, base):
        return lambda at: ref[pl.ds(pl.multiple_of(base + at, 32), 96), :]

    put(0, of(r.hl, 0))
    loop(2, lambda p: put(p + 1, of(r.r2c, p * 576)))
    put(3, of(r.hr, 0))
    kept = fetch(mv, (r.bh, r.oah), (r.bl, r.oal))
    f2[...] = jnp.zeros(f2.shape, f32)
    for p, (src, m) in enumerate(((r.col, sc[4]), (r.co, sc[5]), (r.cor, sc[7]))):
        f2[:24, :24, :] = jnp.where(m > 0, src[...], 0.0)
        im2col(r.cuh, r.cul, p, f2, 24, 24, 128)
    mv.out((r.cuh, r.ocuh), (r.cul, r.ocul))
    weights()
    conv(r.r3, r.bh, r.bl, r.th, r.tl, 576, NN)

    def up(j):
        at = pl.ds(pl.multiple_of((j // 2 + j % 2) * 576, 16), 576)
        out = pl.ds(pl.multiple_of((j // 2) * 576, 16), 576)
        r.r3[out, :] += dot3(r.cuh[at, :], r.cul[at, :], r.uh[j], r.ul[j], NN)

    loop(4, up)
    net.ready()
    net.to_left(r.r3.at[0:576], r.r3r, 0)
    net.to_right(r.r3.at[576:1152], r.r3l, 0)
    s0, q0 = field_sums(r.r3, 0, 576, 23, 23, sc[5])
    s1, q1 = field_sums(r.r3, 1, 576, 23, 23, sc[6])
    put_sums(r.st3, s0 + s1, q0 + q1)
    net.share(r.st3, r.g3, 0)
    mv.out((r.r3, r.or3))
    scale, off = affine(r.par, 1, *moments(r.g2, net.s, sc[8] * 4096.0, 256))

    def pool(t):
        v = jnp.zeros((128, 256), f32)
        for d in range(2):
            x = r.r2[pl.ds(pl.multiple_of(d * 1024 + t * 128, 128), 128), :]
            v = v + sc[1 + d] * silu(x * scale + off)
        v = v[:, :128] + v[:, 128:]
        v = (v + pltpu.roll(v, 64, 1)) * 0.125
        r.pooled[pl.ds(pl.multiple_of(t * 128, 128), 128), :] = v[:, :64]

    ready_r2()
    loop(8, pool)
    toeplitz(r.w4, 0, 64, r.th, r.tl, r.d4h, r.d4l)
    net.shared(r.st3, r.g3, 0)

    avg3, inv3 = moments(r.g3, None, sc[9] * 2116.0, 256)
    scale3, off3 = affine(par, 2, avg3, inv3)

    def put_act(p, get):
        m = sc[4 + p]

        def rows(t):
            x = silu(get(t * 96) * scale3 + off3).reshape(4, 24, 256)
            f[pl.ds(4 * t, 4), :24, :] = jnp.where(m > 0, x, 0.0)

        loop(6, rows)
        im2col(r.ah, r.al, p, f, 22, 24, 256)

    def part_of(ref, base, step):
        return lambda at: ref[pl.ds(pl.multiple_of(base + at, 16), step), :]

    loop(2, lambda p: put_act(p + 1, part_of(r.r3, p * 576, 96)))
    net.sides()
    net.halos = []
    mv.out((r.r3l, r.or3l), (r.r3r, r.or3r))
    put_act(0, part_of(r.r3l, 0, 96))
    put_act(3, part_of(r.r3r, 0, 96))
    conv(r.r4, r.ah, r.al, r.th, r.tl, 528, NN)
    net.to_left(r.r4.at[0:528], r.r4r, 1)
    net.to_right(r.r4.at[528:1056], r.r4l, 1)
    s0, q0 = field_sums(r.r4, 0, 528, 22, 22, sc[5])
    s1, q1 = field_sums(r.r4, 1, 528, 22, 22, sc[6])
    put_sums(r.st4, s0 + s1, q0 + q1)
    net.share(r.st4, r.g4, 1)
    ready_og()
    net.shared(r.st4, r.g4, 1)

    count = sc[9] * 1936.0
    avg, inv = moments(r.g4, None, count, 256)
    scale4, off4 = affine(par, 3, avg, inv)
    s = jnp.zeros((1, 256), f32)
    q = jnp.zeros((1, 256), f32)
    for d in range(2):
        m = sc[5 + d]

        def part(t, c):
            x = r.r4[pl.ds(pl.multiple_of(d * 528 + t * 48, 16), 48), :]
            b = x * scale4 + off4
            sg = 1.0 / (1.0 + jnp.exp(-b))
            r.dec[d, pl.ds(2 * t, 2)] = (m * (b * sg)).reshape(2, 24, 256)
            bg = r.og[d, pl.ds(2 * t, 2)].reshape(48, 256) * sg * (1.0 + b * (1.0 - sg))
            normed = (x - avg) * inv
            return (
                c[0] + jnp.sum(bg.reshape(6, 8, 256), axis=0),
                c[1] + jnp.sum((bg * normed).reshape(6, 8, 256), axis=0),
            )

        ps, pq = lax.fori_loop(0, 11, part, (jnp.zeros((8, 256), f32), jnp.zeros((8, 256), f32)))
        s = s + m * jnp.sum(ps, axis=0, keepdims=True)
        q = q + m * jnp.sum(pq, axis=0, keepdims=True)
    put_sums(r.st5, s, q)
    net.share(r.st5, r.g5, 2)

    def spread(t):
        for d in range(2):
            for py in range(2):
                v = r.dec[d, t, pl.ds(0, 22), py * 128 : py * 128 + 128]
                r.decoded[d, 2 * t + py, pl.ds(0, 22, stride=2), :] = v[:, :64]
                r.decoded[d, 2 * t + py, pl.ds(1, 22, stride=2), :] = v[:, 64:]

    loop(22, spread)
    mv.out((r.decoded, r.odecoded))
    net.shared(r.st5, r.g5, 2)
    net.sides()
    net.halos = []
    kept()

    tg, tc = totals(r.g5, None, 256)
    f[...] = jnp.zeros(f.shape, f32)

    def put_back(p, get_r, get_a, keep):
        m = sc[4 + p]

        def rows(t):
            a = get_a(2 * t).reshape(48, 256)
            e = response_back(par, 3, avg, inv, tg, tc, count, get_r(t * 48), a).reshape(2, 24, 256)
            e = jnp.where(cells(e.shape, 22, 22, 0) & (m > 0), e, 0.0)
            f[pl.ds(1 + 2 * t, 2), 8:32, :] = e
            if keep is not None:
                hi, lo = split(e.reshape(48, 256))
                at = pl.ds(pl.multiple_of(keep * 528 + t * 48, 16), 48)
                r.eh[at, :] = hi
                r.el[at, :] = lo

        loop(11, rows)
        im2col(r.bh, r.bl, p, f, 24, 24, 256, x0=7)

    put_back(0, part_of(r.r4l, 0, 48), lambda y: r.ogl[pl.ds(y, 2)], None)
    loop(2, lambda p: put_back(p + 1, part_of(r.r4, p * 528, 48), lambda y: r.og[p, pl.ds(y, 2)], p))
    put_back(3, part_of(r.r4r, 0, 48), lambda y: r.ogr[pl.ds(y, 2)], None)
    conv(r.a3, r.bh, r.bl, r.d4h, r.d4l, 576, NT)
    net.to_left(r.a3.at[0:576], r.a3r, 2)
    net.to_right(r.a3.at[576:1152], r.a3l, 2)
    mv.out((r.a3, r.oa3))
    s = jnp.zeros((1, 256), f32)
    q = jnp.zeros((1, 256), f32)
    for d in range(2):
        def part(t, c):
            at = pl.ds(pl.multiple_of(d * 576 + t * 48, 16), 48)
            normed, bg = back_parts(par, 2, avg3, inv3, r.r3[at, :], r.a3[at, :])
            bg = bg.reshape(2, 24, 256)
            bg = jnp.where(cells(bg.shape, 23, 23, 2 * t), bg, 0.0)
            return c[0] + jnp.sum(bg, axis=0), c[1] + jnp.sum(bg * normed.reshape(2, 24, 256), axis=0)

        ps, pq = lax.fori_loop(0, 12, part, (jnp.zeros((24, 256), f32), jnp.zeros((24, 256), f32)))
        s = s + sc[5 + d] * jnp.sum(ps, axis=0, keepdims=True)
        q = q + sc[5 + d] * jnp.sum(pq, axis=0, keepdims=True)
    put_sums(r.st6, s, q)
    net.share(r.st6, r.g6, 3)

    def tap(i):
        at = pl.ds(pl.multiple_of(i * 528, 16), 1056)
        r.g[...] = dot3(r.ah[at, :], r.al[at, :], r.eh[...], r.el[...], TN)
        put_taps(r.dw4, r.g, i, 64, 64, 0, 0)

    loop(3, tap)
    net.shared(r.st6, r.g6, 3)
    net.sides()
    mv.finish()


def put_taps(out, g, i, chans, total, row0, base):
    def rows(p):
        return pl.ds(pl.multiple_of(base + (i * 5 + p // 2) * total + row0, 8), chans)

    for p in range(9):
        v = folded(g, p // 3, p % 3, chans)
        v = v if p % 2 == 0 else pltpu.roll(v, 64, 1)
        at = 64 * (p % 2)
        out[rows(p), at : at + 64] = v[:, at : at + 64]
    out[rows(8), 64:] = jnp.zeros((chans, 64), f32)


def decode(dims, k, co, w4):
    n = dims[1] * dims[2]
    V = pltpu.VMEM
    box = (22, 24, 256)
    return launch(
        functools.partial(decode_kernel, dims), "decode", 2,
        [("ir2", k.or2, HB), ("r2c", k.or2c, VM), ("hl", k.hl, VM), ("hr", k.hr, VM), ("co", co[0], VM),
         ("col", k.col, VM), ("cor", k.cor, VM), ("g2", k.g2, VM), ("par", k.par, VM), ("iuh", k.ouh, HB),
         ("iul", k.oul, HB), ("w3", k.ow3c, VM), ("w4", w4, VM), ("iog", k.oog, HB), ("iogl", k.ogl, HB),
         ("iogr", k.ogr, HB), ("sc", k.sc, SM)],
        [("pooled", (1024, 64), f32, VM), ("g3", (n, 1, 512), f32, VM), ("or3", (1152, 256), f32, HB),
         ("or3l", (576, 256), f32, HB), ("or3r", (576, 256), f32, HB), ("odecoded", (2, 44, 44, 64), f32, HB),
         ("oa3", (1152, 256), f32, HB), ("a3l", (576, 256), f32, HB), ("a3r", (576, 256), f32, HB),
         ("g6", (n, 1, 512), f32, VM), ("st5", (1, 512), f32, VM), ("st6", (1, 512), f32, VM),
         ("dw4", (960, 128), f32, VM)]
        + both_out("oa", (2304, 1024)) + both_out("ocu", (1728, 512)),
        both("t", (3, 1024, 256)) + both("d4", (3, 256, 1024)) + both("a", (2112, 1024)) + both("b", (2304, 1024))
        + both("cu", (1728, 512)) + both("u", (4, 512, 256)) + both("e", (1056, 256))
        + [("f", V((26, 40, 256), f32)), ("f2", V((26, 32, 128), f32)), ("r2", V((2048, 256), f32)),
           ("r3", V((1152, 256), f32)), ("r3l", V((576, 256), f32)), ("r3r", V((576, 256), f32)),
           ("r4", V((1056, 256), f32)), ("r4l", V((528, 256), f32)),
           ("r4r", V((528, 256), f32)), ("og", V((2,) + box, f32)), ("ogl", V(box, f32)), ("ogr", V(box, f32)),
           ("dec", V((2,) + box, f32)), ("decoded", V((2, 44, 44, 64), f32)), ("a3", V((1152, 256), f32)),
           ("g", V((1024, 256), f32)), ("g4", V((n, 1, 512), f32)), ("g5", V((n, 1, 512), f32)),
           ("st3", V((1, 512), f32)), ("st4", V((1, 512), f32))]
        + sems(n, n, n, n, n, n, n, n, 6, 6, 24),
    )


def third_back_kernel(dims, r):
    net = Net(dims, False, [])
    barrier = pltpu.get_barrier_semaphore()
    partner = (1 - net.s, net.k, net.b)
    mv = Moves(r.sem0)
    pl.semaphore_signal(barrier, inc=1, device_id=partner, device_id_type=MESH)
    ready_a = fetch(mv, (r.iah, r.ah), (r.ial, r.al))
    ready_u = fetch(mv, (r.icuh, r.cuh), (r.icul, r.cul), (r.iubh, r.ubh), (r.iubl, r.ubl))
    toeplitz(r.w3c, 0, 64, None, None, r.d3h, r.d3l)
    sc, f, par = r.sc, r.f, r.par
    count = sc[9] * 2116.0
    avg, inv = moments(r.g3, None, count, 256)
    tg, tc = totals(r.g6, None, 256)
    f[...] = jnp.zeros(f.shape, f32)

    def of(ref, base):
        return lambda at: ref[pl.ds(pl.multiple_of(base + at, 16), 48), :]

    def put(p, get_r, get_a, keep):
        m = sc[4 + p]

        def rows(t):
            e = response_back(par, 2, avg, inv, tg, tc, count, get_r(t * 48), get_a(t * 48)).reshape(2, 24, 256)
            e = jnp.where(cells(e.shape, 23, 23, 2 * t) & (m > 0), e, 0.0)
            f[pl.ds(1 + 2 * t, 2), 8:32, :] = e
            if keep is not None:
                hi, lo = split(e.reshape(48, 256))
                at = pl.ds(pl.multiple_of(keep * 576 + t * 48, 16), 48)
                r.eh[at, :] = hi
                r.el[at, :] = lo

        loop(12, rows)
        im2col(r.bh, r.bl, p, f, 24, 24, 256, x0=7)

    put(0, of(r.r3l, 0), of(r.a3l, 0), None)
    loop(2, lambda p: put(p + 1, of(r.r3, p * 576), of(r.a3, p * 576), p))
    put(3, of(r.r3r, 0), of(r.a3r, 0), None)
    conv(r.g.at[:1152], r.bh, r.bl, r.d3h, r.d3l, 576, NT)

    def row(t):
        at = pl.ds(pl.multiple_of(t * 24, 24), 24)
        r.skip[2 * t] = r.g[at, :128]
        r.skip[2 * t + 1] = r.g[at, 128:]

    loop(48, row)
    pl.semaphore_wait(barrier, 1)
    across = pltpu.make_async_remote_copy(
        src_ref=r.skip, dst_ref=r.oskip, send_sem=r.sem1.at[0], recv_sem=r.sem1.at[1],
        device_id=partner, device_id_type=MESH,
    )
    across.start()

    ready_a()
    bucket = r.bucket

    def tap(i):
        at = pl.ds(pl.multiple_of(i * 576, 16), 1152)
        r.g[:1024, :] = dot3(r.ah[at, :], r.al[at, :], r.eh[...], r.el[...], TN)
        put_taps(bucket, r.g, i, 64, 192, 128, 0)

    loop(3, tap)
    ready_u()

    def coarse(j):
        at = pl.ds(pl.multiple_of((j // 2 + j % 2) * 576, 16), 576)
        e = pl.ds(pl.multiple_of((j // 2) * 576, 16), 576)
        r.gu[j] = dot3(r.cuh[at, :], r.cul[at, :], r.eh[e, :], r.el[e, :], TN)

    loop(4, coarse)
    r.cg[...] = jnp.zeros(r.cg.shape, f32)

    def back(p):
        at = pl.ds(pl.multiple_of(p * 576, 16), 576)
        r.cg[...] += sc[5] * dot3(r.bh[at, :], r.bl[at, :], r.ubh[p], r.ubl[p], NT)

    loop(4, back)
    up_blocks(r)
    r.gd[...] = jnp.zeros(r.gd.shape, f32)
    for i in range(3):
        loop(1, lambda _, i=i: toeplitz_tap(r.w3u, 0, 128, i, 0, r.tuh, r.tul))

        def block(ab, i=i):
            out = pl.ds(pl.multiple_of(ab * 128, 128), 128)
            p = jnp.concatenate([r.gu[slot_of(i, 0), out, :], r.gu[slot_of(i, 1), out, :]], axis=0)
            ph, plo = split(p)
            rows = pl.ds(pl.multiple_of(ab * 512, 512), 512)
            r.gd[...] += dot3(ph, plo, r.tuh[0, rows, :], r.tul[0, rows, :], NT)
            r.g[rows, :] = dot3(r.uph[...], r.upl[...], ph, plo, TN)

        loop(4, block)
        loop(1, lambda _, i=i: put_taps(bucket, r.g, i, 128, 192, 0, 0))
    bucket[2880:3840, :] = r.dw4[...]
    for ip in range(2):
        for q in range(4):
            at = 3840 + (ip * 4 + q) * 128
            bucket[at : at + 128, :] = r.gd[ip * 128 : ip * 128 + 128, q * 128 : q * 128 + 128]
    if bucket.shape[0] > BUCKET:
        bucket[BUCKET:, :] = jnp.zeros((bucket.shape[0] - BUCKET, 128), f32)
    mv.out((bucket, r.obucket))
    across.wait()
    mv.finish()


def world_rows(dims, rows):
    n = dims[0] * dims[1] * dims[2]
    return -(-rows // (8 * n)) * 8 * n


def bucket_parts(dims):
    first = world_rows(dims, FIRST_HALF)
    return first, world_rows(dims, max(BUCKET - first, 8))


def reduction_buffers(dims, rows, tag):
    S, K, B = dims
    Q = S * K // 2
    V = pltpu.VMEM
    per = rows // (S * K * B)
    return [("mine1" + tag, V((rows // 2, 128), f32)), ("slot1" + tag, V((rows // 2, 128), f32)),
            ("slot2" + tag, V((Q - 1, B * per, 128), f32)), ("mine2" + tag, V((B * per, 128), f32)),
            ("slot3" + tag, V((B - 1, per, 128), f32))]


def reduction_sems(dims):
    Q, B = dims[0] * dims[1] // 2, dims[2]
    return [2, 2 * (Q - 1), 2 * (B - 1), 2 * (B - 1), 2 * (Q - 1), 2]


def third_back(dims, fb, r3, r3l, r3r, g3, k, t, dw4, w3u, w3c, up, par, sc):
    n = dims[0] * dims[1] * dims[2]
    V = pltpu.VMEM
    rows = sum(bucket_parts(dims))
    return launch(
        functools.partial(third_back_kernel, dims), "third_back", 4,
        [("a3", fb.oa3, VM), ("a3l", fb.a3l, VM), ("a3r", fb.a3r, VM), ("r3", r3, VM), ("r3l", r3l, VM),
         ("r3r", r3r, VM), ("g3", g3, VM), ("g6", fb.g6, VM), ("dw4", dw4, VM), ("par", par, VM),
         ("w3u", w3u, VM), ("w3c", w3c, VM), ("up", up, VM), ("iah", t.oah, HB), ("ial", t.oal, HB),
         ("icuh", t.ocuh, HB), ("icul", t.ocul, HB), ("iubh", k.oubh, HB), ("iubl", k.oubl, HB), ("sc", sc, SM)],
        [("oskip", (96, 24, 128), f32, HB), ("cg", (576, 128), f32, VM), ("obucket", (rows, 128), f32, HB)],
        both("tu", (1, 2048, 256)) + both("d3", (3, 256, 1024)) + both("a", (2304, 1024)) + both("cu", (1728, 512))
        + both("up", (256, 512)) + both("ub", (4, 128, 1024)) + both("b", (2304, 1024)) + both("e", (1152, 256))
        + [("f", V((26, 40, 256), f32)), ("skip", V((96, 24, 128), f32)),
           ("g", V((2048, 256), f32)), ("gu", V((4, 512, 256), f32)), ("gd", V((256, 512), f32)),
           ("bucket", V((rows, 128), f32))]
        + sems(24, 2),
    )


class Reduction:
    def __init__(self, dims, net, base, rows, r, tag, sems):
        S, K, B = dims
        self.net, self.base, self.steps = net, base, iter(sems)
        self.per = rows // (S * K * B)
        self.bucket, self.res = r.bucket, r.res
        self.mine1, self.slot1, self.slot2, self.mine2, self.slot3 = (
            getattr(r, name + tag) for name in ("mine1", "slot1", "slot2", "mine2", "slot3")
        )
        self.Q, self.B, self.half = S * K // 2, B, S * K * B // 2
        self.core = net.k % 2
        self.q = net.s * (K // 2) + net.k // 2
        self.rows = K // 2
        self.pair_of = (net.s, net.k + 1 - 2 * self.core, net.b)
        self.place = self.core * self.half + self.q * self.B + net.b

    def ds(self, first, count, base=0):
        return pl.ds(pl.multiple_of(base + first * self.per, 8), count * self.per)

    def whole(self, first, count):
        return self.ds(first, count, self.base)

    def at_square(self, q):
        return (q // self.rows, 2 * (q % self.rows) + self.core, self.net.b)

    def copies(self, items):
        sem = next(self.steps)
        self.open = [
            pltpu.make_async_remote_copy(
                src_ref=src, dst_ref=dst, send_sem=sem.at[2 * j], recv_sem=sem.at[2 * j + 1],
                device_id=dev, device_id_type=MESH,
            )
            for j, (src, dst, dev) in enumerate(items)
        ]
        for c in self.open:
            c.start()

    def wait(self):
        for c in self.open:
            c.wait()

    def pair(self, mv):
        self.own = mv.start(self.bucket.at[self.whole(self.core * self.half, self.half)], self.mine1)
        src = self.bucket.at[self.whole((1 - self.core) * self.half, self.half)]
        self.copies([(src, self.slot1, self.pair_of)])

    def square(self):
        self.wait()
        self.own.wait()
        size = self.half * self.per // 16

        def add(t):
            at = pl.ds(pl.multiple_of(t * size, 8), size)
            self.mine1[at, :] += self.slot1[at, :]

        loop(16, add)
        items = []
        for t in range(1, self.Q):
            q = (self.q + t) % self.Q
            items.append((self.mine1.at[self.ds(q * self.B, self.B)], self.slot2.at[t - 1], self.at_square(q)))
        self.copies(items)

    def line(self):
        self.wait()
        v = self.mine1[self.ds(self.q * self.B, self.B), :]
        for t in range(self.Q - 1):
            v = v + self.slot2[t]
        self.mine2[...] = v
        items = []
        for t in range(1, self.B):
            b = (self.net.b + t) % self.B
            items.append((self.mine2.at[self.ds(b, 1)], self.slot3.at[t - 1], (self.net.s, self.net.k, b)))
        self.copies(items)

    def line_back(self):
        self.wait()
        v = self.mine2[self.ds(self.net.b, 1), :]
        for t in range(self.B - 1):
            v = v + self.slot3[t]
        self.res[self.whole(self.place, 1), :] = v
        own = self.res.at[self.whole(self.place, 1)]
        self.copies([(own, own, (self.net.s, self.net.k, (self.net.b + t) % self.B)) for t in range(1, self.B)])

    def square_back(self):
        self.wait()
        own = self.res.at[self.whole(self.core * self.half + self.q * self.B, self.B)]
        self.copies([(own, own, self.at_square((self.q + t) % self.Q)) for t in range(1, self.Q)])

    def pair_back(self):
        self.wait()
        own = self.res.at[self.whole(self.core * self.half, self.half)]
        self.copies([(own, own, self.pair_of)])


def skip_stage(r, avg, inv, d):
    sc, par = r.sc, r.par
    oy, ox = r.si[0, 0], r.si[0, 1]
    qx = ox // 2
    rx = ox - 2 * qx
    odd = rx > 0
    lane = lax.broadcasted_iota(jnp.int32, (32, 128), 1)
    pad = jnp.zeros((8, 128), f32)

    def placed(row):
        at = row - oy
        v = r.skip[d * 48 + jnp.clip(at, 0, 47)]
        v = jnp.where((at >= 0) & (at < 48), v, 0.0)
        v = jnp.concatenate([v, pad], axis=0)
        v = jnp.where(odd, pltpu.roll(v, 64, 1), v)
        v = pltpu.roll(v, qx, 0)
        return jnp.where((lane < 64) & odd, pltpu.roll(v, 1, 0), v)

    def part(t, c):
        pv = r.pg[t] * 0.125
        pv = jnp.concatenate([pv, pv], axis=1)
        a = jnp.concatenate([placed(2 * t) + pv, placed(2 * t + 1) + pv], axis=1)
        rows = pl.ds(pl.multiple_of(d * 1024 + t * 32, 32), 32)
        normed, bg = back_parts(par, 1, avg, inv, r.r2[rows, :], a)
        bg = sc[1 + d] * bg
        r.bg2[rows, :] = bg
        bg = bg.reshape(4, 8, 256)
        return c[0] + jnp.sum(bg, axis=0), c[1] + jnp.sum(bg * normed.reshape(4, 8, 256), axis=0)

    return lax.fori_loop(0, 32, part, (jnp.zeros((8, 256), f32), jnp.zeros((8, 256), f32)))


def store_slots(slots, x, row0):
    per = slots.shape[1]
    for at in range(0, x.shape[0], per):
        slots[(row0 + at) // per] = x[at : at + per]


def four_rows(st):
    v = st[...]
    return [v[:, 128 * c : 128 * c + 128] for c in range(4)]


def tail_kernel(dims, r):
    net = Net(dims, False, [r.sem0, r.sem1, r.sem2, r.sem3, r.sem4, r.sem5])
    world = Net(dims, True, [r.sem6, r.sem7, r.sem8, r.sem9, r.sem16, r.sem17, r.sem18, r.sem19])
    world.enter()
    mv = Moves(r.sem10)
    ready_a = fetch(mv, (r.iah, r.ah), (r.ial, r.al))
    ready_s = fetch(mv, (r.ish, r.sh), (r.isl, r.sl), (r.ir1.at[1:3], r.r1))
    sc, par, f = r.sc, r.par, r.f
    count = sc[8] * 4096.0
    avg, inv = moments(r.g2, net.s, count, 256)
    toeplitz(r.w2, 0, 32, None, None, r.d2h, r.d2l)
    f[...] = jnp.zeros(f.shape, f32)
    s0, q0 = skip_stage(r, avg, inv, 0)
    world.ready()
    rows_a, rows_b = bucket_parts(dims)
    steps_a = [r.sem11, r.sem12, r.sem13, r.sem14, r.sem15, r.sem20]
    steps_b = [r.sem21, r.sem22, r.sem23, r.sem24, r.sem25, r.sem26]
    big_a = Reduction(dims, net, 0, rows_a, r, "a", steps_a)
    big_b = Reduction(dims, net, rows_a, rows_b, r, "b", steps_b)
    big_a.pair(mv)
    big_b.pair(mv)
    s1, q1 = skip_stage(r, avg, inv, 1)
    put_sums(r.st7, jnp.sum(s0 + s1, axis=0, keepdims=True), jnp.sum(q0 + q1, axis=0, keepdims=True))
    net.share(r.st7, r.g7, 0)
    big_a.square()
    net.shared(r.st7, r.g7, 0)
    big_b.square()

    tg, tc = totals(r.g7, None, 256)
    k = par[2:3, :] * inv

    def put(p):
        m = sc[1 + p]

        def rows(t):
            at = pl.ds(pl.multiple_of(p * 1024 + t * 64, 64), 64)
            normed = (r.r2[at, :] - avg) * inv
            e = k * (r.bg2[at, :] - m * ((tg + normed * tc) / count))
            hi, lo = split(e)
            r.e2h[at, :] = hi
            r.e2l[at, :] = lo
            f[pl.ds(1 + 2 * t, 2), 8:40, :] = e.reshape(2, 32, 256)

        loop(16, rows)
        im2col(r.bh, r.bl, 0, f, 34, 40, 256, x0=7)
        r.v[p] = dot3(r.bh[...], r.bl[...], r.d2h[...].reshape(384, 1024), r.d2l[...].reshape(384, 1024), NT)

    loop(1, lambda _: put(0))
    big_a.line()
    loop(1, lambda _: put(1))
    for d in range(2):
        r.side[d, :1360] = r.v[0, :, 256:] if d == 0 else r.v[1, :, :128]
        r.side[d, 1360:] = jnp.zeros((48, 128), f32)
        if d == 0:
            net.to_left(r.side.at[0], r.fr, 0)
        else:
            net.to_right(r.side.at[1], r.fl, 0)
    r.a1[1, :1360] = r.v[0, :, :128] + r.v[1, :, 128:256]
    r.a1[0, :1360] = r.v[0, :, 128:256] + r.v[1, :, 256:]
    for d in range(2):
        r.a1[d, 1360:] = jnp.zeros((48, 128), f32)
    big_a.line_back()
    big_b.line()

    ready_a()

    def tap(i):
        at = pl.ds(pl.multiple_of(i * 1024, 1024), 2048)
        r.g[...] = dot3(r.ah[at, :], r.al[at, :], r.e2h[...], r.e2l[...], TN)
        put_taps(r.dw2, r.g, i, 32, 32, 0, 0)

    loop(3, tap)
    store_slots(r.small, r.dw2[...], 0)
    rows = jnp.concatenate(
        four_rows(r.st7) + four_rows(r.st6) + four_rows(r.st5) + [jnp.zeros((20, 128), f32)], axis=0
    )
    store_slots(r.small, rows, 480)
    big_a.square_back()
    big_b.line_back()
    net.sides()

    ready_s()
    count1 = sc[8] * 4356.0
    avg1, inv1 = moments(r.g1, net.s, count1, 128)
    s = jnp.zeros((1, 128), f32)
    q = jnp.zeros((1, 128), f32)
    for d in range(2):
        other = r.fl if d == 0 else r.fr
        here = sc[10 + d]

        def part(t, c):
            rows = pl.ds(pl.multiple_of(t * 160, 160), 160)
            a = r.a1[d, rows, :] + jnp.where(here > 0, other[rows, :], 0.0)
            r.a1[d, rows, :] = a
            normed, bg = back_parts(par, 0, avg1, inv1, r.r1[d, rows, :], a)
            bg = bg.reshape(4, 40, 128)
            bg = jnp.where(cells(bg.shape, 33, 33, 4 * t), bg, 0.0)
            return c[0] + jnp.sum(bg, axis=0), c[1] + jnp.sum(bg * normed.reshape(4, 40, 128), axis=0)

        ps, pq = lax.fori_loop(0, 8, part, (jnp.zeros((40, 128), f32), jnp.zeros((40, 128), f32)))
        rows = slice(1280, OWN)
        a = r.a1[d, rows, :] + jnp.where(here > 0, other[rows, :], 0.0)
        r.a1[d, rows, :] = a
        normed, bg = back_parts(par, 0, avg1, inv1, r.r1[d, 1280:1320, :], a[:40])
        bg = jnp.where(lax.broadcasted_iota(jnp.int32, (40, 128), 0) < 33, bg, 0.0)
        ps = ps + bg
        pq = pq + bg * normed
        s = s + sc[1 + d] * jnp.sum(ps, axis=0, keepdims=True)
        q = q + sc[1 + d] * jnp.sum(pq, axis=0, keepdims=True)
    put_sums(r.st8, s, q)
    net.share(r.st8, r.g8, 1)
    world.scatter(r.small, r.slots, 0)
    net.shared(r.st8, r.g8, 1)

    tg1, tc1 = totals(r.g8, None, 128)
    wh, wl = r.w1h[...], r.w1l[...]
    r.dw1[...] = jnp.zeros(r.dw1.shape, f32)

    def put_first(p):
        m = sc[1 + p]
        r.eh[p, 1280:, :] = jnp.zeros((OWN - 1280, 128), bf16)
        r.el[p, 1280:, :] = jnp.zeros((OWN - 1280, 128), bf16)

        def rows(t):
            at = pl.ds(pl.multiple_of(t * 80, 80), 80)
            e = response_back(par, 0, avg1, inv1, tg1, tc1, count1, r.r1[p, at, :], r.a1[p, at, :])
            e = e.reshape(2, 40, 128)
            e = jnp.where(cells(e.shape, 33, 33, 2 * t) & (m > 0), e, 0.0)
            hi, lo = split(e.reshape(80, 128))
            r.eh[p, at, :] = hi
            r.el[p, at, :] = lo

        loop(17, rows)
        rows = pl.ds(pl.multiple_of((p + 1) * 64, 64), 192)
        r.dw1[...] += dot3(r.sh[rows, :], r.sl[rows, :], r.eh[p], r.el[p], NN)

    loop(2, put_first)
    big_a.pair_back()
    big_b.square_back()
    world.scattered(r.small, r.slots, 0)
    r.mine[...] = jnp.sum(r.slots[...], axis=0)
    acc = r.dw1[...]
    lane = lax.broadcasted_iota(jnp.int32, (32, 128), 1)
    tot = jnp.zeros((32, 128), f32)
    for tap in range(4):
        v = jnp.zeros((32, 128), f32)
        for q in range(4):
            x = acc if q == tap else pltpu.roll(acc, ((tap - q) % 4) * 32, 1)
            hi, lo = split(x)
            sel = r.pick[tap * 4 + q]
            v += dot(sel, hi, NN) + dot(sel, lo, NN)
        tot += jnp.where(lane // 32 == tap, v, 0.0)
    last = r.small2.shape[0] * r.small2.shape[1]
    rows = jnp.concatenate([tot] + four_rows(r.st8) + [jnp.zeros((last - 36, 128), f32)], axis=0)
    store_slots(r.small2, rows, 0)
    world.scatter(r.small2, r.slots2, 2)
    world.share(r.mine, r.red, 1)

    def image_part(p):
        v = dot3(wh, wl, r.eh[p], r.el[p], NT)
        for i in range(3):
            tot = jnp.zeros((16, OWN), f32)
            for ab in range(4):
                at = i * 64 + ab * 16
                a, b = ab // 2, ab % 2
                x = v[at : at + 16, :]
                tot += x if ab == 0 else pltpu.roll(x, 40 * a + b, 1)
            r.parts[p, i] = tot

    loop(2, image_part)
    net.halos = []
    net.to_left(r.parts.at[0, 0], r.pr, 1)
    net.to_right(r.parts.at[1, 2], r.pl, 1)
    world.scattered(r.small2, r.slots2, 2)
    r.mine2s[...] = jnp.sum(r.slots2[...], axis=0)
    world.share(r.mine2s, r.red2, 3)
    big_b.pair_back()
    net.sides()
    for d in range(2):
        other = r.pl if d == 0 else r.pr
        tot = r.parts[0, 1 + d] + r.parts[1, d] + jnp.where(sc[10 + d] > 0, other[...], 0.0)
        tot = tot * (r.keep[...] * sc[1 + d])
        rows = []
        for y in range(34):
            tile, off = (40 * y) // 128, (40 * y) % 128
            pair = []
            for px in range(2):
                v = tot[8 * px : 8 * px + 8, 128 * tile : 128 * tile + 128]
                if off + 34 > 128:
                    nxt = tot[8 * px : 8 * px + 8, 128 * tile + 128 : 128 * tile + 256]
                    v = jnp.where(lane[:8] >= off, v, nxt)
                pair.append(v if off == 0 else pltpu.roll(v, 128 - off, 1))
            rows.append(jnp.concatenate(pair, axis=1))
        hi, lo = split(jnp.concatenate(rows, axis=0))
        out = dot(hi, r.even[...], NT) + dot(lo, r.even[...], NT)
        r.ig[d] = out.reshape(34, 8, 68)
    world.shared(r.mine, r.red, 1)
    world.shared(r.mine2s, r.red2, 3)
    big_a.wait()
    big_b.wait()
    mv.finish()


def tail(dims, tb, pg, k, fo, w2, si):
    keep, par, sc = k.keep, k.par, k.sc
    n = dims[0] * dims[1] * dims[2]
    m = dims[1] * dims[2]
    V = pltpu.VMEM
    per = 512 // n
    per2 = max(64, n) // n
    rows_a, rows_b = bucket_parts(dims)
    steps = reduction_sems(dims)
    return launch(
        functools.partial(tail_kernel, dims), "tail", 5,
        [("skip", tb.oskip, VM), ("bucket", tb.obucket, HB), ("pg", pg, VM), ("r2", k.or2, VM), ("g2", k.g2, VM),
         ("g1", k.g1, VM), ("w2", w2, VM), ("keep", keep, VM), ("w1h", k.ow1h, VM), ("w1l", k.ow1l, VM),
         ("pick", tap_picks(), VM), ("even", deinterleave(), VM), ("st5", fo.st5, VM), ("st6", fo.st6, VM),
         ("par", par, VM), ("iah", k.oah, HB), ("ial", k.oal, HB), ("ish", k.osh, HB), ("isl", k.osl, HB),
         ("ir1", k.or1, HB), ("sc", sc, SM), ("si", si, SM)],
        [("ig", (2, 34, 8, 68), f32, VM), ("red", (n, per, 128), f32, VM), ("red2", (n, per2, 128), f32, VM),
         ("res", (rows_a + rows_b, 128), f32, VM)],
        both("d2", (3, 128, 1024)) + both("a", (4096, 512)) + both("b", (1360, 1024)) + both("e2", (2048, 256))
        + both("s", (384, OWN)) + both("e", (2, OWN, 128))
        + [("f", V((36, 56, 256), f32)), ("bg2", V((2048, 256), f32)), ("r1", V((2, 1440, 128), f32)),
           ("a1", V((2, OWN, 128), f32)), ("side", V((2, OWN, 128), f32)), ("fl", V((OWN, 128), f32)),
           ("fr", V((OWN, 128), f32)), ("v", V((2, 1360, 384), f32)), ("parts", V((2, 3, 16, OWN), f32)),
           ("pl", V((16, OWN), f32)), ("pr", V((16, OWN), f32)), ("dw1", V((192, 128), f32)),
           ("g", V((512, 256), f32)), ("dw2", V((480, 128), f32)), ("small", V((n, per, 128), f32)),
           ("slots", V((n, per, 128), f32)), ("mine", V((per, 128), f32)), ("small2", V((n, per2, 128), f32)),
           ("slots2", V((n, per2, 128), f32)), ("mine2s", V((per2, 128), f32)), ("g7", V((m, 1, 512), f32)),
           ("g8", V((m, 1, 512), f32)), ("st7", V((1, 512), f32)), ("st8", V((1, 512), f32))]
        + reduction_buffers(dims, rows_a, "a")
        + reduction_buffers(dims, rows_b, "b")
        + sems(m, m, m, m, 4, 4, n, n, n, n, 8, *steps[:5], n, n, n, n, 2, *steps),
    )


def finish_kernel(r):
    def tap(i):
        for p in range(9):
            at = 64 * (p % 2)

            def get(base, chans, at=at, p=p):
                rows = pl.ds(pl.multiple_of(base + (i * 5 + p // 2) * chans, 8), chans)
                v = r.res[rows, :]
                return (v if at == 0 else pltpu.roll(v, 64, 1))[:, :64]

            r.dw3t[i * 9 + p] = get(0, 192).T
            r.dw4[i * 9 + p] = get(2880, 64)
            rows = pl.ds(pl.multiple_of((i * 5 + p // 2) * 32, 32), 32)
            v = r.red[rows, :]
            r.dw2[i * 9 + p] = (v if at == 0 else pltpu.roll(v, 64, 1))[:, :64]

    loop(3, tap)
    r.pooled[...] = r.ipooled[...]
    r.cg[...] = r.icg[...]
    r.ig[...] = r.iig[...]
    r.dup[...] = r.res[3840:4864, :].reshape(8, 128, 128)
    for t in range(27):
        v = r.red2[4 * (t // 4) : 4 * (t // 4) + 4, :]
        v = v if t % 4 == 0 else pltpu.roll(v, 128 - 32 * (t % 4), 1)
        r.dw1[t] = v[:, :32]
    sums = [r.red2[32:36, :]] + [r.red[480 + 4 * j : 484 + 4 * j, :] for j in range(3)]
    for j, v in enumerate(sums):
        for c, out in ((0, (r.s1, r.s2, r.s3, r.s4)[j]), (2, (r.x1, r.x2, r.x3, r.x4)[j])):
            x = jnp.concatenate([v[c : c + 1], v[c + 1 : c + 2]], axis=1)
            if j == 0:
                x = fold(x[:, :128])
            else:
                x = fold(x)
            out[...] = x[:, : out.shape[1]]


def finish(res, red, red2, pooled, cg, ig):
    vectors = [(f"{a}{j}", (1, 32 if j == 1 else 64), f32, VM) for j in range(1, 5) for a in "sx"]
    return launch(
        finish_kernel, "finish", None,
        [("res", res, VM), ("red", red, VM), ("red2", red2, VM), ("ipooled", pooled, VM),
         ("icg", cg, VM), ("iig", ig, VM)],
        [("dw3t", (27, 64, 192), f32, VM), ("dw4", (27, 64, 64), f32, VM), ("dw2", (27, 32, 64), f32, VM),
         ("dup", (8, 128, 128), f32, VM), ("dw1", (27, 4, 32), f32, VM),
         ("pooled", pooled.shape, f32, VM), ("cg", cg.shape, f32, VM), ("ig", ig.shape, f32, VM)] + vectors,
        [],
    )


def body(
    dims,
    image, modality_mask, extents, crop_offsets, coarse,
    conv_first, gain_first, shift_first, conv_second, gain_second, shift_second,
    up_kernel, conv_third, gain_third, shift_third, conv_fourth, gain_fourth, shift_fourth,
    pool_grad, output_grad,
):
    si = crop_offsets[0]
    img = image[0, 0].transpose(0, 1, 3, 2).reshape(2, 34, 8, 68)
    co = coarse[0, 0]
    w2 = conv_second.reshape(27, 32, 64)
    up = up_kernel.reshape(8, 128, 128)
    k = front(
        dims, img, extents, modality_mask[0], si,
        (gain_first, shift_first, gain_second, shift_second, gain_third, shift_third, gain_fourth, shift_fourth),
        conv_first.reshape(27, 4, 32), w2, conv_third.reshape(27, 192, 64).transpose(0, 2, 1), up, co,
        output_grad[0, 0],
    )
    t = decode(dims, k, co, conv_fourth.reshape(27, 64, 64))
    tb = third_back(dims, t, t.or3, t.or3l, t.or3r, t.g3, k, t, t.dw4, k.ow3u, k.ow3c, up, k.par, k.sc)
    e = tail(dims, tb, pool_grad[0, 0, 0], k, t, w2, si)
    g = finish(e.res, e.red.reshape(512, 128), e.red2.reshape(-1, 128), t.pooled, tb.cg, e.ig)
    return (
        g.pooled.reshape(1, 1, 1, 32, 32, 64),
        t.odecoded[None, None],
        g.ig.reshape(2, 68, 4, 68).transpose(0, 1, 3, 2)[None, None],
        g.cg.reshape(1, 1, 1, 24, 24, 128),
        g.dw1.reshape(3, 3, 3, 4, 32),
        g.x1[0],
        g.s1[0],
        g.dw2.reshape(3, 3, 3, 32, 64),
        g.x2[0],
        g.s2[0],
        g.dup.reshape(2, 2, 2, 128, 128),
        g.dw3t.transpose(0, 2, 1).reshape(3, 3, 3, 192, 64),
        g.x3[0],
        g.s3[0],
        g.dw4.reshape(3, 3, 3, 64, 64),
        g.x4[0],
        g.s4[0],
    )


def solution(mesh):
    dims = tuple(mesh.shape[a] for a in ("section", "slab", "batch"))
    field = P("section", "batch", "slab", None, None, None)
    volume = P("section", "batch", None)
    rep = P()
    return jax.shard_map(
        functools.partial(body, dims),
        mesh=mesh,
        in_specs=(field, volume, rep, volume, field) + (rep,) * 13 + (field, field),
        out_specs=(field,) * 4 + (rep,) * 13,
        check_vma=False,
    )
```

```python
import functools
import types

import jax
import jax.numpy as jnp
import numpy as np
from jax import lax
from jax.experimental import pallas as pl
from jax.experimental.pallas import tpu as pltpu
from jax.sharding import PartitionSpec as P

f32 = jnp.float32
bf16 = jnp.bfloat16
MESH = pl.DeviceIdType.MESH
EPSILON = 1e-05
NN = (((1,), (0,)), ((), ()))
NT = (((1,), (1,)), ((), ()))
TN = (((0,), (0,)), ((), ()))
VM = pl.BlockSpec(memory_space=pltpu.VMEM)
SM = pl.BlockSpec(memory_space=pltpu.SMEM)
HB = pl.BlockSpec(memory_space=pl.ANY)
LIMIT = 62 * 2**20

OWN = 1408
CROP = 896
BUCKET = 2880 + 960 + 1024
FIRST_HALF = 2560


def split(x):
    hi = x.astype(bf16)
    return hi, (x - hi.astype(f32)).astype(bf16)


def dot(a, b, dims):
    return lax.dot_general(a, b, dims, preferred_element_type=f32)


def dot3(ah, al, bh, bl, dims):
    return dot(ah, bh, dims) + dot(al, bh, dims) + dot(ah, bl, dims)


def loop(n, f, unroll=1):
    def step(t, c):
        f(t)
        return c

    lax.fori_loop(0, n, step, 0, unroll=unroll)


def fold(v):
    lanes = v.shape[-1]
    v = jnp.broadcast_to(v, (8, lanes))
    if lanes == 256:
        h = v[:, :128] + v[:, 128:]
        h = h + pltpu.roll(h, 64, 1)
        h = jnp.concatenate([h, h], axis=1)
    else:
        h = v + pltpu.roll(v, 64, 1)
        h = h + pltpu.roll(h, 32, 1)
    return h[:1]


def totals(gath, half, lanes):
    if half is None:
        tot = jnp.sum(gath[...], axis=0)
    else:
        per = gath.shape[0] // 2
        tot = jnp.sum(gath[pl.ds(half * per, per)], axis=0)
    return fold(tot[:, :lanes]), fold(tot[:, 256 : 256 + lanes])


def moments(gath, half, count, lanes):
    s, q = totals(gath, half, lanes)
    avg = s / count
    inv = lax.rsqrt(q / count - avg * avg + EPSILON)
    return avg, inv


def affine(par, layer, avg, inv):
    lanes = avg.shape[-1]
    scale = par[2 * layer : 2 * layer + 1, :lanes] * inv
    return scale, par[2 * layer + 1 : 2 * layer + 2, :lanes] - avg * scale


def silu(b):
    return b / (1.0 + jnp.exp(-b))


def silu_back(a, b):
    s = 1.0 / (1.0 + jnp.exp(-b))
    return a * s * (1.0 + b * (1.0 - s))


def cells(shape, rows, cols, row0):
    y = lax.broadcasted_iota(jnp.int32, shape, 0) + row0
    x = lax.broadcasted_iota(jnp.int32, shape, 1)
    return (y < rows) & (x < cols)


def put_sums(st, s, q):
    lanes = s.shape[-1]
    st[...] = jnp.zeros(st.shape, f32)
    st[:, :lanes] = s
    st[:, 256 : 256 + lanes] = q


def im2col(ah, al, p, f, ny, pitch, lanes, x0=0):
    def pair(t):
        for a in range(2):
            for b in range(2):
                x = f[pl.ds(2 * t + a, 2), x0 + b : x0 + b + pitch, :]
                hi, lo = split(x.reshape(2 * pitch, lanes))
                rows = pl.ds(pl.multiple_of(p * (ny * pitch) + t * (2 * pitch), 16), 2 * pitch)
                at = (2 * a + b) * lanes
                ah[rows, at : at + lanes] = hi
                al[rows, at : at + lanes] = lo

    loop(ny // 2, pair)


def launch(body, name, cid, ins, outs, scratch):
    names = [i[0] for i in ins] + [o[0] for o in outs] + [x[0] for x in scratch]

    def kernel(*refs):
        body(types.SimpleNamespace(**dict(zip(names, refs))))

    res = pl.pallas_call(
        kernel,
        out_shape=[jax.ShapeDtypeStruct(o[1], o[2]) for o in outs],
        in_specs=[i[2] for i in ins],
        out_specs=[o[3] for o in outs],
        scratch_shapes=[x[1] for x in scratch],
        compiler_params=pltpu.CompilerParams(
            vmem_limit_bytes=LIMIT, collective_id=cid, has_side_effects=cid is not None
        ),
        name=name,
    )(*[i[1] for i in ins])
    return types.SimpleNamespace(**dict(zip([o[0] for o in outs], res)))


def both(name, shape):
    return [(name + "h", pltpu.VMEM(shape, bf16)), (name + "l", pltpu.VMEM(shape, bf16))]


def both_out(name, shape):
    return [(name + "h", shape, bf16, HB), (name + "l", shape, bf16, HB)]


def sems(*sizes):
    return [(f"sem{i}", pltpu.SemaphoreType.DMA((n,))) for i, n in enumerate(sizes)]


class Moves:
    def __init__(self, sem):
        self.sem = sem
        self.used = 0
        self.pending = []

    def start(self, src, dst):
        copy = pltpu.make_async_copy(src, dst, self.sem.at[self.used])
        self.used += 1
        copy.start()
        return copy

    def out(self, *pairs):
        for src, dst in pairs:
            self.pending.append(self.start(src, dst))

    def finish(self):
        for copy in self.pending:
            copy.wait()


def fetch(mv, *pairs):
    copies = [mv.start(src, dst) for src, dst in pairs]

    def wait():
        for copy in copies:
            copy.wait()

    return wait


class Net:
    def __init__(self, dims, wide, sems):
        S, K, B = dims
        self.s = lax.axis_index("section")
        self.k = lax.axis_index("slab")
        self.b = lax.axis_index("batch")
        self.K = K
        self.sems = sems
        if wide:
            self.n = S * K * B
            self.me = (self.s * K + self.k) * B + self.b
            self.coords = lambda d: (d // (K * B), (d // B) % K, d % B)
        else:
            self.n = K * B
            self.me = self.k * B + self.b
            self.coords = lambda d: (self.s, d // B, d % B)
        self.halos = []

    def each(self, f):
        def step(p, c):
            f(p)
            return c

        lax.fori_loop(1, self.n, step, 0)

    def enter(self):
        barrier = pltpu.get_barrier_semaphore()
        self.each(
            lambda p: pl.semaphore_signal(
                barrier, inc=1, device_id=self.coords((self.me + p) % self.n), device_id_type=MESH
            )
        )

    def ready(self):
        pl.semaphore_wait(pltpu.get_barrier_semaphore(), self.n - 1)

    def _copy(self, src, dst, p, group):
        return pltpu.make_async_remote_copy(
            src_ref=src,
            dst_ref=dst,
            send_sem=self.sems[2 * group].at[p],
            recv_sem=self.sems[2 * group + 1].at[p],
            device_id=self.coords((self.me + p) % self.n),
            device_id_type=MESH,
        )

    def share(self, src, slots, group=0):
        slots[self.me] = src[...]
        self.each(lambda p: self._copy(src, slots.at[self.me], p, group).start())

    def shared(self, src, slots, group=0):
        n = self.n
        self.each(lambda p: self._copy(src, slots.at[(self.me + n - p) % n], p, group).wait_recv())
        self.each(lambda p: self._copy(src, slots.at[self.me], p, group).wait_send())

    def scatter(self, src, slots, group):
        slots[self.me] = src[self.me]
        n = self.n
        self.each(lambda p: self._copy(src.at[(self.me + p) % n], slots.at[self.me], p, group).start())

    def scattered(self, src, slots, group):
        n = self.n
        self.each(
            lambda p: self._copy(
                src.at[(self.me + p) % n], slots.at[(self.me + n - p) % n], p, group
            ).wait_recv()
        )
        self.each(lambda p: self._copy(src.at[(self.me + p) % n], slots.at[self.me], p, group).wait_send())

    def _side(self, src, dst, j, step):
        return pltpu.make_async_remote_copy(
            src_ref=src,
            dst_ref=dst,
            send_sem=self.sems[-2].at[j],
            recv_sem=self.sems[-1].at[j],
            device_id=(self.s, (self.k + self.K + step) % self.K, self.b),
            device_id_type=MESH,
        )

    def to_left(self, src, dst, j):
        copy = self._side(src, dst, 2 * j, -1)

        @pl.when(self.k > 0)
        def _():
            copy.start()

        self.halos.append((copy, -1))

    def to_right(self, src, dst, j):
        copy = self._side(src, dst, 2 * j + 1, 1)

        @pl.when(self.k < self.K - 1)
        def _():
            copy.start()

        self.halos.append((copy, 1))

    def to_sides(self, left, right, j, first):
        copies = [(self._side(*left, 2 * j, -1), -1), (self._side(*right, 2 * j + 1, 1), 1)]
        even = self.k % 2 == 0

        @pl.when((even if first else ~even) & (self.k > 0))
        def _():
            copies[0][0].start()

        @pl.when((~even if first else even) & (self.k < self.K - 1))
        def _():
            copies[1][0].start()

        if first:
            self.halos += copies

    def sides(self):
        @pl.when(self.k > 0)
        def _():
            for copy, step in self.halos:
                if step < 0:
                    copy.wait_send()
                else:
                    copy.wait_recv()

        @pl.when(self.k < self.K - 1)
        def _():
            for copy, step in self.halos:
                if step > 0:
                    copy.wait_send()
                else:
                    copy.wait_recv()


def toeplitz(w, c0, chans, th, tl, dh=None, dl=None):
    loop(3, lambda i: toeplitz_tap(w, c0, chans, i, i, th, tl, dh, dl))


def toeplitz_tap(w, c0, chans, i, slot, th, tl, dh=None, dl=None):
    zero = jnp.zeros((chans, 64), f32)
    none = jnp.zeros((chans, 128), bf16)
    for s in range(4):
        part = []
        for j in range(3):
            here = w[i * 9 + j * 3 + s, c0 : c0 + chans, :] if s <= 2 else zero
            prev = w[i * 9 + j * 3 + s - 1, c0 : c0 + chans, :] if s >= 1 else zero
            part.append(split(jnp.concatenate([here, prev], axis=1)))
        for r in range(4):
            a, py, b, px = r // 2, r % 2, s // 2, s % 2
            block = (2 * a + b) * 4 + py * 2 + px
            for h in range(2):
                hi, lo = part[r - h] if 0 <= r - h <= 2 else (none, none)
                if th is not None:
                    rows = slice(block * chans, (block + 1) * chans)
                    th[slot, rows, 128 * h : 128 * h + 128] = hi
                    tl[slot, rows, 128 * h : 128 * h + 128] = lo
                if dh is not None:
                    rows = slice((py * 2 + px) * chans, (py * 2 + px + 1) * chans)
                    at = ((1 - a) * 2 + (1 - b)) * 256 + 128 * h
                    dh[2 - i, rows, at : at + 128] = hi
                    dl[2 - i, rows, at : at + 128] = lo


def slot_of(i, ip):
    pd = (ip + i + 1) % 2
    t = (pd + i - 1) // 2 - pd + 1
    return pd * 2 + t


def up_blocks(r):
    for ip in range(2):
        for q in range(4):
            hi, lo = split(r.up[ip * 4 + q])
            r.uph[ip * 128 : ip * 128 + 128, q * 128 : q * 128 + 128] = hi
            r.upl[ip * 128 : ip * 128 + 128, q * 128 : q * 128 + 128] = lo


def compose(r, i):
    def block(ab):
        rows = pl.ds(pl.multiple_of(ab * 512, 512), 512)
        p = dot3(r.uph[...], r.upl[...], r.tuh[i, rows, :], r.tul[i, rows, :], NN)
        out = pl.ds(pl.multiple_of(ab * 128, 128), 128)
        for ip in range(2):
            r.usc[slot_of(i, ip), out, :] += p[ip * 128 : ip * 128 + 128]

    loop(4, block)


def composed(r):
    for e in range(4):
        for ab in range(4):
            hi, lo = split(r.usc[e, ab * 128 : ab * 128 + 128, :])
            r.uh[e, ab * 128 : ab * 128 + 128, :] = hi
            r.ul[e, ab * 128 : ab * 128 + 128, :] = lo
            p = (3, 1, 2, 0)[e]
            at = (3 - ab) * 256
            r.ubh[p, :, at : at + 256] = hi
            r.ubl[p, :, at : at + 256] = lo


def source_copies(dims, own, crop, so, sr, ss, rs):
    K = dims[1]
    s = lax.axis_index("section")
    k = lax.axis_index("slab")
    b = lax.axis_index("batch")
    here, left, right = k, (k + K - 1) % K, (k + 1) % K

    def copy(j, src, dst, dev):
        return pltpu.make_async_remote_copy(
            src_ref=src,
            dst_ref=dst,
            send_sem=ss.at[j],
            recv_sem=rs.at[j],
            device_id=dev,
            device_id_type=MESH,
        )

    so[2:4] = own[...]
    lefts = [
        copy(0, own, so.at[4:6], (s, left, b)),
        copy(1, crop, sr.at[4:6], (1 - s, left, b)),
    ]
    rights = [
        copy(2, own, so.at[0:2], (s, right, b)),
        copy(3, crop, sr.at[0:2], (1 - s, right, b)),
    ]
    across = copy(4, crop, sr.at[2:4], (1 - s, here, b))

    def start():
        across.start()

        @pl.when(k > 0)
        def _():
            for c in lefts:
                c.start()

        @pl.when(k < K - 1)
        def _():
            for c in rights:
                c.start()

    def finish():
        across.wait()

        @pl.when(k > 0)
        def _():
            for c in lefts:
                c.wait_send()
            for c in rights:
                c.wait_recv()

        @pl.when(k < K - 1)
        def _():
            for c in rights:
                c.wait_send()
            for c in lefts:
                c.wait_recv()

        @pl.when(k == 0)
        def _():
            so[0:2] = jnp.zeros((2, 16, OWN), f32)
            sr[0:2] = jnp.zeros((2, 16, CROP), f32)

        @pl.when(k == K - 1)
        def _():
            so[4:6] = jnp.zeros((2, 16, OWN), f32)
            sr[4:6] = jnp.zeros((2, 16, CROP), f32)

    return start, finish


def field_sums(r, d, n, rows, cols, mask):
    base = d * n

    def part(t, c):
        x = r[pl.ds(pl.multiple_of(base + t * 96, 16), 96), :].reshape(4, 24, 256)
        x = jnp.where(cells(x.shape, rows, cols, 4 * t), x, 0.0)
        return c[0] + jnp.sum(x, axis=0), c[1] + jnp.sum(x * x, axis=0)

    zero = jnp.zeros((24, 256), f32)
    full = n // 96
    s, q = lax.fori_loop(0, full, part, (zero, zero))
    if n % 96:
        x = r[base + full * 96 : base + n, :].reshape((n - full * 96) // 24, 24, 256)
        x = jnp.where(cells(x.shape, rows, cols, 4 * full), x, 0.0)
        s = s + jnp.sum(x, axis=0)
        q = q + jnp.sum(x * x, axis=0)
    return mask * jnp.sum(s, axis=0, keepdims=True), mask * jnp.sum(q, axis=0, keepdims=True)


def back_parts(par, layer, avg, inv, r, a):
    lanes = avg.shape[-1]
    normed = (r - avg) * inv
    b = par[2 * layer : 2 * layer + 1, :lanes] * normed + par[2 * layer + 1 : 2 * layer + 2, :lanes]
    return normed, silu_back(a, b)


def response_back(par, layer, avg, inv, tg, tc, count, r, a):
    lanes = avg.shape[-1]
    gain = par[2 * layer : 2 * layer + 1, :lanes]
    normed, bg = back_parts(par, layer, avg, inv, r, a)
    return inv * gain * (bg - (tg + normed * tc) / count)


def folded(g, j, k, chans):
    def block(r, s):
        at = (2 * (r // 2) + s // 2) * 4 + (r % 2) * 2 + s % 2
        return slice(at * chans, (at + 1) * chans)

    x = g[block(j, k), 0:128] + g[block(j + 1, k), 128:256]
    y = g[block(j, k + 1), 0:128] + g[block(j + 1, k + 1), 128:256]
    return x + pltpu.roll(y, 64, 1)


def tap_picks():
    sel = np.zeros((4, 4, 32, 192), np.float32)
    for t in range(27):
        i, j, k = t // 9, (t // 3) % 3, t % 3
        for q in range(4):
            r, s = j + q // 2, k + q % 2
            for c in range(4):
                col = i * 64 + (2 * (r // 2) + s // 2) * 16 + (s % 2) * 8 + (r % 2) * 4 + c
                sel[t % 4, q, (t // 4) * 4 + c, col] = 1.0
    return jnp.asarray(sel.reshape(16, 32, 192), bf16)


def deinterleave():
    sel = np.zeros((68, 256), np.float32)
    for x in range(68):
        sel[x, (x % 2) * 128 + x // 2] = 1.0
    return jnp.asarray(sel, bf16)


def source_stage(r):
    s = lax.axis_index("section")
    k = lax.axis_index("slab")
    b = lax.axis_index("batch")
    ends = (r.ext[s, b], r.ext[1 - s, b])
    for h in range(2):
        for p in range(4):
            g = 2 * k - 1 + p
            r.sc[4 * h + p] = jnp.where((g >= 0) & (g < ends[h]), 1.0, 0.0)
        tot = jnp.int32(0)
        for v in range(r.ext.shape[1]):
            tot = tot + (r.ext[s, v] if h == 0 else r.ext[1 - s, v])
        r.sc[8 + h] = tot.astype(f32)
    r.sc[10] = jnp.where(k > 0, 1.0, 0.0)
    r.sc[11] = jnp.where(k < r.slabs - 1, 1.0, 0.0)
    for j in range(12, 16):
        r.sc[j] = jnp.float32(0.0)
    for j, v in enumerate((r.v0, r.v1, r.v2, r.v3, r.v4, r.v5, r.v6, r.v7)):
        v = v[...]
        while v.shape[1] < 256:
            v = jnp.concatenate([v, v], axis=1)
        r.par[j : j + 1, :] = v
    row = lax.broadcasted_iota(jnp.int32, (16, 1), 0) % 4
    col = jnp.zeros((16, 1), f32)
    for c in range(4):
        col = jnp.where(row == c, r.mods[0, c].astype(f32), col)
    r.keep[...] = col
    img, keep, even, sc, own, crop = r.img, r.keep, r.even, r.sc, r.own, r.crop
    oy, ox = r.si[0, 0], r.si[0, 1]
    x = lax.broadcasted_iota(jnp.int32, (68, 256), 0)
    lane = lax.broadcasted_iota(jnp.int32, (68, 256), 1)
    at = 2 * (lane % 128) + lane // 128
    pick = ((x == at + ox) & (lane % 128 < 26)).astype(f32).astype(bf16)
    r = lax.broadcasted_iota(jnp.int32, (208, 272), 0)
    c = lax.broadcasted_iota(jnp.int32, (208, 272), 1)
    rows = (c == r + 4 * oy).astype(f32).astype(bf16)
    lane = lax.broadcasted_iota(jnp.int32, (8, 128), 1)

    def flat(v, side, pitch, tiles):
        out = [[jnp.zeros((8, 128), f32) for _ in range(tiles)] for _ in range(2)]
        for y in range(side):
            tile, off = (pitch * y) // 128, (pitch * y) % 128
            for px in range(2):
                p = v[8 * y : 8 * y + 8, 128 * px : 128 * px + 128]
                p = p if off == 0 else pltpu.roll(p, off, 1)
                if off + side > 128:
                    out[px][tile + 1] += jnp.where(lane < off, p, 0.0)
                    p = jnp.where(lane >= off, p, 0.0)
                out[px][tile] += p
        return jnp.concatenate([jnp.concatenate(o, axis=1) for o in out], axis=0)

    for d in range(2):
        hi, lo = split(img[d].reshape(272, 68))
        k = keep[...] * sc[1 + d]
        own[d] = flat(dot(hi, even[...], NN) + dot(lo, even[...], NN), 34, 40, OWN // 128) * k
        hi = dot(rows, hi, NN).astype(bf16)
        lo = dot(rows, lo, NN).astype(bf16)
        crop[d] = flat(dot(hi, pick, NN) + dot(lo, pick, NN), 26, 32, CROP // 128) * k


def split_third(r):
    def turn(t):
        v = r.w3t[t].T
        r.w3u[t] = v[:128]
        r.w3c[t] = v[128:]

    loop(27, turn)


def gather_output(r):
    r.og[...] = jnp.zeros(r.og.shape, f32)

    def row(t):
        for py in range(2):
            x0 = r.ograw[2 * t + py, pl.ds(0, 22, stride=2), :, :]
            x1 = r.ograw[2 * t + py, pl.ds(1, 22, stride=2), :, :]
            for d in range(2):
                v = jnp.concatenate([x0[:, d, :], x1[:, d, :]], axis=1)
                r.og[d, t, pl.ds(0, 22), py * 128 : py * 128 + 128] = v

    loop(22, row)


def tap_spread():
    sel = np.zeros((4, 192, 112), np.float32)
    for t in range(27):
        i, j, k = t // 9, (t // 3) % 3, t % 3
        for q in range(4):
            r, s = j + q // 2, k + q % 2
            for c in range(4):
                row = i * 64 + (2 * (r // 2) + s // 2) * 16 + (s % 2) * 8 + (r % 2) * 4 + c
                sel[q, row, t * 4 + c] = 1.0
    return jnp.asarray(sel, bf16)


def first_weights(r):
    r.wf4[...] = jnp.zeros(r.wf4.shape, f32)
    for t in range(27):
        w = r.wf[t]
        r.wf4[4 * t : 4 * t + 4, :] = jnp.concatenate([w, w, w, w], axis=1)
    hi, lo = split(r.wf4[...])
    lane = lax.broadcasted_iota(jnp.int32, (192, 128), 1) // 32
    wh = jnp.zeros((192, 128), f32)
    wl = jnp.zeros((192, 128), f32)
    for q in range(4):
        wh += jnp.where(lane == q, dot(r.spread[q], hi, NN), 0.0)
        wl += jnp.where(lane == q, dot(r.spread[q], lo, NN), 0.0)
    r.w1h[...] = wh.astype(bf16)
    r.w1l[...] = wl.astype(bf16)


def first_stage(r):
    for p in range(6):
        own = r.so[p]
        crop = r.sr[p]
        for ab in range(4):
            a, b = ab // 2, ab % 2
            rows = slice(p * 64 + ab * 16, p * 64 + ab * 16 + 16)
            hi, lo = split(own if ab == 0 else pltpu.roll(own, OWN - 40 * a - b, 1))
            r.sh[rows, :] = hi
            r.sl[rows, :] = lo
            hi, lo = split(crop if ab == 0 else pltpu.roll(crop, CROP - 32 * a - b, 1))
            r.ch[rows, :] = hi
            r.cl[rows, :] = lo
    for w, out in ((r.w1h, r.wdh), (r.w1l, r.wdl)):
        out[...] = jnp.zeros(out.shape, bf16)
        out[:192, :128] = w[...]
        out[64:, 128:] = w[...]
    wh, wl = r.wdh[...], r.wdl[...]
    def pair(t):
        rows = pl.ds(pl.multiple_of(t * 128, 128), 256)
        v = dot3(r.sh[rows, :], r.sl[rows, :], wh, wl, TN)
        r.r1[2 * t, :OWN, :] = v[:, :128]
        r.r1[2 * t + 1, :OWN, :] = v[:, 128:]
        v = dot3(r.ch[rows, :], r.cl[rows, :], wh, wl, TN)
        r.r1c[2 * t] = v[:, :128]
        r.r1c[2 * t + 1] = v[:, 128:]

    loop(2, pair)
    for d in range(4):
        r.r1[d, OWN:, :] = jnp.zeros((1440 - OWN, 128), f32)
    s = jnp.zeros((1, 128), f32)
    q = jnp.zeros((1, 128), f32)
    for d in range(2):
        def part(t, c):
            x = r.r1[1 + d, pl.ds(pl.multiple_of(t * 160, 160), 160), :].reshape(4, 40, 128)
            x = jnp.where(cells(x.shape, 33, 33, 4 * t), x, 0.0)
            return c[0] + jnp.sum(x, axis=0), c[1] + jnp.sum(x * x, axis=0)

        ps, pq = lax.fori_loop(0, 9, part, (jnp.zeros((40, 128), f32), jnp.zeros((40, 128), f32)))
        s = s + r.sc[1 + d] * jnp.sum(ps, axis=0, keepdims=True)
        q = q + r.sc[1 + d] * jnp.sum(pq, axis=0, keepdims=True)
    put_sums(r.st1, s, q)


def front_kernel(dims, r):
    net = Net(dims, True, [r.sem0, r.sem1, r.sem2, r.sem3, r.sem4, r.sem5])
    net.enter()
    mv = Moves(r.sem8)
    ready_og = fetch(mv, (r.iograw, r.ograw))
    r.slabs = dims[1]
    source_stage(r)
    split_third(r)
    mv.out((r.w3u, r.ow3u), (r.w3c, r.ow3c))
    net.ready()
    start, finish = source_copies(dims, r.own, r.crop, r.so, r.sr, r.sem6, r.sem7)
    start()
    net.to_left(r.co.at[0], r.cor, 0)
    net.to_right(r.co.at[0], r.col, 0)
    first_weights(r)
    mv.out((r.w1h, r.ow1h), (r.w1l, r.ow1l))
    toeplitz(r.w2, 0, 32, r.t2h, r.t2l)
    toeplitz(r.w3u, 0, 128, r.tuh, r.tul)
    up_blocks(r)
    r.usc[...] = jnp.zeros(r.usc.shape, f32)
    compose(r, 0)
    finish()
    first_stage(r)
    mv.out((r.sh, r.osh), (r.sl, r.osl), (r.r1, r.or1))
    net.share(r.st1, r.g1, 0)
    ready_og()
    gather_output(r)
    mv.out((r.og, r.oog))
    net.to_left(r.og.at[0], r.ogr, 2)
    net.to_right(r.og.at[1], r.ogl, 2)
    net.shared(r.st1, r.g1, 0)

    half = net.s
    f = r.f
    f[...] = jnp.zeros(f.shape, f32)
    scale_c, off_c = affine(r.par, 0, *moments(r.g1, 1 - half, r.sc[9] * 4356.0, 128))

    def crop(p):
        m = r.sc[4 + p]

        def rows(t):
            x = r.r1c[p, pl.ds(pl.multiple_of(t * 128, 128), 128), :].reshape(4, 32, 128)
            f[pl.ds(4 * t, 4), :32, :] = jnp.where(m > 0, silu(x * scale_c + off_c), 0.0)

        loop(7, rows)
        im2col(r.ah, r.al, p, f, 24, 24, 128)

    loop(4, crop)
    conv(r.r2c, r.ah, r.al, r.t2h, r.t2l, 576, NN)
    net.to_left(r.r2c.at[0:576], r.hr, 1)
    net.to_right(r.r2c.at[576:1152], r.hl, 1)
    mv.out((r.r2c, r.or2c))
    scale, off = affine(r.par, 0, *moments(r.g1, half, r.sc[8] * 4356.0, 128))

    def own(p):
        m = r.sc[p]

        def rows(t):
            x = r.r1[p, pl.ds(pl.multiple_of(t * 160, 160), 160), :].reshape(4, 40, 128)
            f[pl.ds(4 * t, 4), :40, :] = jnp.where(m > 0, silu(x * scale + off), 0.0)

        loop(9, rows)
        im2col(r.ah, r.al, p, f, 32, 32, 128)

    loop(4, own)
    mv.out((r.ah, r.oah), (r.al, r.oal))
    conv(r.r2, r.ah, r.al, r.t2h, r.t2l, 1024, NN)
    mv.out((r.r2, r.or2))
    s = jnp.zeros((1, 256), f32)
    q = jnp.zeros((1, 256), f32)
    for d in range(2):
        def part(t, c):
            x = r.r2[pl.ds(pl.multiple_of(d * 1024 + t * 128, 128), 128), :].reshape(16, 8, 256)
            return c[0] + jnp.sum(x, axis=0), c[1] + jnp.sum(x * x, axis=0)

        ps, pq = lax.fori_loop(0, 8, part, (jnp.zeros((8, 256), f32), jnp.zeros((8, 256), f32)))
        s = s + r.sc[1 + d] * jnp.sum(ps, axis=0, keepdims=True)
        q = q + r.sc[1 + d] * jnp.sum(pq, axis=0, keepdims=True)
    put_sums(r.st2, s, q)
    net.share(r.st2, r.g2, 1)
    compose(r, 1)
    compose(r, 2)
    composed(r)
    mv.out((r.uh, r.ouh), (r.ul, r.oul), (r.ubh, r.oubh), (r.ubl, r.oubl))
    net.shared(r.st2, r.g2, 1)
    net.sides()
    mv.finish()


def conv(out, ah, al, th, tl, rows, dims):
    out[...] = jnp.zeros(out.shape, f32)

    def tap(i):
        at = pl.ds(pl.multiple_of(i * rows, 16), 2 * rows)
        out[...] += dot3(ah[at, :], al[at, :], th[i], tl[i], dims)

    loop(3, tap)


def conv_plane(out, d, ah, al, th, tl, rows, dims):
    to = pl.ds(pl.multiple_of(d * rows, 16), rows)
    out[to, :] = jnp.zeros((rows, out.shape[1]), f32)

    def tap(i):
        at = pl.ds(pl.multiple_of((d + i) * rows, 16), rows)
        out[to, :] += dot3(ah[at, :], al[at, :], th[i], tl[i], dims)

    loop(3, tap)


def front(dims, img, ext, mods, si, vectors, wf, w2, w3t, up, co, og):
    n = dims[0] * dims[1] * dims[2]
    V = pltpu.VMEM
    forms = [("u", (4, 512, 256)), ("ub", (4, 128, 1024)), ("s", (384, OWN)), ("a", (4096, 512)), ("w1", (192, 128))]
    outs = [("g1", (n, 1, 512), f32, VM), ("g2", (n, 1, 512), f32, VM),
            ("or1", (4, 1440, 128), f32, HB), ("or2", (2048, 256), f32, HB), ("or2c", (1152, 256), f32, HB),
            ("col", co.shape[1:], f32, HB), ("cor", co.shape[1:], f32, HB),
            ("par", (8, 256), f32, VM), ("keep", (16, 1), f32, VM), ("sc", (16,), f32, SM),
            ("ow3u", (27, 128, 64), f32, HB), ("ow3c", (27, 64, 64), f32, HB),
            ("oog", (2, 22, 24, 256), f32, HB), ("ogl", (22, 24, 256), f32, HB), ("ogr", (22, 24, 256), f32, HB),
            ("hl", (576, 256), f32, HB), ("hr", (576, 256), f32, HB)]
    scratch = []
    for name, shape in forms:
        outs += both_out("o" + name, shape)
        scratch += both(name, shape)
    scratch += both("t2", (3, 512, 256)) + both("tu", (3, 2048, 256)) + both("up", (256, 512)) + both("c", (384, CROP)) + both("wd", (256, 256))
    scratch += [("st1", V((1, 512), f32)), ("st2", V((1, 512), f32)), ("so", V((6, 16, OWN), f32)),
                ("sr", V((6, 16, CROP), f32)), ("wf4", V((112, 128), f32)), ("usc", V((4, 512, 256), f32)),
                ("r1", V((4, 1440, 128), f32)), ("r1c", V((4, CROP, 128), f32)), ("r2", V((2048, 256), f32)),
                ("r2c", V((1152, 256), f32)), ("f", V((36, 48, 128), f32)), ("own", V((2, 16, OWN), f32)),
                ("crop", V((2, 16, CROP), f32)), ("w3u", V((27, 128, 64), f32)), ("w3c", V((27, 64, 64), f32)),
                ("og", V((2, 22, 24, 256), f32)), ("ograw", V((44, 44, 2, 64), f32))]
    return launch(
        functools.partial(front_kernel, dims), "front", 1,
        [("img", img, VM), ("even", deinterleave(), VM), ("ext", ext, SM), ("mods", mods, SM), ("si", si, SM),
         ("wf", wf, VM), ("spread", tap_spread(), VM), ("w2", w2, VM), ("w3t", w3t, VM), ("up", up, VM),
         ("co", co, HB), ("iograw", og, HB)]
        + [(f"v{j}", v.reshape(1, -1), VM) for j, v in enumerate(vectors)],
        outs, scratch + sems(n, n, n, n, 6, 6, 5, 5, 32),
    )


def decode_kernel(dims, r):
    net = Net(
        dims, False, [r.sem0, r.sem1, r.sem2, r.sem3, r.sem4, r.sem5, r.sem6, r.sem7, r.sem8, r.sem9]
    )
    net.enter()
    mv = Moves(r.sem10)
    par = r.par
    ready_c = fetch(mv, (r.ihl, r.hl), (r.ir2c, r.r2c), (r.ihr, r.hr))
    ready_w3 = fetch(mv, (r.iw3, r.w3))
    ready_co = fetch(mv, (r.icol, r.col), (r.ico.at[0], r.co), (r.icor, r.cor))
    weights = fetch(mv, (r.iuh, r.uh), (r.iul, r.ul))
    ready_w4 = fetch(mv, (r.iw4, r.w4))
    ready_r2 = fetch(mv, (r.ir2, r.r2))
    ready_og = fetch(mv, (r.iog, r.og), (r.iogl, r.ogl), (r.iogr, r.ogr))
    f, f2, sc = r.f, r.f2, r.sc
    scale_c, off_c = affine(r.par, 1, *moments(r.g2, 1 - net.s, sc[9] * 4096.0, 256))
    f[...] = jnp.zeros(f.shape, f32)

    def put(p, get):
        m = sc[4 + p]

        def rows(t):
            x = silu(get(t * 96) * scale_c + off_c).reshape(4, 24, 256)
            f[pl.ds(4 * t, 4), :24, :] = jnp.where(m > 0, x, 0.0)

        loop(6, rows)
        im2col(r.bh, r.bl, p, f, 24, 24, 256)

    def of(ref, base):
        return lambda at: ref[pl.ds(pl.multiple_of(base + at, 32), 96), :]

    ready_c()
    put(0, of(r.hl, 0))
    loop(2, lambda p: put(p + 1, of(r.r2c, p * 576)))
    put(3, of(r.hr, 0))
    kept = fetch(mv, (r.bh, r.oah), (r.bl, r.oal))
    f2[...] = jnp.zeros(f2.shape, f32)
    ready_w3()
    toeplitz(r.w3, 0, 64, r.th, r.tl)
    ready_co()
    for p, (src, m) in enumerate(((r.col, sc[4]), (r.co, sc[5]), (r.cor, sc[7]))):
        f2[:24, :24, :] = jnp.where(m > 0, src[...], 0.0)
        im2col(r.cuh, r.cul, p, f2, 24, 24, 128)
    mv.out((r.cuh, r.ocuh), (r.cul, r.ocul))
    weights()
    sides = ((r.r3.at[0:576], r.r3r), (r.r3.at[576:1152], r.r3l), 0)

    def plane(d):
        conv_plane(r.r3, d, r.bh, r.bl, r.th, r.tl, 576, NN)

        def up(t):
            at = pl.ds(pl.multiple_of((d + t) * 576, 16), 576)
            out = pl.ds(pl.multiple_of(d * 576, 16), 576)
            r.r3[out, :] += dot3(r.cuh[at, :], r.cul[at, :], r.uh[2 * d + t], r.ul[2 * d + t], NN)

        loop(2, up)

    plane(net.k % 2)
    net.ready()
    net.to_sides(*sides, True)
    plane(1 - net.k % 2)
    s0, q0 = field_sums(r.r3, 0, 576, 23, 23, sc[5])
    s1, q1 = field_sums(r.r3, 1, 576, 23, 23, sc[6])
    put_sums(r.st3, s0 + s1, q0 + q1)
    net.share(r.st3, r.g3, 0)
    net.to_sides(*sides, False)
    mv.out((r.r3, r.or3))
    ready_w4()
    toeplitz(r.w4, 0, 64, r.th, r.tl, r.d4h, r.d4l)
    net.shared(r.st3, r.g3, 0)

    avg3, inv3 = moments(r.g3, None, sc[9] * 2116.0, 256)
    scale3, off3 = affine(par, 2, avg3, inv3)

    def put_act(p, get):
        m = sc[4 + p]

        def rows(t):
            x = silu(get(t * 96) * scale3 + off3).reshape(4, 24, 256)
            f[pl.ds(4 * t, 4), :24, :] = jnp.where(m > 0, x, 0.0)

        loop(6, rows)
        im2col(r.ah, r.al, p, f, 22, 24, 256)

    def part_of(ref, base, step):
        return lambda at: ref[pl.ds(pl.multiple_of(base + at, 16), step), :]

    loop(2, lambda p: put_act(p + 1, part_of(r.r3, p * 576, 96)))
    net.sides()
    net.halos = []
    mv.out((r.r3l, r.or3l), (r.r3r, r.or3r))
    put_act(0, part_of(r.r3l, 0, 96))
    put_act(3, part_of(r.r3r, 0, 96))
    conv(r.r4, r.ah, r.al, r.th, r.tl, 528, NN)
    s0, q0 = field_sums(r.r4, 0, 528, 22, 22, sc[5])
    s1, q1 = field_sums(r.r4, 1, 528, 22, 22, sc[6])
    put_sums(r.st4, s0 + s1, q0 + q1)
    net.share(r.st4, r.g4, 1)
    net.to_left(r.r4.at[0:528], r.r4r, 1)
    net.to_right(r.r4.at[528:1056], r.r4l, 1)
    scale, off = affine(r.par, 1, *moments(r.g2, net.s, sc[8] * 4096.0, 256))

    def pool(t):
        v = jnp.zeros((128, 256), f32)
        for d in range(2):
            x = r.r2[pl.ds(pl.multiple_of(d * 1024 + t * 128, 128), 128), :]
            v = v + sc[1 + d] * silu(x * scale + off)
        v = v[:, :128] + v[:, 128:]
        v = (v + pltpu.roll(v, 64, 1)) * 0.125
        r.pooled[pl.ds(pl.multiple_of(t * 128, 128), 128), :] = v[:, :64]

    ready_r2()
    loop(8, pool)
    ready_og()
    net.shared(r.st4, r.g4, 1)

    count = sc[9] * 1936.0
    avg, inv = moments(r.g4, None, count, 256)
    scale4, off4 = affine(par, 3, avg, inv)
    s = jnp.zeros((1, 256), f32)
    q = jnp.zeros((1, 256), f32)
    for d in range(2):
        m = sc[5 + d]

        def part(t, c):
            x = r.r4[pl.ds(pl.multiple_of(d * 528 + t * 48, 16), 48), :]
            b = x * scale4 + off4
            sg = 1.0 / (1.0 + jnp.exp(-b))
            r.dec[d, pl.ds(2 * t, 2)] = (m * (b * sg)).reshape(2, 24, 256)
            bg = r.og[d, pl.ds(2 * t, 2)].reshape(48, 256) * sg * (1.0 + b * (1.0 - sg))
            normed = (x - avg) * inv
            return (
                c[0] + jnp.sum(bg.reshape(6, 8, 256), axis=0),
                c[1] + jnp.sum((bg * normed).reshape(6, 8, 256), axis=0),
            )

        ps, pq = lax.fori_loop(0, 11, part, (jnp.zeros((8, 256), f32), jnp.zeros((8, 256), f32)))
        s = s + m * jnp.sum(ps, axis=0, keepdims=True)
        q = q + m * jnp.sum(pq, axis=0, keepdims=True)
    put_sums(r.st5, s, q)
    net.share(r.st5, r.g5, 2)

    def spread(t):
        for py in range(2):
            for px in range(2):
                at = py * 128 + px * 64
                v = jnp.stack([r.dec[0, t, :22, at : at + 64], r.dec[1, t, :22, at : at + 64]], axis=1)
                r.decoded[2 * t + py, pl.ds(px, 22, stride=2), :, :] = v

    loop(22, spread)
    mv.out((r.decoded, r.odecoded))
    net.shared(r.st5, r.g5, 2)
    net.sides()
    net.halos = []
    kept()

    tg, tc = totals(r.g5, None, 256)
    f[...] = jnp.zeros(f.shape, f32)

    def put_back(p, get_r, get_a, keep):
        m = sc[4 + p]

        def rows(t):
            a = get_a(2 * t).reshape(48, 256)
            e = response_back(par, 3, avg, inv, tg, tc, count, get_r(t * 48), a).reshape(2, 24, 256)
            e = jnp.where(cells(e.shape, 22, 22, 0) & (m > 0), e, 0.0)
            f[pl.ds(1 + 2 * t, 2), 8:32, :] = e
            if keep is not None:
                hi, lo = split(e.reshape(48, 256))
                at = pl.ds(pl.multiple_of(keep * 528 + t * 48, 16), 48)
                r.eh[at, :] = hi
                r.el[at, :] = lo

        loop(11, rows)
        im2col(r.bh, r.bl, p, f, 24, 24, 256, x0=7)

    put_back(0, part_of(r.r4l, 0, 48), lambda y: r.ogl[pl.ds(y, 2)], None)
    loop(2, lambda p: put_back(p + 1, part_of(r.r4, p * 528, 48), lambda y: r.og[p, pl.ds(y, 2)], p))
    put_back(3, part_of(r.r4r, 0, 48), lambda y: r.ogr[pl.ds(y, 2)], None)
    conv(r.a3, r.bh, r.bl, r.d4h, r.d4l, 576, NT)
    mv.out((r.a3, r.oa3))
    s = jnp.zeros((1, 256), f32)
    q = jnp.zeros((1, 256), f32)
    for d in range(2):
        def part(t, c):
            at = pl.ds(pl.multiple_of(d * 576 + t * 48, 16), 48)
            normed, bg = back_parts(par, 2, avg3, inv3, r.r3[at, :], r.a3[at, :])
            bg = bg.reshape(2, 24, 256)
            bg = jnp.where(cells(bg.shape, 23, 23, 2 * t), bg, 0.0)
            return c[0] + jnp.sum(bg, axis=0), c[1] + jnp.sum(bg * normed.reshape(2, 24, 256), axis=0)

        ps, pq = lax.fori_loop(0, 12, part, (jnp.zeros((24, 256), f32), jnp.zeros((24, 256), f32)))
        s = s + sc[5 + d] * jnp.sum(ps, axis=0, keepdims=True)
        q = q + sc[5 + d] * jnp.sum(pq, axis=0, keepdims=True)
    put_sums(r.st6, s, q)
    net.share(r.st6, r.g6, 3)
    net.to_left(r.a3.at[0:576], r.a3r, 2)
    net.to_right(r.a3.at[576:1152], r.a3l, 2)

    def tap(i):
        at = pl.ds(pl.multiple_of(i * 528, 16), 1056)
        r.g[...] = dot3(r.ah[at, :], r.al[at, :], r.eh[...], r.el[...], TN)
        put_taps(r.dw4, r.g, i, 64, 64, 0, 0)

    loop(3, tap)
    net.shared(r.st6, r.g6, 3)
    net.sides()
    mv.finish()


def put_taps(out, g, i, chans, total, row0, base):
    def rows(p):
        return pl.ds(pl.multiple_of(base + (i * 5 + p // 2) * total + row0, 8), chans)

    for p in range(9):
        v = folded(g, p // 3, p % 3, chans)
        v = v if p % 2 == 0 else pltpu.roll(v, 64, 1)
        at = 64 * (p % 2)
        out[rows(p), at : at + 64] = v[:, at : at + 64]
    out[rows(8), 64:] = jnp.zeros((chans, 64), f32)


def decode(dims, k, co, w4):
    n = dims[1] * dims[2]
    V = pltpu.VMEM
    box = (22, 24, 256)
    return launch(
        functools.partial(decode_kernel, dims), "decode", 2,
        [("ir2", k.or2, HB), ("ir2c", k.or2c, HB), ("ihl", k.hl, HB), ("ihr", k.hr, HB), ("ico", co, HB),
         ("icol", k.col, HB), ("icor", k.cor, HB), ("g2", k.g2, VM), ("par", k.par, VM), ("iuh", k.ouh, HB),
         ("iul", k.oul, HB), ("iw3", k.ow3c, HB), ("iw4", w4, HB), ("iog", k.oog, HB), ("iogl", k.ogl, HB),
         ("iogr", k.ogr, HB), ("sc", k.sc, SM)],
        [("pooled", (1024, 64), f32, VM), ("g3", (n, 1, 512), f32, VM), ("or3", (1152, 256), f32, HB),
         ("or3l", (576, 256), f32, HB), ("or3r", (576, 256), f32, HB), ("odecoded", (44, 44, 2, 64), f32, HB),
         ("oa3", (1152, 256), f32, HB), ("a3l", (576, 256), f32, HB), ("a3r", (576, 256), f32, HB),
         ("g6", (n, 1, 512), f32, VM), ("st5", (1, 512), f32, VM), ("st6", (1, 512), f32, VM),
         ("dw4", (960, 128), f32, VM)]
        + both_out("oa", (2304, 1024)) + both_out("ocu", (1728, 512)),
        both("t", (3, 1024, 256)) + both("d4", (3, 256, 1024)) + both("a", (2112, 1024)) + both("b", (2304, 1024))
        + both("cu", (1728, 512)) + both("u", (4, 512, 256)) + both("e", (1056, 256))
        + [("f", V((26, 40, 256), f32)), ("f2", V((26, 32, 128), f32)), ("r2", V((2048, 256), f32)),
           ("r3", V((1152, 256), f32)), ("r3l", V((576, 256), f32)), ("r3r", V((576, 256), f32)),
           ("r4", V((1056, 256), f32)), ("r4l", V((528, 256), f32)),
           ("r4r", V((528, 256), f32)), ("og", V((2,) + box, f32)), ("ogl", V(box, f32)), ("ogr", V(box, f32)),
           ("dec", V((2,) + box, f32)), ("decoded", V((44, 44, 2, 64), f32)), ("a3", V((1152, 256), f32)),
           ("g", V((1024, 256), f32)), ("g4", V((n, 1, 512), f32)), ("g5", V((n, 1, 512), f32)),
           ("st3", V((1, 512), f32)), ("st4", V((1, 512), f32)), ("hl", V((576, 256), f32)),
           ("hr", V((576, 256), f32)), ("r2c", V((1152, 256), f32)), ("co", V((24, 24, 128), f32)),
           ("col", V((24, 24, 128), f32)), ("cor", V((24, 24, 128), f32)), ("w3", V((27, 64, 64), f32)),
           ("w4", V((27, 64, 64), f32))]
        + sems(n, n, n, n, n, n, n, n, 6, 6, 32),
    )


def third_back_kernel(dims, r):
    net = Net(dims, False, [])
    barrier = pltpu.get_barrier_semaphore()
    partner = (1 - net.s, net.k, net.b)
    mv = Moves(r.sem0)
    pl.semaphore_signal(barrier, inc=1, device_id=partner, device_id_type=MESH)
    ready_l = fetch(mv, (r.ir3l, r.r3l), (r.ia3l, r.a3l))
    ready_o = fetch(mv, (r.ir3, r.r3), (r.ia3, r.a3))
    ready_r = fetch(mv, (r.ir3r, r.r3r), (r.ia3r, r.a3r))
    ready_a = fetch(mv, (r.iah, r.ah), (r.ial, r.al))
    ready_u = fetch(mv, (r.icuh, r.cuh), (r.icul, r.cul))
    ready_w = fetch(mv, (r.iw3u, r.w3u), (r.idw4, r.dw4))
    toeplitz(r.w3c, 0, 64, None, None, r.d3h, r.d3l)
    sc, f, par = r.sc, r.f, r.par
    count = sc[9] * 2116.0
    avg, inv = moments(r.g3, None, count, 256)
    tg, tc = totals(r.g6, None, 256)
    f[...] = jnp.zeros(f.shape, f32)

    def of(ref, base):
        return lambda at: ref[pl.ds(pl.multiple_of(base + at, 16), 48), :]

    def put(p, get_r, get_a, keep):
        m = sc[4 + p]

        def rows(t):
            e = response_back(par, 2, avg, inv, tg, tc, count, get_r(t * 48), get_a(t * 48)).reshape(2, 24, 256)
            e = jnp.where(cells(e.shape, 23, 23, 2 * t) & (m > 0), e, 0.0)
            f[pl.ds(1 + 2 * t, 2), 8:32, :] = e
            if keep is not None:
                hi, lo = split(e.reshape(48, 256))
                at = pl.ds(pl.multiple_of(keep * 576 + t * 48, 16), 48)
                r.eh[at, :] = hi
                r.el[at, :] = lo

        loop(12, rows)
        im2col(r.bh, r.bl, p, f, 24, 24, 256, x0=7)

    ready_l()
    put(0, of(r.r3l, 0), of(r.a3l, 0), None)
    ready_o()
    loop(2, lambda p: put(p + 1, of(r.r3, p * 576), of(r.a3, p * 576), p))
    ready_r()
    put(3, of(r.r3r, 0), of(r.a3r, 0), None)
    mv.out((r.bh, r.obh), (r.bl, r.obl))

    across = []
    for d in range(2):
        conv_plane(r.g.at[:1152], d, r.bh, r.bl, r.d3h, r.d3l, 576, NT)

        def row(t):
            at = pl.ds(pl.multiple_of(t * 24, 24), 24)
            r.skip[2 * t] = r.g[at, :128]
            r.skip[2 * t + 1] = r.g[at, 128:]

        loop(24, lambda t, d=d: row(d * 24 + t))
        if d == 0:
            pl.semaphore_wait(barrier, 1)
        copy = pltpu.make_async_remote_copy(
            src_ref=r.skip.at[d * 48 : d * 48 + 48], dst_ref=r.oskip.at[d * 48 : d * 48 + 48],
            send_sem=r.sem1.at[2 * d], recv_sem=r.sem1.at[2 * d + 1],
            device_id=partner, device_id_type=MESH,
        )
        copy.start()
        across.append(copy)

    ready_a()
    bucket = r.bucket

    def tap(i):
        at = pl.ds(pl.multiple_of(i * 576, 16), 1152)
        r.g[:1024, :] = dot3(r.ah[at, :], r.al[at, :], r.eh[...], r.el[...], TN)
        put_taps(bucket, r.g, i, 64, 192, 128, 0)

    loop(3, tap)
    ready_u()

    def coarse(j):
        at = pl.ds(pl.multiple_of((j // 2 + j % 2) * 576, 16), 576)
        e = pl.ds(pl.multiple_of((j // 2) * 576, 16), 576)
        r.gu[j] = dot3(r.cuh[at, :], r.cul[at, :], r.eh[e, :], r.el[e, :], TN)

    loop(4, coarse)
    ready_w()
    up_blocks(r)
    r.gd[...] = jnp.zeros(r.gd.shape, f32)
    for i in range(3):
        loop(1, lambda _, i=i: toeplitz_tap(r.w3u, 0, 128, i, 0, r.tuh, r.tul))

        def block(ab, i=i):
            out = pl.ds(pl.multiple_of(ab * 128, 128), 128)
            p = jnp.concatenate([r.gu[slot_of(i, 0), out, :], r.gu[slot_of(i, 1), out, :]], axis=0)
            ph, plo = split(p)
            rows = pl.ds(pl.multiple_of(ab * 512, 512), 512)
            r.gd[...] += dot3(ph, plo, r.tuh[0, rows, :], r.tul[0, rows, :], NT)
            r.g[rows, :] = dot3(r.uph[...], r.upl[...], ph, plo, TN)

        loop(4, block)
        loop(1, lambda _, i=i: put_taps(bucket, r.g, i, 128, 192, 0, 0))
    bucket[2880:3840, :] = r.dw4[...]
    for ip in range(2):
        for q in range(4):
            at = 3840 + (ip * 4 + q) * 128
            bucket[at : at + 128, :] = r.gd[ip * 128 : ip * 128 + 128, q * 128 : q * 128 + 128]
    if bucket.shape[0] > BUCKET:
        bucket[BUCKET:, :] = jnp.zeros((bucket.shape[0] - BUCKET, 128), f32)
    mv.out((bucket, r.obucket))
    for copy in across:
        copy.wait()
    mv.finish()


def world_rows(dims, rows):
    n = dims[0] * dims[1] * dims[2]
    return -(-rows // (8 * n)) * 8 * n


def bucket_parts(dims):
    first = world_rows(dims, FIRST_HALF)
    return first, world_rows(dims, max(BUCKET - first, 8))


def reduction_buffers(dims, rows, tag):
    S, K, B = dims
    Q = S * K // 2
    V = pltpu.VMEM
    per = rows // (S * K * B)
    return [("mine1" + tag, V((rows // 2, 128), f32)), ("slot1" + tag, V((rows // 2, 128), f32)),
            ("slot2" + tag, V((Q - 1, B * per, 128), f32)), ("mine2" + tag, V((B * per, 128), f32)),
            ("slot3" + tag, V((B - 1, per, 128), f32))]


def reduction_sems(dims):
    Q, B = dims[0] * dims[1] // 2, dims[2]
    return [2, 2 * (Q - 1), 2 * (B - 1), 2 * (B - 1), 2 * (Q - 1), 2]


def third_back(dims, fb, r3, r3l, r3r, g3, k, t, dw4, w3u, w3c, up, par, sc):
    n = dims[0] * dims[1] * dims[2]
    V = pltpu.VMEM
    rows = sum(bucket_parts(dims))
    return launch(
        functools.partial(third_back_kernel, dims), "third_back", 4,
        [("ia3", fb.oa3, HB), ("ia3l", fb.a3l, HB), ("ia3r", fb.a3r, HB), ("ir3", r3, HB), ("ir3l", r3l, HB),
         ("ir3r", r3r, HB), ("g3", g3, VM), ("g6", fb.g6, VM), ("idw4", dw4, HB), ("par", par, VM),
         ("iw3u", w3u, HB), ("w3c", w3c, VM), ("up", up, VM), ("iah", t.oah, HB), ("ial", t.oal, HB),
         ("icuh", t.ocuh, HB), ("icul", t.ocul, HB), ("sc", sc, SM)],
        [("oskip", (96, 24, 128), f32, HB), ("obh", (2304, 1024), bf16, HB), ("obl", (2304, 1024), bf16, HB),
         ("obucket", (rows, 128), f32, HB)],
        both("tu", (1, 2048, 256)) + both("d3", (3, 256, 1024)) + both("a", (2304, 1024)) + both("cu", (1728, 512))
        + both("up", (256, 512)) + both("b", (2304, 1024)) + both("e", (1152, 256))
        + [("f", V((26, 40, 256), f32)), ("skip", V((96, 24, 128), f32)),
           ("g", V((2048, 256), f32)), ("gu", V((4, 512, 256), f32)), ("gd", V((256, 512), f32)),
           ("bucket", V((rows, 128), f32)), ("a3", V((1152, 256), f32)), ("a3l", V((576, 256), f32)),
           ("a3r", V((576, 256), f32)), ("r3", V((1152, 256), f32)), ("r3l", V((576, 256), f32)),
           ("r3r", V((576, 256), f32)), ("w3u", V((27, 128, 64), f32)), ("dw4", V((960, 128), f32))]
        + sems(32, 4),
    )


class Reduction:
    def __init__(self, dims, net, base, rows, r, tag, sems):
        S, K, B = dims
        self.net, self.base, self.steps = net, base, iter(sems)
        self.per = rows // (S * K * B)
        self.bucket, self.res = r.bucket, r.res
        self.mine1, self.slot1, self.slot2, self.mine2, self.slot3 = (
            getattr(r, name + tag) for name in ("mine1", "slot1", "slot2", "mine2", "slot3")
        )
        self.Q, self.B, self.half = S * K // 2, B, S * K * B // 2
        self.core = net.k % 2
        self.q = net.s * (K // 2) + net.k // 2
        self.rows = K // 2
        self.pair_of = (net.s, net.k + 1 - 2 * self.core, net.b)
        self.place = self.core * self.half + self.q * self.B + net.b

    def ds(self, first, count, base=0):
        return pl.ds(pl.multiple_of(base + first * self.per, 8), count * self.per)

    def whole(self, first, count):
        return self.ds(first, count, self.base)

    def at_square(self, q):
        return (q // self.rows, 2 * (q % self.rows) + self.core, self.net.b)

    def copies(self, items):
        sem = next(self.steps)
        self.open = [
            pltpu.make_async_remote_copy(
                src_ref=src, dst_ref=dst, send_sem=sem.at[2 * j], recv_sem=sem.at[2 * j + 1],
                device_id=dev, device_id_type=MESH,
            )
            for j, (src, dst, dev) in enumerate(items)
        ]
        for c in self.open:
            c.start()

    def wait(self):
        for c in self.open:
            c.wait()

    def pair(self, mv):
        self.own = mv.start(self.bucket.at[self.whole(self.core * self.half, self.half)], self.mine1)
        src = self.bucket.at[self.whole((1 - self.core) * self.half, self.half)]
        self.copies([(src, self.slot1, self.pair_of)])

    def square(self):
        self.wait()
        self.own.wait()
        size = self.half * self.per // 16

        def add(t):
            at = pl.ds(pl.multiple_of(t * size, 8), size)
            self.mine1[at, :] += self.slot1[at, :]

        loop(16, add)
        items = []
        for t in range(1, self.Q):
            q = (self.q + t) % self.Q
            items.append((self.mine1.at[self.ds(q * self.B, self.B)], self.slot2.at[t - 1], self.at_square(q)))
        self.copies(items)

    def line(self):
        self.wait()
        v = self.mine1[self.ds(self.q * self.B, self.B), :]
        for t in range(self.Q - 1):
            v = v + self.slot2[t]
        self.mine2[...] = v
        items = []
        for t in range(1, self.B):
            b = (self.net.b + t) % self.B
            items.append((self.mine2.at[self.ds(b, 1)], self.slot3.at[t - 1], (self.net.s, self.net.k, b)))
        self.copies(items)

    def line_back(self):
        self.wait()
        v = self.mine2[self.ds(self.net.b, 1), :]
        for t in range(self.B - 1):
            v = v + self.slot3[t]
        self.res[self.whole(self.place, 1), :] = v
        own = self.res.at[self.whole(self.place, 1)]
        self.copies([(own, own, (self.net.s, self.net.k, (self.net.b + t) % self.B)) for t in range(1, self.B)])

    def square_back(self):
        self.wait()
        own = self.res.at[self.whole(self.core * self.half + self.q * self.B, self.B)]
        self.copies([(own, own, self.at_square((self.q + t) % self.Q)) for t in range(1, self.Q)])

    def pair_back(self):
        self.wait()
        own = self.res.at[self.whole(self.core * self.half, self.half)]
        self.copies([(own, own, self.pair_of)])


def skip_stage(r, avg, inv, d):
    sc, par = r.sc, r.par
    oy, ox = r.si[0, 0], r.si[0, 1]
    qx = ox // 2
    rx = ox - 2 * qx
    odd = rx > 0
    lane = lax.broadcasted_iota(jnp.int32, (32, 128), 1)
    pad = jnp.zeros((8, 128), f32)

    def placed(row):
        at = row - oy
        v = r.skip[d * 48 + jnp.clip(at, 0, 47)]
        v = jnp.where((at >= 0) & (at < 48), v, 0.0)
        v = jnp.concatenate([v, pad], axis=0)
        v = jnp.where(odd, pltpu.roll(v, 64, 1), v)
        v = pltpu.roll(v, qx, 0)
        return jnp.where((lane < 64) & odd, pltpu.roll(v, 1, 0), v)

    def part(t, c):
        pv = r.pg[t] * 0.125
        pv = jnp.concatenate([pv, pv], axis=1)
        a = jnp.concatenate([placed(2 * t) + pv, placed(2 * t + 1) + pv], axis=1)
        rows = pl.ds(pl.multiple_of(d * 1024 + t * 32, 32), 32)
        normed, bg = back_parts(par, 1, avg, inv, r.r2[rows, :], a)
        bg = sc[1 + d] * bg
        r.bg2[rows, :] = bg
        bg = bg.reshape(4, 8, 256)
        return c[0] + jnp.sum(bg, axis=0), c[1] + jnp.sum(bg * normed.reshape(4, 8, 256), axis=0)

    return lax.fori_loop(0, 32, part, (jnp.zeros((8, 256), f32), jnp.zeros((8, 256), f32)))


def store_slots(slots, x, row0):
    per = slots.shape[1]
    for at in range(0, x.shape[0], per):
        slots[(row0 + at) // per] = x[at : at + per]


def four_rows(st):
    v = st[...]
    return [v[:, 128 * c : 128 * c + 128] for c in range(4)]


def tail_kernel(dims, r):
    net = Net(dims, False, [r.sem0, r.sem1, r.sem2, r.sem3, r.sem4, r.sem5])
    world = Net(dims, True, [r.sem6, r.sem7, r.sem8, r.sem9, r.sem16, r.sem17, r.sem18, r.sem19])
    world.enter()
    mv = Moves(r.sem10)
    ready_b = fetch(
        mv, (r.iubh, r.ubh), (r.iubl, r.ubl),
        (r.iebh.at[0:1152], r.bh.at[0:1152]), (r.iebl.at[0:1152], r.bl.at[0:1152]),
    )
    ready_a = fetch(mv, (r.iah, r.ah), (r.ial, r.al))
    ready_s = fetch(mv, (r.ish, r.sh), (r.isl, r.sl), (r.ir1.at[1:3], r.r1))
    sc, par, f = r.sc, r.par, r.f
    count = sc[8] * 4096.0
    avg, inv = moments(r.g2, net.s, count, 256)
    toeplitz(r.w2, 0, 32, None, None, r.d2h, r.d2l)
    f[...] = jnp.zeros(f.shape, f32)
    s0, q0 = skip_stage(r, avg, inv, 0)
    world.ready()
    rows_a, rows_b = bucket_parts(dims)
    steps_a = [r.sem11, r.sem12, r.sem13, r.sem14, r.sem15, r.sem20]
    steps_b = [r.sem21, r.sem22, r.sem23, r.sem24, r.sem25, r.sem26]
    big_a = Reduction(dims, net, 0, rows_a, r, "a", steps_a)
    big_b = Reduction(dims, net, rows_a, rows_b, r, "b", steps_b)
    big_a.pair(mv)
    big_b.pair(mv)
    s1, q1 = skip_stage(r, avg, inv, 1)
    put_sums(r.st7, jnp.sum(s0 + s1, axis=0, keepdims=True), jnp.sum(q0 + q1, axis=0, keepdims=True))
    net.share(r.st7, r.g7, 0)
    big_a.square()
    r.cg[...] = jnp.zeros(r.cg.shape, f32)

    def coarse(p, plane):
        at = pl.ds(pl.multiple_of(plane * 576, 16), 576)
        r.cg[...] += sc[5] * dot3(r.bh[at, :], r.bl[at, :], r.ubh[p], r.ubl[p], NT)

    ready_b()
    loop(2, lambda p: coarse(p, p))
    net.shared(r.st7, r.g7, 0)
    big_b.square()

    tg, tc = totals(r.g7, None, 256)
    k = par[2:3, :] * inv

    def put(p):
        m = sc[1 + p]

        def rows(t):
            at = pl.ds(pl.multiple_of(p * 1024 + t * 64, 64), 64)
            normed = (r.r2[at, :] - avg) * inv
            e = k * (r.bg2[at, :] - m * ((tg + normed * tc) / count))
            hi, lo = split(e)
            r.e2h[at, :] = hi
            r.e2l[at, :] = lo
            f[pl.ds(1 + 2 * t, 2), 8:40, :] = e.reshape(2, 32, 256)

        loop(16, rows)
        im2col(r.bh, r.bl, 0, f, 34, 40, 256, x0=7)
        r.v[p] = dot3(r.bh[...], r.bl[...], r.d2h[...].reshape(384, 1024), r.d2l[...].reshape(384, 1024), NT)

    sides = ((r.side.at[0], r.fr), (r.side.at[1], r.fl), 0)

    def lay(p):
        @pl.when(p == 0)
        def _():
            r.side[0, :1360] = r.v[0, :, 256:]

        @pl.when(p == 1)
        def _():
            r.side[1, :1360] = r.v[1, :, :128]

    for d in range(2):
        r.side[d, 1360:] = jnp.zeros((48, 128), f32)
    put(net.k % 2)
    lay(net.k % 2)
    net.to_sides(*sides, True)
    big_a.line()
    put(1 - net.k % 2)
    lay(1 - net.k % 2)
    net.to_sides(*sides, False)
    ready_b = fetch(
        mv, (r.iebh.at[1152:2304], r.bh.at[0:1152]), (r.iebl.at[1152:2304], r.bl.at[0:1152])
    )
    r.a1[1, :1360] = r.v[0, :, :128] + r.v[1, :, 128:256]
    r.a1[0, :1360] = r.v[0, :, 128:256] + r.v[1, :, 256:]
    for d in range(2):
        r.a1[d, 1360:] = jnp.zeros((48, 128), f32)
    big_a.line_back()
    big_b.line()

    ready_a()

    def tap(i):
        at = pl.ds(pl.multiple_of(i * 1024, 1024), 2048)
        r.g[...] = dot3(r.ah[at, :], r.al[at, :], r.e2h[...], r.e2l[...], TN)
        put_taps(r.dw2, r.g, i, 32, 32, 0, 0)

    loop(3, tap)
    store_slots(r.small, r.dw2[...], 0)
    rows = jnp.concatenate(
        four_rows(r.st7) + four_rows(r.st6) + four_rows(r.st5) + [jnp.zeros((20, 128), f32)], axis=0
    )
    store_slots(r.small, rows, 480)
    world.scatter(r.small, r.slots, 0)
    big_a.square_back()
    big_b.line_back()
    net.sides()

    ready_s()
    count1 = sc[8] * 4356.0
    avg1, inv1 = moments(r.g1, net.s, count1, 128)
    s = jnp.zeros((1, 128), f32)
    q = jnp.zeros((1, 128), f32)
    for d in range(2):
        other = r.fl if d == 0 else r.fr
        here = sc[10 + d]

        def part(t, c):
            rows = pl.ds(pl.multiple_of(t * 160, 160), 160)
            a = r.a1[d, rows, :] + jnp.where(here > 0, other[rows, :], 0.0)
            r.a1[d, rows, :] = a
            normed, bg = back_parts(par, 0, avg1, inv1, r.r1[d, rows, :], a)
            bg = bg.reshape(4, 40, 128)
            bg = jnp.where(cells(bg.shape, 33, 33, 4 * t), bg, 0.0)
            return c[0] + jnp.sum(bg, axis=0), c[1] + jnp.sum(bg * normed.reshape(4, 40, 128), axis=0)

        ps, pq = lax.fori_loop(0, 8, part, (jnp.zeros((40, 128), f32), jnp.zeros((40, 128), f32)))
        rows = slice(1280, OWN)
        a = r.a1[d, rows, :] + jnp.where(here > 0, other[rows, :], 0.0)
        r.a1[d, rows, :] = a
        normed, bg = back_parts(par, 0, avg1, inv1, r.r1[d, 1280:1320, :], a[:40])
        bg = jnp.where(lax.broadcasted_iota(jnp.int32, (40, 128), 0) < 33, bg, 0.0)
        ps = ps + bg
        pq = pq + bg * normed
        s = s + sc[1 + d] * jnp.sum(ps, axis=0, keepdims=True)
        q = q + sc[1 + d] * jnp.sum(pq, axis=0, keepdims=True)
    put_sums(r.st8, s, q)
    net.share(r.st8, r.g8, 1)
    ready_b()
    loop(2, lambda p: coarse(p + 2, p))
    world.scattered(r.small, r.slots, 0)
    r.mine[...] = jnp.sum(r.slots[...], axis=0)
    net.shared(r.st8, r.g8, 1)
    world.share(r.mine, r.red, 1)
    big_b.square_back()
    big_a.pair_back()

    tg1, tc1 = totals(r.g8, None, 128)
    wh, wl = r.w1h[...], r.w1l[...]
    r.dw1[...] = jnp.zeros(r.dw1.shape, f32)

    def put_first(p):
        m = sc[1 + p]
        r.eh[p, 1280:, :] = jnp.zeros((OWN - 1280, 128), bf16)
        r.el[p, 1280:, :] = jnp.zeros((OWN - 1280, 128), bf16)

        def rows(t):
            at = pl.ds(pl.multiple_of(t * 80, 80), 80)
            e = response_back(par, 0, avg1, inv1, tg1, tc1, count1, r.r1[p, at, :], r.a1[p, at, :])
            e = e.reshape(2, 40, 128)
            e = jnp.where(cells(e.shape, 33, 33, 2 * t) & (m > 0), e, 0.0)
            hi, lo = split(e.reshape(80, 128))
            r.eh[p, at, :] = hi
            r.el[p, at, :] = lo

        loop(17, rows)
        rows = pl.ds(pl.multiple_of((p + 1) * 64, 64), 192)
        r.dw1[...] += dot3(r.sh[rows, :], r.sl[rows, :], r.eh[p], r.el[p], NN)

    loop(2, put_first)
    acc = r.dw1[...]
    lane = lax.broadcasted_iota(jnp.int32, (32, 128), 1)
    tot = jnp.zeros((32, 128), f32)
    for tap in range(4):
        v = jnp.zeros((32, 128), f32)
        for q in range(4):
            x = acc if q == tap else pltpu.roll(acc, ((tap - q) % 4) * 32, 1)
            hi, lo = split(x)
            sel = r.pick[tap * 4 + q]
            v += dot(sel, hi, NN) + dot(sel, lo, NN)
        tot += jnp.where(lane // 32 == tap, v, 0.0)
    last = r.small2.shape[0] * r.small2.shape[1]
    rows = jnp.concatenate([tot] + four_rows(r.st8) + [jnp.zeros((last - 36, 128), f32)], axis=0)
    store_slots(r.small2, rows, 0)
    world.scatter(r.small2, r.slots2, 2)

    def image_part(p):
        v = dot3(wh, wl, r.eh[p], r.el[p], NT)
        for i in range(3):
            tot = jnp.zeros((16, OWN), f32)
            for ab in range(4):
                at = i * 64 + ab * 16
                a, b = ab // 2, ab % 2
                x = v[at : at + 16, :]
                tot += x if ab == 0 else pltpu.roll(x, 40 * a + b, 1)
            r.parts[p, i] = tot

    loop(2, image_part)
    net.halos = []
    net.to_left(r.parts.at[0, 0], r.pr, 1)
    net.to_right(r.parts.at[1, 2], r.pl, 1)
    big_b.pair_back()
    world.scattered(r.small2, r.slots2, 2)
    r.mine2s[...] = jnp.sum(r.slots2[...], axis=0)
    world.share(r.mine2s, r.red2, 3)
    net.sides()
    for d in range(2):
        other = r.pl if d == 0 else r.pr
        tot = r.parts[0, 1 + d] + r.parts[1, d] + jnp.where(sc[10 + d] > 0, other[...], 0.0)
        tot = tot * (r.keep[...] * sc[1 + d])
        rows = []
        for y in range(34):
            tile, off = (40 * y) // 128, (40 * y) % 128
            pair = []
            for px in range(2):
                v = tot[8 * px : 8 * px + 8, 128 * tile : 128 * tile + 128]
                if off + 34 > 128:
                    nxt = tot[8 * px : 8 * px + 8, 128 * tile + 128 : 128 * tile + 256]
                    v = jnp.where(lane[:8] >= off, v, nxt)
                pair.append(v if off == 0 else pltpu.roll(v, 128 - off, 1))
            rows.append(jnp.concatenate(pair, axis=1))
        hi, lo = split(jnp.concatenate(rows, axis=0))
        out = dot(hi, r.even[...], NT) + dot(lo, r.even[...], NT)
        r.ig[d] = out.reshape(34, 8, 68)
    world.shared(r.mine, r.red, 1)
    world.shared(r.mine2s, r.red2, 3)
    big_a.wait()
    big_b.wait()
    mv.finish()


def tail(dims, tb, pg, k, fo, w2, si):
    keep, par, sc = k.keep, k.par, k.sc
    n = dims[0] * dims[1] * dims[2]
    m = dims[1] * dims[2]
    V = pltpu.VMEM
    per = 512 // n
    per2 = max(64, n) // n
    rows_a, rows_b = bucket_parts(dims)
    steps = reduction_sems(dims)
    return launch(
        functools.partial(tail_kernel, dims), "tail", 5,
        [("skip", tb.oskip, VM), ("bucket", tb.obucket, HB), ("pg", pg, VM), ("r2", k.or2, VM), ("g2", k.g2, VM),
         ("g1", k.g1, VM), ("w2", w2, VM), ("keep", keep, VM), ("w1h", k.ow1h, VM), ("w1l", k.ow1l, VM),
         ("pick", tap_picks(), VM), ("even", deinterleave(), VM), ("st5", fo.st5, VM), ("st6", fo.st6, VM),
         ("par", par, VM), ("iah", k.oah, HB), ("ial", k.oal, HB), ("ish", k.osh, HB), ("isl", k.osl, HB),
         ("ir1", k.or1, HB), ("iubh", k.oubh, HB), ("iubl", k.oubl, HB), ("iebh", tb.obh, HB),
         ("iebl", tb.obl, HB), ("sc", sc, SM), ("si", si, SM)],
        [("cg", (576, 128), f32, VM), ("ig", (2, 34, 8, 68), f32, VM), ("red", (n, per, 128), f32, VM), ("red2", (n, per2, 128), f32, VM),
         ("res", (rows_a + rows_b, 128), f32, VM)],
        both("d2", (3, 128, 1024)) + both("ub", (4, 128, 1024)) + both("a", (4096, 512)) + both("b", (1360, 1024)) + both("e2", (2048, 256))
        + both("s", (384, OWN)) + both("e", (2, OWN, 128))
        + [("f", V((36, 56, 256), f32)), ("bg2", V((2048, 256), f32)), ("r1", V((2, 1440, 128), f32)),
           ("a1", V((2, OWN, 128), f32)), ("side", V((2, OWN, 128), f32)), ("fl", V((OWN, 128), f32)),
           ("fr", V((OWN, 128), f32)), ("v", V((2, 1360, 384), f32)), ("parts", V((2, 3, 16, OWN), f32)),
           ("pl", V((16, OWN), f32)), ("pr", V((16, OWN), f32)), ("dw1", V((192, 128), f32)),
           ("g", V((512, 256), f32)), ("dw2", V((480, 128), f32)), ("small", V((n, per, 128), f32)),
           ("slots", V((n, per, 128), f32)), ("mine", V((per, 128), f32)), ("small2", V((n, per2, 128), f32)),
           ("slots2", V((n, per2, 128), f32)), ("mine2s", V((per2, 128), f32)), ("g7", V((m, 1, 512), f32)),
           ("g8", V((m, 1, 512), f32)), ("st7", V((1, 512), f32)), ("st8", V((1, 512), f32))]
        + reduction_buffers(dims, rows_a, "a")
        + reduction_buffers(dims, rows_b, "b")
        + sems(m, m, m, m, 4, 4, n, n, n, n, 20, *steps[:5], n, n, n, n, 2, *steps),
    )


def finish_kernel(r):
    def tap(i):
        for p in range(9):
            at = 64 * (p % 2)

            def get(base, chans, at=at, p=p):
                rows = pl.ds(pl.multiple_of(base + (i * 5 + p // 2) * chans, 8), chans)
                v = r.res[rows, :]
                return (v if at == 0 else pltpu.roll(v, 64, 1))[:, :64]

            r.dw3t[i * 9 + p] = get(0, 192).T
            r.dw4[i * 9 + p] = get(2880, 64)
            rows = pl.ds(pl.multiple_of((i * 5 + p // 2) * 32, 32), 32)
            v = r.red[rows, :]
            r.dw2[i * 9 + p] = (v if at == 0 else pltpu.roll(v, 64, 1))[:, :64]

    loop(3, tap)
    r.pooled[...] = r.ipooled[...]
    r.cg[...] = r.icg[...]
    r.ig[...] = r.iig[...]
    r.dup[...] = r.res[3840:4864, :].reshape(8, 128, 128)
    for t in range(27):
        v = r.red2[4 * (t // 4) : 4 * (t // 4) + 4, :]
        v = v if t % 4 == 0 else pltpu.roll(v, 128 - 32 * (t % 4), 1)
        r.dw1[t] = v[:, :32]
    sums = [r.red2[32:36, :]] + [r.red[480 + 4 * j : 484 + 4 * j, :] for j in range(3)]
    for j, v in enumerate(sums):
        for c, out in ((0, (r.s1, r.s2, r.s3, r.s4)[j]), (2, (r.x1, r.x2, r.x3, r.x4)[j])):
            x = jnp.concatenate([v[c : c + 1], v[c + 1 : c + 2]], axis=1)
            if j == 0:
                x = fold(x[:, :128])
            else:
                x = fold(x)
            out[...] = x[:, : out.shape[1]]


def finish(res, red, red2, pooled, cg, ig):
    vectors = [(f"{a}{j}", (1, 32 if j == 1 else 64), f32, VM) for j in range(1, 5) for a in "sx"]
    return launch(
        finish_kernel, "finish", None,
        [("res", res, VM), ("red", red, VM), ("red2", red2, VM), ("ipooled", pooled, VM),
         ("icg", cg, VM), ("iig", ig, VM)],
        [("dw3t", (27, 64, 192), f32, VM), ("dw4", (27, 64, 64), f32, VM), ("dw2", (27, 32, 64), f32, VM),
         ("dup", (8, 128, 128), f32, VM), ("dw1", (27, 4, 32), f32, VM),
         ("pooled", pooled.shape, f32, VM), ("cg", cg.shape, f32, VM), ("ig", ig.shape, f32, VM)] + vectors,
        [],
    )


def body(
    dims,
    image, modality_mask, extents, crop_offsets, coarse,
    conv_first, gain_first, shift_first, conv_second, gain_second, shift_second,
    up_kernel, conv_third, gain_third, shift_third, conv_fourth, gain_fourth, shift_fourth,
    pool_grad, output_grad,
):
    si = crop_offsets[0]
    img = image[0, 0].transpose(0, 1, 3, 2).reshape(2, 34, 8, 68)
    co = coarse[0, 0]
    w2 = conv_second.reshape(27, 32, 64)
    up = up_kernel.reshape(8, 128, 128)
    k = front(
        dims, img, extents, modality_mask[0], si,
        (gain_first, shift_first, gain_second, shift_second, gain_third, shift_third, gain_fourth, shift_fourth),
        conv_first.reshape(27, 4, 32), w2, conv_third.reshape(27, 192, 64).transpose(0, 2, 1), up, co,
        output_grad[0, 0].transpose(1, 2, 0, 3),
    )
    t = decode(dims, k, co, conv_fourth.reshape(27, 64, 64))
    tb = third_back(dims, t, t.or3, t.or3l, t.or3r, t.g3, k, t, t.dw4, k.ow3u, k.ow3c, up, k.par, k.sc)
    e = tail(dims, tb, pool_grad[0, 0, 0], k, t, w2, si)
    g = finish(e.res, e.red.reshape(512, 128), e.red2.reshape(-1, 128), t.pooled, e.cg, e.ig)
    return (
        g.pooled.reshape(1, 1, 1, 32, 32, 64),
        t.odecoded.transpose(2, 0, 1, 3)[None, None],
        g.ig.reshape(2, 68, 4, 68).transpose(0, 1, 3, 2)[None, None],
        g.cg.reshape(1, 1, 1, 24, 24, 128),
        g.dw1.reshape(3, 3, 3, 4, 32),
        g.x1[0],
        g.s1[0],
        g.dw2.reshape(3, 3, 3, 32, 64),
        g.x2[0],
        g.s2[0],
        g.dup.reshape(2, 2, 2, 128, 128),
        g.dw3t.transpose(0, 2, 1).reshape(3, 3, 3, 192, 64),
        g.x3[0],
        g.s3[0],
        g.dw4.reshape(3, 3, 3, 64, 64),
        g.x4[0],
        g.s4[0],
    )


def solution(mesh):
    dims = tuple(mesh.shape[a] for a in ("section", "slab", "batch"))
    field = P("section", "batch", "slab", None, None, None)
    volume = P("section", "batch", None)
    rep = P()
    return jax.shard_map(
        functools.partial(body, dims),
        mesh=mesh,
        in_specs=(field, volume, rep, volume, field) + (rep,) * 13 + (field, field),
        out_specs=(field,) * 4 + (rep,) * 13,
        check_vma=False,
    )
```

```python
import functools
import types

import jax
import jax.numpy as jnp
import numpy as np
from jax import lax
from jax.experimental import pallas as pl
from jax.experimental.pallas import tpu as pltpu
from jax.sharding import PartitionSpec as P

f32 = jnp.float32
bf16 = jnp.bfloat16
MESH = pl.DeviceIdType.MESH
EPSILON = 1e-05
NN = (((1,), (0,)), ((), ()))
NT = (((1,), (1,)), ((), ()))
TN = (((0,), (0,)), ((), ()))
VM = pl.BlockSpec(memory_space=pltpu.VMEM)
SM = pl.BlockSpec(memory_space=pltpu.SMEM)
HB = pl.BlockSpec(memory_space=pl.ANY)
LIMIT = 62 * 2**20

OWN = 1408
CROP = 896
BUCKET = 2880 + 960 + 1024
FIRST_HALF = 2560


def split(x):
    hi = x.astype(bf16)
    return hi, (x - hi.astype(f32)).astype(bf16)


def dot(a, b, dims):
    return lax.dot_general(a, b, dims, preferred_element_type=f32)


def dot3(ah, al, bh, bl, dims):
    return dot(ah, bh, dims) + dot(al, bh, dims) + dot(ah, bl, dims)


def loop(n, f, unroll=1):
    def step(t, c):
        f(t)
        return c

    lax.fori_loop(0, n, step, 0, unroll=unroll)


def fold(v):
    lanes = v.shape[-1]
    v = jnp.broadcast_to(v, (8, lanes))
    if lanes == 256:
        h = v[:, :128] + v[:, 128:]
        h = h + pltpu.roll(h, 64, 1)
        h = jnp.concatenate([h, h], axis=1)
    else:
        h = v + pltpu.roll(v, 64, 1)
        h = h + pltpu.roll(h, 32, 1)
    return h[:1]


def totals(gath, half, lanes):
    if half is None:
        tot = jnp.sum(gath[...], axis=0)
    else:
        per = gath.shape[0] // 2
        tot = jnp.sum(gath[pl.ds(half * per, per)], axis=0)
    return fold(tot[:, :lanes]), fold(tot[:, 256 : 256 + lanes])


def moments(gath, half, count, lanes):
    s, q = totals(gath, half, lanes)
    avg = s / count
    inv = lax.rsqrt(q / count - avg * avg + EPSILON)
    return avg, inv


def affine(par, layer, avg, inv):
    lanes = avg.shape[-1]
    scale = par[2 * layer : 2 * layer + 1, :lanes] * inv
    return scale, par[2 * layer + 1 : 2 * layer + 2, :lanes] - avg * scale


def silu(b):
    return b / (1.0 + jnp.exp(-b))


def silu_back(a, b):
    s = 1.0 / (1.0 + jnp.exp(-b))
    return a * s * (1.0 + b * (1.0 - s))


def cells(shape, rows, cols, row0):
    y = lax.broadcasted_iota(jnp.int32, shape, 0) + row0
    x = lax.broadcasted_iota(jnp.int32, shape, 1)
    return (y < rows) & (x < cols)


def put_sums(st, s, q):
    lanes = s.shape[-1]
    st[...] = jnp.zeros(st.shape, f32)
    st[:, :lanes] = s
    st[:, 256 : 256 + lanes] = q


def im2col(ah, al, p, f, ny, pitch, lanes, x0=0):
    def pair(t):
        for a in range(2):
            for b in range(2):
                x = f[pl.ds(2 * t + a, 2), x0 + b : x0 + b + pitch, :]
                hi, lo = split(x.reshape(2 * pitch, lanes))
                rows = pl.ds(pl.multiple_of(p * (ny * pitch) + t * (2 * pitch), 16), 2 * pitch)
                at = (2 * a + b) * lanes
                ah[rows, at : at + lanes] = hi
                al[rows, at : at + lanes] = lo

    loop(ny // 2, pair)


def launch(body, name, cid, ins, outs, scratch):
    names = [i[0] for i in ins] + [o[0] for o in outs] + [x[0] for x in scratch]

    def kernel(*refs):
        body(types.SimpleNamespace(**dict(zip(names, refs))))

    res = pl.pallas_call(
        kernel,
        out_shape=[jax.ShapeDtypeStruct(o[1], o[2]) for o in outs],
        in_specs=[i[2] for i in ins],
        out_specs=[o[3] for o in outs],
        scratch_shapes=[x[1] for x in scratch],
        compiler_params=pltpu.CompilerParams(
            vmem_limit_bytes=LIMIT, collective_id=cid, has_side_effects=cid is not None
        ),
        name=name,
    )(*[i[1] for i in ins])
    return types.SimpleNamespace(**dict(zip([o[0] for o in outs], res)))


def both(name, shape):
    return [(name + "h", pltpu.VMEM(shape, bf16)), (name + "l", pltpu.VMEM(shape, bf16))]


def both_out(name, shape):
    return [(name + "h", shape, bf16, HB), (name + "l", shape, bf16, HB)]


def sems(*sizes):
    return [(f"sem{i}", pltpu.SemaphoreType.DMA((n,))) for i, n in enumerate(sizes)]


class Moves:
    def __init__(self, sem):
        self.sem = sem
        self.used = 0
        self.pending = []

    def start(self, src, dst):
        copy = pltpu.make_async_copy(src, dst, self.sem.at[self.used])
        self.used += 1
        copy.start()
        return copy

    def out(self, *pairs):
        for src, dst in pairs:
            self.pending.append(self.start(src, dst))

    def finish(self):
        for copy in self.pending:
            copy.wait()


def fetch(mv, *pairs):
    copies = [mv.start(src, dst) for src, dst in pairs]

    def wait():
        for copy in copies:
            copy.wait()

    return wait


class Net:
    def __init__(self, dims, wide, sems):
        S, K, B = dims
        self.s = lax.axis_index("section")
        self.k = lax.axis_index("slab")
        self.b = lax.axis_index("batch")
        self.K = K
        self.sems = sems
        if wide:
            self.n = S * K * B
            self.me = (self.s * K + self.k) * B + self.b
            self.coords = lambda d: (d // (K * B), (d // B) % K, d % B)
        else:
            self.n = K * B
            self.me = self.k * B + self.b
            self.coords = lambda d: (self.s, d // B, d % B)
        self.halos = []

    def each(self, f):
        def step(p, c):
            f(p)
            return c

        lax.fori_loop(1, self.n, step, 0)

    def enter(self):
        barrier = pltpu.get_barrier_semaphore()
        self.each(
            lambda p: pl.semaphore_signal(
                barrier, inc=1, device_id=self.coords((self.me + p) % self.n), device_id_type=MESH
            )
        )

    def ready(self):
        pl.semaphore_wait(pltpu.get_barrier_semaphore(), self.n - 1)

    def _copy(self, src, dst, p, group):
        return pltpu.make_async_remote_copy(
            src_ref=src,
            dst_ref=dst,
            send_sem=self.sems[2 * group].at[p],
            recv_sem=self.sems[2 * group + 1].at[p],
            device_id=self.coords((self.me + p) % self.n),
            device_id_type=MESH,
        )

    def share(self, src, slots, group=0):
        slots[self.me] = src[...]
        self.each(lambda p: self._copy(src, slots.at[self.me], p, group).start())

    def shared(self, src, slots, group=0):
        n = self.n
        self.each(lambda p: self._copy(src, slots.at[(self.me + n - p) % n], p, group).wait_recv())
        self.each(lambda p: self._copy(src, slots.at[self.me], p, group).wait_send())

    def scatter(self, src, slots, group):
        slots[self.me] = src[self.me]
        n = self.n
        self.each(lambda p: self._copy(src.at[(self.me + p) % n], slots.at[self.me], p, group).start())

    def scattered(self, src, slots, group):
        n = self.n
        self.each(
            lambda p: self._copy(
                src.at[(self.me + p) % n], slots.at[(self.me + n - p) % n], p, group
            ).wait_recv()
        )
        self.each(lambda p: self._copy(src.at[(self.me + p) % n], slots.at[self.me], p, group).wait_send())

    def _side(self, src, dst, j, step):
        return pltpu.make_async_remote_copy(
            src_ref=src,
            dst_ref=dst,
            send_sem=self.sems[-2].at[j],
            recv_sem=self.sems[-1].at[j],
            device_id=(self.s, (self.k + self.K + step) % self.K, self.b),
            device_id_type=MESH,
        )

    def to_left(self, src, dst, j):
        copy = self._side(src, dst, 2 * j, -1)

        @pl.when(self.k > 0)
        def _():
            copy.start()

        self.halos.append((copy, -1))

    def to_right(self, src, dst, j):
        copy = self._side(src, dst, 2 * j + 1, 1)

        @pl.when(self.k < self.K - 1)
        def _():
            copy.start()

        self.halos.append((copy, 1))

    def to_sides(self, left, right, j, first):
        copies = [(self._side(*left, 2 * j, -1), -1), (self._side(*right, 2 * j + 1, 1), 1)]
        even = self.k % 2 == 0

        @pl.when((even if first else ~even) & (self.k > 0))
        def _():
            copies[0][0].start()

        @pl.when((~even if first else even) & (self.k < self.K - 1))
        def _():
            copies[1][0].start()

        if first:
            self.halos += copies

    def sides(self):
        @pl.when(self.k > 0)
        def _():
            for copy, step in self.halos:
                if step < 0:
                    copy.wait_send()
                else:
                    copy.wait_recv()

        @pl.when(self.k < self.K - 1)
        def _():
            for copy, step in self.halos:
                if step > 0:
                    copy.wait_send()
                else:
                    copy.wait_recv()


def toeplitz(w, c0, chans, th, tl, dh=None, dl=None):
    loop(3, lambda i: toeplitz_tap(w, c0, chans, i, i, th, tl, dh, dl))


def toeplitz_tap(w, c0, chans, i, slot, th, tl, dh=None, dl=None):
    zero = jnp.zeros((chans, 64), f32)
    none = jnp.zeros((chans, 128), bf16)
    for s in range(4):
        part = []
        for j in range(3):
            here = w[i * 9 + j * 3 + s, c0 : c0 + chans, :] if s <= 2 else zero
            prev = w[i * 9 + j * 3 + s - 1, c0 : c0 + chans, :] if s >= 1 else zero
            part.append(split(jnp.concatenate([here, prev], axis=1)))
        for r in range(4):
            a, py, b, px = r // 2, r % 2, s // 2, s % 2
            block = (2 * a + b) * 4 + py * 2 + px
            for h in range(2):
                hi, lo = part[r - h] if 0 <= r - h <= 2 else (none, none)
                if th is not None:
                    rows = slice(block * chans, (block + 1) * chans)
                    th[slot, rows, 128 * h : 128 * h + 128] = hi
                    tl[slot, rows, 128 * h : 128 * h + 128] = lo
                if dh is not None:
                    rows = slice((py * 2 + px) * chans, (py * 2 + px + 1) * chans)
                    at = ((1 - a) * 2 + (1 - b)) * 256 + 128 * h
                    dh[2 - i, rows, at : at + 128] = hi
                    dl[2 - i, rows, at : at + 128] = lo


def slot_of(i, ip):
    pd = (ip + i + 1) % 2
    t = (pd + i - 1) // 2 - pd + 1
    return pd * 2 + t


def up_blocks(r):
    for ip in range(2):
        for q in range(4):
            hi, lo = split(r.up[ip * 4 + q])
            r.uph[ip * 128 : ip * 128 + 128, q * 128 : q * 128 + 128] = hi
            r.upl[ip * 128 : ip * 128 + 128, q * 128 : q * 128 + 128] = lo


def compose(r, i):
    def block(ab):
        rows = pl.ds(pl.multiple_of(ab * 512, 512), 512)
        p = dot3(r.uph[...], r.upl[...], r.tuh[i, rows, :], r.tul[i, rows, :], NN)
        out = pl.ds(pl.multiple_of(ab * 128, 128), 128)
        for ip in range(2):
            r.usc[slot_of(i, ip), out, :] += p[ip * 128 : ip * 128 + 128]

    loop(4, block)


def composed(r):
    for e in range(4):
        for ab in range(4):
            hi, lo = split(r.usc[e, ab * 128 : ab * 128 + 128, :])
            r.uh[e, ab * 128 : ab * 128 + 128, :] = hi
            r.ul[e, ab * 128 : ab * 128 + 128, :] = lo
            p = (3, 1, 2, 0)[e]
            at = (3 - ab) * 256
            r.ubh[p, :, at : at + 256] = hi
            r.ubl[p, :, at : at + 256] = lo


def source_copies(dims, own, crop, so, sr, ss, rs):
    K = dims[1]
    s = lax.axis_index("section")
    k = lax.axis_index("slab")
    b = lax.axis_index("batch")
    here, left, right = k, (k + K - 1) % K, (k + 1) % K

    def copy(j, src, dst, dev):
        return pltpu.make_async_remote_copy(
            src_ref=src,
            dst_ref=dst,
            send_sem=ss.at[j],
            recv_sem=rs.at[j],
            device_id=dev,
            device_id_type=MESH,
        )

    so[2:4] = own[...]
    lefts = [
        copy(0, own, so.at[4:6], (s, left, b)),
        copy(1, crop, sr.at[4:6], (1 - s, left, b)),
    ]
    rights = [
        copy(2, own, so.at[0:2], (s, right, b)),
        copy(3, crop, sr.at[0:2], (1 - s, right, b)),
    ]
    across = copy(4, crop, sr.at[2:4], (1 - s, here, b))

    def start():
        across.start()

        @pl.when(k > 0)
        def _():
            for c in lefts:
                c.start()

        @pl.when(k < K - 1)
        def _():
            for c in rights:
                c.start()

    def finish(j):
        if j == 1:
            across.wait()
        out = (so, sr)[j]
        none = jnp.zeros((2, 16, (OWN, CROP)[j]), f32)

        @pl.when(k > 0)
        def _():
            lefts[j].wait_send()
            rights[j].wait_recv()

        @pl.when(k < K - 1)
        def _():
            rights[j].wait_send()
            lefts[j].wait_recv()

        @pl.when(k == 0)
        def _():
            out[0:2] = none

        @pl.when(k == K - 1)
        def _():
            out[4:6] = none

    return start, finish


def field_sums(r, d, n, rows, cols, mask):
    base = d * n

    def part(t, c):
        x = r[pl.ds(pl.multiple_of(base + t * 96, 16), 96), :].reshape(4, 24, 256)
        x = jnp.where(cells(x.shape, rows, cols, 4 * t), x, 0.0)
        return c[0] + jnp.sum(x, axis=0), c[1] + jnp.sum(x * x, axis=0)

    zero = jnp.zeros((24, 256), f32)
    full = n // 96
    s, q = lax.fori_loop(0, full, part, (zero, zero))
    if n % 96:
        x = r[base + full * 96 : base + n, :].reshape((n - full * 96) // 24, 24, 256)
        x = jnp.where(cells(x.shape, rows, cols, 4 * full), x, 0.0)
        s = s + jnp.sum(x, axis=0)
        q = q + jnp.sum(x * x, axis=0)
    return mask * jnp.sum(s, axis=0, keepdims=True), mask * jnp.sum(q, axis=0, keepdims=True)


def back_parts(par, layer, avg, inv, r, a):
    lanes = avg.shape[-1]
    normed = (r - avg) * inv
    b = par[2 * layer : 2 * layer + 1, :lanes] * normed + par[2 * layer + 1 : 2 * layer + 2, :lanes]
    return normed, silu_back(a, b)


def response_back(par, layer, avg, inv, tg, tc, count, r, a):
    lanes = avg.shape[-1]
    gain = par[2 * layer : 2 * layer + 1, :lanes]
    normed, bg = back_parts(par, layer, avg, inv, r, a)
    return inv * gain * (bg - (tg + normed * tc) / count)


def folded(g, j, k, chans):
    def block(r, s):
        at = (2 * (r // 2) + s // 2) * 4 + (r % 2) * 2 + s % 2
        return slice(at * chans, (at + 1) * chans)

    x = g[block(j, k), 0:128] + g[block(j + 1, k), 128:256]
    y = g[block(j, k + 1), 0:128] + g[block(j + 1, k + 1), 128:256]
    return x + pltpu.roll(y, 64, 1)


def tap_picks():
    sel = np.zeros((4, 4, 32, 192), np.float32)
    for t in range(27):
        i, j, k = t // 9, (t // 3) % 3, t % 3
        for q in range(4):
            r, s = j + q // 2, k + q % 2
            for c in range(4):
                col = i * 64 + (2 * (r // 2) + s // 2) * 16 + (s % 2) * 8 + (r % 2) * 4 + c
                sel[t % 4, q, (t // 4) * 4 + c, col] = 1.0
    return jnp.asarray(sel.reshape(16, 32, 192), bf16)


def deinterleave():
    sel = np.zeros((68, 256), np.float32)
    for x in range(68):
        sel[x, (x % 2) * 128 + x // 2] = 1.0
    return jnp.asarray(sel, bf16)


def source_stage(r):
    s = lax.axis_index("section")
    k = lax.axis_index("slab")
    b = lax.axis_index("batch")
    ends = (r.ext[s, b], r.ext[1 - s, b])
    for h in range(2):
        for p in range(4):
            g = 2 * k - 1 + p
            r.sc[4 * h + p] = jnp.where((g >= 0) & (g < ends[h]), 1.0, 0.0)
        tot = jnp.int32(0)
        for v in range(r.ext.shape[1]):
            tot = tot + (r.ext[s, v] if h == 0 else r.ext[1 - s, v])
        r.sc[8 + h] = tot.astype(f32)
    r.sc[10] = jnp.where(k > 0, 1.0, 0.0)
    r.sc[11] = jnp.where(k < r.slabs - 1, 1.0, 0.0)
    for j in range(12, 16):
        r.sc[j] = jnp.float32(0.0)
    for j, v in enumerate((r.v0, r.v1, r.v2, r.v3, r.v4, r.v5, r.v6, r.v7)):
        v = v[...]
        while v.shape[1] < 256:
            v = jnp.concatenate([v, v], axis=1)
        r.par[j : j + 1, :] = v
    row = lax.broadcasted_iota(jnp.int32, (16, 1), 0) % 4
    col = jnp.zeros((16, 1), f32)
    for c in range(4):
        col = jnp.where(row == c, r.mods[0, c].astype(f32), col)
    r.keep[...] = col
    img, keep, even, sc, own, crop = r.img, r.keep, r.even, r.sc, r.own, r.crop
    oy, ox = r.si[0, 0], r.si[0, 1]
    x = lax.broadcasted_iota(jnp.int32, (68, 256), 0)
    lane = lax.broadcasted_iota(jnp.int32, (68, 256), 1)
    at = 2 * (lane % 128) + lane // 128
    pick = ((x == at + ox) & (lane % 128 < 26)).astype(f32).astype(bf16)
    r = lax.broadcasted_iota(jnp.int32, (208, 272), 0)
    c = lax.broadcasted_iota(jnp.int32, (208, 272), 1)
    rows = (c == r + 4 * oy).astype(f32).astype(bf16)
    lane = lax.broadcasted_iota(jnp.int32, (8, 128), 1)

    def flat(v, side, pitch, tiles):
        out = [[jnp.zeros((8, 128), f32) for _ in range(tiles)] for _ in range(2)]
        for y in range(side):
            tile, off = (pitch * y) // 128, (pitch * y) % 128
            for px in range(2):
                p = v[8 * y : 8 * y + 8, 128 * px : 128 * px + 128]
                p = p if off == 0 else pltpu.roll(p, off, 1)
                if off + side > 128:
                    out[px][tile + 1] += jnp.where(lane < off, p, 0.0)
                    p = jnp.where(lane >= off, p, 0.0)
                out[px][tile] += p
        return jnp.concatenate([jnp.concatenate(o, axis=1) for o in out], axis=0)

    for d in range(2):
        hi, lo = split(img[d].reshape(272, 68))
        k = keep[...] * sc[1 + d]
        own[d] = flat(dot(hi, even[...], NN) + dot(lo, even[...], NN), 34, 40, OWN // 128) * k
        hi = dot(rows, hi, NN).astype(bf16)
        lo = dot(rows, lo, NN).astype(bf16)
        crop[d] = flat(dot(hi, pick, NN) + dot(lo, pick, NN), 26, 32, CROP // 128) * k


def split_third(r):
    def turn(t):
        v = r.w3t[t].T
        r.w3u[t] = v[:128]
        r.w3c[t] = v[128:]

    loop(27, turn)


def gather_output(r):
    r.og[...] = jnp.zeros(r.og.shape, f32)

    def row(t):
        for py in range(2):
            x0 = r.ograw[2 * t + py, pl.ds(0, 22, stride=2), :, :]
            x1 = r.ograw[2 * t + py, pl.ds(1, 22, stride=2), :, :]
            for d in range(2):
                v = jnp.concatenate([x0[:, d, :], x1[:, d, :]], axis=1)
                r.og[d, t, pl.ds(0, 22), py * 128 : py * 128 + 128] = v

    loop(22, row)


def tap_spread():
    sel = np.zeros((4, 192, 112), np.float32)
    for t in range(27):
        i, j, k = t // 9, (t // 3) % 3, t % 3
        for q in range(4):
            r, s = j + q // 2, k + q % 2
            for c in range(4):
                row = i * 64 + (2 * (r // 2) + s // 2) * 16 + (s % 2) * 8 + (r % 2) * 4 + c
                sel[q, row, t * 4 + c] = 1.0
    return jnp.asarray(sel, bf16)


def first_weights(r):
    r.wf4[...] = jnp.zeros(r.wf4.shape, f32)
    for t in range(27):
        w = r.wf[t]
        r.wf4[4 * t : 4 * t + 4, :] = jnp.concatenate([w, w, w, w], axis=1)
    hi, lo = split(r.wf4[...])
    lane = lax.broadcasted_iota(jnp.int32, (192, 128), 1) // 32
    wh = jnp.zeros((192, 128), f32)
    wl = jnp.zeros((192, 128), f32)
    for q in range(4):
        wh += jnp.where(lane == q, dot(r.spread[q], hi, NN), 0.0)
        wl += jnp.where(lane == q, dot(r.spread[q], lo, NN), 0.0)
    r.w1h[...] = wh.astype(bf16)
    r.w1l[...] = wl.astype(bf16)


def first_stage(r, arrived):
    for j, (src, hi_out, lo_out, pitch, lanes) in enumerate(
        ((r.so, r.sh, r.sl, 40, OWN), (r.sr, r.ch, r.cl, 32, CROP))
    ):
        arrived(j)
        for p in range(6):
            x = src[p]
            for ab in range(4):
                a, b = ab // 2, ab % 2
                rows = slice(p * 64 + ab * 16, p * 64 + ab * 16 + 16)
                hi, lo = split(x if ab == 0 else pltpu.roll(x, lanes - pitch * a - b, 1))
                hi_out[rows, :] = hi
                lo_out[rows, :] = lo
    for w, out in ((r.w1h, r.wdh), (r.w1l, r.wdl)):
        out[...] = jnp.zeros(out.shape, bf16)
        out[:192, :128] = w[...]
        out[64:, 128:] = w[...]
    wh, wl = r.wdh[...], r.wdl[...]
    def pair(t):
        rows = pl.ds(pl.multiple_of(t * 128, 128), 256)
        v = dot3(r.sh[rows, :], r.sl[rows, :], wh, wl, TN)
        r.r1[2 * t, :OWN, :] = v[:, :128]
        r.r1[2 * t + 1, :OWN, :] = v[:, 128:]
        v = dot3(r.ch[rows, :], r.cl[rows, :], wh, wl, TN)
        r.r1c[2 * t] = v[:, :128]
        r.r1c[2 * t + 1] = v[:, 128:]

    loop(2, pair)
    for d in range(4):
        r.r1[d, OWN:, :] = jnp.zeros((1440 - OWN, 128), f32)
    s = jnp.zeros((1, 128), f32)
    q = jnp.zeros((1, 128), f32)
    for d in range(2):
        def part(t, c):
            x = r.r1[1 + d, pl.ds(pl.multiple_of(t * 160, 160), 160), :].reshape(4, 40, 128)
            x = jnp.where(cells(x.shape, 33, 33, 4 * t), x, 0.0)
            return c[0] + jnp.sum(x, axis=0), c[1] + jnp.sum(x * x, axis=0)

        ps, pq = lax.fori_loop(0, 9, part, (jnp.zeros((40, 128), f32), jnp.zeros((40, 128), f32)))
        s = s + r.sc[1 + d] * jnp.sum(ps, axis=0, keepdims=True)
        q = q + r.sc[1 + d] * jnp.sum(pq, axis=0, keepdims=True)
    put_sums(r.st1, s, q)


def front_kernel(dims, r):
    net = Net(dims, True, [r.sem0, r.sem1, r.sem2, r.sem3, r.sem4, r.sem5])
    net.enter()
    mv = Moves(r.sem8)
    ready_w = fetch(mv, (r.iw3t, r.w3t), (r.iw2, r.w2), (r.iup, r.up))
    ready_og = fetch(mv, (r.iograw, r.ograw))
    r.slabs = dims[1]
    source_stage(r)
    net.ready()
    start, finish = source_copies(dims, r.own, r.crop, r.so, r.sr, r.sem6, r.sem7)
    start()
    net.to_left(r.co.at[0], r.cor, 0)
    net.to_right(r.co.at[0], r.col, 0)
    ready_w()
    split_third(r)
    mv.out((r.w3u, r.ow3u), (r.w3c, r.ow3c))
    first_weights(r)
    mv.out((r.w1h, r.ow1h), (r.w1l, r.ow1l))
    toeplitz(r.w2, 0, 32, r.t2h, r.t2l)
    toeplitz(r.w3u, 0, 128, r.tuh, r.tul)
    up_blocks(r)
    r.usc[...] = jnp.zeros(r.usc.shape, f32)
    compose(r, 0)
    first_stage(r, finish)
    mv.out((r.sh, r.osh), (r.sl, r.osl), (r.r1, r.or1))
    net.share(r.st1, r.g1, 0)
    ready_og()
    gather_output(r)
    mv.out((r.og, r.oog))
    net.to_left(r.og.at[0], r.ogr, 2)
    net.to_right(r.og.at[1], r.ogl, 2)
    net.shared(r.st1, r.g1, 0)

    half = net.s
    f = r.f
    f[...] = jnp.zeros(f.shape, f32)
    scale_c, off_c = affine(r.par, 0, *moments(r.g1, 1 - half, r.sc[9] * 4356.0, 128))

    def crop(p):
        m = r.sc[4 + p]

        def rows(t):
            x = r.r1c[p, pl.ds(pl.multiple_of(t * 128, 128), 128), :].reshape(4, 32, 128)
            f[pl.ds(4 * t, 4), :32, :] = jnp.where(m > 0, silu(x * scale_c + off_c), 0.0)

        loop(7, rows)
        im2col(r.ah, r.al, p, f, 24, 24, 128)

    loop(4, crop)
    conv(r.r2c, r.ah, r.al, r.t2h, r.t2l, 576, NN)
    net.to_left(r.r2c.at[0:576], r.hr, 1)
    net.to_right(r.r2c.at[576:1152], r.hl, 1)
    mv.out((r.r2c, r.or2c))
    scale, off = affine(r.par, 0, *moments(r.g1, half, r.sc[8] * 4356.0, 128))

    def own(p):
        m = r.sc[p]

        def rows(t):
            x = r.r1[p, pl.ds(pl.multiple_of(t * 160, 160), 160), :].reshape(4, 40, 128)
            f[pl.ds(4 * t, 4), :40, :] = jnp.where(m > 0, silu(x * scale + off), 0.0)

        loop(9, rows)
        im2col(r.ah, r.al, p, f, 32, 32, 128)

    loop(4, own)
    mv.out((r.ah, r.oah), (r.al, r.oal))
    conv(r.r2, r.ah, r.al, r.t2h, r.t2l, 1024, NN)
    mv.out((r.r2, r.or2))
    s = jnp.zeros((1, 256), f32)
    q = jnp.zeros((1, 256), f32)
    for d in range(2):
        def part(t, c):
            x = r.r2[pl.ds(pl.multiple_of(d * 1024 + t * 128, 128), 128), :].reshape(16, 8, 256)
            return c[0] + jnp.sum(x, axis=0), c[1] + jnp.sum(x * x, axis=0)

        ps, pq = lax.fori_loop(0, 8, part, (jnp.zeros((8, 256), f32), jnp.zeros((8, 256), f32)))
        s = s + r.sc[1 + d] * jnp.sum(ps, axis=0, keepdims=True)
        q = q + r.sc[1 + d] * jnp.sum(pq, axis=0, keepdims=True)
    put_sums(r.st2, s, q)
    net.share(r.st2, r.g2, 1)
    compose(r, 1)
    compose(r, 2)
    composed(r)
    mv.out((r.uh, r.ouh), (r.ul, r.oul), (r.ubh, r.oubh), (r.ubl, r.oubl))
    net.shared(r.st2, r.g2, 1)
    net.sides()
    mv.finish()


def conv(out, ah, al, th, tl, rows, dims):
    out[...] = jnp.zeros(out.shape, f32)

    def tap(i):
        at = pl.ds(pl.multiple_of(i * rows, 16), 2 * rows)
        out[...] += dot3(ah[at, :], al[at, :], th[i], tl[i], dims)

    loop(3, tap)


def conv_plane(out, d, ah, al, th, tl, rows, dims):
    to = pl.ds(pl.multiple_of(d * rows, 16), rows)
    out[to, :] = jnp.zeros((rows, out.shape[1]), f32)

    def tap(i):
        at = pl.ds(pl.multiple_of((d + i) * rows, 16), rows)
        out[to, :] += dot3(ah[at, :], al[at, :], th[i], tl[i], dims)

    loop(3, tap)


def front(dims, img, ext, mods, si, vectors, wf, w2, w3t, up, co, og):
    n = dims[0] * dims[1] * dims[2]
    V = pltpu.VMEM
    forms = [("u", (4, 512, 256)), ("ub", (4, 128, 1024)), ("s", (384, OWN)), ("a", (4096, 512)), ("w1", (192, 128))]
    outs = [("g1", (n, 1, 512), f32, VM), ("g2", (n, 1, 512), f32, VM),
            ("or1", (4, 1440, 128), f32, HB), ("or2", (2048, 256), f32, HB), ("or2c", (1152, 256), f32, HB),
            ("col", co.shape[1:], f32, HB), ("cor", co.shape[1:], f32, HB),
            ("par", (8, 256), f32, VM), ("keep", (16, 1), f32, VM), ("sc", (16,), f32, SM),
            ("ow3u", (27, 128, 64), f32, HB), ("ow3c", (27, 64, 64), f32, HB),
            ("oog", (2, 22, 24, 256), f32, HB), ("ogl", (22, 24, 256), f32, HB), ("ogr", (22, 24, 256), f32, HB),
            ("hl", (576, 256), f32, HB), ("hr", (576, 256), f32, HB)]
    scratch = []
    for name, shape in forms:
        outs += both_out("o" + name, shape)
        scratch += both(name, shape)
    scratch += both("t2", (3, 512, 256)) + both("tu", (3, 2048, 256)) + both("up", (256, 512)) + both("c", (384, CROP)) + both("wd", (256, 256))
    scratch += [("st1", V((1, 512), f32)), ("st2", V((1, 512), f32)), ("so", V((6, 16, OWN), f32)),
                ("sr", V((6, 16, CROP), f32)), ("wf4", V((112, 128), f32)), ("usc", V((4, 512, 256), f32)),
                ("r1", V((4, 1440, 128), f32)), ("r1c", V((4, CROP, 128), f32)), ("r2", V((2048, 256), f32)),
                ("r2c", V((1152, 256), f32)), ("f", V((36, 48, 128), f32)), ("own", V((2, 16, OWN), f32)),
                ("crop", V((2, 16, CROP), f32)), ("w3u", V((27, 128, 64), f32)), ("w3c", V((27, 64, 64), f32)),
                ("og", V((2, 22, 24, 256), f32)), ("ograw", V((44, 44, 2, 64), f32)),
                ("w3t", V((27, 64, 192), f32)), ("w2", V((27, 32, 64), f32)), ("up", V((8, 128, 128), f32))]
    return launch(
        functools.partial(front_kernel, dims), "front", 1,
        [("img", img, VM), ("even", deinterleave(), VM), ("ext", ext, SM), ("mods", mods, SM), ("si", si, SM),
         ("wf", wf, VM), ("spread", tap_spread(), VM), ("iw2", w2, HB), ("iw3t", w3t, HB), ("iup", up, HB),
         ("co", co, HB), ("iograw", og, HB)]
        + [(f"v{j}", v.reshape(1, -1), VM) for j, v in enumerate(vectors)],
        outs, scratch + sems(n, n, n, n, 6, 6, 5, 5, 32),
    )


def decode_kernel(dims, r):
    net = Net(
        dims, False, [r.sem0, r.sem1, r.sem2, r.sem3, r.sem4, r.sem5, r.sem6, r.sem7, r.sem8, r.sem9]
    )
    net.enter()
    mv = Moves(r.sem10)
    par = r.par
    ready_c = fetch(mv, (r.ihl, r.hl), (r.ir2c, r.r2c), (r.ihr, r.hr))
    ready_w3 = fetch(mv, (r.iw3, r.w3))
    ready_co = fetch(mv, (r.icol, r.col), (r.ico.at[0], r.co), (r.icor, r.cor))
    weights = fetch(mv, (r.iuh, r.uh), (r.iul, r.ul))
    ready_w4 = fetch(mv, (r.iw4, r.w4))
    ready_r2 = fetch(mv, (r.ir2, r.r2))
    ready_og = fetch(mv, (r.iog, r.og), (r.iogl, r.ogl), (r.iogr, r.ogr))
    f, f2, sc = r.f, r.f2, r.sc
    scale_c, off_c = affine(r.par, 1, *moments(r.g2, 1 - net.s, sc[9] * 4096.0, 256))
    f[...] = jnp.zeros(f.shape, f32)

    def put(p, get):
        m = sc[4 + p]

        def rows(t):
            x = silu(get(t * 96) * scale_c + off_c).reshape(4, 24, 256)
            f[pl.ds(4 * t, 4), :24, :] = jnp.where(m > 0, x, 0.0)

        loop(6, rows)
        im2col(r.bh, r.bl, p, f, 24, 24, 256)

    def of(ref, base):
        return lambda at: ref[pl.ds(pl.multiple_of(base + at, 32), 96), :]

    ready_c()
    put(0, of(r.hl, 0))
    loop(2, lambda p: put(p + 1, of(r.r2c, p * 576)))
    put(3, of(r.hr, 0))
    kept = fetch(mv, (r.bh, r.oah), (r.bl, r.oal))
    f2[...] = jnp.zeros(f2.shape, f32)
    ready_w3()
    toeplitz(r.w3, 0, 64, r.th, r.tl)
    ready_co()
    for p, (src, m) in enumerate(((r.col, sc[4]), (r.co, sc[5]), (r.cor, sc[7]))):
        f2[:24, :24, :] = jnp.where(m > 0, src[...], 0.0)
        im2col(r.cuh, r.cul, p, f2, 24, 24, 128)
    mv.out((r.cuh, r.ocuh), (r.cul, r.ocul))
    weights()
    sides = ((r.r3.at[0:576], r.r3r), (r.r3.at[576:1152], r.r3l), 0)

    def plane(d):
        conv_plane(r.r3, d, r.bh, r.bl, r.th, r.tl, 576, NN)

        def up(t):
            at = pl.ds(pl.multiple_of((d + t) * 576, 16), 576)
            out = pl.ds(pl.multiple_of(d * 576, 16), 576)
            r.r3[out, :] += dot3(r.cuh[at, :], r.cul[at, :], r.uh[2 * d + t], r.ul[2 * d + t], NN)

        loop(2, up)

    plane(net.k % 2)
    net.ready()
    net.to_sides(*sides, True)
    plane(1 - net.k % 2)
    s0, q0 = field_sums(r.r3, 0, 576, 23, 23, sc[5])
    s1, q1 = field_sums(r.r3, 1, 576, 23, 23, sc[6])
    put_sums(r.st3, s0 + s1, q0 + q1)
    net.share(r.st3, r.g3, 0)
    net.to_sides(*sides, False)
    mv.out((r.r3, r.or3))
    ready_w4()
    toeplitz(r.w4, 0, 64, r.th, r.tl, r.d4h, r.d4l)
    net.shared(r.st3, r.g3, 0)

    avg3, inv3 = moments(r.g3, None, sc[9] * 2116.0, 256)
    scale3, off3 = affine(par, 2, avg3, inv3)

    def put_act(p, get):
        m = sc[4 + p]

        def rows(t):
            x = silu(get(t * 96) * scale3 + off3).reshape(4, 24, 256)
            f[pl.ds(4 * t, 4), :24, :] = jnp.where(m > 0, x, 0.0)

        loop(6, rows)
        im2col(r.ah, r.al, p, f, 22, 24, 256)

    def part_of(ref, base, step):
        return lambda at: ref[pl.ds(pl.multiple_of(base + at, 16), step), :]

    loop(2, lambda p: put_act(p + 1, part_of(r.r3, p * 576, 96)))
    net.sides()
    net.halos = []
    mv.out((r.r3l, r.or3l), (r.r3r, r.or3r))
    put_act(0, part_of(r.r3l, 0, 96))
    put_act(3, part_of(r.r3r, 0, 96))
    conv(r.r4, r.ah, r.al, r.th, r.tl, 528, NN)
    s0, q0 = field_sums(r.r4, 0, 528, 22, 22, sc[5])
    s1, q1 = field_sums(r.r4, 1, 528, 22, 22, sc[6])
    put_sums(r.st4, s0 + s1, q0 + q1)
    net.share(r.st4, r.g4, 1)
    net.to_left(r.r4.at[0:528], r.r4r, 1)
    net.to_right(r.r4.at[528:1056], r.r4l, 1)
    scale, off = affine(r.par, 1, *moments(r.g2, net.s, sc[8] * 4096.0, 256))

    def pool(t):
        v = jnp.zeros((128, 256), f32)
        for d in range(2):
            x = r.r2[pl.ds(pl.multiple_of(d * 1024 + t * 128, 128), 128), :]
            v = v + sc[1 + d] * silu(x * scale + off)
        v = v[:, :128] + v[:, 128:]
        v = (v + pltpu.roll(v, 64, 1)) * 0.125
        r.pooled[pl.ds(pl.multiple_of(t * 128, 128), 128), :] = v[:, :64]

    ready_r2()
    loop(8, pool)
    ready_og()
    net.shared(r.st4, r.g4, 1)

    count = sc[9] * 1936.0
    avg, inv = moments(r.g4, None, count, 256)
    scale4, off4 = affine(par, 3, avg, inv)
    s = jnp.zeros((1, 256), f32)
    q = jnp.zeros((1, 256), f32)
    for d in range(2):
        m = sc[5 + d]

        def part(t, c):
            x = r.r4[pl.ds(pl.multiple_of(d * 528 + t * 48, 16), 48), :]
            b = x * scale4 + off4
            sg = 1.0 / (1.0 + jnp.exp(-b))
            r.dec[d, pl.ds(2 * t, 2)] = (m * (b * sg)).reshape(2, 24, 256)
            bg = r.og[d, pl.ds(2 * t, 2)].reshape(48, 256) * sg * (1.0 + b * (1.0 - sg))
            normed = (x - avg) * inv
            return (
                c[0] + jnp.sum(bg.reshape(6, 8, 256), axis=0),
                c[1] + jnp.sum((bg * normed).reshape(6, 8, 256), axis=0),
            )

        ps, pq = lax.fori_loop(0, 11, part, (jnp.zeros((8, 256), f32), jnp.zeros((8, 256), f32)))
        s = s + m * jnp.sum(ps, axis=0, keepdims=True)
        q = q + m * jnp.sum(pq, axis=0, keepdims=True)
    put_sums(r.st5, s, q)
    net.share(r.st5, r.g5, 2)

    def spread(t):
        for py in range(2):
            for px in range(2):
                at = py * 128 + px * 64
                v = jnp.stack([r.dec[0, t, :22, at : at + 64], r.dec[1, t, :22, at : at + 64]], axis=1)
                r.decoded[2 * t + py, pl.ds(px, 22, stride=2), :, :] = v

    loop(22, spread)
    mv.out((r.decoded, r.odecoded))
    net.shared(r.st5, r.g5, 2)
    net.sides()
    net.halos = []
    kept()

    tg, tc = totals(r.g5, None, 256)
    f[...] = jnp.zeros(f.shape, f32)

    def put_back(p, get_r, get_a, keep):
        m = sc[4 + p]

        def rows(t):
            a = get_a(2 * t).reshape(48, 256)
            e = response_back(par, 3, avg, inv, tg, tc, count, get_r(t * 48), a).reshape(2, 24, 256)
            e = jnp.where(cells(e.shape, 22, 22, 0) & (m > 0), e, 0.0)
            f[pl.ds(1 + 2 * t, 2), 8:32, :] = e
            if keep is not None:
                hi, lo = split(e.reshape(48, 256))
                at = pl.ds(pl.multiple_of(keep * 528 + t * 48, 16), 48)
                r.eh[at, :] = hi
                r.el[at, :] = lo

        loop(11, rows)
        im2col(r.bh, r.bl, p, f, 24, 24, 256, x0=7)

    put_back(0, part_of(r.r4l, 0, 48), lambda y: r.ogl[pl.ds(y, 2)], None)
    loop(2, lambda p: put_back(p + 1, part_of(r.r4, p * 528, 48), lambda y: r.og[p, pl.ds(y, 2)], p))
    put_back(3, part_of(r.r4r, 0, 48), lambda y: r.ogr[pl.ds(y, 2)], None)
    conv(r.a3, r.bh, r.bl, r.d4h, r.d4l, 576, NT)
    mv.out((r.a3, r.oa3))
    s = jnp.zeros((1, 256), f32)
    q = jnp.zeros((1, 256), f32)
    for d in range(2):
        def part(t, c):
            at = pl.ds(pl.multiple_of(d * 576 + t * 48, 16), 48)
            normed, bg = back_parts(par, 2, avg3, inv3, r.r3[at, :], r.a3[at, :])
            bg = bg.reshape(2, 24, 256)
            bg = jnp.where(cells(bg.shape, 23, 23, 2 * t), bg, 0.0)
            return c[0] + jnp.sum(bg, axis=0), c[1] + jnp.sum(bg * normed.reshape(2, 24, 256), axis=0)

        ps, pq = lax.fori_loop(0, 12, part, (jnp.zeros((24, 256), f32), jnp.zeros((24, 256), f32)))
        s = s + sc[5 + d] * jnp.sum(ps, axis=0, keepdims=True)
        q = q + sc[5 + d] * jnp.sum(pq, axis=0, keepdims=True)
    put_sums(r.st6, s, q)
    net.share(r.st6, r.g6, 3)
    net.to_left(r.a3.at[0:576], r.a3r, 2)
    net.to_right(r.a3.at[576:1152], r.a3l, 2)

    def tap(i):
        at = pl.ds(pl.multiple_of(i * 528, 16), 1056)
        r.g[...] = dot3(r.ah[at, :], r.al[at, :], r.eh[...], r.el[...], TN)
        put_taps(r.dw4, r.g, i, 64, 64, 0, 0)

    loop(3, tap)
    net.shared(r.st6, r.g6, 3)
    net.sides()
    mv.finish()


def put_taps(out, g, i, chans, total, row0, base):
    def rows(p):
        return pl.ds(pl.multiple_of(base + (i * 5 + p // 2) * total + row0, 8), chans)

    for p in range(9):
        v = folded(g, p // 3, p % 3, chans)
        v = v if p % 2 == 0 else pltpu.roll(v, 64, 1)
        at = 64 * (p % 2)
        out[rows(p), at : at + 64] = v[:, at : at + 64]
    out[rows(8), 64:] = jnp.zeros((chans, 64), f32)


def decode(dims, k, co, w4):
    n = dims[1] * dims[2]
    V = pltpu.VMEM
    box = (22, 24, 256)
    return launch(
        functools.partial(decode_kernel, dims), "decode", 2,
        [("ir2", k.or2, HB), ("ir2c", k.or2c, HB), ("ihl", k.hl, HB), ("ihr", k.hr, HB), ("ico", co, HB),
         ("icol", k.col, HB), ("icor", k.cor, HB), ("g2", k.g2, VM), ("par", k.par, VM), ("iuh", k.ouh, HB),
         ("iul", k.oul, HB), ("iw3", k.ow3c, HB), ("iw4", w4, HB), ("iog", k.oog, HB), ("iogl", k.ogl, HB),
         ("iogr", k.ogr, HB), ("sc", k.sc, SM)],
        [("pooled", (1024, 64), f32, VM), ("g3", (n, 1, 512), f32, VM), ("or3", (1152, 256), f32, HB),
         ("or3l", (576, 256), f32, HB), ("or3r", (576, 256), f32, HB), ("odecoded", (44, 44, 2, 64), f32, HB),
         ("oa3", (1152, 256), f32, HB), ("a3l", (576, 256), f32, HB), ("a3r", (576, 256), f32, HB),
         ("g6", (n, 1, 512), f32, VM), ("st5", (1, 512), f32, VM), ("st6", (1, 512), f32, VM),
         ("dw4", (960, 128), f32, VM)]
        + both_out("oa", (2304, 1024)) + both_out("ocu", (1728, 512)),
        both("t", (3, 1024, 256)) + both("d4", (3, 256, 1024)) + both("a", (2112, 1024)) + both("b", (2304, 1024))
        + both("cu", (1728, 512)) + both("u", (4, 512, 256)) + both("e", (1056, 256))
        + [("f", V((26, 40, 256), f32)), ("f2", V((26, 32, 128), f32)), ("r2", V((2048, 256), f32)),
           ("r3", V((1152, 256), f32)), ("r3l", V((576, 256), f32)), ("r3r", V((576, 256), f32)),
           ("r4", V((1056, 256), f32)), ("r4l", V((528, 256), f32)),
           ("r4r", V((528, 256), f32)), ("og", V((2,) + box, f32)), ("ogl", V(box, f32)), ("ogr", V(box, f32)),
           ("dec", V((2,) + box, f32)), ("decoded", V((44, 44, 2, 64), f32)), ("a3", V((1152, 256), f32)),
           ("g", V((1024, 256), f32)), ("g4", V((n, 1, 512), f32)), ("g5", V((n, 1, 512), f32)),
           ("st3", V((1, 512), f32)), ("st4", V((1, 512), f32)), ("hl", V((576, 256), f32)),
           ("hr", V((576, 256), f32)), ("r2c", V((1152, 256), f32)), ("co", V((24, 24, 128), f32)),
           ("col", V((24, 24, 128), f32)), ("cor", V((24, 24, 128), f32)), ("w3", V((27, 64, 64), f32)),
           ("w4", V((27, 64, 64), f32))]
        + sems(n, n, n, n, n, n, n, n, 6, 6, 32),
    )


def third_back_kernel(dims, r):
    net = Net(dims, False, [])
    barrier = pltpu.get_barrier_semaphore()
    partner = (1 - net.s, net.k, net.b)
    mv = Moves(r.sem0)
    pl.semaphore_signal(barrier, inc=1, device_id=partner, device_id_type=MESH)
    ready_l = fetch(mv, (r.ir3l, r.r3l), (r.ia3l, r.a3l))
    ready_o = fetch(mv, (r.ir3, r.r3), (r.ia3, r.a3))
    ready_r = fetch(mv, (r.ir3r, r.r3r), (r.ia3r, r.a3r))
    ready_a = fetch(mv, (r.iah, r.ah), (r.ial, r.al))
    ready_u = fetch(mv, (r.icuh, r.cuh), (r.icul, r.cul))
    ready_w = fetch(mv, (r.iw3u, r.w3u), (r.idw4, r.dw4))
    toeplitz(r.w3c, 0, 64, None, None, r.d3h, r.d3l)
    sc, f, par = r.sc, r.f, r.par
    count = sc[9] * 2116.0
    avg, inv = moments(r.g3, None, count, 256)
    tg, tc = totals(r.g6, None, 256)
    f[...] = jnp.zeros(f.shape, f32)

    def of(ref, base):
        return lambda at: ref[pl.ds(pl.multiple_of(base + at, 16), 48), :]

    def put(p, get_r, get_a, keep):
        m = sc[4 + p]

        def rows(t):
            e = response_back(par, 2, avg, inv, tg, tc, count, get_r(t * 48), get_a(t * 48)).reshape(2, 24, 256)
            e = jnp.where(cells(e.shape, 23, 23, 2 * t) & (m > 0), e, 0.0)
            f[pl.ds(1 + 2 * t, 2), 8:32, :] = e
            if keep is not None:
                hi, lo = split(e.reshape(48, 256))
                at = pl.ds(pl.multiple_of(keep * 576 + t * 48, 16), 48)
                r.eh[at, :] = hi
                r.el[at, :] = lo

        loop(12, rows)
        im2col(r.bh, r.bl, p, f, 24, 24, 256, x0=7)

    ready_l()
    put(0, of(r.r3l, 0), of(r.a3l, 0), None)
    ready_o()
    loop(2, lambda p: put(p + 1, of(r.r3, p * 576), of(r.a3, p * 576), p))
    ready_r()
    put(3, of(r.r3r, 0), of(r.a3r, 0), None)
    mv.out((r.bh, r.obh), (r.bl, r.obl))

    across = []
    for d in range(2):
        conv_plane(r.g.at[:1152], d, r.bh, r.bl, r.d3h, r.d3l, 576, NT)

        def row(t):
            at = pl.ds(pl.multiple_of(t * 24, 24), 24)
            r.skip[2 * t] = r.g[at, :128]
            r.skip[2 * t + 1] = r.g[at, 128:]

        loop(24, lambda t, d=d: row(d * 24 + t))
        if d == 0:
            pl.semaphore_wait(barrier, 1)
        copy = pltpu.make_async_remote_copy(
            src_ref=r.skip.at[d * 48 : d * 48 + 48], dst_ref=r.oskip.at[d * 48 : d * 48 + 48],
            send_sem=r.sem1.at[2 * d], recv_sem=r.sem1.at[2 * d + 1],
            device_id=partner, device_id_type=MESH,
        )
        copy.start()
        across.append(copy)

    ready_a()
    bucket = r.bucket

    def tap(i):
        at = pl.ds(pl.multiple_of(i * 576, 16), 1152)
        r.g[:1024, :] = dot3(r.ah[at, :], r.al[at, :], r.eh[...], r.el[...], TN)
        put_taps(bucket, r.g, i, 64, 192, 128, 0)

    loop(3, tap)
    ready_u()

    def coarse(j):
        at = pl.ds(pl.multiple_of((j // 2 + j % 2) * 576, 16), 576)
        e = pl.ds(pl.multiple_of((j // 2) * 576, 16), 576)
        r.gu[j] = dot3(r.cuh[at, :], r.cul[at, :], r.eh[e, :], r.el[e, :], TN)

    loop(4, coarse)
    ready_w()
    up_blocks(r)
    r.gd[...] = jnp.zeros(r.gd.shape, f32)
    for i in range(3):
        loop(1, lambda _, i=i: toeplitz_tap(r.w3u, 0, 128, i, 0, r.tuh, r.tul))

        def block(ab, i=i):
            out = pl.ds(pl.multiple_of(ab * 128, 128), 128)
            p = jnp.concatenate([r.gu[slot_of(i, 0), out, :], r.gu[slot_of(i, 1), out, :]], axis=0)
            ph, plo = split(p)
            rows = pl.ds(pl.multiple_of(ab * 512, 512), 512)
            r.gd[...] += dot3(ph, plo, r.tuh[0, rows, :], r.tul[0, rows, :], NT)
            r.g[rows, :] = dot3(r.uph[...], r.upl[...], ph, plo, TN)

        loop(4, block)
        loop(1, lambda _, i=i: put_taps(bucket, r.g, i, 128, 192, 0, 0))
    bucket[2880:3840, :] = r.dw4[...]
    for ip in range(2):
        for q in range(4):
            at = 3840 + (ip * 4 + q) * 128
            bucket[at : at + 128, :] = r.gd[ip * 128 : ip * 128 + 128, q * 128 : q * 128 + 128]
    if bucket.shape[0] > BUCKET:
        bucket[BUCKET:, :] = jnp.zeros((bucket.shape[0] - BUCKET, 128), f32)
    mv.out((bucket, r.obucket))
    for copy in across:
        copy.wait()
    mv.finish()


def world_rows(dims, rows):
    n = dims[0] * dims[1] * dims[2]
    return -(-rows // (8 * n)) * 8 * n


def bucket_parts(dims):
    first = world_rows(dims, FIRST_HALF)
    return first, world_rows(dims, max(BUCKET - first, 8))


def reduction_buffers(dims, rows, tag):
    S, K, B = dims
    Q = S * K // 2
    V = pltpu.VMEM
    per = rows // (S * K * B)
    return [("mine1" + tag, V((rows // 2, 128), f32)), ("slot1" + tag, V((rows // 2, 128), f32)),
            ("slot2" + tag, V((Q - 1, B * per, 128), f32)), ("mine2" + tag, V((B * per, 128), f32)),
            ("slot3" + tag, V((B - 1, per, 128), f32))]


def reduction_sems(dims):
    Q, B = dims[0] * dims[1] // 2, dims[2]
    return [2, 2 * (Q - 1), 2 * (B - 1), 2 * (B - 1), 2 * (Q - 1), 2]


def third_back(dims, fb, r3, r3l, r3r, g3, k, t, dw4, w3u, w3c, up, par, sc):
    n = dims[0] * dims[1] * dims[2]
    V = pltpu.VMEM
    rows = sum(bucket_parts(dims))
    return launch(
        functools.partial(third_back_kernel, dims), "third_back", 4,
        [("ia3", fb.oa3, HB), ("ia3l", fb.a3l, HB), ("ia3r", fb.a3r, HB), ("ir3", r3, HB), ("ir3l", r3l, HB),
         ("ir3r", r3r, HB), ("g3", g3, VM), ("g6", fb.g6, VM), ("idw4", dw4, HB), ("par", par, VM),
         ("iw3u", w3u, HB), ("w3c", w3c, VM), ("up", up, VM), ("iah", t.oah, HB), ("ial", t.oal, HB),
         ("icuh", t.ocuh, HB), ("icul", t.ocul, HB), ("sc", sc, SM)],
        [("oskip", (96, 24, 128), f32, HB), ("obh", (2304, 1024), bf16, HB), ("obl", (2304, 1024), bf16, HB),
         ("obucket", (rows, 128), f32, HB)],
        both("tu", (1, 2048, 256)) + both("d3", (3, 256, 1024)) + both("a", (2304, 1024)) + both("cu", (1728, 512))
        + both("up", (256, 512)) + both("b", (2304, 1024)) + both("e", (1152, 256))
        + [("f", V((26, 40, 256), f32)), ("skip", V((96, 24, 128), f32)),
           ("g", V((2048, 256), f32)), ("gu", V((4, 512, 256), f32)), ("gd", V((256, 512), f32)),
           ("bucket", V((rows, 128), f32)), ("a3", V((1152, 256), f32)), ("a3l", V((576, 256), f32)),
           ("a3r", V((576, 256), f32)), ("r3", V((1152, 256), f32)), ("r3l", V((576, 256), f32)),
           ("r3r", V((576, 256), f32)), ("w3u", V((27, 128, 64), f32)), ("dw4", V((960, 128), f32))]
        + sems(32, 4),
    )


class Reduction:
    def __init__(self, dims, net, base, rows, r, tag, sems):
        S, K, B = dims
        self.net, self.base, self.steps = net, base, iter(sems)
        self.per = rows // (S * K * B)
        self.bucket, self.res = r.bucket, r.res
        self.mine1, self.slot1, self.slot2, self.mine2, self.slot3 = (
            getattr(r, name + tag) for name in ("mine1", "slot1", "slot2", "mine2", "slot3")
        )
        self.Q, self.B, self.half = S * K // 2, B, S * K * B // 2
        self.core = net.k % 2
        self.q = net.s * (K // 2) + net.k // 2
        self.rows = K // 2
        self.pair_of = (net.s, net.k + 1 - 2 * self.core, net.b)
        self.place = self.core * self.half + self.q * self.B + net.b

    def ds(self, first, count, base=0):
        return pl.ds(pl.multiple_of(base + first * self.per, 8), count * self.per)

    def whole(self, first, count):
        return self.ds(first, count, self.base)

    def at_square(self, q):
        return (q // self.rows, 2 * (q % self.rows) + self.core, self.net.b)

    def copies(self, items):
        sem = next(self.steps)
        self.open = [
            pltpu.make_async_remote_copy(
                src_ref=src, dst_ref=dst, send_sem=sem.at[2 * j], recv_sem=sem.at[2 * j + 1],
                device_id=dev, device_id_type=MESH,
            )
            for j, (src, dst, dev) in enumerate(items)
        ]
        for c in self.open:
            c.start()

    def wait(self):
        for c in self.open:
            c.wait()

    def pair(self, mv):
        self.own = mv.start(self.bucket.at[self.whole(self.core * self.half, self.half)], self.mine1)
        src = self.bucket.at[self.whole((1 - self.core) * self.half, self.half)]
        self.copies([(src, self.slot1, self.pair_of)])

    def square(self):
        self.wait()
        self.own.wait()
        size = self.half * self.per // 16

        def add(t):
            at = pl.ds(pl.multiple_of(t * size, 8), size)
            self.mine1[at, :] += self.slot1[at, :]

        loop(16, add)
        items = []
        for t in range(1, self.Q):
            q = (self.q + t) % self.Q
            items.append((self.mine1.at[self.ds(q * self.B, self.B)], self.slot2.at[t - 1], self.at_square(q)))
        self.copies(items)

    def line(self):
        self.wait()
        v = self.mine1[self.ds(self.q * self.B, self.B), :]
        for t in range(self.Q - 1):
            v = v + self.slot2[t]
        self.mine2[...] = v
        items = []
        for t in range(1, self.B):
            b = (self.net.b + t) % self.B
            items.append((self.mine2.at[self.ds(b, 1)], self.slot3.at[t - 1], (self.net.s, self.net.k, b)))
        self.copies(items)

    def line_back(self):
        self.wait()
        v = self.mine2[self.ds(self.net.b, 1), :]
        for t in range(self.B - 1):
            v = v + self.slot3[t]
        self.res[self.whole(self.place, 1), :] = v
        own = self.res.at[self.whole(self.place, 1)]
        self.copies([(own, own, (self.net.s, self.net.k, (self.net.b + t) % self.B)) for t in range(1, self.B)])

    def square_back(self):
        self.wait()
        own = self.res.at[self.whole(self.core * self.half + self.q * self.B, self.B)]
        self.copies([(own, own, self.at_square((self.q + t) % self.Q)) for t in range(1, self.Q)])

    def pair_back(self):
        self.wait()
        own = self.res.at[self.whole(self.core * self.half, self.half)]
        self.copies([(own, own, self.pair_of)])


def skip_stage(r, avg, inv, d):
    sc, par = r.sc, r.par
    oy, ox = r.si[0, 0], r.si[0, 1]
    qx = ox // 2
    rx = ox - 2 * qx
    odd = rx > 0
    lane = lax.broadcasted_iota(jnp.int32, (32, 128), 1)
    pad = jnp.zeros((8, 128), f32)

    def placed(row):
        at = row - oy
        v = r.skip[d * 48 + jnp.clip(at, 0, 47)]
        v = jnp.where((at >= 0) & (at < 48), v, 0.0)
        v = jnp.concatenate([v, pad], axis=0)
        v = jnp.where(odd, pltpu.roll(v, 64, 1), v)
        v = pltpu.roll(v, qx, 0)
        return jnp.where((lane < 64) & odd, pltpu.roll(v, 1, 0), v)

    def part(t, c):
        pv = r.pg[t] * 0.125
        pv = jnp.concatenate([pv, pv], axis=1)
        a = jnp.concatenate([placed(2 * t) + pv, placed(2 * t + 1) + pv], axis=1)
        rows = pl.ds(pl.multiple_of(d * 1024 + t * 32, 32), 32)
        normed, bg = back_parts(par, 1, avg, inv, r.r2[rows, :], a)
        bg = sc[1 + d] * bg
        r.bg2[rows, :] = bg
        bg = bg.reshape(4, 8, 256)
        return c[0] + jnp.sum(bg, axis=0), c[1] + jnp.sum(bg * normed.reshape(4, 8, 256), axis=0)

    return lax.fori_loop(0, 32, part, (jnp.zeros((8, 256), f32), jnp.zeros((8, 256), f32)))


def store_slots(slots, x, row0):
    per = slots.shape[1]
    for at in range(0, x.shape[0], per):
        slots[(row0 + at) // per] = x[at : at + per]


def four_rows(st):
    v = st[...]
    return [v[:, 128 * c : 128 * c + 128] for c in range(4)]


def tail_kernel(dims, r):
    net = Net(dims, False, [r.sem0, r.sem1, r.sem2, r.sem3, r.sem4, r.sem5])
    world = Net(dims, True, [r.sem6, r.sem7, r.sem8, r.sem9, r.sem16, r.sem17, r.sem18, r.sem19])
    world.enter()
    mv = Moves(r.sem10)
    ready_0 = fetch(mv, (r.iskip, r.skip), (r.ipg, r.pg), (r.ir2, r.r2), (r.iw2, r.w2))
    ready_b = fetch(
        mv, (r.iubh, r.ubh), (r.iubl, r.ubl),
        (r.iebh.at[0:1152], r.bh.at[0:1152]), (r.iebl.at[0:1152], r.bl.at[0:1152]),
    )
    ready_a = fetch(mv, (r.iah, r.ah), (r.ial, r.al))
    ready_s = fetch(mv, (r.ish, r.sh), (r.isl, r.sl), (r.ir1.at[1:3], r.r1))
    sc, par, f = r.sc, r.par, r.f
    count = sc[8] * 4096.0
    avg, inv = moments(r.g2, net.s, count, 256)
    f[...] = jnp.zeros(f.shape, f32)
    ready_0()
    toeplitz(r.w2, 0, 32, None, None, r.d2h, r.d2l)
    s0, q0 = skip_stage(r, avg, inv, 0)
    world.ready()
    rows_a, rows_b = bucket_parts(dims)
    steps_a = [r.sem11, r.sem12, r.sem13, r.sem14, r.sem15, r.sem20]
    steps_b = [r.sem21, r.sem22, r.sem23, r.sem24, r.sem25, r.sem26]
    big_a = Reduction(dims, net, 0, rows_a, r, "a", steps_a)
    big_b = Reduction(dims, net, rows_a, rows_b, r, "b", steps_b)
    big_a.pair(mv)
    big_b.pair(mv)
    s1, q1 = skip_stage(r, avg, inv, 1)
    put_sums(r.st7, jnp.sum(s0 + s1, axis=0, keepdims=True), jnp.sum(q0 + q1, axis=0, keepdims=True))
    net.share(r.st7, r.g7, 0)
    big_a.square()
    r.cg[...] = jnp.zeros(r.cg.shape, f32)

    def coarse(p, plane):
        at = pl.ds(pl.multiple_of(plane * 576, 16), 576)
        r.cg[...] += sc[5] * dot3(r.bh[at, :], r.bl[at, :], r.ubh[p], r.ubl[p], NT)

    ready_b()
    loop(2, lambda p: coarse(p, p))
    big_b.square()
    net.shared(r.st7, r.g7, 0)

    tg, tc = totals(r.g7, None, 256)
    k = par[2:3, :] * inv

    def put(p):
        m = sc[1 + p]

        def rows(t):
            at = pl.ds(pl.multiple_of(p * 1024 + t * 64, 64), 64)
            normed = (r.r2[at, :] - avg) * inv
            e = k * (r.bg2[at, :] - m * ((tg + normed * tc) / count))
            hi, lo = split(e)
            r.e2h[at, :] = hi
            r.e2l[at, :] = lo
            f[pl.ds(1 + 2 * t, 2), 8:40, :] = e.reshape(2, 32, 256)

        loop(16, rows)
        im2col(r.bh, r.bl, 0, f, 34, 40, 256, x0=7)
        r.v[p] = dot3(r.bh[...], r.bl[...], r.d2h[...].reshape(384, 1024), r.d2l[...].reshape(384, 1024), NT)

    sides = ((r.side.at[0], r.fr), (r.side.at[1], r.fl), 0)

    def lay(p):
        @pl.when(p == 0)
        def _():
            r.side[0, :1360] = r.v[0, :, 256:]

        @pl.when(p == 1)
        def _():
            r.side[1, :1360] = r.v[1, :, :128]

    for d in range(2):
        r.side[d, 1360:] = jnp.zeros((48, 128), f32)
    put(net.k % 2)
    lay(net.k % 2)
    net.to_sides(*sides, True)
    big_a.line()
    put(1 - net.k % 2)
    lay(1 - net.k % 2)
    net.to_sides(*sides, False)
    ready_b = fetch(
        mv, (r.iebh.at[1152:2304], r.bh.at[0:1152]), (r.iebl.at[1152:2304], r.bl.at[0:1152])
    )
    r.a1[1, :1360] = r.v[0, :, :128] + r.v[1, :, 128:256]
    r.a1[0, :1360] = r.v[0, :, 128:256] + r.v[1, :, 256:]
    for d in range(2):
        r.a1[d, 1360:] = jnp.zeros((48, 128), f32)
    big_a.line_back()
    big_b.line()

    ready_a()

    def tap(i):
        at = pl.ds(pl.multiple_of(i * 1024, 1024), 2048)
        r.g[...] = dot3(r.ah[at, :], r.al[at, :], r.e2h[...], r.e2l[...], TN)
        put_taps(r.dw2, r.g, i, 32, 32, 0, 0)

    loop(3, tap)
    store_slots(r.small, r.dw2[...], 0)
    rows = jnp.concatenate(
        four_rows(r.st7) + four_rows(r.st6) + four_rows(r.st5) + [jnp.zeros((20, 128), f32)], axis=0
    )
    store_slots(r.small, rows, 480)
    world.scatter(r.small, r.slots, 0)
    big_a.square_back()
    big_b.line_back()
    net.sides()

    ready_s()
    count1 = sc[8] * 4356.0
    avg1, inv1 = moments(r.g1, net.s, count1, 128)
    s = jnp.zeros((1, 128), f32)
    q = jnp.zeros((1, 128), f32)
    for d in range(2):
        other = r.fl if d == 0 else r.fr
        here = sc[10 + d]

        def part(t, c):
            rows = pl.ds(pl.multiple_of(t * 160, 160), 160)
            a = r.a1[d, rows, :] + jnp.where(here > 0, other[rows, :], 0.0)
            r.a1[d, rows, :] = a
            normed, bg = back_parts(par, 0, avg1, inv1, r.r1[d, rows, :], a)
            bg = bg.reshape(4, 40, 128)
            bg = jnp.where(cells(bg.shape, 33, 33, 4 * t), bg, 0.0)
            return c[0] + jnp.sum(bg, axis=0), c[1] + jnp.sum(bg * normed.reshape(4, 40, 128), axis=0)

        ps, pq = lax.fori_loop(0, 8, part, (jnp.zeros((40, 128), f32), jnp.zeros((40, 128), f32)))
        rows = slice(1280, OWN)
        a = r.a1[d, rows, :] + jnp.where(here > 0, other[rows, :], 0.0)
        r.a1[d, rows, :] = a
        normed, bg = back_parts(par, 0, avg1, inv1, r.r1[d, 1280:1320, :], a[:40])
        bg = jnp.where(lax.broadcasted_iota(jnp.int32, (40, 128), 0) < 33, bg, 0.0)
        ps = ps + bg
        pq = pq + bg * normed
        s = s + sc[1 + d] * jnp.sum(ps, axis=0, keepdims=True)
        q = q + sc[1 + d] * jnp.sum(pq, axis=0, keepdims=True)
    put_sums(r.st8, s, q)
    net.share(r.st8, r.g8, 1)
    ready_b()
    loop(2, lambda p: coarse(p + 2, p))
    big_b.square_back()
    world.scattered(r.small, r.slots, 0)
    r.mine[...] = jnp.sum(r.slots[...], axis=0)
    net.shared(r.st8, r.g8, 1)
    world.share(r.mine, r.red, 1)
    big_a.pair_back()

    tg1, tc1 = totals(r.g8, None, 128)
    wh, wl = r.w1h[...], r.w1l[...]
    r.dw1[...] = jnp.zeros(r.dw1.shape, f32)

    def put_first(p):
        m = sc[1 + p]
        r.eh[p, 1280:, :] = jnp.zeros((OWN - 1280, 128), bf16)
        r.el[p, 1280:, :] = jnp.zeros((OWN - 1280, 128), bf16)

        def rows(t):
            at = pl.ds(pl.multiple_of(t * 80, 80), 80)
            e = response_back(par, 0, avg1, inv1, tg1, tc1, count1, r.r1[p, at, :], r.a1[p, at, :])
            e = e.reshape(2, 40, 128)
            e = jnp.where(cells(e.shape, 33, 33, 2 * t) & (m > 0), e, 0.0)
            hi, lo = split(e.reshape(80, 128))
            r.eh[p, at, :] = hi
            r.el[p, at, :] = lo

        loop(17, rows)
        rows = pl.ds(pl.multiple_of((p + 1) * 64, 64), 192)
        r.dw1[...] += dot3(r.sh[rows, :], r.sl[rows, :], r.eh[p], r.el[p], NN)

    loop(2, put_first)
    acc = r.dw1[...]
    lane = lax.broadcasted_iota(jnp.int32, (32, 128), 1)
    tot = jnp.zeros((32, 128), f32)
    for tap in range(4):
        v = jnp.zeros((32, 128), f32)
        for q in range(4):
            x = acc if q == tap else pltpu.roll(acc, ((tap - q) % 4) * 32, 1)
            hi, lo = split(x)
            sel = r.pick[tap * 4 + q]
            v += dot(sel, hi, NN) + dot(sel, lo, NN)
        tot += jnp.where(lane // 32 == tap, v, 0.0)
    last = r.small2.shape[0] * r.small2.shape[1]
    rows = jnp.concatenate([tot] + four_rows(r.st8) + [jnp.zeros((last - 36, 128), f32)], axis=0)
    store_slots(r.small2, rows, 0)
    world.scatter(r.small2, r.slots2, 2)

    def image_part(p):
        v = dot3(wh, wl, r.eh[p], r.el[p], NT)
        for i in range(3):
            tot = jnp.zeros((16, OWN), f32)
            for ab in range(4):
                at = i * 64 + ab * 16
                a, b = ab // 2, ab % 2
                x = v[at : at + 16, :]
                tot += x if ab == 0 else pltpu.roll(x, 40 * a + b, 1)
            r.parts[p, i] = tot

    loop(2, image_part)
    net.halos = []
    net.to_left(r.parts.at[0, 0], r.pr, 1)
    net.to_right(r.parts.at[1, 2], r.pl, 1)
    big_b.pair_back()
    world.scattered(r.small2, r.slots2, 2)
    r.mine2s[...] = jnp.sum(r.slots2[...], axis=0)
    world.share(r.mine2s, r.red2, 3)
    net.sides()
    for d in range(2):
        other = r.pl if d == 0 else r.pr
        tot = r.parts[0, 1 + d] + r.parts[1, d] + jnp.where(sc[10 + d] > 0, other[...], 0.0)
        tot = tot * (r.keep[...] * sc[1 + d])
        rows = []
        for y in range(34):
            tile, off = (40 * y) // 128, (40 * y) % 128
            pair = []
            for px in range(2):
                v = tot[8 * px : 8 * px + 8, 128 * tile : 128 * tile + 128]
                if off + 34 > 128:
                    nxt = tot[8 * px : 8 * px + 8, 128 * tile + 128 : 128 * tile + 256]
                    v = jnp.where(lane[:8] >= off, v, nxt)
                pair.append(v if off == 0 else pltpu.roll(v, 128 - off, 1))
            rows.append(jnp.concatenate(pair, axis=1))
        hi, lo = split(jnp.concatenate(rows, axis=0))
        out = dot(hi, r.even[...], NT) + dot(lo, r.even[...], NT)
        r.ig[d] = out.reshape(34, 8, 68)
    world.shared(r.mine, r.red, 1)
    world.shared(r.mine2s, r.red2, 3)
    big_a.wait()
    big_b.wait()
    mv.finish()


def tail(dims, tb, pg, k, fo, w2, si):
    keep, par, sc = k.keep, k.par, k.sc
    n = dims[0] * dims[1] * dims[2]
    m = dims[1] * dims[2]
    V = pltpu.VMEM
    per = 512 // n
    per2 = max(64, n) // n
    rows_a, rows_b = bucket_parts(dims)
    steps = reduction_sems(dims)
    return launch(
        functools.partial(tail_kernel, dims), "tail", 5,
        [("iskip", tb.oskip, HB), ("bucket", tb.obucket, HB), ("ipg", pg, HB), ("ir2", k.or2, HB), ("g2", k.g2, VM),
         ("g1", k.g1, VM), ("iw2", w2, HB), ("keep", keep, VM), ("w1h", k.ow1h, VM), ("w1l", k.ow1l, VM),
         ("pick", tap_picks(), VM), ("even", deinterleave(), VM), ("st5", fo.st5, VM), ("st6", fo.st6, VM),
         ("par", par, VM), ("iah", k.oah, HB), ("ial", k.oal, HB), ("ish", k.osh, HB), ("isl", k.osl, HB),
         ("ir1", k.or1, HB), ("iubh", k.oubh, HB), ("iubl", k.oubl, HB), ("iebh", tb.obh, HB),
         ("iebl", tb.obl, HB), ("sc", sc, SM), ("si", si, SM)],
        [("cg", (576, 128), f32, VM), ("ig", (2, 34, 8, 68), f32, VM), ("red", (n, per, 128), f32, VM), ("red2", (n, per2, 128), f32, VM),
         ("res", (rows_a + rows_b, 128), f32, VM)],
        both("d2", (3, 128, 1024)) + both("ub", (4, 128, 1024)) + both("a", (4096, 512)) + both("b", (1360, 1024)) + both("e2", (2048, 256))
        + both("s", (384, OWN)) + both("e", (2, OWN, 128))
        + [("f", V((36, 56, 256), f32)), ("bg2", V((2048, 256), f32)), ("r1", V((2, 1440, 128), f32)),
           ("a1", V((2, OWN, 128), f32)), ("side", V((2, OWN, 128), f32)), ("fl", V((OWN, 128), f32)),
           ("fr", V((OWN, 128), f32)), ("v", V((2, 1360, 384), f32)), ("parts", V((2, 3, 16, OWN), f32)),
           ("pl", V((16, OWN), f32)), ("pr", V((16, OWN), f32)), ("dw1", V((192, 128), f32)),
           ("skip", V((96, 24, 128), f32)), ("pg", V((32, 32, 64), f32)), ("r2", V((2048, 256), f32)),
           ("w2", V((27, 32, 64), f32)), ("g", V((512, 256), f32)), ("dw2", V((480, 128), f32)), ("small", V((n, per, 128), f32)),
           ("slots", V((n, per, 128), f32)), ("mine", V((per, 128), f32)), ("small2", V((n, per2, 128), f32)),
           ("slots2", V((n, per2, 128), f32)), ("mine2s", V((per2, 128), f32)), ("g7", V((m, 1, 512), f32)),
           ("g8", V((m, 1, 512), f32)), ("st7", V((1, 512), f32)), ("st8", V((1, 512), f32))]
        + reduction_buffers(dims, rows_a, "a")
        + reduction_buffers(dims, rows_b, "b")
        + sems(m, m, m, m, 4, 4, n, n, n, n, 24, *steps[:5], n, n, n, n, 2, *steps),
    )


def finish_kernel(r):
    def tap(i):
        for p in range(9):
            at = 64 * (p % 2)

            def get(base, chans, at=at, p=p):
                rows = pl.ds(pl.multiple_of(base + (i * 5 + p // 2) * chans, 8), chans)
                v = r.res[rows, :]
                return (v if at == 0 else pltpu.roll(v, 64, 1))[:, :64]

            r.dw3t[i * 9 + p] = get(0, 192).T
            r.dw4[i * 9 + p] = get(2880, 64)
            rows = pl.ds(pl.multiple_of((i * 5 + p // 2) * 32, 32), 32)
            v = r.red[rows, :]
            r.dw2[i * 9 + p] = (v if at == 0 else pltpu.roll(v, 64, 1))[:, :64]

    loop(3, tap)
    r.dup[...] = r.res[3840:4864, :].reshape(8, 128, 128)
    for t in range(27):
        v = r.red2[4 * (t // 4) : 4 * (t // 4) + 4, :]
        v = v if t % 4 == 0 else pltpu.roll(v, 128 - 32 * (t % 4), 1)
        r.dw1[t] = v[:, :32]
    sums = [r.red2[32:36, :]] + [r.red[480 + 4 * j : 484 + 4 * j, :] for j in range(3)]
    for j, v in enumerate(sums):
        for c, out in ((0, (r.s1, r.s2, r.s3, r.s4)[j]), (2, (r.x1, r.x2, r.x3, r.x4)[j])):
            x = jnp.concatenate([v[c : c + 1], v[c + 1 : c + 2]], axis=1)
            if j == 0:
                x = fold(x[:, :128])
            else:
                x = fold(x)
            out[...] = x[:, : out.shape[1]]
    r.pooled[...] = r.ipooled[...]
    r.cg[...] = r.icg[...]
    r.ig[...] = r.iig[...]


def finish(res, red, red2, pooled, cg, ig):
    vectors = [(f"{a}{j}", (1, 32 if j == 1 else 64), f32, VM) for j in range(1, 5) for a in "sx"]
    return launch(
        finish_kernel, "finish", None,
        [("res", res, VM), ("red", red, VM), ("red2", red2, VM), ("ipooled", pooled, VM),
         ("icg", cg, VM), ("iig", ig, VM)],
        [("dw3t", (27, 64, 192), f32, VM), ("dw4", (27, 64, 64), f32, VM), ("dw2", (27, 32, 64), f32, VM),
         ("dup", (8, 128, 128), f32, VM), ("dw1", (27, 4, 32), f32, VM),
         ("pooled", pooled.shape, f32, VM), ("cg", cg.shape, f32, VM), ("ig", ig.shape, f32, VM)] + vectors,
        [],
    )


def body(
    dims,
    image, modality_mask, extents, crop_offsets, coarse,
    conv_first, gain_first, shift_first, conv_second, gain_second, shift_second,
    up_kernel, conv_third, gain_third, shift_third, conv_fourth, gain_fourth, shift_fourth,
    pool_grad, output_grad,
):
    si = crop_offsets[0]
    img = image[0, 0].transpose(0, 1, 3, 2).reshape(2, 34, 8, 68)
    co = coarse[0, 0]
    w2 = conv_second.reshape(27, 32, 64)
    up = up_kernel.reshape(8, 128, 128)
    k = front(
        dims, img, extents, modality_mask[0], si,
        (gain_first, shift_first, gain_second, shift_second, gain_third, shift_third, gain_fourth, shift_fourth),
        conv_first.reshape(27, 4, 32), w2, conv_third.reshape(27, 192, 64).transpose(0, 2, 1), up, co,
        output_grad[0, 0].transpose(1, 2, 0, 3),
    )
    t = decode(dims, k, co, conv_fourth.reshape(27, 64, 64))
    tb = third_back(dims, t, t.or3, t.or3l, t.or3r, t.g3, k, t, t.dw4, k.ow3u, k.ow3c, up, k.par, k.sc)
    e = tail(dims, tb, pool_grad[0, 0, 0], k, t, w2, si)
    g = finish(e.res, e.red.reshape(512, 128), e.red2.reshape(-1, 128), t.pooled, e.cg, e.ig)
    return (
        g.pooled.reshape(1, 1, 1, 32, 32, 64),
        t.odecoded.transpose(2, 0, 1, 3)[None, None],
        g.ig.reshape(2, 68, 4, 68).transpose(0, 1, 3, 2)[None, None],
        g.cg.reshape(1, 1, 1, 24, 24, 128),
        g.dw1.reshape(3, 3, 3, 4, 32),
        g.x1[0],
        g.s1[0],
        g.dw2.reshape(3, 3, 3, 32, 64),
        g.x2[0],
        g.s2[0],
        g.dup.reshape(2, 2, 2, 128, 128),
        g.dw3t.transpose(0, 2, 1).reshape(3, 3, 3, 192, 64),
        g.x3[0],
        g.s3[0],
        g.dw4.reshape(3, 3, 3, 64, 64),
        g.x4[0],
        g.s4[0],
    )


def solution(mesh):
    dims = tuple(mesh.shape[a] for a in ("section", "slab", "batch"))
    field = P("section", "batch", "slab", None, None, None)
    volume = P("section", "batch", None)
    rep = P()
    return jax.shard_map(
        functools.partial(body, dims),
        mesh=mesh,
        in_specs=(field, volume, rep, volume, field) + (rep,) * 13 + (field, field),
        out_specs=(field,) * 4 + (rep,) * 13,
        check_vma=False,
    )
```
